128 devices in a mesh: ctx: 64 (over z, y_hi, x, core), wsh: 2 (over y_lo).
Axes of the slice: x: 4, y: 4 (y_hi: 2, y_lo: 2; y = y_hi * 2 + y_lo), z: 4, core: 2. Of those that a mesh axis runs over, the one named last changes fastest.
Arguments:
- tokens: bfloat16 [8192, 2048], P('ctx'), may hold values from -6 to 6
- cotangent: bfloat16 [8192, 2048], P('ctx'), may hold values from -6 to 6
- seq_lengths: int32 [4], replicated, may hold values from 1 to 4096, 8192 in all
- block_order: int32 [128], replicated, may hold values from 0 to 127, as said below
- routes: int32 [8192, 8], P('ctx'), may hold values from 0 to 127, all different within a row; in each aligned block of 128 rows (0 to 127, 128 to 255, ...) at most 12 rows name the same one
- w_query: float32 [2048, 4096], P('ctx', 'wsh'), may hold values from -0.125 to 0.125
- key_weight: float32 [2048, 512], P('ctx', 'wsh'), may hold values from -0.125 to 0.125
- value_weight: float32 [2048, 512], P('ctx', 'wsh'), may hold values from -0.125 to 0.125
- w_out: float32 [4096, 2048], P('wsh', 'ctx'), may hold values from -0.75 to 0.75
- gain_attn: float32 [2048], P('ctx'), may hold values from 0.5 to 1.5
- gain_query: float32 [128], replicated, may hold values from 0.5 to 1.5
- gain_key: float32 [128], replicated, may hold values from 0.5 to 1.5
- gain_ffn: float32 [2048], P('ctx'), may hold values from 0.5 to 1.5
- w_router: float32 [2048, 128], P('ctx'), may hold values from -0.0625 to 0.0625
- w_gate: float32 [128, 2048, 768], P('ctx', None, 'wsh'), may hold values from -0.125 to 0.125
- w_up: float32 [128, 2048, 768], P('ctx', None, 'wsh'), may hold values from -0.125 to 0.125
- w_down: float32 [128, 768, 2048], P('ctx', 'wsh'), may hold values from -0.875 to 0.875
Outputs:
- out_stream: float32 [8192, 2048], P('ctx')
- grad_tokens: float32 [8192, 2048], P('ctx')
- grad_query: float32 [2048, 4096], P('ctx', 'wsh')
- grad_key: float32 [2048, 512], P('ctx', 'wsh')
- grad_value: float32 [2048, 512], P('ctx', 'wsh')
- grad_out: float32 [4096, 2048], P('wsh', 'ctx')
- grad_gain_attn: float32 [2048], P('ctx')
- grad_gain_query: float32 [128], replicated
- grad_gain_key: float32 [128], replicated
- grad_gain_ffn: float32 [2048], P('ctx')
- grad_router: float32 [2048, 128], P('ctx')
- grad_gate: float32 [128, 2048, 768], P('ctx', None, 'wsh')
- grad_up: float32 [128, 2048, 768], P('ctx', None, 'wsh')
- grad_down: float32 [128, 768, 2048], P('ctx', 'wsh')
The draws below stay inside these ranges and needn't reach their ends.
Inputs may be any that keep to these rules, and one draw needn't show every extreme that they name: `seq_lengths`: the lengths of the 4 sequences sum to 8192; the longest is exactly 4096. `block_order`: A permutation of the 128 natural blocks. The blocks of one device, entries c * 2 to c * 2 + 1, lie one in each aligned run of 64 consecutive natural blocks. `routes`: each row names 8 different experts; within the rows of one device no expert is named more than 12 times.
All inputs are finite; a program needn't handle non-finite values.
Results may differ from the reference program's by a relative error of at most 0.03.
Values may be sent and summed in bfloat16 or wider, within the bound.
A program may use at most 384 MiB of HBM per device.

```python
import math
import jax
import jax.numpy as jnp
import numpy as np
from jax import lax

HIDDEN_WIDTH = 2048
QUERY_HEADS = 32
KEY_VALUE_HEADS = 4
HEAD_WIDTH = 128
FF = 768
TOPK = 8
BLK = 64
MAX_SEQ_TOKENS = 4096
EXPERTS = 128
ROWS_DEV = 128
TOKENS = 8192
NSEQ = 4
NBLK = 128
BPD = 2
CAP = 12
N_CTX = 64


def draw_block_order(key, part):
    key = jax.random.fold_in(key, 7)
    per_device = BPD
    devices = NBLK // BPD
    turning = jax.random.randint(jax.random.fold_in(key, 1), (), 0, devices)
    priority = jax.random.randint(jax.random.fold_in(key, 2), (devices, per_device), 0, 1 << 20)
    priority = priority * per_device + jnp.arange(per_device, dtype=jnp.int32)[None, :]
    runs_held = jnp.argsort(priority, axis=1, stable=True).astype(jnp.int32)
    device_ids = jnp.arange(devices, dtype=jnp.int32)[:, None]
    return (runs_held * devices + (device_ids + turning) % devices).reshape(-1).astype(jnp.int32)


def steps_of(stream_key, dims, split, least, largest):
    level, own = 1.0, jax.random.fold_in(stream_key, 6)
    for axis_at, shards_of in split:
        draws = jnp.exp(jax.random.uniform(jax.random.fold_in(own, axis_at), (shards_of,), jnp.float32, least / len(split), largest / len(split)))
        level = level * jnp.repeat(draws, dims[axis_at] // shards_of).reshape([-1 if axis == axis_at else 1 for axis in range(len(dims))])
    return level


def profile(amount, total, bound, skew):
    weights = [(1 << 20) // math.isqrt(standing ** skew) + 1 for standing in range(2, amount + 1)]
    spare, counts = total - bound - (amount - 1), [1] * (amount - 1)
    while spare > 0:
        free = [i for i in range(amount - 1) if counts[i] < bound]
        pool, left = sum([weights[i] for i in free]), spare
        for i in free:
            more = min(bound - counts[i], max(1, left * weights[i] // pool), spare)
            counts[i] = counts[i] + more
            spare = spare - more
    return np.array([bound] + counts)


def uneven(key, number_of, total, most, slope):
    if number_of == 2:
        one = jax.random.randint(key, (), max(1, total - most), min(most, total - 1) + 1)
        return jnp.stack([one, total - one])
    sizes = jnp.asarray(profile(number_of, total, most, slope), jnp.int32)
    couples = (number_of - 1) // 2
    donor, sink = sizes[1:1 + 2 * couples:2], sizes[2:2 + 2 * couples:2]
    room = jnp.minimum(donor - 1, most - sink)
    shifted = jax.random.randint(jax.random.fold_in(key, 1), (couples,), 0, 1 << 20) % (room + 1)
    sizes = sizes.at[1:1 + 2 * couples:2].set(donor - shifted).at[2:2 + 2 * couples:2].set(sink + shifted)
    return sizes[jax.random.permutation(jax.random.fold_in(key, 2), number_of)]


def assign_block(rng, own, number, rows, count, top, limit, skew):
    order = jax.random.permutation(rng, count)
    crowded, ordinary = load_shares(count, rows * top, limit, skew, True), load_shares(count, rows * top, limit, skew, False)
    places = jnp.arange(count)

    def named(sizes, turn):
        used = int((sizes > 0).sum())
        fixed = max(1, used // 4)
        passed = fixed + (places - fixed + turn * (used - fixed)) % max(1, count - fixed)
        return jnp.zeros((count,), jnp.int32).at[order[jnp.where(places < fixed, places, passed)]].set(jnp.asarray(sizes, jnp.int32))

    sizes = jnp.where(number % 4 == 0, named(crowded, number // 4), named(ordinary, number - number // 4 - 1))
    mixed = jax.random.permutation(jax.random.fold_in(own, 3), count)
    giver, sink = mixed[0:count // 2 * 2:2], mixed[1:count // 2 * 2:2]
    room = jnp.minimum(sizes[giver] - 1, limit - sizes[sink]) // 2
    room = jnp.where((giver == order[0]) | (sink == order[0]) | (sizes[sink] == 0), 0, jnp.maximum(room, 0))
    passed = jax.random.randint(jax.random.fold_in(own, 4), (count // 2,), 0, 1 << 20) % (room + 1)
    sizes = sizes.at[giver].add(-passed).at[sink].add(passed)
    items = jnp.searchsorted(jnp.cumsum(sizes), jnp.arange(rows * top), side="right").astype(jnp.int32)
    grid = items.reshape(top, rows).T
    grid = grid[jax.random.permutation(jax.random.fold_in(own, 1), rows)]
    turn = jax.random.randint(jax.random.fold_in(own, 2), (rows, 1), 0, top)
    return jnp.take_along_axis(grid, (jnp.arange(top)[None, :] + turn) % top, axis=1)


def load_shares(number_of, total, bound, slope, full):
    loads = [(1 << 20) // math.isqrt(rank ** slope) + 1 for rank in range(1, number_of + 1)]
    largest = bound if full else min(bound, max(-(-total // number_of), total * loads[0] // sum(loads)))
    least = 1 if total - largest >= number_of - 1 else 0
    counts, rest = [largest] + [least] * (number_of - 1), total - largest - least * (number_of - 1)
    while rest > 0:
        movable = [i for i in range(1, number_of) if counts[i] < largest] or [i for i in range(1, number_of) if counts[i] < bound]
        mass, left = sum([loads[i] for i in movable]), rest
        for i in movable:
            addition = min(bound - counts[i], max(1, left * loads[i] // mass), rest)
            counts[i] = counts[i] + addition
            rest = rest - addition
    return np.array(counts)


def noise(rng, extent, width, limit, shards=(), held_as=jnp.bfloat16):
    entries = jax.random.normal(rng, extent, jnp.float32) * width
    if len(shards) > 0:
        entries = steps_of(rng, extent, shards, -0.22, 0.18) * entries
    return jnp.clip(entries, min=-limit, max=limit).astype(held_as)


def setup_inputs(seed: int = 0) -> dict:
    keys = jax.random.split(jax.random.key(seed), 18)
    tokens = noise(keys[0], (TOKENS, HIDDEN_WIDTH), 1.0, 6.0, ((0, 64),))
    cotangent = noise(keys[1], (TOKENS, HIDDEN_WIDTH), 1.0, 6.0, ((0, 64),))
    seq_lengths = uneven(keys[2], NSEQ, TOKENS, MAX_SEQ_TOKENS, 1).astype(jnp.int32)
    block_order = draw_block_order(jax.random.fold_in(keys[17], 71), 0)
    routes_keys = jax.random.split(jax.random.fold_in(keys[4], 1), TOKENS // ROWS_DEV)
    routes_turns = jax.random.permutation(jax.random.fold_in(keys[4], 3), TOKENS // ROWS_DEV)
    routes = jax.vmap(lambda own, number: assign_block(jax.random.fold_in(keys[4], 2), own, number, ROWS_DEV, EXPERTS, TOPK, CAP, 1))(routes_keys, routes_turns).reshape((TOKENS, TOPK))
    w_query = noise(keys[5], (HIDDEN_WIDTH, QUERY_HEADS * HEAD_WIDTH), HIDDEN_WIDTH ** -0.5, 0.125, ((0, 64), (1, 2)), jnp.float32)
    key_weight = noise(keys[6], (HIDDEN_WIDTH, KEY_VALUE_HEADS * HEAD_WIDTH), HIDDEN_WIDTH ** -0.5, 0.125, ((0, 64), (1, 2)), jnp.float32)
    value_weight = noise(keys[7], (HIDDEN_WIDTH, KEY_VALUE_HEADS * HEAD_WIDTH), HIDDEN_WIDTH ** -0.5, 0.125, ((0, 64), (1, 2)), jnp.float32)
    w_out = noise(keys[8], (QUERY_HEADS * HEAD_WIDTH, HIDDEN_WIDTH), (QUERY_HEADS * HEAD_WIDTH // 64) ** -0.5, 0.75, ((0, 2), (1, 64)), jnp.float32)
    gain_attn = jnp.clip(1.0 + 0.1 * jax.random.normal(keys[9], (HIDDEN_WIDTH,), jnp.float32), 0.5, 1.5)
    gain_query = jnp.clip(1.0 + 0.1 * jax.random.normal(keys[10], (HEAD_WIDTH,), jnp.float32), 0.5, 1.5)
    gain_key = jnp.clip(1.0 + 0.1 * jax.random.normal(keys[11], (HEAD_WIDTH,), jnp.float32), 0.5, 1.5)
    gain_ffn = jnp.clip(1.0 + 0.1 * jax.random.normal(keys[12], (HIDDEN_WIDTH,), jnp.float32), 0.5, 1.5)
    w_router = noise(keys[13], (HIDDEN_WIDTH, EXPERTS), (4 * HIDDEN_WIDTH) ** -0.5, 0.0625, ((0, 64),), jnp.float32)
    w_gate = noise(keys[14], (EXPERTS, HIDDEN_WIDTH, FF), HIDDEN_WIDTH ** -0.5, 0.125, ((0, 64), (2, 2)), jnp.float32)
    w_up = noise(keys[15], (EXPERTS, HIDDEN_WIDTH, FF), HIDDEN_WIDTH ** -0.5, 0.125, ((0, 64), (2, 2)), jnp.float32)
    w_down = noise(keys[16], (EXPERTS, FF, HIDDEN_WIDTH), (FF // 16) ** -0.5, 0.875, ((0, 64), (1, 2)), jnp.float32)
    return {"tokens": tokens, "cotangent": cotangent, "seq_lengths": seq_lengths, "block_order": block_order, "routes": routes, "w_query": w_query, "key_weight": key_weight, "value_weight": value_weight, "w_out": w_out, "gain_attn": gain_attn, "gain_query": gain_query, "gain_key": gain_key, "gain_ffn": gain_ffn, "w_router": w_router, "w_gate": w_gate, "w_up": w_up, "w_down": w_down}


EPSILON = 1e-06
ROPE_BASE = 1000000.0
MASKED = -1e+30
PRECISE = lax.Precision.HIGHEST

@jax.custom_vjp
def reduced_precision(v):
    return lax.optimization_barrier(v.astype(jnp.bfloat16)).astype(jnp.float32)

@jax.custom_vjp
def reduced_backward(v):
    return v

def low_keep(v):
    return (reduced_precision(v), None)

def low_pass(kept, grad):
    return (grad,)

def back_keep(v):
    return (v, None)

def back_low(kept, grad):
    return (reduced_precision(grad),)
reduced_precision.defvjp(low_keep, low_pass)
reduced_backward.defvjp(back_keep, back_low)

def matrix_result(left, right):
    return jnp.dot(left, right, precision=PRECISE, preferred_element_type=jnp.float32)

def norm_rows(value_rows, gain_vec):
    inverse_rms = lax.rsqrt(lax.optimization_barrier(jnp.mean(value_rows * value_rows, axis=-1, keepdims=True)) + EPSILON)
    return value_rows * inverse_rms * gain_vec

def rope_tables(positions):
    half_dim = HEAD_WIDTH // 2
    frequency = jnp.power(ROPE_BASE, -2.0 * jnp.arange(half_dim, dtype=jnp.float32) / HEAD_WIDTH)
    angles = positions.astype(jnp.float32)[:, None] * frequency[None, :]
    angles = jnp.concatenate([angles, angles], axis=-1)
    return (jnp.cos(angles)[:, None, :], jnp.sin(angles)[:, None, :])

def rotate(value_rows, cosine, sine_tab):
    half_dim = value_rows.shape[-1] // 2
    turned = jnp.concatenate([-value_rows[..., half_dim:], value_rows[..., :half_dim]], axis=-1)
    return value_rows * cosine + turned * sine_tab

def seq_starts(positions, seq_lengths):
    offsets = (jnp.cumsum(seq_lengths) - seq_lengths).astype(jnp.int32)
    inside = offsets[None, :] <= positions[:, None]
    return lax.optimization_barrier(jnp.max(jnp.where(inside, offsets[None, :], 0), axis=1)).astype(jnp.int32)

def attend(query_matrix, key_rows, value_rows, starts):
    every_row = query_matrix.shape[0]
    query_per_key_head = QUERY_HEADS // KEY_VALUE_HEADS
    query_row_count = math.gcd(512, every_row)
    score_scale = 1.0 / math.sqrt(HEAD_WIDTH)
    padded_keys = jnp.concatenate([jnp.zeros((MAX_SEQ_TOKENS, KEY_VALUE_HEADS, HEAD_WIDTH), jnp.float32), key_rows], axis=0)
    padded_values = jnp.concatenate([jnp.zeros((MAX_SEQ_TOKENS, KEY_VALUE_HEADS, HEAD_WIDTH), jnp.float32), value_rows], axis=0)

    def block(block_index):
        leading_part = (block_index * query_row_count).astype(jnp.int32)
        query_block = lax.dynamic_slice_in_dim(query_matrix, leading_part, query_row_count, 0).reshape(query_row_count, KEY_VALUE_HEADS, query_per_key_head, HEAD_WIDTH)
        k_block = lax.dynamic_slice_in_dim(padded_keys, leading_part, MAX_SEQ_TOKENS + query_row_count, 0)
        v_block = lax.dynamic_slice_in_dim(padded_values, leading_part, MAX_SEQ_TOKENS + query_row_count, 0)
        q_pos = leading_part + jnp.arange(query_row_count, dtype=jnp.int32)
        k_pos = leading_part - MAX_SEQ_TOKENS + jnp.arange(MAX_SEQ_TOKENS + query_row_count, dtype=jnp.int32)
        q_start = lax.dynamic_slice_in_dim(starts, leading_part, query_row_count, 0)
        allowed = (k_pos[None, :] <= q_pos[:, None]) & (k_pos[None, :] >= q_start[:, None])
        scored = reduced_backward(jnp.einsum('qkgd,skd->kgqs', query_block, k_block, precision=PRECISE) * score_scale)
        masked = jnp.where(allowed[None, None], scored, MASKED)
        highest = lax.optimization_barrier(jnp.max(masked, axis=-1, keepdims=True))
        exps = jnp.exp(masked - highest)
        probs = reduced_precision(exps / lax.optimization_barrier(jnp.sum(exps, axis=-1, keepdims=True)))
        mixed = jnp.einsum('kgqs,skd->qkgd', probs, v_block, precision=PRECISE)
        return mixed.reshape(query_row_count, QUERY_HEADS * HEAD_WIDTH)
    blocks = lax.map(jax.checkpoint(block), jnp.arange(every_row // query_row_count, dtype=jnp.int32))
    return blocks.reshape(every_row, QUERY_HEADS * HEAD_WIDTH)

def expert_ranks(device_routes):
    flat_routes = device_routes.reshape(-1)
    expert_hits = (flat_routes[:, None] == jnp.arange(EXPERTS, dtype=jnp.int32)[None, :]).astype(jnp.int32)
    return lax.optimization_barrier(jnp.sum((jnp.cumsum(expert_hits, axis=0) - expert_hits) * expert_hits, axis=1)).astype(jnp.int32)

def expert(weights):
    gate_w, up_w, down_w, rows_in = weights
    gate_pre = reduced_backward(matrix_result(rows_in, reduced_precision(gate_w)))
    up_pre = reduced_backward(matrix_result(rows_in, reduced_precision(up_w)))
    activated = reduced_precision(gate_pre * jax.nn.sigmoid(gate_pre) * up_pre)
    return reduced_backward(matrix_result(activated, reduced_precision(down_w)))

def reference(tokens, cotangent, seq_lengths, block_order, routes, w_query, key_weight, value_weight, w_out, gain_attn, gain_query, gain_key, gain_ffn, w_router, w_gate, w_up, w_down):
    every_row = tokens.shape[0]
    row_ids = jnp.arange(every_row, dtype=jnp.int32)
    natural = (block_order[:, None] * BLK + jnp.arange(BLK, dtype=jnp.int32)[None, :]).reshape(every_row).astype(jnp.int32)
    inverse = jnp.zeros((every_row,), jnp.int32).at[natural].set(row_ids)
    starts_dealt = seq_starts(natural, seq_lengths)
    starts_natural = seq_starts(row_ids, seq_lengths)
    cosine, sine_tab = rope_tables(natural - starts_dealt)
    slot_rank = lax.map(expert_ranks, routes.reshape(N_CTX, ROWS_DEV, TOPK)).reshape(-1)
    flat_routes = routes.reshape(-1)
    pair_ids = jnp.arange(every_row * TOPK, dtype=jnp.int32)
    slot_index = (flat_routes * (N_CTX * CAP) + pair_ids // (ROWS_DEV * TOPK) * CAP + slot_rank).astype(jnp.int32)
    slot_rows = jnp.full((EXPERTS * N_CTX * CAP,), every_row, jnp.int32).at[slot_index].set(pair_ids // TOPK)

    def forward(stream, wq, key_matrix, value_matrix, wo, ga, gq, gk, gf, wr, wg, wu, wd):
        hidden_after_attn = reduced_precision(norm_rows(stream, reduced_precision(ga)))
        q_pre = reduced_backward(matrix_result(hidden_after_attn, reduced_precision(wq))).reshape(every_row, QUERY_HEADS, HEAD_WIDTH)
        key_before_norm = reduced_backward(matrix_result(hidden_after_attn, reduced_precision(key_matrix))).reshape(every_row, KEY_VALUE_HEADS, HEAD_WIDTH)
        value_rows = reduced_precision(reduced_backward(matrix_result(hidden_after_attn, reduced_precision(value_matrix)))).reshape(every_row, KEY_VALUE_HEADS, HEAD_WIDTH)
        query_matrix = reduced_precision(rotate(norm_rows(q_pre, reduced_precision(gq)), cosine, sine_tab))
        key_rows = reduced_precision(rotate(norm_rows(key_before_norm, reduced_precision(gk)), cosine, sine_tab))
        mixed = attend(query_matrix[inverse], key_rows[inverse], value_rows[inverse], starts_natural)[natural]
        heads = reduced_precision(reduced_backward(mixed))
        residual = stream + reduced_backward(matrix_result(heads, reduced_precision(wo)))
        hidden_two = reduced_precision(norm_rows(residual, reduced_precision(gf)))
        logits = reduced_backward(matrix_result(hidden_two, reduced_precision(wr)))
        chosen = jnp.take_along_axis(logits, routes, axis=1)
        highest = lax.optimization_barrier(jnp.max(chosen, axis=-1, keepdims=True))
        exps = jnp.exp(chosen - highest)
        gates = exps / lax.optimization_barrier(jnp.sum(exps, axis=-1, keepdims=True))
        padded = jnp.concatenate([hidden_two, jnp.zeros((1, HIDDEN_WIDTH), jnp.float32)], axis=0)
        buffers = padded[slot_rows].reshape(EXPERTS, N_CTX * CAP, HIDDEN_WIDTH)
        outputs = lax.map(jax.checkpoint(expert), (wg, wu, wd, buffers))
        per_pair = outputs.reshape(EXPERTS * N_CTX * CAP, HIDDEN_WIDTH)[slot_index].reshape(every_row, TOPK, HIDDEN_WIDTH)
        return residual + lax.optimization_barrier(jnp.sum(gates[:, :, None] * per_pair, axis=1))
    primals = (tokens.astype(jnp.float32), w_query, key_weight, value_weight, w_out, gain_attn, gain_query, gain_key, gain_ffn, w_router, w_gate, w_up, w_down)
    out_stream, pullback = jax.vjp(forward, *primals)
    grads = pullback(cotangent.astype(jnp.float32))
    return (out_stream, grads[0], grads[1], grads[2], grads[3], grads[4], grads[5], grads[6], grads[7], grads[8], grads[9], grads[10], grads[11], grads[12])
```

```python
import functools
import math

import jax
import jax.numpy as jnp
from jax import lax
from jax.experimental import pallas as pl
from jax.experimental.pallas import tpu as pltpu
from jax.sharding import PartitionSpec as P

HEAD_WIDTH = 128
TOPK = 8
BLK = 64
MAX_SEQ_TOKENS = 4096
CAP = 12
CHUNK = 512

EPSILON = 1e-06
ROPE_BASE = 1000000.0
MASKED = -1e30
MESH = pl.DeviceIdType.MESH
BF = jnp.bfloat16
F32 = jnp.float32


def to_low(value_rows):
    return value_rows.astype(jnp.bfloat16)


def rounded(value_rows):
    return lax.optimization_barrier(value_rows.astype(jnp.bfloat16)).astype(jnp.float32)


def matmul(left, right):
    return jnp.dot(left, right, preferred_element_type=jnp.float32)


def times_transposed(left, right):
    return lax.dot_general(
        left, right, (((1,), (1,)), ((), ())), preferred_element_type=jnp.float32
    )


def transposed_times(left, right):
    return lax.dot_general(
        left, right, (((0,), (0,)), ((), ())), preferred_element_type=jnp.float32
    )


def norm_back(value_rows, inverse_rms, gain_vec, gradient):
    weighted = gradient * gain_vec
    mean_term = jnp.mean(weighted * value_rows, axis=-1, keepdims=True)
    d_values = (
        inverse_rms * weighted - value_rows * (inverse_rms * inverse_rms * inverse_rms) * mean_term
    )
    return (d_values, gradient * value_rows * inverse_rms)


def inverse_root(value_rows):
    return lax.rsqrt(jnp.mean(value_rows * value_rows, axis=-1, keepdims=True) + EPSILON)


def rope_tables(positions):
    half_dim = HEAD_WIDTH // 2
    frequency = jnp.power(ROPE_BASE, -2.0 * jnp.arange(half_dim, dtype=jnp.float32) / HEAD_WIDTH)
    angles = positions.astype(jnp.float32)[:, None] * frequency[None, :]
    cosine, sine_tab = jnp.cos(angles), jnp.sin(angles)
    return (
        jnp.concatenate([cosine, cosine], axis=-1),
        jnp.concatenate([sine_tab, sine_tab], axis=-1),
    )


def rotate(value_rows, cosine, sine_tab):
    half_dim = value_rows.shape[-1] // 2
    turned = jnp.concatenate([-value_rows[..., half_dim:], value_rows[..., :half_dim]], axis=-1)
    return value_rows * cosine + turned * sine_tab


def rotate_back(gradient, cosine, sine_tab):
    half_dim = gradient.shape[-1] // 2
    shifted = gradient * sine_tab
    return gradient * cosine + jnp.concatenate(
        [shifted[..., half_dim:], -shifted[..., :half_dim]], axis=-1
    )


def seq_starts(positions, seq_lengths):
    offsets = jnp.cumsum(seq_lengths) - seq_lengths
    inside = offsets[None, :] <= positions[:, None]
    return jnp.max(jnp.where(inside, offsets[None, :], 0), axis=1)


def coords(c):
    return (
        lax.div(c, 16),
        lax.rem(lax.div(c, 8), 2),
        lax.rem(lax.div(c, 2), 4),
        lax.rem(c, 2),
    )


def index_of(z, y, x, k):
    return ((z * 2 + y) * 4 + x) * 2 + k


def shifted(me, dz, dy, dx, dk):
    z, y, x, k = coords(me)
    return index_of(lax.rem(z + dz, 4), lax.rem(y + dy, 2), lax.rem(x + dx, 4), lax.rem(k + dk, 2))


def remote(src, dst, send, recv, ctx, wsh):
    return pltpu.make_async_remote_copy(
        src_ref=src,
        dst_ref=dst,
        send_sem=send,
        recv_sem=recv,
        device_id=(ctx, wsh),
        device_id_type=MESH,
    )


def greet(targets):
    barrier = pltpu.get_barrier_semaphore()
    for ctx, wsh in targets:
        pl.semaphore_signal(barrier, inc=1, device_id=(ctx, wsh), device_id_type=MESH)
    return barrier, len(targets)


def greet_many(count, target, wsh):
    barrier = pltpu.get_barrier_semaphore()

    def one(step, carried):
        pl.semaphore_signal(barrier, inc=1, device_id=(target(step), wsh), device_id_type=MESH)
        return carried

    lax.fori_loop(1, count, one, 0)
    return barrier, count - 1


ANY = pl.BlockSpec(memory_space=pl.ANY)
VMEM = pl.BlockSpec(memory_space=pltpu.VMEM)
DMA = pltpu.SemaphoreType.DMA


def call_params(collective_id, limit=None):
    return pltpu.CompilerParams(
        collective_id=collective_id, has_side_effects=True, vmem_limit_bytes=limit
    )


def row_gather_start(src, out, me, wsh, send, recv):
    place = lax.rem(me, 8)
    copies = []
    for at, (dx, dk) in enumerate(((1, 0), (3, 0), (2, 0), (0, 1))):
        copy = remote(
            src, out.at[place], send.at[at], recv.at[at], shifted(me, 0, 0, dx, dk), wsh
        )
        copy.start()
        copies.append(copy)
    return copies


def row_gather_finish(out, me, wsh, copies, send, recv):
    partner = shifted(me, 0, 0, 0, 1)
    forwards = []
    for at, dx in enumerate((1, 3, 2)):
        copies[at].wait_recv()
        from_place = lax.rem(shifted(me, 0, 0, 4 - dx, 0), 8)
        forward = remote(
            out.at[from_place],
            out.at[from_place],
            send.at[4 + at],
            recv.at[4 + at],
            partner,
            wsh,
        )
        forward.start()
        forwards.append(forward)
    for copy in copies:
        copy.wait_send()
    copies[3].wait_recv()
    for forward in forwards:
        forward.wait()


def gather_first(weights, tokens, small, routes, cotangent):
    def body(w_in, t_in, s_in, r_in, c_in, w_out, t_out, s_out, r_out, c_out, wide, row_s, row_r, pair, local):
        me, wsh = lax.axis_index("ctx"), lax.axis_index("wsh")
        core = lax.rem(me, 2)
        place = lax.rem(me, 8)

        def target(step):
            return shifted(
                me, lax.div(step, 16), lax.rem(lax.div(step, 8), 2), lax.rem(lax.div(step, 2), 4), lax.rem(step, 2)
            )

        barrier, amount = greet_many(64, target, wsh)
        locals_ = [
            pltpu.make_async_copy(t_in, t_out.at[place], local.at[0]),
            pltpu.make_async_copy(w_in.at[place], w_out.at[me], local.at[1]),
            pltpu.make_async_copy(s_in, s_out.at[me], local.at[2]),
            pltpu.make_async_copy(r_in, r_out.at[core], local.at[3]),
            pltpu.make_async_copy(c_in, c_out.at[core], local.at[4]),
        ]
        for copy in locals_:
            copy.start()
        pl.semaphore_wait(barrier, amount)
        row_copies = row_gather_start(t_in, t_out, me, wsh, row_s, row_r)

        def send(step, carried):
            turned = lax.rem(step * 13, 64)
            ctx = target(turned)
            remote(s_in, s_out.at[me], wide.at[0], wide.at[1], ctx, wsh).start()
            remote(w_in.at[lax.rem(ctx, 8)], w_out.at[me], wide.at[2], wide.at[3], ctx, wsh).start()
            return carried

        lax.fori_loop(1, 64, send, 0)
        partner = shifted(me, 0, 0, 0, 1)
        pair_copies = [
            remote(r_in, r_out.at[core], pair.at[0], pair.at[1], partner, wsh),
            remote(c_in, c_out.at[core], pair.at[2], pair.at[3], partner, wsh),
        ]
        for copy in pair_copies:
            copy.start()
        row_gather_finish(t_out, me, wsh, row_copies, row_s, row_r)
        for copy in pair_copies:
            copy.wait()
        for copy in locals_:
            copy.wait()
        for at, out in ((0, s_out), (2, w_out)):
            rest = out.at[pl.ds(0, 63)]
            done = remote(rest, rest, wide.at[at], wide.at[at + 1], partner, wsh)
            done.wait_send()
            done.wait_recv()

    sds = jax.ShapeDtypeStruct
    return pl.pallas_call(
        body,
        out_shape=(
            sds((64,) + weights.shape[1:], weights.dtype),
            sds((8,) + tokens.shape, tokens.dtype),
            sds((64,) + small.shape, small.dtype),
            sds((2,) + routes.shape, routes.dtype),
            sds((2,) + cotangent.shape, cotangent.dtype),
        ),
        in_specs=[ANY] * 5,
        out_specs=[ANY] * 5,
        scratch_shapes=[DMA((4,)), DMA((7,)), DMA((7,)), DMA((4,)), DMA((5,))],
        compiler_params=call_params(0),
        name="gather_first",
    )(weights, tokens, small, routes, cotangent)


def gather_row(block, collective_id):
    def body(src, out, row_s, row_r, local):
        me, wsh = lax.axis_index("ctx"), lax.axis_index("wsh")
        barrier, amount = greet([(shifted(me, 0, 0, dx, dk), wsh) for dx, dk in ((1, 0), (3, 0), (2, 0), (0, 1))])
        mine = pltpu.make_async_copy(src, out.at[lax.rem(me, 8)], local)
        mine.start()
        pl.semaphore_wait(barrier, amount)
        copies = row_gather_start(src, out, me, wsh, row_s, row_r)
        row_gather_finish(out, me, wsh, copies, row_s, row_r)
        mine.wait()

    return pl.pallas_call(
        body,
        out_shape=jax.ShapeDtypeStruct((8,) + block.shape, block.dtype),
        in_specs=[ANY],
        out_specs=ANY,
        scratch_shapes=[DMA((7,)), DMA((7,)), DMA],
        compiler_params=call_params(collective_id),
        name="gather_row",
    )(block)


COLUMN_STEPS = ((1, 0), (3, 0), (0, 1), (2, 0), (1, 1), (3, 1), (2, 1))


def gather_keys(rows, collective_id):
    count = rows.shape[0]
    half = count // 2

    def body(src, out, send, recv, local):
        me, wsh = lax.axis_index("ctx"), lax.axis_index("wsh")
        core = lax.rem(me, 2)
        group = lax.div(me, 8)
        partner = shifted(me, 0, 0, 0, 1)
        peers = [shifted(me, dz, dy, 0, 0) for dz, dy in COLUMN_STEPS]
        barrier, amount = greet([(peer, wsh) for peer in peers + [partner]])
        mine = pltpu.make_async_copy(src, out.at[group], local)
        mine.start()
        pl.semaphore_wait(barrier, amount)
        my_half = pl.ds(pl.multiple_of(core * half, half), half)
        copies = []
        for at, peer in enumerate(peers):
            copy = remote(src.at[my_half], out.at[group, my_half], send.at[at], recv.at[at], peer, wsh)
            copy.start()
            copies.append(copy)
        forwards = []
        for at, (dz, dy) in enumerate(COLUMN_STEPS):
            copies[at].wait_recv()
            origin = lax.div(shifted(me, 4 - dz, 2 - dy, 0, 0), 8)
            part = out.at[origin, my_half]
            forward = remote(part, part, send.at[7 + at], recv.at[7 + at], partner, wsh)
            forward.start()
            forwards.append(forward)
        for copy in copies:
            copy.wait_send()
        for forward in forwards:
            forward.wait()
        mine.wait()

    return pl.pallas_call(
        body,
        out_shape=jax.ShapeDtypeStruct((8,) + rows.shape, rows.dtype),
        in_specs=[ANY],
        out_specs=ANY,
        scratch_shapes=[DMA((14,)), DMA((14,)), DMA],
        compiler_params=call_params(collective_id),
        name="gather_keys",
    )(rows)


def reduce_row(parts, collective_id, both):
    _, rows, width = parts.shape
    block = (rows, width)

    def body(src, out, arrived, summed, landed, swapped, total, send, recv, local):
        me, wsh = lax.axis_index("ctx"), lax.axis_index("wsh")
        other = 1 - wsh
        core = lax.rem(me, 2)
        _, _, x, _ = coords(me)
        partner = shifted(me, 0, 0, 0, 1)
        peers = [shifted(me, 0, 0, dx, 0) for dx in (1, 2, 3)]
        barrier, amount = greet([(peer, wsh) for peer in peers + [partner]] + [(me, other)])
        pl.semaphore_wait(barrier, amount)
        first = []
        for at, dx in enumerate((2, 1, 3, 0)):
            chip = lax.rem(x + dx, 4)
            copy = remote(
                src.at[chip * 2 + 1 - core], arrived.at[at], send.at[at], recv.at[at], partner, wsh
            )
            copy.start()
            first.append(copy)
        second = []
        for at, dx in enumerate((2, 1, 3)):
            chip = lax.rem(x + dx, 4)
            first[at].wait_recv()
            summed[at] = (src[chip * 2 + core].astype(F32) + arrived[at].astype(F32)).astype(BF)
            copy = remote(
                summed.at[at],
                landed.at[at],
                send.at[4 + at],
                recv.at[4 + at],
                shifted(me, 0, 0, dx, 0),
                wsh,
            )
            copy.start()
            second.append(copy)
        first[3].wait_recv()
        total[...] = src[x * 2 + core].astype(F32) + arrived[3].astype(F32)
        for at in (1, 2, 0):
            second[at].wait_recv()
        swapped[0] = (
            total[...] + landed[0].astype(F32) + landed[1].astype(F32) + landed[2].astype(F32)
        ).astype(BF)
        swap = remote(swapped.at[0], swapped.at[1], send.at[7], recv.at[7], me, other)
        swap.start()
        swap.wait()
        total[...] = swapped[0].astype(F32) + swapped[1].astype(F32)
        if both:
            keep = pltpu.make_async_copy(total, out.at[core], local)
            keep.start()
            give = remote(total, out.at[core], send.at[8], recv.at[8], partner, wsh)
            give.start()
            give.wait()
            keep.wait()
        else:
            out[...] = total[...]
        for copy in first + second:
            copy.wait_send()

    return pl.pallas_call(
        body,
        out_shape=jax.ShapeDtypeStruct((2,) + block if both else block, F32),
        in_specs=[VMEM],
        out_specs=VMEM,
        scratch_shapes=[
            pltpu.VMEM((4,) + block, BF),
            pltpu.VMEM((3,) + block, BF),
            pltpu.VMEM((3,) + block, BF),
            pltpu.VMEM((2,) + block, BF),
            pltpu.VMEM(block, F32),
            DMA((9,)),
            DMA((9,)),
            DMA,
        ],
        compiler_params=call_params(collective_id, 40 * 1024 * 1024),
        name="reduce_row",
    )(parts)


def reduce_chip(parts, extra, collective_id):
    _, rows, width = parts.shape
    extra_block = None if extra is None else extra.shape[1:]

    def body(*refs):
        if extra is None:
            src, out, arrived, swapped, total, send, recv = refs
        else:
            src, src2, out, out2, arrived, swapped, total, arrived2, swapped2, send, recv = refs
        me, wsh = lax.axis_index("ctx"), lax.axis_index("wsh")
        other = 1 - wsh
        core = lax.rem(me, 2)
        partner = shifted(me, 0, 0, 0, 1)
        barrier, amount = greet([(partner, wsh), (me, other)])
        pl.semaphore_wait(barrier, amount)
        give = remote(src.at[1 - core], arrived, send.at[0], recv.at[0], partner, wsh)
        give.start()
        if extra is not None:
            give2 = remote(src2.at[1 - core], arrived2, send.at[2], recv.at[2], partner, wsh)
            give2.start()
        give.wait()
        swapped[0] = (src[core].astype(F32) + arrived[...].astype(F32)).astype(BF)
        swap = remote(swapped.at[0], swapped.at[1], send.at[1], recv.at[1], me, other)
        swap.start()
        if extra is not None:
            give2.wait()
            swapped2[0] = src2[core] + arrived2[...]
            swap2 = remote(swapped2.at[0], swapped2.at[1], send.at[3], recv.at[3], me, other)
            swap2.start()
            swap2.wait()
            out2[...] = swapped2[0] + swapped2[1]
        swap.wait()
        out[...] = swapped[0].astype(F32) + swapped[1].astype(F32)

    sds = jax.ShapeDtypeStruct
    block = (rows, width)
    shapes = [sds(block, F32)]
    scratch = [pltpu.VMEM(block, BF), pltpu.VMEM((2,) + block, BF), pltpu.VMEM(block, F32)]
    operands = [parts]
    if extra is not None:
        shapes.append(sds(extra_block, F32))
        scratch += [pltpu.VMEM(extra_block, F32), pltpu.VMEM((2,) + extra_block, F32)]
        operands.append(extra)
    scratch += [DMA((4,)), DMA((4,))]
    return pl.pallas_call(
        body,
        out_shape=shapes,
        in_specs=[VMEM] * len(operands),
        out_specs=[VMEM] * len(operands),
        scratch_shapes=scratch,
        compiler_params=call_params(collective_id, 40 * 1024 * 1024),
        name="reduce_chip",
    )(*operands)


def reduce_keys(parts, collective_id):
    _, groups, _, rows, width = parts.shape

    def body(src, out, arrived, summed, landed, send, recv, fsend, frecv):
        me, wsh = lax.axis_index("ctx"), lax.axis_index("wsh")
        core = lax.rem(me, 2)
        z, y, x, _ = coords(me)
        pair = lax.div(x, 2) * 2
        side = lax.rem(x, 2)
        partner = shifted(me, 0, 0, 0, 1)

        def target(step):
            dz, dy, db = lax.div(step, 4), lax.rem(lax.div(step, 2), 2), lax.rem(step, 2)
            return (
                lax.rem(z + dz, 4) * 2 + lax.rem(y + dy, 2),
                lax.rem(side + db, 2),
            )

        barrier = pltpu.get_barrier_semaphore()
        pl.semaphore_signal(barrier, inc=1, device_id=(partner, wsh), device_id_type=MESH)
        for step in range(1, 16):
            group, b = target(step)
            pl.semaphore_signal(
                barrier, inc=1, device_id=((group * 4 + pair + b) * 2 + core, wsh), device_id_type=MESH
            )
        pl.semaphore_wait(barrier, 16)
        order = (1, 4, 2, 8, 12, 3, 5, 6, 9, 13, 10, 14, 7, 11, 15, 0)
        first = []
        for at, step in enumerate(order):
            group, b = target(step)
            copy = remote(
                src.at[1 - core, group, b], arrived.at[step], fsend.at[at], frecv.at[at], partner, wsh
            )
            copy.start()
            first.append(copy)
        second = []
        for at, step in enumerate(order):
            group, b = target(step)
            first[at].wait_recv()
            value = src[core, group, b].astype(F32) + arrived[step].astype(F32)
            if step == 0:
                out[...] = value
            else:
                summed[step] = value.astype(BF)
                copy = remote(
                    summed.at[step],
                    landed.at[step],
                    send.at[at],
                    recv.at[at],
                    (group * 4 + pair + b) * 2 + core,
                    wsh,
                )
                copy.start()
                second.append((step, copy))
        for step, copy in second:
            copy.wait_recv()
            out[...] += landed[step].astype(F32)
        for copy in first:
            copy.wait_send()
        for _, copy in second:
            copy.wait_send()

    block = (rows, width)
    return pl.pallas_call(
        body,
        out_shape=jax.ShapeDtypeStruct(block, F32),
        in_specs=[VMEM],
        out_specs=VMEM,
        scratch_shapes=[
            pltpu.VMEM((16,) + block, BF),
            pltpu.VMEM((16,) + block, BF),
            pltpu.VMEM((16,) + block, BF),
            DMA((16,)),
            DMA((16,)),
            DMA((16,)),
            DMA((16,)),
        ],
        compiler_params=call_params(collective_id, 40 * 1024 * 1024),
        name="reduce_keys",
    )(parts)


def exchange_same_core(arrays, collective_id):
    amount = len(arrays)

    def body(*refs):
        ins, outs = refs[:amount], refs[amount : 2 * amount]
        send, recv, local = refs[2 * amount :]
        me, wsh = lax.axis_index("ctx"), lax.axis_index("wsh")
        chip = lax.div(me, 2)

        def target(step):
            return shifted(me, lax.div(step, 8), lax.rem(lax.div(step, 4), 2), lax.rem(step, 4), 0)

        barrier, count = greet_many(32, target, wsh)
        locals_ = []
        for at in range(amount):
            copy = pltpu.make_async_copy(ins[at].at[chip], outs[at].at[chip], local.at[at])
            copy.start()
            locals_.append(copy)
        pl.semaphore_wait(barrier, count)

        def one(step, carried):
            ctx = target(lax.rem(step * 13, 32))
            for at in range(amount):
                remote(
                    ins[at].at[lax.div(ctx, 2)], outs[at].at[chip], send.at[at], recv.at[at], ctx, wsh
                ).start()
            return carried

        lax.fori_loop(1, 32, one, 0)
        for copy in locals_:
            copy.wait()
        for at in range(amount):
            rest = outs[at].at[pl.ds(0, 31)]
            done = remote(rest, rest, send.at[at], recv.at[at], me, wsh)
            done.wait_send()
            done.wait_recv()

    return pl.pallas_call(
        body,
        out_shape=[jax.ShapeDtypeStruct(a.shape, a.dtype) for a in arrays],
        in_specs=[ANY] * amount,
        out_specs=[ANY] * amount,
        scratch_shapes=[DMA((amount,)), DMA((amount,)), DMA((amount,))],
        compiler_params=call_params(collective_id),
        name="exchange_same_core",
    )(*arrays)


def same_core_groups():
    return [[2 * i + core for i in range(32)] for core in range(2)]


def natural_order(inverse, kv_ref, keys, values, transposed):
    def one(block, carried):
        rows = kv_ref[pl.ds(pl.multiple_of(inverse[block] * BLK, BLK), BLK), :]
        at = pl.ds(pl.multiple_of(block * BLK, BLK), BLK)
        keys[at, :] = rows[:, :HEAD_WIDTH]
        values[at, :] = rows[:, HEAD_WIDTH:]
        return carried

    lax.fori_loop(0, kv_ref.shape[0] // BLK, one, 0)
    source, turned = transposed

    def turn(chunk, carried):
        at = pl.ds(pl.multiple_of(chunk * CHUNK, CHUNK), CHUNK)
        turned[:, at] = source[at, :].T
        return carried

    lax.fori_loop(0, kv_ref.shape[0] // CHUNK, turn, 0)


def stacked(ref, first, second):
    rows = [ref[pl.ds(pl.multiple_of(at * BLK, BLK), BLK), :] for at in (first, second)]
    return jnp.concatenate(
        [rows[0][:, :HEAD_WIDTH], rows[0][:, HEAD_WIDTH:], rows[1][:, :HEAD_WIDTH], rows[1][:, HEAD_WIDTH:]],
        axis=0,
    )


def unstacked(ref, first, second, value):
    for at, begin in ((first, 0), (second, 2 * BLK)):
        ref[pl.ds(pl.multiple_of(at * BLK, BLK), BLK), :] = jnp.concatenate(
            [value[begin : begin + BLK], value[begin + BLK : begin + 2 * BLK]], axis=1
        )


def forward_kernel(order, low, high, inverse, q_ref, kv_ref, pos_ref, start_ref, out_ref, lse_ref, keys, values, values_t, acc):
    step = pl.program_id(0)

    @pl.when(step == 0)
    def _():
        natural_order(inverse, kv_ref, keys, values, (values, values_t))

    first, second = order[2 * step], order[2 * step + 1]
    q_t = stacked(q_ref, first, second).astype(F32).T.astype(BF)
    q_pos, q_start = pos_ref[0], start_ref[0]
    scale = 1.0 / math.sqrt(HEAD_WIDTH)
    width = 4 * BLK
    acc[...] = jnp.zeros_like(acc)

    def chunk(index, carried):
        highest, total = carried
        at = pl.multiple_of(index * CHUNK, CHUNK)
        scores = matmul(keys[pl.ds(at, CHUNK), :], q_t) * scale
        k_pos = at + lax.broadcasted_iota(jnp.int32, (CHUNK, width), 0)
        scores = jnp.where((k_pos <= q_pos) & (k_pos >= q_start), scores, MASKED)
        top = jnp.maximum(highest, jnp.max(scores, axis=0, keepdims=True))
        probs = jnp.exp(scores - top)
        fade = jnp.exp(highest - top)
        acc[...] = acc[...] * fade + matmul(values_t[:, pl.ds(at, CHUNK)], probs.astype(BF))
        return top, total * fade + jnp.sum(probs, axis=0, keepdims=True)

    highest, total = lax.fori_loop(
        low[step],
        high[step],
        chunk,
        (jnp.full((1, width), MASKED, F32), jnp.zeros((1, width), F32)),
    )
    lse_ref[0] = highest + jnp.log(total)
    unstacked(out_ref, first, second, (acc[...] / total).T.astype(BF))


def attend(order, low, high, inverse, queries, kv, positions, starts):
    rows = queries.shape[0]
    steps = rows // (2 * BLK)
    everything = pl.BlockSpec(queries.shape, lambda i, *_: (0, 0))
    strip = pl.BlockSpec((1, 1, 4 * BLK), lambda i, *_: (i, 0, 0))
    sds = jax.ShapeDtypeStruct
    return pl.pallas_call(
        forward_kernel,
        out_shape=(sds(queries.shape, BF), sds((steps, 1, 4 * BLK), F32)),
        grid_spec=pltpu.PrefetchScalarGridSpec(
            num_scalar_prefetch=4,
            grid=(steps,),
            in_specs=[everything, pl.BlockSpec(kv.shape, lambda i, *_: (0, 0)), strip, strip],
            out_specs=[everything, strip],
            scratch_shapes=[
                pltpu.VMEM((kv.shape[0], HEAD_WIDTH), BF),
                pltpu.VMEM((kv.shape[0], HEAD_WIDTH), BF),
                pltpu.VMEM((HEAD_WIDTH, kv.shape[0]), BF),
                pltpu.VMEM((HEAD_WIDTH, 4 * BLK), F32),
            ],
        ),
        compiler_params=pltpu.CompilerParams(vmem_limit_bytes=50 * 1024 * 1024),
        name="attend",
    )(order, low, high, inverse, queries, kv, positions, starts)


def backward_kernel(order, low, high, inverse, q_ref, do_ref, kv_ref, pos_ref, start_ref, lse_ref, dot_ref, dq_ref, dkv_ref, keys, values, keys_t, d_keys, d_values, acc):
    step = pl.program_id(0)

    @pl.when(step == 0)
    def _():
        natural_order(inverse, kv_ref, keys, values, (keys, keys_t))
        d_keys[...] = jnp.zeros_like(d_keys)
        d_values[...] = jnp.zeros_like(d_values)

    first, second = order[2 * step], order[2 * step + 1]
    q = stacked(q_ref, first, second)
    d_out = stacked(do_ref, first, second)
    q_t = q.astype(F32).T.astype(BF)
    d_out_t = d_out.astype(F32).T.astype(BF)
    q_pos, q_start = pos_ref[0], start_ref[0]
    lse, dots = lse_ref[0], dot_ref[0]
    scale = 1.0 / math.sqrt(HEAD_WIDTH)
    width = 4 * BLK
    acc[...] = jnp.zeros_like(acc)

    def chunk(index, carried):
        at = pl.multiple_of(index * CHUNK, CHUNK)
        here = pl.ds(at, CHUNK)
        scores = matmul(keys[here, :], q_t) * scale
        k_pos = at + lax.broadcasted_iota(jnp.int32, (CHUNK, width), 0)
        scores = jnp.where((k_pos <= q_pos) & (k_pos >= q_start), scores, MASKED)
        probs = jnp.exp(scores - lse)
        d_probs = matmul(values[here, :], d_out_t)
        d_scores = (probs * (d_probs - dots)).astype(BF)
        d_values[here, :] += matmul(probs.astype(BF), d_out)
        d_keys[here, :] += matmul(d_scores, q)
        acc[...] += matmul(keys_t[:, here], d_scores)
        return carried

    lax.fori_loop(low[step], high[step], chunk, 0)
    unstacked(dq_ref, first, second, (acc[...] * scale).T)

    @pl.when(step == pl.num_programs(0) - 1)
    def _():
        def one(block, carried):
            dealt = inverse[block]
            group, inside = dealt // 16, dealt % 16
            half, rest = inside // 8, inside % 8
            at = pl.ds(pl.multiple_of(block * BLK, BLK), BLK)
            to = pl.ds(pl.multiple_of(rest * BLK, BLK), BLK)
            dkv_ref[half, group, 0, to, :] = (d_keys[at, :] * scale).astype(BF)
            dkv_ref[half, group, 1, to, :] = d_values[at, :].astype(BF)
            return carried

        lax.fori_loop(0, kv_ref.shape[0] // BLK, one, 0)


def attend_back(order, low, high, inverse, queries, d_heads, kv, positions, starts, lse, dots):
    rows = queries.shape[0]
    total = kv.shape[0]
    steps = rows // (2 * BLK)
    everything = pl.BlockSpec(queries.shape, lambda i, *_: (0, 0))
    strip = pl.BlockSpec((1, 1, 4 * BLK), lambda i, *_: (i, 0, 0))
    sds = jax.ShapeDtypeStruct
    dkv_shape = (2, total // rows, 2, rows // 2, HEAD_WIDTH)
    return pl.pallas_call(
        backward_kernel,
        out_shape=(sds(queries.shape, F32), sds(dkv_shape, BF)),
        grid_spec=pltpu.PrefetchScalarGridSpec(
            num_scalar_prefetch=4,
            grid=(steps,),
            in_specs=[everything, everything, pl.BlockSpec(kv.shape, lambda i, *_: (0, 0)), strip, strip, strip, strip],
            out_specs=[everything, pl.BlockSpec(dkv_shape, lambda i, *_: (0, 0, 0, 0, 0))],
            scratch_shapes=[
                pltpu.VMEM((total, HEAD_WIDTH), BF),
                pltpu.VMEM((total, HEAD_WIDTH), BF),
                pltpu.VMEM((HEAD_WIDTH, total), BF),
                pltpu.VMEM((total, HEAD_WIDTH), F32),
                pltpu.VMEM((total, HEAD_WIDTH), F32),
                pltpu.VMEM((HEAD_WIDTH, 4 * BLK), F32),
            ],
        ),
        compiler_params=pltpu.CompilerParams(vmem_limit_bytes=55 * 1024 * 1024),
        name="attend_back",
    )(order, low, high, inverse, queries, d_heads, kv, positions, starts, lse, dots)


def lanes_to(row, lanes=128):
    return jnp.pad(row, ((0, 0),) * (row.ndim - 1) + ((0, lanes - row.shape[-1]),))


def local(
    tokens,
    cotangent,
    seq_lengths,
    block_order,
    routes,
    w_query,
    key_weight,
    value_weight,
    w_out,
    gain_attn,
    gain_query,
    gain_key,
    gain_ffn,
    w_router,
    w_gate,
    w_up,
    w_down,
):
    rows = tokens.shape[0]
    width = tokens.shape[1]
    experts = w_router.shape[1]
    block_count = block_order.shape[0]
    wsh = lax.axis_index("wsh")
    me = lax.axis_index("ctx")
    core = lax.rem(me, 2)
    place = lax.rem(me, 8)
    group = lax.div(me, 8)
    row_tokens = 8 * rows
    row_blocks = row_tokens // BLK

    def of_mine(weight):
        return to_low(lax.dynamic_index_in_dim(weight, wsh, 0, keepdims=False))

    def of_other(weight):
        return to_low(lax.dynamic_index_in_dim(weight, 1 - wsh, 0, keepdims=False))

    def swap(value):
        return lax.ppermute(value, "wsh", [(0, 1), (1, 0)])

    gate_w = (of_mine(w_gate), swap(of_other(w_gate)))
    up_w = (of_mine(w_up), swap(of_other(w_up)))
    down_w = (of_mine(w_down), swap(of_other(w_down)))

    depth = w_query.shape[0]
    q_part = to_low(w_query).reshape(depth, 8, 256).transpose(1, 0, 2)
    k_part = jnp.repeat(to_low(key_weight).reshape(depth, 2, 128).transpose(1, 0, 2), 4, axis=0)
    v_part = jnp.repeat(to_low(value_weight).reshape(depth, 2, 128).transpose(1, 0, 2), 4, axis=0)
    w_pack = jnp.concatenate([q_part, k_part, v_part], axis=2)
    small = jnp.concatenate(
        [lanes_to(gain_attn[None, :]), lanes_to(gain_ffn[None, :]), jnp.zeros((6, 128), F32)], axis=0
    )
    w_all, row_rows, small_all, chip_routes, chip_cot = gather_first(
        w_pack, tokens, small, routes.T, cotangent
    )
    w_qkv = w_all.reshape(width, 512)
    g_attn = to_low(small_all[:, 0, :depth].reshape(width)).astype(F32)
    g_ffn = to_low(small_all[:, 1, :depth].reshape(width)).astype(F32)
    g_query = rounded(gain_query)
    g_key = rounded(gain_key)

    o_part = to_low(w_out).T.reshape(depth, 8, 256).transpose(1, 0, 2)
    r_part = jnp.broadcast_to(to_low(w_router)[None], (8, depth, experts))
    late_pack = jnp.tile(jnp.concatenate([o_part, r_part], axis=2), (8, 1, 1))
    late_all = lax.all_to_all(late_pack, "ctx", split_axis=0, concat_axis=0, tiled=True).reshape(width, 384)
    wo_t = late_all[:, :256]
    wr = late_all[:, 256:]

    route_rows = chip_routes.transpose(0, 2, 1)
    hits = jnp.any(
        route_rows[:, :, :, None] == jnp.arange(experts, dtype=jnp.int32)[None, None, None, :], axis=2
    )
    before = jnp.tril(jnp.ones((rows, rows), BF), -1)
    ranks = jnp.einsum("ts,hse->hte", before, hits.astype(BF), preferred_element_type=F32).astype(jnp.int32)
    ranks = jnp.where(hits, ranks + jnp.array([0, CAP], jnp.int32)[:, None, None], -1)
    hits = hits.reshape(2 * rows, experts)
    quarter = core * 2 + wsh
    my_ranks = lax.dynamic_index_in_dim(
        ranks.reshape(2 * rows, experts).T.reshape(experts // 4, 4, 2 * rows), quarter, 1, keepdims=False
    )
    chips = experts // 4
    slots = 2 * CAP
    pick = my_ranks[:, None, :] == jnp.arange(slots, dtype=jnp.int32)[None, :, None]
    pick_low = pick.astype(BF).reshape(chips * slots, 2 * rows)
    cot_rows = matmul(pick_low, chip_cot.reshape(2 * rows, width)).astype(BF)
    cot_there = lax.all_to_all(
        cot_rows.reshape(chips, slots, width),
        "ctx",
        split_axis=0,
        concat_axis=0,
        tiled=True,
        axis_index_groups=same_core_groups(),
    ).reshape(chips * slots, width)

    my_blocks = lax.dynamic_slice_in_dim(block_order, group * row_blocks, row_blocks, 0)
    positions = (my_blocks[:, None] * BLK + jnp.arange(BLK, dtype=jnp.int32)[None, :]).reshape(row_tokens)
    starts = seq_starts(positions, seq_lengths)
    cosine, sine_tab = rope_tables(positions - starts)
    inverse_order = (
        jnp.zeros((block_count,), jnp.int32)
        .at[block_order]
        .set(jnp.arange(block_count, dtype=jnp.int32))
    )
    smaller = jnp.sum((my_blocks[None, :] < my_blocks[:, None]).astype(jnp.int32), axis=1)
    order = jnp.sum(
        jnp.where(
            smaller[None, :] == jnp.arange(row_blocks, dtype=jnp.int32)[:, None],
            jnp.arange(row_blocks, dtype=jnp.int32)[None, :],
            0,
        ),
        axis=1,
    )
    first_start = starts.reshape(row_blocks, BLK)[:, 0]
    low = jnp.min(jnp.take(first_start, order).reshape(-1, 2), axis=1) // CHUNK
    high = jnp.max(jnp.take(my_blocks, order).reshape(-1, 2), axis=1) * BLK // CHUNK + 1

    def strips(per_token):
        by_block = jnp.take(per_token.reshape(row_blocks, BLK), order, axis=0).reshape(-1, 2, 1, BLK)
        return jnp.broadcast_to(by_block, (row_blocks // 2, 2, 2, BLK)).reshape(-1, 1, 4 * BLK)

    q_pos, q_start = strips(positions), strips(starts)

    stream = row_rows.reshape(row_tokens, width).astype(F32)
    inverse_one = inverse_root(stream)
    hidden_one = to_low(stream * inverse_one * g_attn)
    qkv = matmul(hidden_one, w_qkv)
    q_pre = qkv[:, :256].reshape(row_tokens, 2, HEAD_WIDTH)
    k_pre = qkv[:, 256:384]
    q_inverse = inverse_root(q_pre)
    k_inverse = inverse_root(k_pre)
    queries = to_low(rotate(q_pre * q_inverse * g_query, cosine[:, None], sine_tab[:, None]))
    queries = queries.reshape(row_tokens, 256)
    keys = to_low(rotate(k_pre * k_inverse * g_key, cosine, sine_tab))
    kv = jnp.concatenate([keys, to_low(qkv[:, 384:])], axis=1)
    kv_all = gather_keys(kv, 1).reshape(block_count * BLK, 256)
    heads, lse = attend(order, low, high, inverse_order, queries, kv_all, q_pos, q_start)

    attn_parts = to_low(times_transposed(heads, wo_t)).reshape(8, rows, width)
    attn_total = reduce_row(attn_parts, 2, True).reshape(2 * rows, width)
    chip_stream = lax.dynamic_slice_in_dim(stream, (place - core) * rows, 2 * rows, 0)
    chip_residual = chip_stream + attn_total
    chip_inverse_two = inverse_root(chip_residual)
    chip_hidden = to_low(chip_residual * chip_inverse_two * g_ffn)
    logits = matmul(chip_hidden, wr)
    masked_logits = jnp.where(hits, logits, MASKED)
    gate_exps = jnp.where(
        hits, jnp.exp(masked_logits - jnp.max(masked_logits, axis=-1, keepdims=True)), 0.0
    )
    gates = gate_exps / jnp.sum(gate_exps, axis=-1, keepdims=True)

    def my_rows(value):
        return lax.dynamic_slice_in_dim(value, core * rows, rows, 0)

    out_rows = matmul(pick_low, chip_hidden).astype(BF).reshape(chips, slots, width)
    my_gates = lax.dynamic_index_in_dim(
        gates.T.reshape(chips, 4, 2 * rows), quarter, 1, keepdims=False
    )
    slot_gates = jnp.sum(jnp.where(pick, my_gates[:, None, :], 0.0), axis=2)
    gate_tile = jnp.pad(slot_gates[:, None, :], ((0, 0), (0, 7), (0, 128 - slots)))
    arrived, gate_there = exchange_same_core([out_rows, gate_tile], 3)
    arrived = arrived.reshape(chips * slots, width)
    gate_col = gate_there[:, 0, :slots].reshape(chips * slots, 1)
    d_pairs = to_low(gate_col * cot_there.astype(F32))
    expert_out = 0.0
    d_rows = 0.0
    grads = []
    for gate_half, up_half, down_half in zip(gate_w, up_w, down_w):
        gate_pre = matmul(arrived, gate_half)
        up_pre = matmul(arrived, up_half)
        sigma = jax.nn.sigmoid(gate_pre)
        activated = to_low(gate_pre * sigma * up_pre)
        expert_out = expert_out + matmul(activated, down_half)
        d_act = times_transposed(d_pairs, down_half)
        grad_down = transposed_times(activated, d_pairs)
        d_gate_pre = to_low(d_act * up_pre * sigma * (1.0 + gate_pre * (1.0 - sigma)))
        d_up_pre = to_low(d_act * gate_pre * sigma)
        grad_gate = transposed_times(arrived, d_gate_pre)
        grad_up = transposed_times(arrived, d_up_pre)
        d_rows = (
            d_rows + times_transposed(d_gate_pre, gate_half) + times_transposed(d_up_pre, up_half)
        )
        grads.append((grad_gate, grad_up, grad_down))
    d_gate_slots = jnp.sum(expert_out * cot_there.astype(F32), axis=1).reshape(chips, 1, slots)
    d_gate_tile = jnp.pad(d_gate_slots, ((0, 0), (0, 7), (0, 128 - slots)))
    d_back, d_gate_back = exchange_same_core(
        [to_low(d_rows).reshape(chips, slots, width), d_gate_tile], 4
    )
    y_back = lax.all_to_all(
        to_low(gate_col * expert_out).reshape(chips, slots, width),
        "ctx",
        split_axis=0,
        concat_axis=0,
        tiled=True,
        axis_index_groups=same_core_groups(),
    )

    def paired(own, back):
        back = swap(to_low(back)).astype(F32)
        return jnp.where(wsh == 0, jnp.stack([own, back]), jnp.stack([back, own]))

    grad_gate, grad_up, grad_down = [paired(own, back) for own, back in zip(*grads)]

    def collect(back):
        return to_low(transposed_times(pick_low, back.reshape(chips * slots, width))).reshape(2, rows, width)

    d_gate_slots = d_gate_back[:, 0, :slots]
    d_gates_mine = jnp.sum(jnp.where(pick, d_gate_slots[:, :, None], 0.0), axis=1)
    d_gates_part = jnp.sum(
        jnp.where(
            jnp.arange(4, dtype=jnp.int32)[None, :, None] == quarter, d_gates_mine[:, None, :], 0.0
        ),
        axis=0,
        keepdims=True,
    ) if False else jnp.where(
        jnp.arange(4, dtype=jnp.int32)[None, :, None] == quarter, d_gates_mine[:, None, :], 0.0
    ).reshape(experts, 2 * rows)
    d_gates_part = d_gates_part.T.reshape(2, rows, experts)
    d_hidden_moe, d_gates = reduce_chip(collect(d_back), d_gates_part, 5)
    (moe_total,) = reduce_chip(collect(y_back), None, 6)
    residual = my_rows(chip_residual)
    out_stream = residual + moe_total

    own_gates = my_rows(gates)
    hidden_two = my_rows(chip_hidden)
    inverse_two = my_rows(chip_inverse_two)
    d_chosen = own_gates * (d_gates - jnp.sum(own_gates * d_gates, axis=-1, keepdims=True))
    d_logits = to_low(d_chosen)
    grad_router = transposed_times(hidden_two, d_logits)
    d_hidden_two = d_hidden_moe + times_transposed(d_logits, wr)
    d_res_norm, ffn_gain_terms = norm_back(residual, inverse_two, g_ffn, d_hidden_two)
    d_residual = cotangent.astype(F32) + d_res_norm
    gain_ffn_part = jnp.sum(ffn_gain_terms, axis=0)

    d_attn = gather_row(to_low(d_residual), 7).reshape(row_tokens, width)
    grad_out_t = transposed_times(d_attn, heads)
    d_heads = to_low(matmul(d_attn, wo_t))
    dots = jnp.sum(
        d_heads.astype(F32).reshape(row_tokens, 2, HEAD_WIDTH)
        * heads.astype(F32).reshape(row_tokens, 2, HEAD_WIDTH),
        axis=-1,
    )
    dot_strips = (
        jnp.take(dots.reshape(row_blocks, BLK, 2), order, axis=0)
        .transpose(0, 2, 1)
        .reshape(row_blocks // 2, 1, 4 * BLK)
    )
    early = jnp.concatenate(
        [
            to_low(grad_out_t[:, :128]).reshape(64, depth, 128),
            to_low(grad_out_t[:, 128:]).reshape(64, depth, 128),
            to_low(grad_router).reshape(64, depth, 128),
            jnp.pad(
                to_low(gain_ffn_part).reshape(64, 1, depth), ((0, 0), (0, 15), (0, 128 - depth))
            ),
        ],
        axis=1,
    )
    early = lax.all_to_all(early, "ctx", split_axis=0, concat_axis=0, tiled=True)
    d_queries, d_kv = attend_back(
        order, low, high, inverse_order, queries, d_heads, kv_all, q_pos, q_start, lse, dot_strips
    )
    d_side = reduce_keys(d_kv, 8)
    is_key = lax.rem(lax.div(me, 2), 2) == 0
    half_rows = row_tokens // 2

    def half_of(value):
        return lax.dynamic_slice_in_dim(value, core * half_rows, half_rows, 0)

    d_k_norm = rotate_back(d_side, half_of(cosine), half_of(sine_tab))
    d_k_pre, key_gain_terms = norm_back(half_of(k_pre), half_of(k_inverse), g_key, d_k_norm)
    key_gain_part = jnp.where(is_key, jnp.sum(key_gain_terms, axis=0), 0.0)
    d_side_pre = to_low(jnp.where(is_key, d_k_pre, d_side))
    d_q_norm = rotate_back(
        d_queries.reshape(row_tokens, 2, HEAD_WIDTH), cosine[:, None], sine_tab[:, None]
    )
    d_q_pre, query_gain_terms = norm_back(q_pre, q_inverse, g_query, d_q_norm)
    query_gain_part = jnp.sum(query_gain_terms, axis=(0, 1))
    d_q_pre = to_low(d_q_pre.reshape(row_tokens, 256))
    side_w = jnp.where(is_key, w_qkv[:, 256:384], w_qkv[:, 384:])
    d_side_full = jnp.where(
        (jnp.arange(row_tokens, dtype=jnp.int32) // half_rows == core)[:, None],
        jnp.concatenate([d_side_pre, d_side_pre], axis=0),
        jnp.zeros((), BF),
    )
    d_all = jnp.concatenate([d_q_pre, d_side_full], axis=1)
    d_hidden_parts = to_low(
        times_transposed(d_all, jnp.concatenate([w_qkv[:, :256], side_w], axis=1))
    ).reshape(8, rows, width)
    grad_in = to_low(transposed_times(hidden_one, d_all))
    tail = jnp.broadcast_to(
        jnp.pad(to_low(jnp.stack([query_gain_part, key_gain_part])), ((0, 14), (0, 0)))[None],
        (64, 16, 128),
    )
    late = jnp.concatenate(
        [grad_in[:, 128 * i : 128 * i + 128].reshape(64, depth, 128) for i in range(3)] + [tail], axis=1
    )
    late = lax.all_to_all(late, "ctx", split_axis=0, concat_axis=0, tiled=True)
    d_hidden_one = reduce_row(d_hidden_parts, 9, False)
    own_stream = tokens.astype(F32)
    d_stream_norm, _ = norm_back(own_stream, inverse_root(own_stream), g_attn, d_hidden_one)
    grad_tokens = d_residual + d_stream_norm

    def summed(value, terms):
        return jnp.sum(value.astype(F32).reshape((8,) + terms + value.shape[1:]), axis=0)

    early_q = summed(early[:, : 2 * depth], (8,)).reshape(8, 2, depth, 128)
    grad_out = early_q.transpose(0, 1, 3, 2).reshape(8 * 256, depth)
    grad_router = jnp.sum(early[:, 2 * depth : 3 * depth].astype(F32), axis=0)
    grad_gain_ffn = jnp.sum(early[:, 3 * depth, :depth].astype(F32), axis=0)
    late_q = summed(late[:, : 2 * depth], (8,)).reshape(8, 2, depth, 128)
    grad_query = late_q.transpose(2, 0, 1, 3).reshape(depth, 8 * 256)
    late_kv = jnp.sum(
        late[:, 2 * depth : 3 * depth].astype(F32).reshape(8, 2, 2, 2, depth, 128), axis=(0, 3)
    )
    grad_key = late_kv[:, 0].transpose(1, 0, 2).reshape(depth, 256)
    grad_value = late_kv[:, 1].transpose(1, 0, 2).reshape(depth, 256)
    gain_parts = jnp.sum(late[:, 3 * depth : 3 * depth + 2].astype(F32), axis=0)
    gain_attn_part = (
        jnp.sum(rounded(w_query) * grad_query, axis=1)
        + jnp.sum(rounded(key_weight) * grad_key, axis=1)
        + jnp.sum(rounded(value_weight) * grad_value, axis=1)
    ) / rounded(gain_attn)
    gain_parts = lax.psum(jnp.concatenate([gain_parts, lanes_to(gain_attn_part[None, :])], axis=0), "wsh")
    return (
        out_stream,
        grad_tokens,
        grad_query,
        grad_key,
        grad_value,
        grad_out,
        gain_parts[2, :depth],
        gain_parts[0],
        gain_parts[1],
        grad_gain_ffn,
        grad_router,
        grad_gate,
        grad_up,
        grad_down,
    )


def solution(mesh):
    in_specs = (
        P("ctx", None),
        P("ctx", None),
        P(),
        P(),
        P("ctx", None),
        P("ctx", "wsh"),
        P("ctx", "wsh"),
        P("ctx", "wsh"),
        P("wsh", "ctx"),
        P("ctx"),
        P(),
        P(),
        P("ctx"),
        P("ctx", None),
        P("ctx", None, "wsh"),
        P("ctx", None, "wsh"),
        P("ctx", "wsh", None),
    )
    out_specs = (
        P("ctx", None),
        P("ctx", None),
        P("ctx", "wsh"),
        P("ctx", "wsh"),
        P("ctx", "wsh"),
        P("wsh", "ctx"),
        P("ctx"),
        P(),
        P(),
        P("ctx"),
        P("ctx", None),
        P("ctx", None, "wsh"),
        P("ctx", None, "wsh"),
        P("ctx", "wsh", None),
    )
    return jax.shard_map(local, mesh=mesh, in_specs=in_specs, out_specs=out_specs, check_vma=False)
```

```python
import functools
import math

import jax
import jax.numpy as jnp
from jax import lax
from jax.experimental import pallas as pl
from jax.experimental.pallas import tpu as pltpu
from jax.sharding import PartitionSpec as P

HEAD_WIDTH = 128
TOPK = 8
BLK = 64
MAX_SEQ_TOKENS = 4096
CAP = 12
CHUNK = 512

EPSILON = 1e-06
ROPE_BASE = 1000000.0
MASKED = -1e30
MESH = pl.DeviceIdType.MESH
BF = jnp.bfloat16
F32 = jnp.float32


def to_low(value_rows):
    return value_rows.astype(jnp.bfloat16)


def rounded(value_rows):
    return lax.optimization_barrier(value_rows.astype(jnp.bfloat16)).astype(jnp.float32)


def matmul(left, right):
    return jnp.dot(left, right, preferred_element_type=jnp.float32)


def times_transposed(left, right):
    return lax.dot_general(
        left, right, (((1,), (1,)), ((), ())), preferred_element_type=jnp.float32
    )


def transposed_times(left, right):
    return lax.dot_general(
        left, right, (((0,), (0,)), ((), ())), preferred_element_type=jnp.float32
    )


def norm_back(value_rows, inverse_rms, gain_vec, gradient):
    weighted = gradient * gain_vec
    mean_term = jnp.mean(weighted * value_rows, axis=-1, keepdims=True)
    d_values = (
        inverse_rms * weighted - value_rows * (inverse_rms * inverse_rms * inverse_rms) * mean_term
    )
    return (d_values, gradient * value_rows * inverse_rms)


def inverse_root(value_rows):
    return lax.rsqrt(jnp.mean(value_rows * value_rows, axis=-1, keepdims=True) + EPSILON)


def rope_tables(positions):
    half_dim = HEAD_WIDTH // 2
    frequency = jnp.power(ROPE_BASE, -2.0 * jnp.arange(half_dim, dtype=jnp.float32) / HEAD_WIDTH)
    angles = positions.astype(jnp.float32)[:, None] * frequency[None, :]
    cosine, sine_tab = jnp.cos(angles), jnp.sin(angles)
    return (
        jnp.concatenate([cosine, cosine], axis=-1),
        jnp.concatenate([sine_tab, sine_tab], axis=-1),
    )


def rotate(value_rows, cosine, sine_tab):
    half_dim = value_rows.shape[-1] // 2
    turned = jnp.concatenate([-value_rows[..., half_dim:], value_rows[..., :half_dim]], axis=-1)
    return value_rows * cosine + turned * sine_tab


def rotate_back(gradient, cosine, sine_tab):
    half_dim = gradient.shape[-1] // 2
    shifted = gradient * sine_tab
    return gradient * cosine + jnp.concatenate(
        [shifted[..., half_dim:], -shifted[..., :half_dim]], axis=-1
    )


def seq_starts(positions, seq_lengths):
    offsets = jnp.cumsum(seq_lengths) - seq_lengths
    inside = offsets[None, :] <= positions[:, None]
    return jnp.max(jnp.where(inside, offsets[None, :], 0), axis=1)


def coords(c):
    return (
        lax.div(c, 16),
        lax.rem(lax.div(c, 8), 2),
        lax.rem(lax.div(c, 2), 4),
        lax.rem(c, 2),
    )


def index_of(z, y, x, k):
    return ((z * 2 + y) * 4 + x) * 2 + k


def shifted(me, dz, dy, dx, dk):
    z, y, x, k = coords(me)
    return index_of(lax.rem(z + dz, 4), lax.rem(y + dy, 2), lax.rem(x + dx, 4), lax.rem(k + dk, 2))


def remote(src, dst, send, recv, ctx, wsh):
    return pltpu.make_async_remote_copy(
        src_ref=src,
        dst_ref=dst,
        send_sem=send,
        recv_sem=recv,
        device_id=(ctx, wsh),
        device_id_type=MESH,
    )


def greet(targets):
    barrier = pltpu.get_barrier_semaphore()
    for ctx, wsh in targets:
        pl.semaphore_signal(barrier, inc=1, device_id=(ctx, wsh), device_id_type=MESH)
    return barrier, len(targets)


def greet_many(count, target):
    barrier = pltpu.get_barrier_semaphore()

    def one(step, carried):
        pl.semaphore_signal(barrier, inc=1, device_id=target(step), device_id_type=MESH)
        return carried

    lax.fori_loop(1, count, one, 0)
    return barrier, count - 1


ANY = pl.BlockSpec(memory_space=pl.ANY)
VMEM = pl.BlockSpec(memory_space=pltpu.VMEM)
DMA = pltpu.SemaphoreType.DMA


def cost(microseconds):
    return pl.CostEstimate(flops=0, bytes_accessed=int(microseconds * 3.6e6), transcendentals=0)


def call_params(collective_id, limit=None):
    return pltpu.CompilerParams(
        collective_id=collective_id, has_side_effects=True, vmem_limit_bytes=limit
    )


def row_gather_start(src, out, me, wsh, send, recv):
    place = lax.rem(me, 8)
    copies = []
    for at, (dx, dk) in enumerate(((1, 0), (3, 0), (0, 1))):
        copy = remote(
            src, out.at[place], send.at[at], recv.at[at], shifted(me, 0, 0, dx, dk), wsh
        )
        copy.start()
        copies.append(copy)
    return copies


def row_gather_finish(out, me, wsh, copies, send, recv):
    partner = shifted(me, 0, 0, 0, 1)
    half = out.shape[1] // 2
    onward = []
    forwards = []
    for at, dx in enumerate((1, 3)):
        copies[at].wait_recv()
        from_place = lax.rem(shifted(me, 0, 0, 4 - dx, 0), 8)
        part = out.at[from_place, pl.ds(at * half, half)]
        step = remote(part, part, send.at[3 + at], recv.at[3 + at], shifted(me, 0, 0, dx, 0), wsh)
        step.start()
        onward.append(step)
        block = out.at[from_place]
        forward = remote(block, block, send.at[5 + at], recv.at[5 + at], partner, wsh)
        forward.start()
        forwards.append(forward)
    far = lax.rem(shifted(me, 0, 0, 2, 0), 8)
    for at in (0, 1):
        onward[at].wait_recv()
        part = out.at[far, pl.ds(at * half, half)]
        forward = remote(part, part, send.at[7 + at], recv.at[7 + at], partner, wsh)
        forward.start()
        forwards.append(forward)
    copies[2].wait_recv()
    for copy in copies + onward:
        copy.wait_send()
    for forward in forwards:
        forward.wait()


def gather_first(weights, tokens, small, routes, cotangent):
    def body(w_in, t_in, s_in, r_in, c_in, w_out, t_out, s_out, r_out, c_out, wide, row_s, row_r, pair, local):
        me, wsh = lax.axis_index("ctx"), lax.axis_index("wsh")
        core = lax.rem(me, 2)
        place = lax.rem(me, 8)

        def target(step):
            return shifted(
                me, lax.div(step, 16), lax.rem(lax.div(step, 8), 2), lax.rem(lax.div(step, 2), 4), lax.rem(step, 2)
            )

        barrier, amount = greet_many(64, lambda step: (target(step), wsh))
        locals_ = [
            pltpu.make_async_copy(t_in, t_out.at[place], local.at[0]),
            pltpu.make_async_copy(w_in.at[place], w_out.at[me], local.at[1]),
            pltpu.make_async_copy(s_in, s_out.at[me], local.at[2]),
            pltpu.make_async_copy(r_in, r_out.at[core], local.at[3]),
            pltpu.make_async_copy(c_in, c_out.at[core], local.at[4]),
        ]
        for copy in locals_:
            copy.start()
        pl.semaphore_wait(barrier, amount)
        row_copies = row_gather_start(t_in, t_out, me, wsh, row_s, row_r)

        def send(step, carried):
            turned = lax.rem(step * 13, 64)
            ctx = target(turned)
            remote(s_in, s_out.at[me], wide.at[0], wide.at[1], ctx, wsh).start()
            remote(w_in.at[lax.rem(ctx, 8)], w_out.at[me], wide.at[2], wide.at[3], ctx, wsh).start()
            return carried

        lax.fori_loop(1, 64, send, 0)
        partner = shifted(me, 0, 0, 0, 1)
        pair_copies = [
            remote(r_in, r_out.at[core], pair.at[0], pair.at[1], partner, wsh),
            remote(c_in, c_out.at[core], pair.at[2], pair.at[3], partner, wsh),
        ]
        for copy in pair_copies:
            copy.start()
        row_gather_finish(t_out, me, wsh, row_copies, row_s, row_r)
        for copy in pair_copies:
            copy.wait()
        for copy in locals_:
            copy.wait()
        for at, out in ((0, s_out), (2, w_out)):
            rest = out.at[pl.ds(0, 63)]
            done = remote(rest, rest, wide.at[at], wide.at[at + 1], partner, wsh)
            done.wait_send()
            done.wait_recv()

    sds = jax.ShapeDtypeStruct
    return pl.pallas_call(
        body,
        out_shape=(
            sds((64,) + weights.shape[1:], weights.dtype),
            sds((8,) + tokens.shape, tokens.dtype),
            sds((64,) + small.shape, small.dtype),
            sds((2,) + routes.shape, routes.dtype),
            sds((2,) + cotangent.shape, cotangent.dtype),
        ),
        in_specs=[ANY] * 5,
        out_specs=[ANY] * 5,
        scratch_shapes=[DMA((4,)), DMA((9,)), DMA((9,)), DMA((4,)), DMA((5,))],
        compiler_params=call_params(0),
        name="gather_first",
        cost_estimate=cost(60),
    )(weights, tokens, small, routes, cotangent)


def gather_row(block, collective_id):
    def body(src, out, row_s, row_r, local):
        me, wsh = lax.axis_index("ctx"), lax.axis_index("wsh")
        barrier, amount = greet([(shifted(me, 0, 0, dx, dk), wsh) for dx, dk in ((1, 0), (3, 0), (0, 1))])
        mine = pltpu.make_async_copy(src, out.at[lax.rem(me, 8)], local)
        mine.start()
        pl.semaphore_wait(barrier, amount)
        copies = row_gather_start(src, out, me, wsh, row_s, row_r)
        row_gather_finish(out, me, wsh, copies, row_s, row_r)
        mine.wait()

    return pl.pallas_call(
        body,
        out_shape=jax.ShapeDtypeStruct((8,) + block.shape, block.dtype),
        in_specs=[ANY],
        out_specs=ANY,
        scratch_shapes=[DMA((9,)), DMA((9,)), DMA],
        compiler_params=call_params(collective_id),
        name="gather_row",
        cost_estimate=cost(26),
    )(block)


COLUMN_STEPS = ((1, 0), (3, 0), (0, 1), (2, 0), (1, 1), (3, 1), (2, 1))


def gather_keys(rows, collective_id):
    count = rows.shape[0]
    half = count // 2

    def body(src, out, send, recv, local):
        me, wsh = lax.axis_index("ctx"), lax.axis_index("wsh")
        core = lax.rem(me, 2)
        group = lax.div(me, 8)
        partner = shifted(me, 0, 0, 0, 1)
        peers = [shifted(me, dz, dy, 0, 0) for dz, dy in COLUMN_STEPS]
        barrier, amount = greet([(peer, wsh) for peer in peers + [partner]])
        mine = pltpu.make_async_copy(src, out.at[group], local)
        mine.start()
        pl.semaphore_wait(barrier, amount)
        my_half = pl.ds(pl.multiple_of(core * half, half), half)
        copies = []
        for at, peer in enumerate(peers):
            copy = remote(src.at[my_half], out.at[group, my_half], send.at[at], recv.at[at], peer, wsh)
            copy.start()
            copies.append(copy)
        forwards = []
        for at, (dz, dy) in enumerate(COLUMN_STEPS):
            copies[at].wait_recv()
            origin = lax.div(shifted(me, 4 - dz, 2 - dy, 0, 0), 8)
            part = out.at[origin, my_half]
            forward = remote(part, part, send.at[7 + at], recv.at[7 + at], partner, wsh)
            forward.start()
            forwards.append(forward)
        for copy in copies:
            copy.wait_send()
        for forward in forwards:
            forward.wait()
        mine.wait()

    return pl.pallas_call(
        body,
        out_shape=jax.ShapeDtypeStruct((8,) + rows.shape, rows.dtype),
        in_specs=[ANY],
        out_specs=ANY,
        scratch_shapes=[DMA((14,)), DMA((14,)), DMA],
        compiler_params=call_params(collective_id),
        name="gather_keys",
        cost_estimate=cost(30),
    )(rows)


def reduce_row(parts, collective_id, both, extra=None):
    _, rows, width = parts.shape
    block = (rows, width)
    pieces = 2
    columns = width // pieces
    has_extra = extra is not None

    def body(*refs):
        refs = list(refs)
        src = refs.pop(0)
        src2 = refs.pop(0) if has_extra else None
        out = refs.pop(0)
        out2 = refs.pop(0) if has_extra else None
        arrived, summed, landed, swapped, total, send, recv, local = refs[:8]
        me, wsh = lax.axis_index("ctx"), lax.axis_index("wsh")
        other = 1 - wsh
        core = lax.rem(me, 2)
        _, _, x, _ = coords(me)
        partner = shifted(me, 0, 0, 0, 1)
        peers = [shifted(me, 0, 0, dx, 0) for dx in (1, 2, 3)]
        barrier, amount = greet([(peer, wsh) for peer in peers + [partner]] + [(me, other)])
        pl.semaphore_wait(barrier, amount)
        spans = [pl.ds(piece * columns, columns) for piece in range(pieces)]
        everything = pl.ds(0, rows)
        first = []
        for piece, span in enumerate(spans):
            for at, dx in enumerate((2, 1, 3, 0)):
                chip = lax.rem(x + dx, 4)
                copy = remote(
                    src.at[chip * 2 + 1 - core, everything, span],
                    arrived.at[at, everything, span],
                    send.at[piece, at],
                    recv.at[piece, at],
                    partner,
                    wsh,
                )
                copy.start()
                first.append(copy)
        if has_extra:
            arrived2, swapped2 = refs[8:]
            give2 = remote(src2.at[1 - core], arrived2, send.at[0, 8], recv.at[0, 8], partner, wsh)
            give2.start()
        second = []
        for piece, span in enumerate(spans):
            for at, dx in enumerate((2, 1, 3)):
                chip = lax.rem(x + dx, 4)
                first[piece * 4 + at].wait_recv()
                summed[at, :, span] = (
                    src[chip * 2 + core, :, span].astype(F32) + arrived[at, :, span].astype(F32)
                ).astype(BF)
                copy = remote(
                    summed.at[at, everything, span],
                    landed.at[at, everything, span],
                    send.at[piece, 4 + at],
                    recv.at[piece, 4 + at],
                    shifted(me, 0, 0, dx, 0),
                    wsh,
                )
                copy.start()
                second.append(copy)
            first[piece * 4 + 3].wait_recv()
            total[:, span] = src[x * 2 + core, :, span].astype(F32) + arrived[3, :, span].astype(F32)
        if has_extra:
            give2.wait()
            swapped2[0] = (src2[core].astype(F32) + arrived2[...].astype(F32)).astype(BF)
            swap2 = remote(swapped2.at[0], swapped2.at[1], send.at[1, 8], recv.at[1, 8], me, other)
            swap2.start()
        swaps = []
        for piece, span in enumerate(spans):
            for at in (1, 2, 0):
                second[piece * 3 + at].wait_recv()
            swapped[0, :, span] = (
                total[:, span]
                + landed[0, :, span].astype(F32)
                + landed[1, :, span].astype(F32)
                + landed[2, :, span].astype(F32)
            ).astype(BF)
            swap = remote(
                swapped.at[0, everything, span],
                swapped.at[1, everything, span],
                send.at[piece, 7],
                recv.at[piece, 7],
                me,
                other,
            )
            swap.start()
            swaps.append(swap)
        if has_extra:
            swap2.wait()
            out2[...] = swapped2[0].astype(F32) + swapped2[1].astype(F32)
        for piece, span in enumerate(spans):
            swaps[piece].wait()
            if both:
                total[:, span] = swapped[0, :, span].astype(F32) + swapped[1, :, span].astype(F32)
            else:
                out[:, span] = swapped[0, :, span].astype(F32) + swapped[1, :, span].astype(F32)
        if both:
            keep = pltpu.make_async_copy(total, out.at[core], local)
            keep.start()
            give = remote(total, out.at[core], send.at[0, 9], recv.at[0, 9], partner, wsh)
            give.start()
            give.wait()
            keep.wait()
        for copy in first + second:
            copy.wait_send()

    shapes = [jax.ShapeDtypeStruct((2,) + block if both else block, F32)]
    scratch = [
        pltpu.VMEM((4,) + block, BF),
        pltpu.VMEM((3,) + block, BF),
        pltpu.VMEM((3,) + block, BF),
        pltpu.VMEM((2,) + block, BF),
        pltpu.VMEM(block, F32),
        DMA((pieces, 10)),
        DMA((pieces, 10)),
        DMA,
    ]
    operands = [parts]
    if has_extra:
        shapes.append(jax.ShapeDtypeStruct(block, F32))
        scratch += [pltpu.VMEM(block, BF), pltpu.VMEM((2,) + block, BF)]
        operands.append(extra)
    return pl.pallas_call(
        body,
        out_shape=shapes,
        in_specs=[VMEM] * len(operands),
        out_specs=[VMEM] * len(operands),
        scratch_shapes=scratch,
        compiler_params=call_params(collective_id, 40 * 1024 * 1024),
        name="reduce_row",
        cost_estimate=cost(40),
    )(*operands)


def reduce_chip(parts, extra, collective_id):
    _, rows, width = parts.shape
    extra_block = None if extra is None else extra.shape[1:]

    def body(*refs):
        if extra is None:
            src, out, arrived, swapped, total, send, recv = refs
        else:
            src, src2, out, out2, arrived, swapped, total, arrived2, swapped2, send, recv = refs
        me, wsh = lax.axis_index("ctx"), lax.axis_index("wsh")
        other = 1 - wsh
        core = lax.rem(me, 2)
        partner = shifted(me, 0, 0, 0, 1)
        barrier, amount = greet([(partner, wsh), (me, other)])
        pl.semaphore_wait(barrier, amount)
        give = remote(src.at[1 - core], arrived, send.at[0], recv.at[0], partner, wsh)
        give.start()
        if extra is not None:
            give2 = remote(src2.at[1 - core], arrived2, send.at[2], recv.at[2], partner, wsh)
            give2.start()
        give.wait()
        swapped[0] = (src[core].astype(F32) + arrived[...].astype(F32)).astype(BF)
        swap = remote(swapped.at[0], swapped.at[1], send.at[1], recv.at[1], me, other)
        swap.start()
        if extra is not None:
            give2.wait()
            swapped2[0] = src2[core] + arrived2[...]
            swap2 = remote(swapped2.at[0], swapped2.at[1], send.at[3], recv.at[3], me, other)
            swap2.start()
            swap2.wait()
            out2[...] = swapped2[0] + swapped2[1]
        swap.wait()
        out[...] = swapped[0].astype(F32) + swapped[1].astype(F32)

    sds = jax.ShapeDtypeStruct
    block = (rows, width)
    shapes = [sds(block, F32)]
    scratch = [pltpu.VMEM(block, BF), pltpu.VMEM((2,) + block, BF), pltpu.VMEM(block, F32)]
    operands = [parts]
    if extra is not None:
        shapes.append(sds(extra_block, F32))
        scratch += [pltpu.VMEM(extra_block, F32), pltpu.VMEM((2,) + extra_block, F32)]
        operands.append(extra)
    scratch += [DMA((4,)), DMA((4,))]
    return pl.pallas_call(
        body,
        out_shape=shapes,
        in_specs=[VMEM] * len(operands),
        out_specs=[VMEM] * len(operands),
        scratch_shapes=scratch,
        compiler_params=call_params(collective_id, 40 * 1024 * 1024),
        name="reduce_chip",
        cost_estimate=cost(17),
    )(*operands)


def reduce_keys(parts, collective_id):
    _, groups, _, rows, width = parts.shape

    def body(src, out, arrived, mid, beside, summed, landed, send, recv):
        me, wsh = lax.axis_index("ctx"), lax.axis_index("wsh")
        core = lax.rem(me, 2)
        _, _, x, _ = coords(me)
        side = lax.rem(x, 2)
        partner = shifted(me, 0, 0, 0, 1)
        neighbour = me + 2 - 4 * side
        steps = COLUMN_STEPS + ((0, 0),)
        peers = [shifted(me, dz, dy, 0, 0) for dz, dy in steps]
        barrier, amount = greet([(peer, wsh) for peer in peers[:-1] + [partner, neighbour]])
        pl.semaphore_wait(barrier, amount)
        first = []
        for at, peer in enumerate(peers):
            group = lax.div(peer, 8)
            for turn, b in enumerate((1 - side, side)):
                copy = remote(
                    src.at[1 - core, group, b],
                    arrived.at[turn, at],
                    send.at[turn, at],
                    recv.at[turn, at],
                    partner,
                    wsh,
                )
                copy.start()
                first.append(copy)
        across = []
        for at, peer in enumerate(peers):
            group = lax.div(peer, 8)
            first[2 * at].wait_recv()
            mid[at] = (src[core, group, 1 - side].astype(F32) + arrived[0, at].astype(F32)).astype(BF)
            copy = remote(mid.at[at], beside.at[at], send.at[2, at], recv.at[2, at], neighbour, wsh)
            copy.start()
            across.append(copy)
        last = []
        for at, peer in enumerate(peers):
            group = lax.div(peer, 8)
            first[2 * at + 1].wait_recv()
            across[at].wait_recv()
            value = (
                src[core, group, side].astype(F32)
                + arrived[1, at].astype(F32)
                + beside[at].astype(F32)
            )
            if at == groups - 1:
                out[...] = value
            else:
                summed[at] = value.astype(BF)
                copy = remote(summed.at[at], landed.at[at], send.at[3, at], recv.at[3, at], peer, wsh)
                copy.start()
                last.append(copy)
        for at, copy in enumerate(last):
            copy.wait_recv()
            out[...] += landed[at].astype(F32)
        for copy in first + across + last:
            copy.wait_send()

    block = (rows, width)
    return pl.pallas_call(
        body,
        out_shape=jax.ShapeDtypeStruct(block, F32),
        in_specs=[VMEM],
        out_specs=VMEM,
        scratch_shapes=[
            pltpu.VMEM((2, groups) + block, BF),
            pltpu.VMEM((groups,) + block, BF),
            pltpu.VMEM((groups,) + block, BF),
            pltpu.VMEM((groups,) + block, BF),
            pltpu.VMEM((groups,) + block, BF),
            DMA((4, groups)),
            DMA((4, groups)),
        ],
        compiler_params=call_params(collective_id, 40 * 1024 * 1024),
        name="reduce_keys",
        cost_estimate=cost(40),
    )(parts)


def exchange(arrays, collective_id):
    amount = len(arrays)

    def body(*refs):
        ins, outs = refs[:amount], refs[amount : 2 * amount]
        send, recv, local = refs[2 * amount :]
        me, wsh = lax.axis_index("ctx"), lax.axis_index("wsh")
        chip = lax.div(me, 2)

        def target(step):
            dy = lax.rem(lax.div(step, 4), 2)
            return shifted(me, lax.div(step, 8), dy, lax.rem(step, 4), 0), lax.rem(wsh + dy, 2)

        barrier, count = greet_many(32, target)
        locals_ = []
        for at in range(amount):
            copy = pltpu.make_async_copy(ins[at].at[chip], outs[at].at[chip], local.at[at])
            copy.start()
            locals_.append(copy)
        pl.semaphore_wait(barrier, count)

        def one(step, carried):
            ctx, side = target(lax.rem(step * 13, 32))
            for at in range(amount):
                remote(
                    ins[at].at[lax.div(ctx, 2)], outs[at].at[chip], send.at[at], recv.at[at], ctx, side
                ).start()
            return carried

        lax.fori_loop(1, 32, one, 0)
        for copy in locals_:
            copy.wait()
        for at in range(amount):
            rest = outs[at].at[pl.ds(0, 31)]
            done = remote(rest, rest, send.at[at], recv.at[at], me, wsh)
            done.wait_send()
            done.wait_recv()

    return pl.pallas_call(
        body,
        out_shape=[jax.ShapeDtypeStruct(a.shape, a.dtype) for a in arrays],
        in_specs=[ANY] * amount,
        out_specs=[ANY] * amount,
        scratch_shapes=[DMA((amount,)), DMA((amount,)), DMA((amount,))],
        compiler_params=call_params(collective_id),
        name="exchange",
        cost_estimate=cost(48),
    )(*arrays)


def exchange_behind(value):
    groups = []
    for core in range(2):
        for parity in range(2):
            groups.append(
                [(chip * 2 + core) * 2 + (parity + chip // 4) % 2 for chip in range(32)]
            )
    return lax.all_to_all(
        value, ("ctx", "wsh"), split_axis=0, concat_axis=0, tiled=True, axis_index_groups=groups
    )


def natural_order(inverse, kv_ref, keys, values, transposed):
    def one(block, carried):
        rows = kv_ref[pl.ds(pl.multiple_of(inverse[block] * BLK, BLK), BLK), :]
        at = pl.ds(pl.multiple_of(block * BLK, BLK), BLK)
        keys[at, :] = rows[:, :HEAD_WIDTH]
        values[at, :] = rows[:, HEAD_WIDTH:]
        return carried

    lax.fori_loop(0, kv_ref.shape[0] // BLK, one, 0)
    source, turned = transposed

    def turn(chunk, carried):
        at = pl.ds(pl.multiple_of(chunk * CHUNK, CHUNK), CHUNK)
        turned[:, at] = source[at, :].T
        return carried

    lax.fori_loop(0, kv_ref.shape[0] // CHUNK, turn, 0)


def stacked(ref, first, second):
    rows = [ref[pl.ds(pl.multiple_of(at * BLK, BLK), BLK), :] for at in (first, second)]
    return jnp.concatenate(
        [rows[0][:, :HEAD_WIDTH], rows[0][:, HEAD_WIDTH:], rows[1][:, :HEAD_WIDTH], rows[1][:, HEAD_WIDTH:]],
        axis=0,
    )


def unstacked(ref, first, second, value):
    for at, begin in ((first, 0), (second, 2 * BLK)):
        ref[pl.ds(pl.multiple_of(at * BLK, BLK), BLK), :] = jnp.concatenate(
            [value[begin : begin + BLK], value[begin + BLK : begin + 2 * BLK]], axis=1
        )


def three_loops(step, low, inner_low, inner_high, high, chunk, state):
    state = lax.fori_loop(low[step], inner_low[step], functools.partial(chunk, True), state)
    state = lax.fori_loop(inner_low[step], inner_high[step], functools.partial(chunk, False), state)
    return lax.fori_loop(inner_high[step], high[step], functools.partial(chunk, True), state)


def kept(scores, at, q_pos, q_start):
    k_pos = at + lax.broadcasted_iota(jnp.int32, scores.shape, 0)
    return jnp.where((k_pos <= q_pos) & (k_pos >= q_start), scores, MASKED)


SCORE_SCALE = 1.0 / math.sqrt(HEAD_WIDTH)
TWO_SCALE = SCORE_SCALE / math.log(2.0)


def forward_kernel(order, low, inner_low, inner_high, high, inverse, q_ref, kv_ref, pos_ref, start_ref, out_ref, lse_ref, keys, values, values_t, acc):
    step = pl.program_id(0)

    @pl.when(step == 0)
    def _():
        natural_order(inverse, kv_ref, keys, values, (values, values_t))

    first, second = order[2 * step], order[2 * step + 1]
    q_t = stacked(q_ref, first, second).astype(F32).T.astype(BF)
    q_pos, q_start = pos_ref[0], start_ref[0]
    width = 4 * BLK
    acc[...] = jnp.zeros_like(acc)

    def chunk(masked, index, carried):
        highest, total = carried
        at = pl.multiple_of(index * CHUNK, CHUNK)
        scores = matmul(keys[pl.ds(at, CHUNK), :], q_t)
        if masked:
            scores = kept(scores, at, q_pos, q_start)
        top = jnp.maximum(highest, jnp.max(scores, axis=0, keepdims=True))
        probs = jnp.exp2((scores - top) * TWO_SCALE)
        fade = jnp.exp2((highest - top) * TWO_SCALE)
        acc[...] = acc[...] * fade + matmul(values_t[:, pl.ds(at, CHUNK)], probs.astype(BF))
        return top, total * fade + jnp.sum(probs, axis=0, keepdims=True)

    highest, total = three_loops(
        step,
        low,
        inner_low,
        inner_high,
        high,
        chunk,
        (jnp.full((1, width), MASKED, F32), jnp.zeros((1, width), F32)),
    )
    lse_ref[0] = highest * TWO_SCALE + jnp.log2(total)
    unstacked(out_ref, first, second, (acc[...] / total).T.astype(BF))


def attend(plan, queries, kv, positions, starts):
    rows = queries.shape[0]
    steps = rows // (2 * BLK)
    everything = pl.BlockSpec(queries.shape, lambda i, *_: (0, 0))
    strip = pl.BlockSpec((1, 1, 4 * BLK), lambda i, *_: (i, 0, 0))
    sds = jax.ShapeDtypeStruct
    return pl.pallas_call(
        forward_kernel,
        out_shape=(sds(queries.shape, BF), sds((steps, 1, 4 * BLK), F32)),
        grid_spec=pltpu.PrefetchScalarGridSpec(
            num_scalar_prefetch=6,
            grid=(steps,),
            in_specs=[everything, pl.BlockSpec(kv.shape, lambda i, *_: (0, 0)), strip, strip],
            out_specs=[everything, strip],
            scratch_shapes=[
                pltpu.VMEM((kv.shape[0], HEAD_WIDTH), BF),
                pltpu.VMEM((kv.shape[0], HEAD_WIDTH), BF),
                pltpu.VMEM((HEAD_WIDTH, kv.shape[0]), BF),
                pltpu.VMEM((HEAD_WIDTH, 4 * BLK), F32),
            ],
        ),
        compiler_params=pltpu.CompilerParams(vmem_limit_bytes=50 * 1024 * 1024),
        name="attend",
        cost_estimate=cost(17),
    )(*plan, queries, kv, positions, starts)


def backward_kernel(order, low, inner_low, inner_high, high, inverse, q_ref, do_ref, kv_ref, pos_ref, start_ref, lse_ref, dot_ref, dq_ref, dkv_ref, keys, values, keys_t, d_keys, d_values, acc):
    step = pl.program_id(0)

    @pl.when(step == 0)
    def _():
        natural_order(inverse, kv_ref, keys, values, (keys, keys_t))
        d_keys[...] = jnp.zeros_like(d_keys)
        d_values[...] = jnp.zeros_like(d_values)

    first, second = order[2 * step], order[2 * step + 1]
    q = stacked(q_ref, first, second)
    d_out = stacked(do_ref, first, second)
    q_t = q.astype(F32).T.astype(BF)
    d_out_t = d_out.astype(F32).T.astype(BF)
    q_pos, q_start = pos_ref[0], start_ref[0]
    lse, dots = lse_ref[0], dot_ref[0]
    acc[...] = jnp.zeros_like(acc)

    def chunk(masked, index, carried):
        at = pl.multiple_of(index * CHUNK, CHUNK)
        here = pl.ds(at, CHUNK)
        scores = matmul(keys[here, :], q_t)
        if masked:
            scores = kept(scores, at, q_pos, q_start)
        probs = jnp.exp2(scores * TWO_SCALE - lse)
        d_probs = matmul(values[here, :], d_out_t)
        d_scores = (probs * (d_probs - dots)).astype(BF)
        d_values[here, :] += matmul(probs.astype(BF), d_out)
        d_keys[here, :] += matmul(d_scores, q)
        acc[...] += matmul(keys_t[:, here], d_scores)
        return carried

    three_loops(step, low, inner_low, inner_high, high, chunk, 0)
    unstacked(dq_ref, first, second, (acc[...] * SCORE_SCALE).T)

    @pl.when(step == pl.num_programs(0) - 1)
    def _():
        def one(block, carried):
            dealt = inverse[block]
            group, inside = dealt // 16, dealt % 16
            half, rest = inside // 8, inside % 8
            at = pl.ds(pl.multiple_of(block * BLK, BLK), BLK)
            to = pl.ds(pl.multiple_of(rest * BLK, BLK), BLK)
            dkv_ref[half, group, 0, to, :] = (d_keys[at, :] * SCORE_SCALE).astype(BF)
            dkv_ref[half, group, 1, to, :] = d_values[at, :].astype(BF)
            return carried

        lax.fori_loop(0, kv_ref.shape[0] // BLK, one, 0)


def attend_back(plan, queries, d_heads, kv, positions, starts, lse, dots):
    rows = queries.shape[0]
    total = kv.shape[0]
    steps = rows // (2 * BLK)
    everything = pl.BlockSpec(queries.shape, lambda i, *_: (0, 0))
    strip = pl.BlockSpec((1, 1, 4 * BLK), lambda i, *_: (i, 0, 0))
    sds = jax.ShapeDtypeStruct
    dkv_shape = (2, total // rows, 2, rows // 2, HEAD_WIDTH)
    return pl.pallas_call(
        backward_kernel,
        out_shape=(sds(queries.shape, F32), sds(dkv_shape, BF)),
        grid_spec=pltpu.PrefetchScalarGridSpec(
            num_scalar_prefetch=6,
            grid=(steps,),
            in_specs=[everything, everything, pl.BlockSpec(kv.shape, lambda i, *_: (0, 0)), strip, strip, strip, strip],
            out_specs=[everything, pl.BlockSpec(dkv_shape, lambda i, *_: (0, 0, 0, 0, 0))],
            scratch_shapes=[
                pltpu.VMEM((total, HEAD_WIDTH), BF),
                pltpu.VMEM((total, HEAD_WIDTH), BF),
                pltpu.VMEM((HEAD_WIDTH, total), BF),
                pltpu.VMEM((total, HEAD_WIDTH), F32),
                pltpu.VMEM((total, HEAD_WIDTH), F32),
                pltpu.VMEM((HEAD_WIDTH, 4 * BLK), F32),
            ],
        ),
        compiler_params=pltpu.CompilerParams(vmem_limit_bytes=55 * 1024 * 1024),
        name="attend_back",
        cost_estimate=cost(24),
    )(*plan, queries, d_heads, kv, positions, starts, lse, dots)


def after(value, earlier):
    return lax.optimization_barrier((value, earlier))


def lanes_to(row, lanes=128):
    return jnp.pad(row, ((0, 0),) * (row.ndim - 1) + ((0, lanes - row.shape[-1]),))


def local(
    tokens,
    cotangent,
    seq_lengths,
    block_order,
    routes,
    w_query,
    key_weight,
    value_weight,
    w_out,
    gain_attn,
    gain_query,
    gain_key,
    gain_ffn,
    w_router,
    w_gate,
    w_up,
    w_down,
):
    rows = tokens.shape[0]
    width = tokens.shape[1]
    experts = w_router.shape[1]
    block_count = block_order.shape[0]
    wsh = lax.axis_index("wsh")
    me = lax.axis_index("ctx")
    core = lax.rem(me, 2)
    place = lax.rem(me, 8)
    group = lax.div(me, 8)
    row_tokens = 8 * rows
    row_blocks = row_tokens // BLK

    def of_mine(weight):
        return to_low(lax.dynamic_index_in_dim(weight, wsh, 0, keepdims=False))

    def of_other(weight):
        return to_low(lax.dynamic_index_in_dim(weight, 1 - wsh, 0, keepdims=False))

    def swap(value):
        return lax.ppermute(value, "wsh", [(0, 1), (1, 0)])

    depth = w_query.shape[0]
    q_part = to_low(w_query).reshape(depth, 8, 256).transpose(1, 0, 2)
    k_part = jnp.repeat(to_low(key_weight).reshape(depth, 2, 128).transpose(1, 0, 2), 4, axis=0)
    v_part = jnp.repeat(to_low(value_weight).reshape(depth, 2, 128).transpose(1, 0, 2), 4, axis=0)
    w_pack = jnp.concatenate([q_part, k_part, v_part], axis=2)
    small = jnp.concatenate(
        [lanes_to(gain_attn[None, :]), lanes_to(gain_ffn[None, :]), jnp.zeros((6, 128), F32)], axis=0
    )
    w_all, row_rows, small_all, chip_routes, chip_cot = gather_first(
        w_pack, tokens, small, routes.T, cotangent
    )
    other_gate, small_all = after(of_other(w_gate), small_all)
    gate_back = swap(other_gate)
    w_qkv = w_all.reshape(width, 512)
    g_attn = to_low(small_all[:, 0, :depth].reshape(width)).astype(F32)
    g_ffn = to_low(small_all[:, 1, :depth].reshape(width)).astype(F32)
    g_query = rounded(gain_query)
    g_key = rounded(gain_key)

    o_part = to_low(w_out).T.reshape(depth, 8, 256).transpose(1, 0, 2)
    r_part = jnp.broadcast_to(to_low(w_router)[None], (8, depth, experts))
    late_pack = jnp.tile(jnp.concatenate([o_part, r_part], axis=2), (8, 1, 1))
    late_pack, small_all = after(late_pack, small_all)
    late_all = lax.all_to_all(late_pack, "ctx", split_axis=0, concat_axis=0, tiled=True).reshape(width, 384)

    route_rows = chip_routes.transpose(0, 2, 1)
    hits = jnp.any(
        route_rows[:, :, :, None] == jnp.arange(experts, dtype=jnp.int32)[None, None, None, :], axis=2
    )
    before = jnp.tril(jnp.ones((rows, rows), BF), -1)
    ranks = jnp.einsum("ts,hse->hte", before, hits.astype(BF), preferred_element_type=F32).astype(jnp.int32)
    ranks = jnp.where(hits, ranks + jnp.array([0, CAP], jnp.int32)[:, None, None], -1)
    hits = hits.reshape(2 * rows, experts)
    chips = experts // 4
    chip_ids = jnp.arange(chips, dtype=jnp.int32)
    quarter = core * 2 + (wsh + chip_ids // 4 + lax.div(me, 8)) % 2

    def my_quarter(value):
        by_chip = value.reshape(2 * rows, experts).T.reshape(chips, 4, 2 * rows)
        two = lax.dynamic_slice_in_dim(by_chip, core * 2, 2, 1)
        return jnp.where((quarter % 2 == 0)[:, None], two[:, 0], two[:, 1])

    my_ranks = my_quarter(ranks)
    slots = 2 * CAP
    pick = my_ranks[:, None, :] == jnp.arange(slots, dtype=jnp.int32)[None, :, None]
    pick_low = pick.astype(BF).reshape(chips * slots, 2 * rows)
    cot_rows = matmul(pick_low, chip_cot.reshape(2 * rows, width)).astype(BF)
    my_blocks = lax.dynamic_slice_in_dim(block_order, group * row_blocks, row_blocks, 0)
    positions = (my_blocks[:, None] * BLK + jnp.arange(BLK, dtype=jnp.int32)[None, :]).reshape(row_tokens)
    starts = seq_starts(positions, seq_lengths)
    cosine, sine_tab = rope_tables(positions - starts)
    inverse_order = (
        jnp.zeros((block_count,), jnp.int32)
        .at[block_order]
        .set(jnp.arange(block_count, dtype=jnp.int32))
    )
    smaller = jnp.sum((my_blocks[None, :] < my_blocks[:, None]).astype(jnp.int32), axis=1)
    order = jnp.sum(
        jnp.where(
            smaller[None, :] == jnp.arange(row_blocks, dtype=jnp.int32)[:, None],
            jnp.arange(row_blocks, dtype=jnp.int32)[None, :],
            0,
        ),
        axis=1,
    )
    block_starts = starts.reshape(row_blocks, BLK)
    pair_blocks = jnp.take(my_blocks, order).reshape(-1, 2)
    low = jnp.min(jnp.take(block_starts[:, 0], order).reshape(-1, 2), axis=1) // CHUNK
    high = jnp.max(pair_blocks, axis=1) * BLK // CHUNK + 1
    last_start = jnp.max(jnp.take(block_starts[:, BLK - 1], order).reshape(-1, 2), axis=1)
    inner_low = jnp.clip((last_start + CHUNK - 1) // CHUNK, low, high)
    inner_high = jnp.clip((jnp.min(pair_blocks, axis=1) * BLK + 1) // CHUNK, inner_low, high)
    plan = (order, low, inner_low, inner_high, high, inverse_order)

    def strips(per_token):
        by_block = jnp.take(per_token.reshape(row_blocks, BLK), order, axis=0).reshape(-1, 2, 1, BLK)
        return jnp.broadcast_to(by_block, (row_blocks // 2, 2, 2, BLK)).reshape(-1, 1, 4 * BLK)

    q_pos, q_start = strips(positions), strips(starts)

    stream = row_rows.reshape(row_tokens, width).astype(F32)
    inverse_one = inverse_root(stream)
    hidden_one = to_low(stream * inverse_one * g_attn)
    qkv = matmul(hidden_one, w_qkv)
    q_pre = qkv[:, :256].reshape(row_tokens, 2, HEAD_WIDTH)
    k_pre = qkv[:, 256:384]
    q_inverse = inverse_root(q_pre)
    k_inverse = inverse_root(k_pre)
    queries = to_low(rotate(q_pre * q_inverse * g_query, cosine[:, None], sine_tab[:, None]))
    queries = queries.reshape(row_tokens, 256)
    keys = to_low(rotate(k_pre * k_inverse * g_key, cosine, sine_tab))
    kv = jnp.concatenate([keys, to_low(qkv[:, 384:])], axis=1)
    (gate_back, late_all), kv = after((gate_back, late_all), kv)
    wo_t = late_all[:, :256]
    wr = late_all[:, 256:]
    kv_all = gather_keys(kv, 1).reshape(block_count * BLK, 256)
    (cot_rows, other_up), kv_all = after((cot_rows, of_other(w_up)), kv_all)
    up_back = swap(other_up)
    cot_there = exchange_behind(cot_rows.reshape(chips, slots, width)).reshape(chips * slots, width)
    heads, lse = attend(plan, queries, kv_all, q_pos, q_start)

    attn_parts = to_low(times_transposed(heads, wo_t)).reshape(8, rows, width)
    (up_back, cot_there, other_down), attn_parts = after((up_back, cot_there, of_other(w_down)), attn_parts)
    down_back = swap(other_down)
    attn_total = reduce_row(attn_parts, 2, True)[0].reshape(2 * rows, width)
    chip_stream = lax.dynamic_slice_in_dim(stream, (place - core) * rows, 2 * rows, 0)
    chip_residual = chip_stream + attn_total
    chip_inverse_two = inverse_root(chip_residual)
    chip_hidden = to_low(chip_residual * chip_inverse_two * g_ffn)
    logits = matmul(chip_hidden, wr)
    masked_logits = jnp.where(hits, logits, MASKED)
    gate_exps = jnp.where(
        hits, jnp.exp(masked_logits - jnp.max(masked_logits, axis=-1, keepdims=True)), 0.0
    )
    gates = gate_exps / jnp.sum(gate_exps, axis=-1, keepdims=True)

    def my_rows(value):
        return lax.dynamic_slice_in_dim(value, core * rows, rows, 0)

    out_rows = matmul(pick_low, chip_hidden).astype(BF).reshape(chips, slots, width)
    my_gates = my_quarter(gates)
    slot_gates = jnp.sum(jnp.where(pick, my_gates[:, None, :], 0.0), axis=2)
    gate_tile = jnp.pad(slot_gates[:, None, :], ((0, 0), (0, 7), (0, 128 - slots)))
    arrived, gate_there = exchange([out_rows, gate_tile], 3)
    arrived = arrived.reshape(chips * slots, width)
    gate_col = gate_there[:, 0, :slots].reshape(chips * slots, 1)
    d_pairs = to_low(gate_col * cot_there.astype(F32))
    gate_w = (of_mine(w_gate), gate_back)
    up_w = (of_mine(w_up), up_back)
    down_w = (of_mine(w_down), down_back)
    expert_out = 0.0
    d_rows = 0.0
    grads = []
    for gate_half, up_half, down_half in zip(gate_w, up_w, down_w):
        gate_pre = matmul(arrived, gate_half)
        up_pre = matmul(arrived, up_half)
        sigma = jax.nn.sigmoid(gate_pre)
        activated = to_low(gate_pre * sigma * up_pre)
        expert_out = expert_out + matmul(activated, down_half)
        d_act = times_transposed(d_pairs, down_half)
        grad_down = transposed_times(activated, d_pairs)
        d_gate_pre = to_low(d_act * up_pre * sigma * (1.0 + gate_pre * (1.0 - sigma)))
        d_up_pre = to_low(d_act * gate_pre * sigma)
        grad_gate = transposed_times(arrived, d_gate_pre)
        grad_up = transposed_times(arrived, d_up_pre)
        d_rows = (
            d_rows + times_transposed(d_gate_pre, gate_half) + times_transposed(d_up_pre, up_half)
        )
        grads.append((grad_gate, grad_up, grad_down))
    d_gate_slots = jnp.sum(expert_out * cot_there.astype(F32), axis=1).reshape(chips, 1, slots)
    d_gate_tile = jnp.pad(d_gate_slots, ((0, 0), (0, 7), (0, 128 - slots)))
    d_back, d_gate_back = exchange(
        [to_low(d_rows).reshape(chips, slots, width), d_gate_tile], 4
    )
    y_back = exchange_behind(to_low(gate_col * expert_out).reshape(chips, slots, width))
    swapped_grads = [swap(to_low(back)) for back in grads[1]]

    def collect(back):
        return to_low(transposed_times(pick_low, back.reshape(chips * slots, width))).reshape(2, rows, width)

    d_gate_slots = d_gate_back[:, 0, :slots]
    d_gates_mine = jnp.sum(jnp.where(pick, d_gate_slots[:, :, None], 0.0), axis=1)
    d_gates_part = jnp.where(
        jnp.arange(4, dtype=jnp.int32)[None, :, None] == quarter[:, None, None], d_gates_mine[:, None, :], 0.0
    ).reshape(experts, 2 * rows)
    d_gates_part = d_gates_part.T.reshape(2, rows, experts)
    d_hidden_moe, d_gates = reduce_chip(collect(d_back), d_gates_part, 5)
    residual = my_rows(chip_residual)

    own_gates = my_rows(gates)
    hidden_two = my_rows(chip_hidden)
    inverse_two = my_rows(chip_inverse_two)
    d_chosen = own_gates * (d_gates - jnp.sum(own_gates * d_gates, axis=-1, keepdims=True))
    d_logits = to_low(d_chosen)
    grad_router = transposed_times(hidden_two, d_logits)
    d_hidden_two = d_hidden_moe + times_transposed(d_logits, wr)
    d_res_norm, ffn_gain_terms = norm_back(residual, inverse_two, g_ffn, d_hidden_two)
    d_residual = cotangent.astype(F32) + d_res_norm
    gain_ffn_part = jnp.sum(ffn_gain_terms, axis=0)

    d_attn = gather_row(to_low(d_residual), 7).reshape(row_tokens, width)
    grad_out_t = transposed_times(d_attn, heads)
    d_heads = to_low(matmul(d_attn, wo_t))
    dots = jnp.sum(
        d_heads.astype(F32).reshape(row_tokens, 2, HEAD_WIDTH)
        * heads.astype(F32).reshape(row_tokens, 2, HEAD_WIDTH),
        axis=-1,
    )
    dot_strips = (
        jnp.take(dots.reshape(row_blocks, BLK, 2), order, axis=0)
        .transpose(0, 2, 1)
        .reshape(row_blocks // 2, 1, 4 * BLK)
    )
    early = jnp.concatenate(
        [
            to_low(grad_out_t[:, :128]).reshape(64, depth, 128),
            to_low(grad_out_t[:, 128:]).reshape(64, depth, 128),
            to_low(grad_router).reshape(64, depth, 128),
            jnp.pad(
                to_low(gain_ffn_part).reshape(64, 1, depth), ((0, 0), (0, 15), (0, 128 - depth))
            ),
        ],
        axis=1,
    )
    early = lax.all_to_all(early, "ctx", split_axis=0, concat_axis=0, tiled=True)
    y_back, d_heads = after(y_back, d_heads)
    d_queries, d_kv = attend_back(plan, queries, d_heads, kv_all, q_pos, q_start, lse, dot_strips)
    (early, swapped_grads), d_kv = after((early, swapped_grads), d_kv)
    d_side = reduce_keys(d_kv, 8)
    is_key = lax.rem(lax.div(me, 2), 2) == 0
    half_rows = row_tokens // 2

    def half_of(value):
        return lax.dynamic_slice_in_dim(value, core * half_rows, half_rows, 0)

    d_k_norm = rotate_back(d_side, half_of(cosine), half_of(sine_tab))
    d_k_pre, key_gain_terms = norm_back(half_of(k_pre), half_of(k_inverse), g_key, d_k_norm)
    key_gain_part = jnp.where(is_key, jnp.sum(key_gain_terms, axis=0), 0.0)
    d_side_pre = to_low(jnp.where(is_key, d_k_pre, d_side))
    d_q_norm = rotate_back(
        d_queries.reshape(row_tokens, 2, HEAD_WIDTH), cosine[:, None], sine_tab[:, None]
    )
    d_q_pre, query_gain_terms = norm_back(q_pre, q_inverse, g_query, d_q_norm)
    query_gain_part = jnp.sum(query_gain_terms, axis=(0, 1))
    d_q_pre = to_low(d_q_pre.reshape(row_tokens, 256))
    side_w = jnp.where(is_key, w_qkv[:, 256:384], w_qkv[:, 384:])
    d_side_full = jnp.where(
        (jnp.arange(row_tokens, dtype=jnp.int32) // half_rows == core)[:, None],
        jnp.concatenate([d_side_pre, d_side_pre], axis=0),
        jnp.zeros((), BF),
    )
    d_all = jnp.concatenate([d_q_pre, d_side_full], axis=1)
    d_hidden_parts = to_low(
        times_transposed(d_all, jnp.concatenate([w_qkv[:, :256], side_w], axis=1))
    ).reshape(8, rows, width)
    grad_in = to_low(transposed_times(hidden_one, d_all))
    tail = jnp.broadcast_to(
        jnp.pad(to_low(jnp.stack([query_gain_part, key_gain_part])), ((0, 14), (0, 0)))[None],
        (64, 16, 128),
    )
    late = jnp.concatenate(
        [grad_in[:, 128 * i : 128 * i + 128].reshape(64, depth, 128) for i in range(3)] + [tail], axis=1
    )
    late, d_hidden_parts = after(late, d_hidden_parts)
    late = lax.all_to_all(late, "ctx", split_axis=0, concat_axis=0, tiled=True)
    d_hidden_one, moe_total = reduce_row(d_hidden_parts, 9, False, collect(y_back))
    out_stream = residual + moe_total
    own_stream = tokens.astype(F32)
    d_stream_norm, _ = norm_back(own_stream, inverse_root(own_stream), g_attn, d_hidden_one)
    grad_tokens = d_residual + d_stream_norm


    def paired(own, back):
        back = back.astype(F32)
        return jnp.where(wsh == 0, jnp.stack([own, back]), jnp.stack([back, own]))

    grad_gate, grad_up, grad_down = [paired(own, back) for own, back in zip(grads[0], swapped_grads)]

    def summed(value, terms):
        return jnp.sum(value.astype(F32).reshape((8,) + terms + value.shape[1:]), axis=0)

    early_q = summed(early[:, : 2 * depth], (8,)).reshape(8, 2, depth, 128)
    grad_out = early_q.transpose(0, 1, 3, 2).reshape(8 * 256, depth)
    grad_router = jnp.sum(early[:, 2 * depth : 3 * depth].astype(F32), axis=0)
    grad_gain_ffn = jnp.sum(early[:, 3 * depth, :depth].astype(F32), axis=0)
    late_q = summed(late[:, : 2 * depth], (8,)).reshape(8, 2, depth, 128)
    grad_query = late_q.transpose(2, 0, 1, 3).reshape(depth, 8 * 256)
    late_kv = jnp.sum(
        late[:, 2 * depth : 3 * depth].astype(F32).reshape(8, 2, 2, 2, depth, 128), axis=(0, 3)
    )
    grad_key = late_kv[:, 0].transpose(1, 0, 2).reshape(depth, 256)
    grad_value = late_kv[:, 1].transpose(1, 0, 2).reshape(depth, 256)
    gain_parts = jnp.sum(late[:, 3 * depth : 3 * depth + 2].astype(F32), axis=0)
    gain_attn_part = (
        jnp.sum(rounded(w_query) * grad_query, axis=1)
        + jnp.sum(rounded(key_weight) * grad_key, axis=1)
        + jnp.sum(rounded(value_weight) * grad_value, axis=1)
    ) / rounded(gain_attn)
    gain_parts = lax.psum(jnp.concatenate([gain_parts, lanes_to(gain_attn_part[None, :])], axis=0), "wsh")
    return (
        out_stream,
        grad_tokens,
        grad_query,
        grad_key,
        grad_value,
        grad_out,
        gain_parts[2, :depth],
        gain_parts[0],
        gain_parts[1],
        grad_gain_ffn,
        grad_router,
        grad_gate,
        grad_up,
        grad_down,
    )


def solution(mesh):
    in_specs = (
        P("ctx", None),
        P("ctx", None),
        P(),
        P(),
        P("ctx", None),
        P("ctx", "wsh"),
        P("ctx", "wsh"),
        P("ctx", "wsh"),
        P("wsh", "ctx"),
        P("ctx"),
        P(),
        P(),
        P("ctx"),
        P("ctx", None),
        P("ctx", None, "wsh"),
        P("ctx", None, "wsh"),
        P("ctx", "wsh", None),
    )
    out_specs = (
        P("ctx", None),
        P("ctx", None),
        P("ctx", "wsh"),
        P("ctx", "wsh"),
        P("ctx", "wsh"),
        P("wsh", "ctx"),
        P("ctx"),
        P(),
        P(),
        P("ctx"),
        P("ctx", None),
        P("ctx", None, "wsh"),
        P("ctx", None, "wsh"),
        P("ctx", "wsh", None),
    )
    return jax.shard_map(local, mesh=mesh, in_specs=in_specs, out_specs=out_specs, check_vma=False)
```

```python
import functools
import math

import jax
import jax.numpy as jnp
from jax import lax
from jax.experimental import pallas as pl
from jax.experimental.pallas import tpu as pltpu
from jax.sharding import PartitionSpec as P

HEAD_WIDTH = 128
TOPK = 8
BLK = 64
MAX_SEQ_TOKENS = 4096
CAP = 12
CHUNK = 1024

EPSILON = 1e-06
ROPE_BASE = 1000000.0
MASKED = -1e30
MESH = pl.DeviceIdType.MESH
BF = jnp.bfloat16
F32 = jnp.float32


def to_low(value_rows):
    return value_rows.astype(jnp.bfloat16)


def rounded(value_rows):
    return lax.optimization_barrier(value_rows.astype(jnp.bfloat16)).astype(jnp.float32)


def matmul(left, right):
    return jnp.dot(left, right, preferred_element_type=jnp.float32)


def times_transposed(left, right):
    return lax.dot_general(
        left, right, (((1,), (1,)), ((), ())), preferred_element_type=jnp.float32
    )


def transposed_times(left, right):
    return lax.dot_general(
        left, right, (((0,), (0,)), ((), ())), preferred_element_type=jnp.float32
    )


def norm_back(value_rows, inverse_rms, gain_vec, gradient):
    weighted = gradient * gain_vec
    mean_term = jnp.mean(weighted * value_rows, axis=-1, keepdims=True)
    d_values = (
        inverse_rms * weighted - value_rows * (inverse_rms * inverse_rms * inverse_rms) * mean_term
    )
    return (d_values, gradient * value_rows * inverse_rms)


def inverse_root(value_rows):
    return lax.rsqrt(jnp.mean(value_rows * value_rows, axis=-1, keepdims=True) + EPSILON)


def rope_tables(positions):
    half_dim = HEAD_WIDTH // 2
    frequency = jnp.power(ROPE_BASE, -2.0 * jnp.arange(half_dim, dtype=jnp.float32) / HEAD_WIDTH)
    angles = positions.astype(jnp.float32)[:, None] * frequency[None, :]
    cosine, sine_tab = jnp.cos(angles), jnp.sin(angles)
    return (
        jnp.concatenate([cosine, cosine], axis=-1),
        jnp.concatenate([-sine_tab, sine_tab], axis=-1),
    )


def seq_starts(positions, seq_lengths):
    offsets = jnp.cumsum(seq_lengths) - seq_lengths
    inside = offsets[None, :] <= positions[:, None]
    return jnp.max(jnp.where(inside, offsets[None, :], 0), axis=1)


def coords(c):
    return (
        lax.div(c, 16),
        lax.rem(lax.div(c, 8), 2),
        lax.rem(lax.div(c, 2), 4),
        lax.rem(c, 2),
    )


def index_of(z, y, x, k):
    return ((z * 2 + y) * 4 + x) * 2 + k


def shifted(me, dz, dy, dx, dk):
    z, y, x, k = coords(me)
    return index_of(lax.rem(z + dz, 4), lax.rem(y + dy, 2), lax.rem(x + dx, 4), lax.rem(k + dk, 2))


def remote(src, dst, send, recv, ctx, wsh):
    return pltpu.make_async_remote_copy(
        src_ref=src,
        dst_ref=dst,
        send_sem=send,
        recv_sem=recv,
        device_id=(ctx, wsh),
        device_id_type=MESH,
    )


def greet(targets):
    barrier = pltpu.get_barrier_semaphore()
    for ctx, wsh in targets:
        pl.semaphore_signal(barrier, inc=1, device_id=(ctx, wsh), device_id_type=MESH)
    return barrier, len(targets)


def greet_many(count, target):
    barrier = pltpu.get_barrier_semaphore()

    def one(step, carried):
        pl.semaphore_signal(barrier, inc=1, device_id=target(step), device_id_type=MESH)
        return carried

    lax.fori_loop(1, count, one, 0)
    return barrier, count - 1


ANY = pl.BlockSpec(memory_space=pl.ANY)
VMEM = pl.BlockSpec(memory_space=pltpu.VMEM)
DMA = pltpu.SemaphoreType.DMA


def cost(microseconds):
    return pl.CostEstimate(flops=0, bytes_accessed=int(microseconds * 1.2e6), transcendentals=0)


ROOM = 56 * 1024 * 1024


def call_params(collective_id):
    return pltpu.CompilerParams(
        collective_id=collective_id, has_side_effects=True, vmem_limit_bytes=ROOM
    )


def row_gather_start(src, out, me, wsh, send, recv):
    place = lax.rem(me, 8)
    copies = []
    for at, (dx, dk) in enumerate(((1, 0), (3, 0), (0, 1))):
        copy = remote(
            src, out.at[place], send.at[at], recv.at[at], shifted(me, 0, 0, dx, dk), wsh
        )
        copy.start()
        copies.append(copy)
    return copies


def row_gather_finish(out, me, wsh, copies, send, recv):
    partner = shifted(me, 0, 0, 0, 1)
    half = out.shape[1] // 2
    onward = []
    forwards = []
    for at, dx in enumerate((1, 3)):
        copies[at].wait_recv()
        from_place = lax.rem(shifted(me, 0, 0, 4 - dx, 0), 8)
        part = out.at[from_place, pl.ds(at * half, half)]
        step = remote(part, part, send.at[3 + at], recv.at[3 + at], shifted(me, 0, 0, dx, 0), wsh)
        step.start()
        onward.append(step)
        block = out.at[from_place]
        forward = remote(block, block, send.at[5 + at], recv.at[5 + at], partner, wsh)
        forward.start()
        forwards.append(forward)
    far = lax.rem(shifted(me, 0, 0, 2, 0), 8)
    for at in (0, 1):
        onward[at].wait_recv()
        part = out.at[far, pl.ds(at * half, half)]
        forward = remote(part, part, send.at[7 + at], recv.at[7 + at], partner, wsh)
        forward.start()
        forwards.append(forward)
    copies[2].wait_recv()
    for copy in copies + onward:
        copy.wait_send()
    for forward in forwards:
        forward.wait()


def cast_steps(wide, narrow, side):
    sources, staging, lows, in_sems, out_sems = wide
    steps = []
    for src, dst in zip(sources, narrow):
        at = 0 if src.shape[1] > src.shape[2] else 1
        rows = staging[at].shape[1]
        for chunk in range(src.shape[1] // rows):
            steps.append((src, dst, at, pl.ds(chunk * rows, rows)))
    loads, stores = [], []
    for index, (src, dst, at, span) in enumerate(steps):
        slot = index % 2
        loads.append(pltpu.make_async_copy(src.at[side, span], staging[at].at[slot], in_sems.at[slot]))
        stores.append(pltpu.make_async_copy(lows[at].at[slot], dst.at[span], out_sems.at[slot]))
    loads[0].start()
    loads[1].start()
    for index, (_, _, at, _) in enumerate(steps):
        slot = index % 2
        loads[index].wait()
        if index >= 2:
            stores[index - 2].wait()
        lows[at][slot] = staging[at][slot].astype(BF)
        stores[index].start()
        if index + 2 < len(steps):
            loads[index + 2].start()
    stores[-2].wait()
    stores[-1].wait()


def gather_first(weights, tokens, small, routes, cotangent, expert_weights):
    def body(w_in, t_in, s_in, r_in, c_in, *refs):
        sources, refs = refs[:3], refs[3:]
        w_out, t_out, s_out, r_out, c_out = refs[:5]
        lows, side_out, refs = refs[5:8], refs[8], refs[9:]
        wide, row_s, row_r, pair, local, tall_f, flat_f, tall_b, flat_b, in_sems, out_sems = refs
        me, wsh = lax.axis_index("ctx"), lax.axis_index("wsh")
        core = lax.rem(me, 2)
        place = lax.rem(me, 8)

        def target(step):
            return shifted(
                me, lax.div(step, 16), lax.rem(lax.div(step, 8), 2), lax.rem(lax.div(step, 2), 4), lax.rem(step, 2)
            )

        barrier, amount = greet_many(64, lambda step: (target(step), wsh))
        locals_ = [
            pltpu.make_async_copy(t_in, t_out.at[place], local.at[0]),
            pltpu.make_async_copy(w_in.at[place], w_out.at[me], local.at[1]),
            pltpu.make_async_copy(s_in, s_out.at[me], local.at[2]),
            pltpu.make_async_copy(r_in, r_out.at[core], local.at[3]),
            pltpu.make_async_copy(c_in, c_out.at[core], local.at[4]),
        ]
        for copy in locals_:
            copy.start()
        pl.semaphore_wait(barrier, amount)
        row_copies = row_gather_start(t_in, t_out, me, wsh, row_s, row_r)

        def send(step, carried):
            turned = lax.rem(step * 13, 64)
            ctx = target(turned)
            remote(s_in, s_out.at[me], wide.at[0], wide.at[1], ctx, wsh).start()
            remote(w_in.at[lax.rem(ctx, 8)], w_out.at[me], wide.at[2], wide.at[3], ctx, wsh).start()
            return carried

        lax.fori_loop(1, 64, send, 0)
        partner = shifted(me, 0, 0, 0, 1)
        pair_copies = [
            remote(r_in, r_out.at[core], pair.at[0], pair.at[1], partner, wsh),
            remote(c_in, c_out.at[core], pair.at[2], pair.at[3], partner, wsh),
        ]
        for copy in pair_copies:
            copy.start()
        cast_steps((sources, (tall_f, flat_f), (tall_b, flat_b), in_sems, out_sems), lows, 1 - wsh)
        row_gather_finish(t_out, me, wsh, row_copies, row_s, row_r)
        for copy in pair_copies:
            copy.wait()
        for copy in locals_[:1] + locals_[2:]:
            copy.wait()
        for at, out in ((0, s_out), (2, w_out)):
            rest = out.at[pl.ds(0, 63)]
            done = remote(rest, rest, wide.at[at], wide.at[at + 1], partner, wsh)
            done.wait_send()
            done.wait_recv()
        locals_[1].wait()
        lanes = side_out.shape[2]
        share = w_out.at[pl.ds(0, 64), pl.ds(0, w_out.shape[1]), pl.ds(w_out.shape[2] - lanes, lanes)]
        give = remote(share, side_out, pair.at[4], pair.at[5], partner, wsh)
        give.start()
        give.wait()

    sds = jax.ShapeDtypeStruct
    tall = (expert_weights[0].shape[1] // 4, expert_weights[0].shape[2])
    flat = (expert_weights[2].shape[1] // 4, expert_weights[2].shape[2])
    return pl.pallas_call(
        body,
        out_shape=(
            sds((64,) + weights.shape[1:], weights.dtype),
            sds((8,) + tokens.shape, tokens.dtype),
            sds((64,) + small.shape, small.dtype),
            sds((2,) + routes.shape, routes.dtype),
            sds((2,) + cotangent.shape, cotangent.dtype),
        )
        + tuple(sds(value.shape[1:], BF) for value in expert_weights)
        + (sds((64, weights.shape[1], 128), weights.dtype),),
        in_specs=[ANY] * 8,
        out_specs=[ANY] * 9,
        scratch_shapes=[
            DMA((4,)),
            DMA((9,)),
            DMA((9,)),
            DMA((6,)),
            DMA((5,)),
            pltpu.VMEM((2,) + tall, F32),
            pltpu.VMEM((2,) + flat, F32),
            pltpu.VMEM((2,) + tall, BF),
            pltpu.VMEM((2,) + flat, BF),
            DMA((2,)),
            DMA((2,)),
        ],
        compiler_params=call_params(0),
        name="gather_first",
        cost_estimate=cost(60),
    )(weights, tokens, small, routes, cotangent, *expert_weights)


def gather_row(block, collective_id):
    def body(src, out, row_s, row_r, local):
        me, wsh = lax.axis_index("ctx"), lax.axis_index("wsh")
        barrier, amount = greet([(shifted(me, 0, 0, dx, dk), wsh) for dx, dk in ((1, 0), (3, 0), (0, 1))])
        mine = pltpu.make_async_copy(src, out.at[lax.rem(me, 8)], local)
        mine.start()
        pl.semaphore_wait(barrier, amount)
        copies = row_gather_start(src, out, me, wsh, row_s, row_r)
        row_gather_finish(out, me, wsh, copies, row_s, row_r)
        mine.wait()

    return pl.pallas_call(
        body,
        out_shape=jax.ShapeDtypeStruct((8,) + block.shape, block.dtype),
        in_specs=[ANY],
        out_specs=ANY,
        scratch_shapes=[DMA((9,)), DMA((9,)), DMA],
        compiler_params=call_params(collective_id),
        name="gather_row",
        cost_estimate=cost(26),
    )(block)


COLUMN_STEPS = ((1, 0), (3, 0), (0, 1), (2, 0), (1, 1), (3, 1), (2, 1))


def gather_keys(rows, collective_id):
    count = rows.shape[0]
    half = count // 2

    def body(src, out, send, recv, local):
        me, wsh = lax.axis_index("ctx"), lax.axis_index("wsh")
        core = lax.rem(me, 2)
        group = lax.div(me, 8)
        partner = shifted(me, 0, 0, 0, 1)
        peers = [shifted(me, dz, dy, 0, 0) for dz, dy in COLUMN_STEPS]
        barrier, amount = greet([(peer, wsh) for peer in peers + [partner]])
        mine = pltpu.make_async_copy(src, out.at[group], local)
        mine.start()
        pl.semaphore_wait(barrier, amount)
        my_half = pl.ds(pl.multiple_of(core * half, half), half)
        copies = []
        for at, peer in enumerate(peers):
            copy = remote(src.at[my_half], out.at[group, my_half], send.at[at], recv.at[at], peer, wsh)
            copy.start()
            copies.append(copy)
        forwards = []
        for at, (dz, dy) in enumerate(COLUMN_STEPS):
            copies[at].wait_recv()
            origin = lax.div(shifted(me, 4 - dz, 2 - dy, 0, 0), 8)
            part = out.at[origin, my_half]
            forward = remote(part, part, send.at[7 + at], recv.at[7 + at], partner, wsh)
            forward.start()
            forwards.append(forward)
        for copy in copies:
            copy.wait_send()
        for forward in forwards:
            forward.wait()
        mine.wait()

    return pl.pallas_call(
        body,
        out_shape=jax.ShapeDtypeStruct((8,) + rows.shape, rows.dtype),
        in_specs=[ANY],
        out_specs=ANY,
        scratch_shapes=[DMA((14,)), DMA((14,)), DMA],
        compiler_params=call_params(collective_id),
        name="gather_keys",
        cost_estimate=cost(30),
    )(rows)


def reduce_row(parts, collective_id, both, extra=None):
    _, rows, width = parts.shape
    block = (rows, width)
    pieces = 4
    columns = width // pieces
    has_extra = extra is not None

    def body(*refs):
        refs = list(refs)
        src = refs.pop(0)
        src2 = refs.pop(0) if has_extra else None
        out = refs.pop(0)
        out2 = refs.pop(0) if has_extra else None
        arrived, summed, landed, swapped, total, send, recv, local = refs[:8]
        me, wsh = lax.axis_index("ctx"), lax.axis_index("wsh")
        other = 1 - wsh
        core = lax.rem(me, 2)
        _, _, x, _ = coords(me)
        partner = shifted(me, 0, 0, 0, 1)
        peers = [shifted(me, 0, 0, dx, 0) for dx in (1, 2, 3)]
        barrier, amount = greet([(peer, wsh) for peer in peers + [partner]] + [(me, other)])
        pl.semaphore_wait(barrier, amount)
        spans = [pl.ds(piece * columns, columns) for piece in range(pieces)]
        everything = pl.ds(0, rows)
        first = []
        for piece, span in enumerate(spans):
            for at, dx in enumerate((2, 1, 3, 0)):
                chip = lax.rem(x + dx, 4)
                copy = remote(
                    src.at[chip * 2 + 1 - core, everything, span],
                    arrived.at[at, everything, span],
                    send.at[piece, at],
                    recv.at[piece, at],
                    partner,
                    wsh,
                )
                copy.start()
                first.append(copy)
        if has_extra:
            arrived2, swapped2 = refs[8:]
            give2 = remote(src2.at[1 - core], arrived2, send.at[0, 8], recv.at[0, 8], partner, wsh)
            give2.start()
        second = []
        for piece, span in enumerate(spans):
            for at, dx in enumerate((2, 1, 3)):
                chip = lax.rem(x + dx, 4)
                first[piece * 4 + at].wait_recv()
                summed[at, :, span] = (
                    src[chip * 2 + core, :, span].astype(F32) + arrived[at, :, span].astype(F32)
                ).astype(BF)
                copy = remote(
                    summed.at[at, everything, span],
                    landed.at[at, everything, span],
                    send.at[piece, 4 + at],
                    recv.at[piece, 4 + at],
                    shifted(me, 0, 0, dx, 0),
                    wsh,
                )
                copy.start()
                second.append(copy)
            first[piece * 4 + 3].wait_recv()
            total[:, span] = src[x * 2 + core, :, span].astype(F32) + arrived[3, :, span].astype(F32)
        if has_extra:
            give2.wait()
            swapped2[0] = (src2[core].astype(F32) + arrived2[...].astype(F32)).astype(BF)
            swap2 = remote(swapped2.at[0], swapped2.at[1], send.at[1, 8], recv.at[1, 8], me, other)
            swap2.start()
        swaps = []
        for piece, span in enumerate(spans):
            for at in (1, 2, 0):
                second[piece * 3 + at].wait_recv()
            swapped[0, :, span] = (
                total[:, span]
                + landed[0, :, span].astype(F32)
                + landed[1, :, span].astype(F32)
                + landed[2, :, span].astype(F32)
            ).astype(BF)
            swap = remote(
                swapped.at[0, everything, span],
                swapped.at[1, everything, span],
                send.at[piece, 7],
                recv.at[piece, 7],
                me,
                other,
            )
            swap.start()
            swaps.append(swap)
        if has_extra:
            swap2.wait()
            out2[...] = swapped2[0].astype(F32) + swapped2[1].astype(F32)
        for piece, span in enumerate(spans):
            swaps[piece].wait()
            if both:
                total[:, span] = swapped[0, :, span].astype(F32) + swapped[1, :, span].astype(F32)
            else:
                out[:, span] = swapped[0, :, span].astype(F32) + swapped[1, :, span].astype(F32)
        if both:
            keep = pltpu.make_async_copy(total, out.at[core], local)
            keep.start()
            give = remote(total, out.at[core], send.at[0, 9], recv.at[0, 9], partner, wsh)
            give.start()
            give.wait()
            keep.wait()
        for copy in first + second:
            copy.wait_send()

    shapes = [jax.ShapeDtypeStruct((2,) + block if both else block, F32)]
    scratch = [
        pltpu.VMEM((4,) + block, BF),
        pltpu.VMEM((3,) + block, BF),
        pltpu.VMEM((3,) + block, BF),
        pltpu.VMEM((2,) + block, BF),
        pltpu.VMEM(block, F32),
        DMA((pieces, 10)),
        DMA((pieces, 10)),
        DMA,
    ]
    operands = [parts]
    if has_extra:
        shapes.append(jax.ShapeDtypeStruct(block, F32))
        scratch += [pltpu.VMEM(block, BF), pltpu.VMEM((2,) + block, BF)]
        operands.append(extra)
    return pl.pallas_call(
        body,
        out_shape=shapes,
        in_specs=[VMEM] * len(operands),
        out_specs=[VMEM] * len(operands),
        scratch_shapes=scratch,
        compiler_params=call_params(collective_id),
        name="reduce_row",
        cost_estimate=cost(40),
    )(*operands)


def reduce_chip(parts, extra, collective_id):
    _, rows, width = parts.shape
    extra_block = None if extra is None else extra.shape[1:]

    def body(*refs):
        if extra is None:
            src, out, arrived, swapped, total, send, recv = refs
        else:
            src, src2, out, out2, arrived, swapped, total, arrived2, swapped2, send, recv = refs
        me, wsh = lax.axis_index("ctx"), lax.axis_index("wsh")
        other = 1 - wsh
        core = lax.rem(me, 2)
        partner = shifted(me, 0, 0, 0, 1)
        barrier, amount = greet([(partner, wsh), (me, other)])
        pl.semaphore_wait(barrier, amount)
        give = remote(src.at[1 - core], arrived, send.at[0], recv.at[0], partner, wsh)
        give.start()
        if extra is not None:
            give2 = remote(src2.at[1 - core], arrived2, send.at[2], recv.at[2], partner, wsh)
            give2.start()
        give.wait()
        swapped[0] = (src[core].astype(F32) + arrived[...].astype(F32)).astype(BF)
        swap = remote(swapped.at[0], swapped.at[1], send.at[1], recv.at[1], me, other)
        swap.start()
        if extra is not None:
            give2.wait()
            swapped2[0] = src2[core] + arrived2[...]
            swap2 = remote(swapped2.at[0], swapped2.at[1], send.at[3], recv.at[3], me, other)
            swap2.start()
            swap2.wait()
            out2[...] = swapped2[0] + swapped2[1]
        swap.wait()
        out[...] = swapped[0].astype(F32) + swapped[1].astype(F32)

    sds = jax.ShapeDtypeStruct
    block = (rows, width)
    shapes = [sds(block, F32)]
    scratch = [pltpu.VMEM(block, BF), pltpu.VMEM((2,) + block, BF), pltpu.VMEM(block, F32)]
    operands = [parts]
    if extra is not None:
        shapes.append(sds(extra_block, F32))
        scratch += [pltpu.VMEM(extra_block, F32), pltpu.VMEM((2,) + extra_block, F32)]
        operands.append(extra)
    scratch += [DMA((4,)), DMA((4,))]
    return pl.pallas_call(
        body,
        out_shape=shapes,
        in_specs=[VMEM] * len(operands),
        out_specs=[VMEM] * len(operands),
        scratch_shapes=scratch,
        compiler_params=call_params(collective_id),
        name="reduce_chip",
        cost_estimate=cost(17),
    )(*operands)


def reduce_keys(parts, collective_id):
    _, groups, _, rows, width = parts.shape

    def body(src, out, arrived, mid, beside, summed, landed, send, recv):
        me, wsh = lax.axis_index("ctx"), lax.axis_index("wsh")
        core = lax.rem(me, 2)
        _, _, x, _ = coords(me)
        side = lax.rem(x, 2)
        partner = shifted(me, 0, 0, 0, 1)
        neighbour = me + 2 - 4 * side
        steps = COLUMN_STEPS + ((0, 0),)
        peers = [shifted(me, dz, dy, 0, 0) for dz, dy in steps]
        barrier, amount = greet([(peer, wsh) for peer in peers[:-1] + [partner, neighbour]])
        pl.semaphore_wait(barrier, amount)
        first = []
        for at, peer in enumerate(peers):
            group = lax.div(peer, 8)
            for turn, b in enumerate((1 - side, side)):
                copy = remote(
                    src.at[1 - core, group, b],
                    arrived.at[turn, at],
                    send.at[turn, at],
                    recv.at[turn, at],
                    partner,
                    wsh,
                )
                copy.start()
                first.append(copy)
        across = []
        for at, peer in enumerate(peers):
            group = lax.div(peer, 8)
            first[2 * at].wait_recv()
            mid[at] = (src[core, group, 1 - side].astype(F32) + arrived[0, at].astype(F32)).astype(BF)
            copy = remote(mid.at[at], beside.at[at], send.at[2, at], recv.at[2, at], neighbour, wsh)
            copy.start()
            across.append(copy)
        last = []
        for at, peer in enumerate(peers):
            group = lax.div(peer, 8)
            first[2 * at + 1].wait_recv()
            across[at].wait_recv()
            value = (
                src[core, group, side].astype(F32)
                + arrived[1, at].astype(F32)
                + beside[at].astype(F32)
            )
            if at == groups - 1:
                out[...] = value
            else:
                summed[at] = value.astype(BF)
                copy = remote(summed.at[at], landed.at[at], send.at[3, at], recv.at[3, at], peer, wsh)
                copy.start()
                last.append(copy)
        for at, copy in enumerate(last):
            copy.wait_recv()
            out[...] += landed[at].astype(F32)
        for copy in first + across + last:
            copy.wait_send()

    block = (rows, width)
    return pl.pallas_call(
        body,
        out_shape=jax.ShapeDtypeStruct(block, F32),
        in_specs=[VMEM],
        out_specs=VMEM,
        scratch_shapes=[
            pltpu.VMEM((2, groups) + block, BF),
            pltpu.VMEM((groups,) + block, BF),
            pltpu.VMEM((groups,) + block, BF),
            pltpu.VMEM((groups,) + block, BF),
            pltpu.VMEM((groups,) + block, BF),
            DMA((4, groups)),
            DMA((4, groups)),
        ],
        compiler_params=call_params(collective_id),
        name="reduce_keys",
        cost_estimate=cost(40),
    )(parts)


def exchange(arrays, collective_id):
    amount = len(arrays)

    def body(*refs):
        ins, outs = refs[:amount], refs[amount : 2 * amount]
        send, recv, local = refs[2 * amount :]
        me, wsh = lax.axis_index("ctx"), lax.axis_index("wsh")
        chip = lax.div(me, 2)

        def target(step):
            dy = lax.rem(lax.div(step, 4), 2)
            return shifted(me, lax.div(step, 8), dy, lax.rem(step, 4), 0), lax.rem(wsh + dy, 2)

        barrier, count = greet_many(32, target)
        locals_ = []
        for at in range(amount):
            copy = pltpu.make_async_copy(ins[at].at[chip], outs[at].at[chip], local.at[at])
            copy.start()
            locals_.append(copy)
        pl.semaphore_wait(barrier, count)

        def one(step, carried):
            ctx, side = target(lax.rem(step * 13, 32))
            for at in range(amount):
                remote(
                    ins[at].at[lax.div(ctx, 2)], outs[at].at[chip], send.at[at], recv.at[at], ctx, side
                ).start()
            return carried

        lax.fori_loop(1, 32, one, 0)
        for copy in locals_:
            copy.wait()
        for at in range(amount):
            rest = outs[at].at[pl.ds(0, 31)]
            done = remote(rest, rest, send.at[at], recv.at[at], me, wsh)
            done.wait_send()
            done.wait_recv()

    return pl.pallas_call(
        body,
        out_shape=[jax.ShapeDtypeStruct(a.shape, a.dtype) for a in arrays],
        in_specs=[ANY] * amount,
        out_specs=[ANY] * amount,
        scratch_shapes=[DMA((amount,)), DMA((amount,)), DMA((amount,))],
        compiler_params=call_params(collective_id),
        name="exchange",
        cost_estimate=cost(48),
    )(*arrays)


def exchange_behind(value):
    groups = []
    for core in range(2):
        for parity in range(2):
            groups.append(
                [(chip * 2 + core) * 2 + (parity + chip // 4) % 2 for chip in range(32)]
            )
    return lax.all_to_all(
        value, ("ctx", "wsh"), split_axis=0, concat_axis=0, tiled=True, axis_index_groups=groups
    )


def natural_order(inverse, kv_ref, keys, values, transposed):
    def one(block, carried):
        rows = kv_ref[pl.ds(pl.multiple_of(inverse[block] * BLK, BLK), BLK), :]
        at = pl.ds(pl.multiple_of(block * BLK, BLK), BLK)
        keys[at, :] = rows[:, :HEAD_WIDTH]
        values[at, :] = rows[:, HEAD_WIDTH:]
        return carried

    lax.fori_loop(0, kv_ref.shape[0] // BLK, one, 0, unroll=8)
    source, turned = transposed

    def turn(chunk, carried):
        at = pl.ds(pl.multiple_of(chunk * CHUNK, CHUNK), CHUNK)
        turned[:, at] = source[at, :].T
        return carried

    lax.fori_loop(0, kv_ref.shape[0] // CHUNK, turn, 0, unroll=4)


def stacked(ref, first, second):
    rows = [ref[pl.ds(pl.multiple_of(at * BLK, BLK), BLK), :] for at in (first, second)]
    return jnp.concatenate(
        [rows[0][:, :HEAD_WIDTH], rows[0][:, HEAD_WIDTH:], rows[1][:, :HEAD_WIDTH], rows[1][:, HEAD_WIDTH:]],
        axis=0,
    )


def unstacked(ref, first, second, value):
    for at, begin in ((first, 0), (second, 2 * BLK)):
        ref[pl.ds(pl.multiple_of(at * BLK, BLK), BLK), :] = jnp.concatenate(
            [value[begin : begin + BLK], value[begin + BLK : begin + 2 * BLK]], axis=1
        )


def three_loops(step, low, inner_low, inner_high, high, chunk, state):
    state = lax.fori_loop(low[step], inner_low[step], functools.partial(chunk, True), state)
    state = lax.fori_loop(inner_low[step], inner_high[step], functools.partial(chunk, False), state)
    return lax.fori_loop(inner_high[step], high[step], functools.partial(chunk, True), state)


def kept(scores, at, q_pos, q_start):
    k_pos = at + lax.broadcasted_iota(jnp.int32, scores.shape, 0)
    return jnp.where((k_pos <= q_pos) & (k_pos >= q_start), scores, MASKED)


SCORE_SCALE = 1.0 / math.sqrt(HEAD_WIDTH)
TWO_SCALE = SCORE_SCALE / math.log(2.0)


def forward_kernel(order, low, inner_low, inner_high, high, inverse, q_ref, kv_ref, pos_ref, start_ref, out_ref, lse_ref, keys, values, values_t, acc):
    step = pl.program_id(0)

    @pl.when(step == 0)
    def _():
        natural_order(inverse, kv_ref, keys, values, (values, values_t))

    first, second = order[2 * step], order[2 * step + 1]
    q_t = stacked(q_ref, first, second).astype(F32).T.astype(BF)
    q_pos, q_start = pos_ref[0], start_ref[0]
    width = 4 * BLK
    acc[...] = jnp.zeros_like(acc)

    def chunk(masked, index, total):
        at = pl.multiple_of(index * CHUNK, CHUNK)
        scores = matmul(keys[pl.ds(at, CHUNK), :], q_t)
        if masked:
            scores = kept(scores, at, q_pos, q_start)
        probs = jnp.exp2(scores * TWO_SCALE)
        acc[...] += matmul(values_t[:, pl.ds(at, CHUNK)], probs.astype(BF))
        return total + jnp.sum(probs, axis=0, keepdims=True)

    total = three_loops(
        step, low, inner_low, inner_high, high, chunk, jnp.zeros((1, width), F32)
    )
    lse_ref[0] = jnp.log2(total)
    unstacked(out_ref, first, second, (acc[...] / total).T.astype(BF))


def attend(plan, queries, kv, positions, starts):
    rows = queries.shape[0]
    steps = rows // (2 * BLK)
    everything = pl.BlockSpec(queries.shape, lambda i, *_: (0, 0))
    strip = pl.BlockSpec((1, 1, 4 * BLK), lambda i, *_: (i, 0, 0))
    sds = jax.ShapeDtypeStruct
    return pl.pallas_call(
        forward_kernel,
        out_shape=(sds(queries.shape, BF), sds((steps, 1, 4 * BLK), F32)),
        grid_spec=pltpu.PrefetchScalarGridSpec(
            num_scalar_prefetch=6,
            grid=(steps,),
            in_specs=[everything, pl.BlockSpec(kv.shape, lambda i, *_: (0, 0)), strip, strip],
            out_specs=[everything, strip],
            scratch_shapes=[
                pltpu.VMEM((kv.shape[0], HEAD_WIDTH), BF),
                pltpu.VMEM((kv.shape[0], HEAD_WIDTH), BF),
                pltpu.VMEM((HEAD_WIDTH, kv.shape[0]), BF),
                pltpu.VMEM((HEAD_WIDTH, 4 * BLK), F32),
            ],
        ),
        compiler_params=pltpu.CompilerParams(vmem_limit_bytes=ROOM),
        name="attend",
        cost_estimate=cost(17),
    )(*plan, queries, kv, positions, starts)


def backward_kernel(order, low, inner_low, inner_high, high, inverse, q_ref, heads_ref, da_ref, wo_ref, kv_ref, pos_ref, start_ref, lse_ref, dq_ref, dkv_ref, keys, values, keys_t, d_keys, d_values, acc):
    step = pl.program_id(0)

    @pl.when(step == 0)
    def _():
        natural_order(inverse, kv_ref, keys, values, (keys, keys_t))
        d_keys[...] = jnp.zeros_like(d_keys)
        d_values[...] = jnp.zeros_like(d_values)

    first, second = order[2 * step], order[2 * step + 1]
    q = stacked(q_ref, first, second)
    d_rows = matmul(
        jnp.concatenate(
            [da_ref[pl.ds(pl.multiple_of(at * BLK, BLK), BLK), :] for at in (first, second)], axis=0
        ),
        wo_ref[...],
    )
    d_out = jnp.concatenate(
        [
            d_rows[begin : begin + BLK, head : head + HEAD_WIDTH]
            for begin in (0, BLK)
            for head in (0, HEAD_WIDTH)
        ],
        axis=0,
    ).astype(BF)
    q_t = q.astype(F32).T.astype(BF)
    d_out_wide = d_out.astype(F32).T
    d_out_t = d_out_wide.astype(BF)
    q_pos, q_start = pos_ref[0], start_ref[0]
    lse = lse_ref[0]
    dots = jnp.sum(d_out_wide * stacked(heads_ref, first, second).astype(F32).T, axis=0, keepdims=True)
    acc[...] = jnp.zeros_like(acc)

    def chunk(masked, index, carried):
        at = pl.multiple_of(index * CHUNK, CHUNK)
        here = pl.ds(at, CHUNK)
        scores = matmul(keys[here, :], q_t)
        if masked:
            scores = kept(scores, at, q_pos, q_start)
        probs = jnp.exp2(scores * TWO_SCALE - lse)
        d_probs = matmul(values[here, :], d_out_t)
        d_scores = (probs * (d_probs - dots)).astype(BF)
        d_values[here, :] += matmul(probs.astype(BF), d_out)
        d_keys[here, :] += matmul(d_scores, q)
        acc[...] += matmul(keys_t[:, here], d_scores)
        return carried

    three_loops(step, low, inner_low, inner_high, high, chunk, 0)
    unstacked(dq_ref, first, second, (acc[...] * SCORE_SCALE).T)

    @pl.when(step == pl.num_programs(0) - 1)
    def _():
        def one(block, carried):
            dealt = inverse[block]
            group, inside = dealt // 16, dealt % 16
            half, rest = inside // 8, inside % 8
            at = pl.ds(pl.multiple_of(block * BLK, BLK), BLK)
            to = pl.ds(pl.multiple_of(rest * BLK, BLK), BLK)
            dkv_ref[half, group, 0, to, :] = (d_keys[at, :] * SCORE_SCALE).astype(BF)
            dkv_ref[half, group, 1, to, :] = d_values[at, :].astype(BF)
            return carried

        lax.fori_loop(0, kv_ref.shape[0] // BLK, one, 0, unroll=4)


def attend_back(plan, queries, heads, d_attn, wo_t, kv, positions, starts, lse):
    rows = queries.shape[0]
    total = kv.shape[0]
    steps = rows // (2 * BLK)
    everything = pl.BlockSpec(queries.shape, lambda i, *_: (0, 0))
    strip = pl.BlockSpec((1, 1, 4 * BLK), lambda i, *_: (i, 0, 0))
    sds = jax.ShapeDtypeStruct
    dkv_shape = (2, total // rows, 2, rows // 2, HEAD_WIDTH)
    return pl.pallas_call(
        backward_kernel,
        out_shape=(sds(queries.shape, F32), sds(dkv_shape, BF)),
        grid_spec=pltpu.PrefetchScalarGridSpec(
            num_scalar_prefetch=6,
            grid=(steps,),
            in_specs=[
                everything,
                everything,
                pl.BlockSpec(d_attn.shape, lambda i, *_: (0, 0)),
                pl.BlockSpec(wo_t.shape, lambda i, *_: (0, 0)),
                pl.BlockSpec(kv.shape, lambda i, *_: (0, 0)),
                strip,
                strip,
                strip,
            ],
            out_specs=[everything, pl.BlockSpec(dkv_shape, lambda i, *_: (0, 0, 0, 0, 0))],
            scratch_shapes=[
                pltpu.VMEM((total, HEAD_WIDTH), BF),
                pltpu.VMEM((total, HEAD_WIDTH), BF),
                pltpu.VMEM((HEAD_WIDTH, total), BF),
                pltpu.VMEM((total, HEAD_WIDTH), F32),
                pltpu.VMEM((total, HEAD_WIDTH), F32),
                pltpu.VMEM((HEAD_WIDTH, 4 * BLK), F32),
            ],
        ),
        compiler_params=pltpu.CompilerParams(vmem_limit_bytes=ROOM),
        name="attend_back",
        cost_estimate=cost(24),
    )(*plan, queries, heads, d_attn, wo_t, kv, positions, starts, lse)


def expert_kernel(side, x_ref, cot_ref, gate_ref, g_own, u_own, d_own, g_other, u_other, d_other, y_ref, dx_ref, dot_ref, a_ref, dg_ref, du_ref, dy_ref, gate_w, up_w, down_w, gate_f, up_f, down_f, sems):
    half = g_other.shape[1]
    own_copies, other_copies = [], []
    for at, (own, other, whole, stage, columns) in enumerate(
        (
            (g_own, g_other, gate_w, gate_f, True),
            (u_own, u_other, up_w, up_f, True),
            (d_own, d_other, down_w, down_f, False),
        )
    ):
        span = pl.ds(half, half)
        target = whole.at[pl.ds(0, whole.shape[0]), span] if columns else whole.at[span]
        own_copies.append(pltpu.make_async_copy(own.at[side[0]], stage, sems.at[at, 0]))
        other_copies.append(pltpu.make_async_copy(other, target, sems.at[at, 1]))

    @pl.when(pl.program_id(0) == 0)
    def _():
        for copy in own_copies + other_copies:
            copy.start()
        own_copies[0].wait()
        gate_w[:, :half] = gate_f[...].astype(BF)
        own_copies[1].wait()
        up_w[:, :half] = up_f[...].astype(BF)
        own_copies[2].wait()
        down_w[:half, :] = down_f[...].astype(BF)
        for copy in other_copies:
            copy.wait()

    x = x_ref[...]
    gate_pre = matmul(x, gate_w[...])
    up_pre = matmul(x, up_w[...])
    sigma = 1.0 / (1.0 + jnp.exp(-gate_pre))
    silu = gate_pre * sigma
    activated = (silu * up_pre).astype(BF)
    a_ref[...] = activated
    gates = gate_ref[:, 0:1].astype(F32) + gate_ref[:, 64:65].astype(F32)
    cot = cot_ref[...].astype(F32)
    out = matmul(activated, down_w[...])
    y_ref[...] = (out * gates).astype(BF)
    dots = jnp.sum(out * cot, axis=1, keepdims=True)
    high = dots.astype(BF).astype(F32)
    lane = lax.broadcasted_iota(jnp.int32, dot_ref.shape, 1)
    dot_ref[...] = jnp.where(lane < 64, high, dots - high).astype(BF)
    d_pairs = (cot * gates).astype(BF)
    dy_ref[...] = d_pairs
    d_act = times_transposed(d_pairs, down_w[...])
    d_gate = (d_act * up_pre * sigma * (1.0 + gate_pre * (1.0 - sigma))).astype(BF)
    d_up = (d_act * silu).astype(BF)
    dg_ref[...] = d_gate
    du_ref[...] = d_up
    dx_ref[...] = (times_transposed(d_gate, gate_w[...]) + times_transposed(d_up, up_w[...])).astype(BF)


def run_expert(side, rows_in, cot, gates, own, other):
    count, width = rows_in.shape
    half = other[0].shape[1]
    tile = 256
    sds = jax.ShapeDtypeStruct

    def by_rows(columns):
        return pl.BlockSpec((tile, columns), lambda i, side: (i, 0))

    return pl.pallas_call(
        expert_kernel,
        out_shape=(
            sds((count, width), BF),
            sds((count, width), BF),
            sds((count, 128), BF),
            sds((count, 2 * half), BF),
            sds((count, 2 * half), BF),
            sds((count, 2 * half), BF),
            sds((count, width), BF),
        ),
        grid_spec=pltpu.PrefetchScalarGridSpec(
            num_scalar_prefetch=1,
            grid=(count // tile,),
            in_specs=[by_rows(width), by_rows(width), by_rows(128)] + [ANY] * 6,
            out_specs=[
                by_rows(width),
                by_rows(width),
                by_rows(128),
                by_rows(2 * half),
                by_rows(2 * half),
                by_rows(2 * half),
                by_rows(width),
            ],
            scratch_shapes=[
                pltpu.VMEM((width, 2 * half), BF),
                pltpu.VMEM((width, 2 * half), BF),
                pltpu.VMEM((2 * half, width), BF),
                pltpu.VMEM((width, half), F32),
                pltpu.VMEM((width, half), F32),
                pltpu.VMEM((half, width), F32),
                DMA((3, 2)),
            ],
        ),
        compiler_params=pltpu.CompilerParams(vmem_limit_bytes=ROOM),
        name="run_expert",
        cost_estimate=cost(25),
    )(side, rows_in, cot, gates, *own, *other)


def expert_grads_kernel(side, x_ref, dy_ref, a_ref, dg_ref, du_ref, gate_ref, up_ref, down_ref, gate_out, up_out, down_out, a_t):
    half = gate_ref.shape[-1]

    @pl.when(pl.program_id(0) == 0)
    def _():
        a_t[...] = a_ref[...].T

    x_t = x_ref[...].T
    for grad_ref, own, other in ((dg_ref, gate_ref, gate_out), (du_ref, up_ref, up_out)):
        value = matmul(x_t, grad_ref[...])
        own[0] = value[:, :half]
        other[...] = value[:, half:].astype(BF)
    value = matmul(a_t[...], dy_ref[...])
    down_ref[0] = value[:half]
    down_out[...] = value[half:].astype(BF)


def expert_grads(side, rows_in, d_pairs, activated, d_gate, d_up):
    count, width = rows_in.shape
    whole = activated.shape[1]
    half = whole // 2
    tile = 256
    sds = jax.ShapeDtypeStruct
    columns = pl.BlockSpec((count, tile), lambda i, side: (0, i))
    full = pl.BlockSpec((count, whole), lambda i, side: (0, 0))
    own_rows = pl.BlockSpec((1, tile, half), lambda i, side: (side[0], i, 0))
    other_rows = pl.BlockSpec((tile, half), lambda i, side: (i, 0))
    return pl.pallas_call(
        expert_grads_kernel,
        out_shape=(
            sds((2, width, half), F32),
            sds((2, width, half), F32),
            sds((2, half, width), F32),
            sds((width, half), BF),
            sds((width, half), BF),
            sds((half, width), BF),
        ),
        grid_spec=pltpu.PrefetchScalarGridSpec(
            num_scalar_prefetch=1,
            grid=(width // tile,),
            in_specs=[columns, columns, full, full, full],
            out_specs=[
                own_rows,
                own_rows,
                pl.BlockSpec((1, half, tile), lambda i, side: (side[0], 0, i)),
                other_rows,
                other_rows,
                pl.BlockSpec((half, tile), lambda i, side: (0, i)),
            ],
            scratch_shapes=[pltpu.VMEM((whole, count), BF)],
        ),
        compiler_params=pltpu.CompilerParams(vmem_limit_bytes=ROOM),
        name="expert_grads",
        cost_estimate=cost(12),
    )(side, rows_in, d_pairs, activated, d_gate, d_up)


def place_kernel(side, *refs):
    for at in range(3):
        refs[6 + at][0] = refs[at][...].astype(F32)


def place_other(side, arrived, placed):
    tile = 256
    width, half = arrived[0].shape
    rows_in = pl.BlockSpec((tile, half), lambda i, side: (i, 0))
    rows_out = pl.BlockSpec((1, tile, half), lambda i, side: (1 - side[0], i, 0))
    return pl.pallas_call(
        place_kernel,
        out_shape=[jax.ShapeDtypeStruct(value.shape, F32) for value in placed],
        grid_spec=pltpu.PrefetchScalarGridSpec(
            num_scalar_prefetch=1,
            grid=(width // tile,),
            in_specs=[rows_in, rows_in, pl.BlockSpec((half, tile), lambda i, side: (0, i))] + [ANY] * 3,
            out_specs=[
                rows_out,
                rows_out,
                pl.BlockSpec((1, half, tile), lambda i, side: (1 - side[0], 0, i)),
            ],
        ),
        input_output_aliases={4: 0, 5: 1, 6: 2},
        compiler_params=pltpu.CompilerParams(vmem_limit_bytes=ROOM),
        name="place_other",
        cost_estimate=cost(5),
    )(side, *arrived, *placed)


def project_kernel(t_ref, w_ref, side_ref, flag_ref, cos_ref, sin_ref, ga_ref, gq_ref, gk_ref, h_ref, q_ref, kv_ref, qp_ref, kp_ref):
    rows = t_ref[...].astype(F32)
    inverse = lax.rsqrt(jnp.mean(rows * rows, axis=1, keepdims=True) + EPSILON)
    hidden = (rows * inverse * ga_ref[...]).astype(BF)
    h_ref[...] = hidden
    qkv = matmul(hidden, w_ref[...])
    own = qkv[:, 2 * HEAD_WIDTH :]
    other = matmul(hidden, side_ref[...])
    first = flag_ref[0:1, :] > 0.5
    cosine, sine_tab = cos_ref[...], sin_ref[...]

    def turned(value, gain):
        root = lax.rsqrt(jnp.mean(value * value, axis=1, keepdims=True) + EPSILON)
        value = value * root * gain
        return (value * cosine + pltpu.roll(value, HEAD_WIDTH // 2, 1) * sine_tab).astype(BF)

    for head in range(2):
        span = slice(head * HEAD_WIDTH, (head + 1) * HEAD_WIDTH)
        q_ref[:, span] = turned(qkv[:, span], gq_ref[...])
    qp_ref[...] = qkv[:, : 2 * HEAD_WIDTH]
    keys = jnp.where(first, own, other)
    kp_ref[...] = keys
    kv_ref[:, :HEAD_WIDTH] = turned(keys, gk_ref[...])
    kv_ref[:, HEAD_WIDTH:] = jnp.where(first, other, own).astype(BF)


def project(tokens, weights, side, first, cosine, sine_tab, gain, gain_query, gain_key):
    rows, width = tokens.shape
    tile = 256
    sds = jax.ShapeDtypeStruct

    def by_rows(columns):
        return pl.BlockSpec((tile, columns), lambda i: (i, 0))

    def whole(value):
        return pl.BlockSpec(value.shape, lambda i: (0, 0))

    return pl.pallas_call(
        project_kernel,
        grid=(rows // tile,),
        out_shape=(
            sds((rows, width), BF),
            sds((rows, 256), BF),
            sds((rows, 256), BF),
            sds((rows, 256), F32),
            sds((rows, 128), F32),
        ),
        in_specs=[
            by_rows(width),
            whole(weights),
            whole(side),
            whole(first),
            by_rows(128),
            by_rows(128),
            whole(gain),
            whole(gain_query),
            whole(gain_key),
        ],
        out_specs=[by_rows(width), by_rows(256), by_rows(256), by_rows(256), by_rows(128)],
        compiler_params=pltpu.CompilerParams(vmem_limit_bytes=ROOM),
        name="project",
        cost_estimate=cost(8),
    )(tokens, weights, side, first, cosine, sine_tab, gain, gain_query, gain_key)


def project_back_kernel(dq_ref, ds_ref, qp_ref, kp_ref, cos_ref, sin_ref, h_ref, w_ref, side_ref, gq_ref, gk_ref, flag_ref, part_ref, late_ref, side_w, total, gains):
    step = pl.program_id(0)
    cosine, sine_tab = cos_ref[...], sin_ref[...]
    key, first, own = flag_ref[0:1, :], flag_ref[1:2, :], flag_ref[2:3, :]
    heads = 2 * HEAD_WIDTH

    @pl.when(step == 0)
    def _():
        gains[...] = jnp.zeros_like(gains)
        total[...] = jnp.zeros_like(total)
        side_w[...] = jnp.where(
            own > 0.5, w_ref[:, heads:].astype(F32), side_ref[...].astype(F32)
        ).astype(BF)

    def back(gradient, value, gain):
        gradient = gradient * cosine - pltpu.roll(gradient, HEAD_WIDTH // 2, 1) * sine_tab
        root = lax.rsqrt(jnp.mean(value * value, axis=1, keepdims=True) + EPSILON)
        weighted = gradient * gain
        mean_term = jnp.mean(weighted * value, axis=1, keepdims=True)
        terms = jnp.sum(gradient * value * root, axis=0, keepdims=True)
        return root * weighted - value * (root * root * root) * mean_term, terms

    columns = []
    for head in range(2):
        span = slice(head * HEAD_WIDTH, (head + 1) * HEAD_WIDTH)
        value, terms = back(dq_ref[:, span], qp_ref[:, span], gq_ref[...])
        columns.append(value.astype(BF))
        gains[0:1, :] += terms
    d_side = ds_ref[...]
    value, terms = back(d_side, kp_ref[...], gk_ref[...])
    mine = jnp.where(first == (step // 2).astype(F32), 1.0, 0.0)
    columns.append((jnp.where(key > 0.5, value, d_side) * mine).astype(BF))
    gains[1:2, :] += terms * key * mine
    d_all = jnp.concatenate(columns, axis=1)
    part_ref[...] = (
        times_transposed(d_all[:, :heads], w_ref[:, :heads])
        + times_transposed(d_all[:, heads:], side_w[...])
    ).astype(BF)
    total[...] += transposed_times(h_ref[...], d_all)

    @pl.when(step == pl.num_programs(0) - 1)
    def _():
        pieces, depth = late_ref.shape[0], h_ref.shape[1] // late_ref.shape[0]
        for at in range(3):
            value = total[:, at * HEAD_WIDTH : (at + 1) * HEAD_WIDTH].astype(BF)
            late_ref[:, at * depth : (at + 1) * depth, :] = value.reshape(pieces, depth, HEAD_WIDTH)
        late_ref[:, 3 * depth :, :] = jnp.broadcast_to(
            gains[...].astype(BF)[None], (pieces,) + gains.shape
        )


def project_back(d_queries, d_side, q_pre, k_pre, cosine, sine_tab, hidden, weights, side, gain_query, gain_key, flags):
    rows = d_queries.shape[0]
    width = hidden.shape[1]
    tile = 256
    tiles = rows // tile
    owners = 64
    sds = jax.ShapeDtypeStruct
    late = (owners, 3 * width // owners + 16, 128)

    def by_rows(columns):
        return pl.BlockSpec((tile, columns), lambda i: (i, 0))

    def whole(value):
        return pl.BlockSpec(value.shape, lambda i: (0, 0))

    half_rows = pl.BlockSpec((tile, 128), lambda i: (i % (tiles // 2), 0))
    return pl.pallas_call(
        project_back_kernel,
        grid=(tiles,),
        out_shape=(sds((rows, width), BF), sds(late, BF)),
        in_specs=[
            by_rows(256),
            half_rows,
            by_rows(256),
            by_rows(128),
            by_rows(128),
            by_rows(128),
            by_rows(width),
            whole(weights),
            whole(side),
            whole(gain_query),
            whole(gain_key),
            whole(flags),
        ],
        out_specs=[by_rows(width), pl.BlockSpec(late, lambda i: (0, 0, 0))],
        scratch_shapes=[
            pltpu.VMEM((width, 128), BF),
            pltpu.VMEM((width, 384), F32),
            pltpu.VMEM((16, 128), F32),
        ],
        compiler_params=pltpu.CompilerParams(vmem_limit_bytes=ROOM),
        name="project_back",
        cost_estimate=cost(12),
    )(
        d_queries, d_side, q_pre, k_pre, cosine, sine_tab, hidden, weights, side, gain_query, gain_key, flags
    )


def after(value, earlier):
    return lax.optimization_barrier((value, earlier))


def lanes_to(row, lanes=128):
    return jnp.pad(row, ((0, 0),) * (row.ndim - 1) + ((0, lanes - row.shape[-1]),))


def local(
    tokens,
    cotangent,
    seq_lengths,
    block_order,
    routes,
    w_query,
    key_weight,
    value_weight,
    w_out,
    gain_attn,
    gain_query,
    gain_key,
    gain_ffn,
    w_router,
    w_gate,
    w_up,
    w_down,
):
    rows = tokens.shape[0]
    width = tokens.shape[1]
    experts = w_router.shape[1]
    block_count = block_order.shape[0]
    wsh = lax.axis_index("wsh")
    me = lax.axis_index("ctx")
    core = lax.rem(me, 2)
    place = lax.rem(me, 8)
    group = lax.div(me, 8)
    row_tokens = 8 * rows
    row_blocks = row_tokens // BLK

    def swap(value):
        return lax.ppermute(value, "wsh", [(0, 1), (1, 0)])

    depth = w_query.shape[0]
    q_part = to_low(w_query).reshape(depth, 8, 256).transpose(1, 0, 2)
    sides = [
        to_low(value[:, head * 128 : head * 128 + 128])
        for head in (0, 0, 1, 1)
        for value in (key_weight, value_weight)
    ]
    w_pack = jnp.concatenate([q_part, jnp.stack(sides)], axis=2)
    small = jnp.concatenate(
        [lanes_to(gain_attn[None, :]), lanes_to(gain_ffn[None, :]), jnp.zeros((6, 128), F32)], axis=0
    )
    w_all, row_rows, small_all, chip_routes, chip_cot, other_gate, other_up, other_down, w_side = gather_first(
        w_pack, tokens, small, routes.T, cotangent, (w_gate, w_up, w_down)
    )
    w_main = w_all.reshape(width, 384)
    w_side = w_side.reshape(width, 128)
    is_key = lax.rem(lax.div(me, 2), 2) == 0

    def flag(value):
        return jnp.broadcast_to(value.astype(F32).reshape(1, 1), (8, 128))

    g_attn = to_low(small_all[:, 0, :depth].reshape(width)).astype(F32)
    g_ffn = to_low(small_all[:, 1, :depth].reshape(width)).astype(F32)
    g_query = rounded(gain_query)
    g_key = rounded(gain_key)

    o_part = to_low(w_out).T.reshape(depth, 8, 256).transpose(1, 0, 2)
    r_part = jnp.broadcast_to(to_low(w_router)[None], (8, depth, experts))
    late_pack = jnp.tile(jnp.concatenate([o_part, r_part], axis=2), (8, 1, 1))
    late_pack, small_all = after(late_pack, small_all)
    late_all = lax.all_to_all(late_pack, "ctx", split_axis=0, concat_axis=0, tiled=True).reshape(width, 384)

    route_rows = chip_routes.transpose(0, 2, 1)
    hits = jnp.any(
        route_rows[:, :, :, None] == jnp.arange(experts, dtype=jnp.int32)[None, None, None, :], axis=2
    )
    before = jnp.tril(jnp.ones((rows, rows), BF), -1)
    ranks = jnp.einsum("ts,hse->hte", before, hits.astype(BF), preferred_element_type=F32).astype(jnp.int32)
    ranks = jnp.where(hits, ranks + jnp.array([0, CAP], jnp.int32)[:, None, None], -1)
    hits = hits.reshape(2 * rows, experts)
    chips = experts // 4
    chip_ids = jnp.arange(chips, dtype=jnp.int32)
    quarter = core * 2 + (wsh + chip_ids // 4 + lax.div(me, 8)) % 2

    def my_quarter(value):
        by_chip = value.reshape(2 * rows, experts).T.reshape(chips, 4, 2 * rows)
        two = lax.dynamic_slice_in_dim(by_chip, core * 2, 2, 1)
        return jnp.where((quarter % 2 == 0)[:, None], two[:, 0], two[:, 1])

    my_ranks = my_quarter(ranks)
    slots = 2 * CAP
    pick = my_ranks[:, None, :] == jnp.arange(slots, dtype=jnp.int32)[None, :, None]
    pick_low = pick.astype(BF).reshape(chips * slots, 2 * rows)
    cot_rows = matmul(pick_low, chip_cot.reshape(2 * rows, width)).astype(BF)
    my_blocks = lax.dynamic_slice_in_dim(block_order, group * row_blocks, row_blocks, 0)
    positions = (my_blocks[:, None] * BLK + jnp.arange(BLK, dtype=jnp.int32)[None, :]).reshape(row_tokens)
    starts = seq_starts(positions, seq_lengths)
    cosine, sine_tab = rope_tables(positions - starts)
    inverse_order = (
        jnp.zeros((block_count,), jnp.int32)
        .at[block_order]
        .set(jnp.arange(block_count, dtype=jnp.int32))
    )
    smaller = jnp.sum((my_blocks[None, :] < my_blocks[:, None]).astype(jnp.int32), axis=1)
    order = jnp.sum(
        jnp.where(
            smaller[None, :] == jnp.arange(row_blocks, dtype=jnp.int32)[:, None],
            jnp.arange(row_blocks, dtype=jnp.int32)[None, :],
            0,
        ),
        axis=1,
    )
    block_starts = starts.reshape(row_blocks, BLK)
    pair_blocks = jnp.take(my_blocks, order).reshape(-1, 2)
    low = jnp.min(jnp.take(block_starts[:, 0], order).reshape(-1, 2), axis=1) // CHUNK
    high = jnp.max(pair_blocks, axis=1) * BLK // CHUNK + 1
    last_start = jnp.max(jnp.take(block_starts[:, BLK - 1], order).reshape(-1, 2), axis=1)
    inner_low = jnp.clip((last_start + CHUNK - 1) // CHUNK, low, high)
    inner_high = jnp.clip((jnp.min(pair_blocks, axis=1) * BLK + 1) // CHUNK, inner_low, high)
    plan = (order, low, inner_low, inner_high, high, inverse_order)

    def strips(per_token):
        by_block = jnp.take(per_token.reshape(row_blocks, BLK), order, axis=0).reshape(-1, 2, 1, BLK)
        return jnp.broadcast_to(by_block, (row_blocks // 2, 2, 2, BLK)).reshape(-1, 1, 4 * BLK)

    q_pos, q_start = strips(positions), strips(starts)

    row_rows = row_rows.reshape(row_tokens, width)
    hidden_one, queries, kv, q_pre, k_pre = project(
        row_rows, w_main, w_side, flag(core == 0), cosine, sine_tab, g_attn[None, :], g_query[None, :], g_key[None, :]
    )
    kv_all = gather_keys(kv, 1).reshape(block_count * BLK, 256)
    late_all, kv_all = after(late_all, kv_all)
    wo_t = late_all[:, :256]
    wr = late_all[:, 256:]
    (cot_rows, other_gate), kv_all = after((cot_rows, other_gate), kv_all)
    gate_back = swap(other_gate)
    cot_there = exchange_behind(cot_rows.reshape(chips, slots, width)).reshape(chips * slots, width)
    heads, lse = attend(plan, queries, kv_all, q_pos, q_start)

    attn_parts = to_low(times_transposed(heads, wo_t)).reshape(8, rows, width)
    (gate_back, cot_there, other_up, other_down), attn_parts = after(
        (gate_back, cot_there, other_up, other_down), attn_parts
    )
    up_back = swap(other_up)
    attn_total = reduce_row(attn_parts, 2, True)[0].reshape(2 * rows, width)
    chip_stream = lax.dynamic_slice_in_dim(row_rows, (place - core) * rows, 2 * rows, 0).astype(F32)
    chip_residual = chip_stream + attn_total
    chip_inverse_two = inverse_root(chip_residual)
    chip_hidden = to_low(chip_residual * chip_inverse_two * g_ffn)
    logits = matmul(chip_hidden, wr)
    masked_logits = jnp.where(hits, logits, MASKED)
    gate_exps = jnp.where(
        hits, jnp.exp(masked_logits - jnp.max(masked_logits, axis=-1, keepdims=True)), 0.0
    )
    gates = gate_exps / jnp.sum(gate_exps, axis=-1, keepdims=True)

    def my_rows(value):
        return lax.dynamic_slice_in_dim(value, core * rows, rows, 0)

    out_rows = matmul(pick_low, chip_hidden).astype(BF).reshape(chips, slots, width)
    expert_of = jnp.repeat(4 * chip_ids + quarter, slots)
    of_expert = expert_of[:, None] == jnp.arange(experts, dtype=jnp.int32)[None, :]

    def parted(value):
        high = to_low(value)
        return high, to_low(value - high.astype(F32))

    slot_gates = [
        jnp.sum(jnp.where(of_expert, matmul(pick_low, part), 0.0), axis=1, keepdims=True)
        for part in parted(gates)
    ]
    gate_tile = to_low(
        jnp.where(jnp.arange(128)[None, :] < 64, slot_gates[0], slot_gates[1])
    ).reshape(chips, slots, 128)
    (up_back, other_down), gate_tile = after((up_back, other_down), gate_tile)
    down_back = swap(other_down)
    arrived, gate_there = exchange([out_rows, gate_tile], 3)
    arrived = arrived.reshape(chips * slots, width)
    side = wsh.reshape(1)
    gate_there = gate_there.reshape(chips * slots, 128)
    y_rows, d_rows, d_gate_slots, activated, d_gate_pre, d_up_pre, d_pairs = run_expert(
        side, arrived, cot_there, gate_there, (w_gate, w_up, w_down), (gate_back, up_back, down_back)
    )
    *own_grads, other_gate, other_up, other_down = expert_grads(
        side, arrived, d_pairs, activated, d_gate_pre, d_up_pre
    )
    gate_grad_back = swap(other_gate)
    (other_up, other_down), d_gate_slots = after((other_up, other_down), d_gate_slots)
    d_back, d_gate_back = exchange(
        [d_rows.reshape(chips, slots, width), d_gate_slots.reshape(chips, slots, 128)], 4
    )
    (y_rows, gate_grad_back), d_back = after((y_rows, gate_grad_back), d_back)
    y_back = exchange_behind(y_rows.reshape(chips, slots, width))

    def collect(back):
        return to_low(transposed_times(pick_low, back.reshape(chips * slots, width))).reshape(2, rows, width)

    d_gate_back = d_gate_back.reshape(chips * slots, 128)
    d_gates_part = sum(
        transposed_times(
            pick_low, jnp.where(of_expert, d_gate_back[:, at : at + 1], jnp.zeros((), BF))
        )
        for at in (0, 64)
    ).reshape(2, rows, experts)
    d_hidden_moe, d_gates = reduce_chip(collect(d_back), d_gates_part, 5)
    residual = my_rows(chip_residual)

    own_gates = my_rows(gates)
    hidden_two = my_rows(chip_hidden)
    inverse_two = my_rows(chip_inverse_two)
    d_chosen = own_gates * (d_gates - jnp.sum(own_gates * d_gates, axis=-1, keepdims=True))
    d_logits = to_low(d_chosen)
    grad_router = transposed_times(hidden_two, d_logits)
    d_hidden_two = d_hidden_moe + times_transposed(d_logits, wr)
    d_res_norm, ffn_gain_terms = norm_back(residual, inverse_two, g_ffn, d_hidden_two)
    d_residual = cotangent.astype(F32) + d_res_norm
    gain_ffn_part = jnp.sum(ffn_gain_terms, axis=0)

    other_up, d_residual = after(other_up, d_residual)
    up_grad_back = swap(other_up)
    d_attn = gather_row(to_low(d_residual), 7).reshape(row_tokens, width)
    (y_back, up_grad_back), d_attn_late = after((y_back, up_grad_back), d_attn)
    other_down, up_grad_back = after(other_down, up_grad_back)
    down_grad_back = swap(other_down)
    grad_out_t = transposed_times(d_attn, heads)
    early = jnp.concatenate(
        [
            to_low(grad_out_t[:, :128]).reshape(64, depth, 128),
            to_low(grad_out_t[:, 128:]).reshape(64, depth, 128),
            to_low(grad_router).reshape(64, depth, 128),
            jnp.pad(
                to_low(gain_ffn_part).reshape(64, 1, depth), ((0, 0), (0, 15), (0, 128 - depth))
            ),
        ],
        axis=1,
    )
    early = lax.all_to_all(early, "ctx", split_axis=0, concat_axis=0, tiled=True)
    d_queries, d_kv = attend_back(plan, queries, heads, d_attn_late, wo_t, kv_all, q_pos, q_start, lse)
    (early, down_grad_back), d_kv = after((early, down_grad_back), d_kv)
    swapped_grads = (gate_grad_back, up_grad_back, down_grad_back)
    d_side = reduce_keys(d_kv, 8)
    flags = jnp.concatenate(
        [
            flag(is_key)[:1],
            flag(core)[:1],
            flag(is_key == (core == 0))[:1],
            jnp.zeros((5, 128), F32),
        ],
        axis=0,
    )
    d_hidden_parts, late = project_back(
        d_queries,
        d_side,
        q_pre,
        k_pre,
        cosine,
        sine_tab,
        hidden_one,
        w_main,
        w_side,
        g_query[None, :],
        g_key[None, :],
        flags,
    )
    d_hidden_parts = d_hidden_parts.reshape(8, rows, width)
    late, d_hidden_parts = after(late, d_hidden_parts)
    late = lax.all_to_all(late, "ctx", split_axis=0, concat_axis=0, tiled=True)
    d_hidden_one, moe_total = reduce_row(d_hidden_parts, 9, False, collect(y_back))
    out_stream = residual + moe_total
    own_stream = tokens.astype(F32)
    d_stream_norm, _ = norm_back(own_stream, inverse_root(own_stream), g_attn, d_hidden_one)
    grad_tokens = d_residual + d_stream_norm


    grad_gate, grad_up, grad_down = place_other(side, swapped_grads, own_grads)

    def summed(value, terms):
        return jnp.sum(value.astype(F32).reshape((8,) + terms + value.shape[1:]), axis=0)

    early_q = summed(early[:, : 2 * depth], (8,)).reshape(8, 2, depth, 128)
    grad_out = early_q.transpose(0, 1, 3, 2).reshape(8 * 256, depth)
    grad_router = jnp.sum(early[:, 2 * depth : 3 * depth].astype(F32), axis=0)
    grad_gain_ffn = jnp.sum(early[:, 3 * depth, :depth].astype(F32), axis=0)
    late_q = summed(late[:, : 2 * depth], (8,)).reshape(8, 2, depth, 128)
    grad_query = late_q.transpose(2, 0, 1, 3).reshape(depth, 8 * 256)
    late_kv = jnp.sum(
        late[:, 2 * depth : 3 * depth].astype(F32).reshape(8, 2, 2, 2, depth, 128), axis=(0, 3)
    )
    grad_key = late_kv[:, 0].transpose(1, 0, 2).reshape(depth, 256)
    grad_value = late_kv[:, 1].transpose(1, 0, 2).reshape(depth, 256)
    gain_parts = jnp.sum(late[:, 3 * depth : 3 * depth + 2].astype(F32), axis=0)
    gain_attn_part = (
        jnp.sum(rounded(w_query) * grad_query, axis=1)
        + jnp.sum(rounded(key_weight) * grad_key, axis=1)
        + jnp.sum(rounded(value_weight) * grad_value, axis=1)
    ) / rounded(gain_attn)
    gain_parts = lax.psum(jnp.concatenate([gain_parts, lanes_to(gain_attn_part[None, :])], axis=0), "wsh")
    return (
        out_stream,
        grad_tokens,
        grad_query,
        grad_key,
        grad_value,
        grad_out,
        gain_parts[2, :depth],
        gain_parts[0],
        gain_parts[1],
        grad_gain_ffn,
        grad_router,
        grad_gate,
        grad_up,
        grad_down,
    )


def solution(mesh):
    in_specs = (
        P("ctx", None),
        P("ctx", None),
        P(),
        P(),
        P("ctx", None),
        P("ctx", "wsh"),
        P("ctx", "wsh"),
        P("ctx", "wsh"),
        P("wsh", "ctx"),
        P("ctx"),
        P(),
        P(),
        P("ctx"),
        P("ctx", None),
        P("ctx", None, "wsh"),
        P("ctx", None, "wsh"),
        P("ctx", "wsh", None),
    )
    out_specs = (
        P("ctx", None),
        P("ctx", None),
        P("ctx", "wsh"),
        P("ctx", "wsh"),
        P("ctx", "wsh"),
        P("wsh", "ctx"),
        P("ctx"),
        P(),
        P(),
        P("ctx"),
        P("ctx", None),
        P("ctx", None, "wsh"),
        P("ctx", None, "wsh"),
        P("ctx", "wsh", None),
    )
    return jax.shard_map(local, mesh=mesh, in_specs=in_specs, out_specs=out_specs, check_vma=False)
```

```python
import functools
import math

import jax
import jax.numpy as jnp
from jax import lax
from jax.experimental import pallas as pl
from jax.experimental.pallas import tpu as pltpu
from jax.sharding import PartitionSpec as P

HEAD_WIDTH = 128
TOPK = 8
BLK = 64
MAX_SEQ_TOKENS = 4096
CAP = 12
CHUNK = 1024

EPSILON = 1e-06
ROPE_BASE = 1000000.0
MASKED = -1e30
MESH = pl.DeviceIdType.MESH
BF = jnp.bfloat16
F32 = jnp.float32


def to_low(value_rows):
    return value_rows.astype(jnp.bfloat16)


def rounded(value_rows):
    return lax.optimization_barrier(value_rows.astype(jnp.bfloat16)).astype(jnp.float32)


def matmul(left, right):
    return jnp.dot(left, right, preferred_element_type=jnp.float32)


def times_transposed(left, right):
    return lax.dot_general(
        left, right, (((1,), (1,)), ((), ())), preferred_element_type=jnp.float32
    )


def transposed_times(left, right):
    return lax.dot_general(
        left, right, (((0,), (0,)), ((), ())), preferred_element_type=jnp.float32
    )


def norm_back(value_rows, inverse_rms, gain_vec, gradient):
    weighted = gradient * gain_vec
    mean_term = jnp.mean(weighted * value_rows, axis=-1, keepdims=True)
    d_values = (
        inverse_rms * weighted - value_rows * (inverse_rms * inverse_rms * inverse_rms) * mean_term
    )
    return (d_values, gradient * value_rows * inverse_rms)


def inverse_root(value_rows):
    return lax.rsqrt(jnp.mean(value_rows * value_rows, axis=-1, keepdims=True) + EPSILON)


def coords(c):
    return (
        lax.div(c, 16),
        lax.rem(lax.div(c, 8), 2),
        lax.rem(lax.div(c, 2), 4),
        lax.rem(c, 2),
    )


def index_of(z, y, x, k):
    return ((z * 2 + y) * 4 + x) * 2 + k


def shifted(me, dz, dy, dx, dk):
    z, y, x, k = coords(me)
    return index_of(lax.rem(z + dz, 4), lax.rem(y + dy, 2), lax.rem(x + dx, 4), lax.rem(k + dk, 2))


def remote(src, dst, send, recv, ctx, wsh):
    return pltpu.make_async_remote_copy(
        src_ref=src,
        dst_ref=dst,
        send_sem=send,
        recv_sem=recv,
        device_id=(ctx, wsh),
        device_id_type=MESH,
    )


def greet(targets):
    barrier = pltpu.get_barrier_semaphore()
    for ctx, wsh in targets:
        pl.semaphore_signal(barrier, inc=1, device_id=(ctx, wsh), device_id_type=MESH)
    return barrier, len(targets)


def greet_many(count, target):
    barrier = pltpu.get_barrier_semaphore()

    def one(step, carried):
        pl.semaphore_signal(barrier, inc=1, device_id=target(step), device_id_type=MESH)
        return carried

    lax.fori_loop(1, count, one, 0)
    return barrier, count - 1


ANY = pl.BlockSpec(memory_space=pl.ANY)
VMEM = pl.BlockSpec(memory_space=pltpu.VMEM)
DMA = pltpu.SemaphoreType.DMA


def cost(microseconds):
    return pl.CostEstimate(flops=0, bytes_accessed=int(microseconds * 1.2e6), transcendentals=0)


ROOM = 56 * 1024 * 1024


def call_params(collective_id):
    return pltpu.CompilerParams(
        collective_id=collective_id, has_side_effects=True, vmem_limit_bytes=ROOM
    )


def row_gather_start(src, out, me, wsh, send, recv):
    place = lax.rem(me, 8)
    copies = []
    for at, (dx, dk) in enumerate(((1, 0), (3, 0), (0, 1))):
        copy = remote(
            src, out.at[place], send.at[at], recv.at[at], shifted(me, 0, 0, dx, dk), wsh
        )
        copy.start()
        copies.append(copy)
    return copies


def row_gather_onward(out, me, wsh, copies, send, recv):
    partner = shifted(me, 0, 0, 0, 1)
    half = out.shape[1] // 2
    onward = []
    forwards = []
    for at, dx in enumerate((1, 3)):
        copies[at].wait_recv()
        from_place = lax.rem(shifted(me, 0, 0, 4 - dx, 0), 8)
        part = out.at[from_place, pl.ds(at * half, half)]
        step = remote(part, part, send.at[3 + at], recv.at[3 + at], shifted(me, 0, 0, dx, 0), wsh)
        step.start()
        onward.append(step)
        block = out.at[from_place]
        forward = remote(block, block, send.at[5 + at], recv.at[5 + at], partner, wsh)
        forward.start()
        forwards.append(forward)
    return onward, forwards


def row_gather_end(out, me, wsh, copies, onward, forwards, send, recv):
    partner = shifted(me, 0, 0, 0, 1)
    half = out.shape[1] // 2
    far = lax.rem(shifted(me, 0, 0, 2, 0), 8)
    for at in (0, 1):
        onward[at].wait_recv()
        part = out.at[far, pl.ds(at * half, half)]
        forward = remote(part, part, send.at[7 + at], recv.at[7 + at], partner, wsh)
        forward.start()
        forwards.append(forward)
    copies[2].wait_recv()
    for copy in copies + onward:
        copy.wait_send()
    for forward in forwards:
        forward.wait()


def cast_steps(wide, narrow, side):
    sources, staging, lows, in_sems, out_sems = wide
    steps = []
    for src, dst in zip(sources, narrow):
        at = 0 if src.shape[1] > src.shape[2] else 1
        rows = staging[at].shape[1]
        for chunk in range(src.shape[1] // rows):
            steps.append((src, dst, at, pl.ds(chunk * rows, rows)))
    loads, stores = [], []
    for index, (src, dst, at, span) in enumerate(steps):
        slot = index % 2
        loads.append(pltpu.make_async_copy(src.at[side, span], staging[at].at[slot], in_sems.at[slot]))
        stores.append(pltpu.make_async_copy(lows[at].at[slot], dst.at[span], out_sems.at[slot]))
    loads[0].start()
    loads[1].start()
    for index, (_, _, at, _) in enumerate(steps):
        slot = index % 2
        loads[index].wait()
        if index >= 2:
            stores[index - 2].wait()
        lows[at][slot] = staging[at][slot].astype(BF)
        stores[index].start()
        if index + 2 < len(steps):
            loads[index + 2].start()
    stores[-2].wait()
    stores[-1].wait()


COLUMN_STEPS = ((1, 0), (3, 0), (0, 1), (2, 0), (1, 1), (3, 1), (2, 1))
ROW_STEPS = ((1, 0), (3, 0), (1, 1), (3, 1), (0, 1), (2, 0), (2, 1))


def gather_first(weights, tokens, small, routes, cotangent, expert_weights):
    def body(w_in, t_in, s_in, r_in, c_in, *refs):
        sources, refs = refs[:3], refs[3:]
        w_out, t_out, s_out, r_out, c_out = refs[:5]
        lows, side_out, refs = refs[5:8], refs[8], refs[9:]
        wide, row_s, row_r, pair, local, col_s, col_r, tall_f, flat_f, tall_b, flat_b, in_sems, out_sems = refs
        me, wsh = lax.axis_index("ctx"), lax.axis_index("wsh")
        core = lax.rem(me, 2)
        place = lax.rem(me, 8)
        group = lax.div(me, 8)
        partner = shifted(me, 0, 0, 0, 1)
        row_peers = [shifted(me, 0, 0, dx, dk) for dx, dk in ROW_STEPS]
        col_peers = [shifted(me, dz, dy, 0, 0) for dz, dy in COLUMN_STEPS]
        barrier, amount = greet([(peer, wsh) for peer in row_peers + col_peers])
        locals_ = [
            pltpu.make_async_copy(w_in.at[place], w_out.at[me], local.at[0]),
            pltpu.make_async_copy(s_in, s_out.at[me], local.at[1]),
            pltpu.make_async_copy(t_in, t_out.at[place], local.at[2]),
            pltpu.make_async_copy(r_in, r_out.at[core], local.at[3]),
            pltpu.make_async_copy(c_in, c_out.at[core], local.at[4]),
        ]
        for copy in locals_:
            copy.start()
        pl.semaphore_wait(barrier, amount)
        for peer in row_peers:
            remote(w_in.at[lax.rem(peer, 8)], w_out.at[me], wide.at[0], wide.at[1], peer, wsh).start()
            remote(s_in, s_out.at[me], wide.at[2], wide.at[3], peer, wsh).start()
        row_copies = row_gather_start(t_in, t_out, me, wsh, row_s, row_r)
        pair_copies = [
            remote(r_in, r_out.at[core], pair.at[0], pair.at[1], partner, wsh),
            remote(c_in, c_out.at[core], pair.at[2], pair.at[3], partner, wsh),
        ]
        for copy in pair_copies:
            copy.start()
        locals_[0].wait()
        locals_[1].wait()
        for at, out in ((0, w_out), (2, s_out)):
            rest = out.at[pl.ds(0, 7)]
            done = remote(rest, rest, wide.at[at], wide.at[at + 1], partner, wsh)
            done.wait_recv()
            done.wait_send()
        lanes = side_out.shape[2]
        depth, columns = w_out.shape[1], w_out.shape[2]

        def share(origin, at):
            blocks = pl.ds(origin * 8, 8)
            part = w_out.at[blocks, pl.ds(0, depth), pl.ds(columns - lanes, lanes)]
            give = remote(part, side_out.at[blocks], col_s.at[2, at], col_r.at[2, at], partner, wsh)
            give.start()
            return give

        mine = pl.ds(group * 8, 8)
        col_copies = []
        for at, peer in enumerate(col_peers):
            for kind, out in enumerate((w_out, s_out)):
                copy = remote(out.at[mine], out.at[mine], col_s.at[kind, at], col_r.at[kind, at], peer, wsh)
                copy.start()
                col_copies.append(copy)
        shares = [share(group, 7)]
        onward, forwards = row_gather_onward(t_out, me, wsh, row_copies, row_s, row_r)
        cast_steps((sources, (tall_f, flat_f), (tall_b, flat_b), in_sems, out_sems), lows, 1 - wsh)
        row_gather_end(t_out, me, wsh, row_copies, onward, forwards, row_s, row_r)
        for at, (dz, dy) in enumerate(COLUMN_STEPS):
            col_copies[2 * at].wait_recv()
            col_copies[2 * at + 1].wait_recv()
            shares.append(share(lax.div(shifted(me, 4 - dz, 2 - dy, 0, 0), 8), at))
        for copy in pair_copies + shares:
            copy.wait()
        for copy in locals_[2:]:
            copy.wait()
        for copy in col_copies:
            copy.wait_send()

    sds = jax.ShapeDtypeStruct
    tall = (expert_weights[0].shape[1] // 4, expert_weights[0].shape[2])
    flat = (expert_weights[2].shape[1] // 4, expert_weights[2].shape[2])
    return pl.pallas_call(
        body,
        out_shape=(
            sds((64,) + weights.shape[1:], weights.dtype),
            sds((8,) + tokens.shape, tokens.dtype),
            sds((64,) + small.shape, small.dtype),
            sds((2,) + routes.shape, routes.dtype),
            sds((2,) + cotangent.shape, cotangent.dtype),
        )
        + tuple(sds(value.shape[1:], BF) for value in expert_weights)
        + (sds((64, weights.shape[1], 128), weights.dtype),),
        in_specs=[ANY] * 8,
        out_specs=[ANY] * 9,
        scratch_shapes=[
            DMA((4,)),
            DMA((9,)),
            DMA((9,)),
            DMA((4,)),
            DMA((5,)),
            DMA((3, 8)),
            DMA((3, 8)),
            pltpu.VMEM((2,) + tall, F32),
            pltpu.VMEM((2,) + flat, F32),
            pltpu.VMEM((2,) + tall, BF),
            pltpu.VMEM((2,) + flat, BF),
            DMA((2,)),
            DMA((2,)),
        ],
        compiler_params=call_params(0),
        name="gather_first",
        cost_estimate=cost(40),
    )(weights, tokens, small, routes, cotangent, *expert_weights)


def gather_row(block, collective_id):
    def body(src, out, row_s, row_r, local):
        me, wsh = lax.axis_index("ctx"), lax.axis_index("wsh")
        barrier, amount = greet([(shifted(me, 0, 0, dx, dk), wsh) for dx, dk in ((1, 0), (3, 0), (0, 1))])
        mine = pltpu.make_async_copy(src, out.at[lax.rem(me, 8)], local)
        mine.start()
        pl.semaphore_wait(barrier, amount)
        copies = row_gather_start(src, out, me, wsh, row_s, row_r)
        onward, forwards = row_gather_onward(out, me, wsh, copies, row_s, row_r)
        row_gather_end(out, me, wsh, copies, onward, forwards, row_s, row_r)
        mine.wait()

    return pl.pallas_call(
        body,
        out_shape=jax.ShapeDtypeStruct((8,) + block.shape, block.dtype),
        in_specs=[ANY],
        out_specs=ANY,
        scratch_shapes=[DMA((9,)), DMA((9,)), DMA],
        compiler_params=call_params(collective_id),
        name="gather_row",
        cost_estimate=cost(26),
    )(block)


def gather_keys(rows, collective_id):
    count = rows.shape[0]
    half = count // 2

    def body(src, out, send, recv, local):
        me, wsh = lax.axis_index("ctx"), lax.axis_index("wsh")
        core = lax.rem(me, 2)
        group = lax.div(me, 8)
        partner = shifted(me, 0, 0, 0, 1)
        peers = [shifted(me, dz, dy, 0, 0) for dz, dy in COLUMN_STEPS]
        barrier, amount = greet([(peer, wsh) for peer in peers + [partner]])
        mine = pltpu.make_async_copy(src, out.at[group], local)
        mine.start()
        pl.semaphore_wait(barrier, amount)
        my_half = pl.ds(pl.multiple_of(core * half, half), half)
        copies = []
        for at, peer in enumerate(peers):
            copy = remote(src.at[my_half], out.at[group, my_half], send.at[at], recv.at[at], peer, wsh)
            copy.start()
            copies.append(copy)
        forwards = []
        for at, (dz, dy) in enumerate(COLUMN_STEPS):
            copies[at].wait_recv()
            origin = lax.div(shifted(me, 4 - dz, 2 - dy, 0, 0), 8)
            part = out.at[origin, my_half]
            forward = remote(part, part, send.at[7 + at], recv.at[7 + at], partner, wsh)
            forward.start()
            forwards.append(forward)
        for copy in copies:
            copy.wait_send()
        for forward in forwards:
            forward.wait()
        mine.wait()

    return pl.pallas_call(
        body,
        out_shape=jax.ShapeDtypeStruct((8,) + rows.shape, rows.dtype),
        in_specs=[ANY],
        out_specs=ANY,
        scratch_shapes=[DMA((14,)), DMA((14,)), DMA],
        compiler_params=call_params(collective_id),
        name="gather_keys",
        cost_estimate=cost(30),
    )(rows)


class Owned:
    SCRATCH = 10

    def __init__(self, src, out, scratch):
        self.src, self.out = src, out
        self.land_z, self.sum_z, self.land_y, self.reduced, *self.sems = scratch

    @staticmethod
    def scratch(value):
        inner = value.shape[1:]
        return [
            pltpu.VMEM((3, 16) + inner, BF),
            pltpu.VMEM((16,) + inner, BF),
            pltpu.VMEM((8,) + inner, BF),
            pltpu.VMEM((8,) + inner, BF),
            DMA((3,)),
            DMA((3,)),
            DMA((1,)),
            DMA((1,)),
            DMA((7,)),
            DMA((7,)),
        ]

    def along_z(self, me, wsh):
        z, _, _, _ = coords(me)
        self.copies_z = []
        for at, dz in enumerate((1, 3, 2)):
            blocks = pl.ds(lax.rem(z + dz, 4) * 16, 16)
            copy = remote(
                self.src.at[blocks],
                self.land_z.at[at],
                self.sems[0].at[at],
                self.sems[1].at[at],
                shifted(me, dz, 0, 0, 0),
                wsh,
            )
            copy.start()
            self.copies_z.append(copy)

    def along_y(self, me, wsh):
        z, y, _, _ = coords(me)
        value = self.src[pl.ds(z * 16, 16)].astype(F32)
        for at, copy in enumerate(self.copies_z):
            copy.wait_recv()
            value = value + self.land_z[at].astype(F32)
        self.sum_z[...] = value.astype(BF)
        self.copy_y = remote(
            self.sum_z.at[pl.ds((1 - y) * 8, 8)],
            self.land_y,
            self.sems[2].at[0],
            self.sems[3].at[0],
            shifted(me, 0, 1, 0, 0),
            wsh,
        )
        self.copy_y.start()

    def along_row(self, me, wsh):
        _, y, _, _ = coords(me)
        self.copy_y.wait_recv()
        value = self.sum_z[pl.ds(y * 8, 8)].astype(F32) + self.land_y[...].astype(F32)
        self.reduced[...] = value.astype(BF)
        place = lax.rem(me, 8)
        self.copies_row = []
        for at, (dx, dk) in enumerate(ROW_STEPS):
            peer = shifted(me, 0, 0, dx, dk)
            copy = remote(
                self.reduced.at[lax.rem(peer, 8)],
                self.out.at[place],
                self.sems[4].at[at],
                self.sems[5].at[at],
                peer,
                wsh,
            )
            copy.start()
            self.copies_row.append(copy)
        self.out[place] = self.reduced[place]

    def finish(self):
        for copy in self.copies_row:
            copy.wait()
        for copy in self.copies_z + [self.copy_y]:
            copy.wait_send()


def reduce_row(parts, collective_id, both, extra=None, swapped_whole=None, owned=()):
    has_whole = swapped_whole is not None
    _, rows, width = parts.shape
    block = (rows, width)
    pieces = 4
    columns = width // pieces
    has_extra = extra is not None

    def body(*refs):
        refs = list(refs)
        src = refs.pop(0)
        src2 = refs.pop(0) if has_extra else None
        src3 = refs.pop(0) if has_whole else None
        mine_in = [refs.pop(0) for _ in owned]
        out = refs.pop(0)
        out2 = refs.pop(0) if has_extra else None
        out3 = refs.pop(0) if has_whole else None
        mine_out = [refs.pop(0) for _ in owned]
        blocks = []
        for src4, out4 in reversed(list(zip(mine_in, mine_out))):
            blocks.append(Owned(src4, out4, refs[-Owned.SCRATCH :]))
            refs = refs[: -Owned.SCRATCH]
        arrived, summed, landed, swapped, total, send, recv, local = refs[:8]
        me, wsh = lax.axis_index("ctx"), lax.axis_index("wsh")
        other = 1 - wsh
        core = lax.rem(me, 2)
        _, _, x, _ = coords(me)
        partner = shifted(me, 0, 0, 0, 1)
        peers = [shifted(me, 0, 0, dx, 0) for dx in (1, 2, 3)]
        row_peers = [shifted(me, 0, 0, dx, dk) for dx, dk in ROW_STEPS]
        col_peers = [shifted(me, dz, dy, 0, 0) for dz, dy in COLUMN_STEPS]
        greeted = row_peers + col_peers if owned else peers + [partner]
        barrier, amount = greet([(peer, wsh) for peer in greeted] + [(me, other)])
        pl.semaphore_wait(barrier, amount)
        if has_whole:
            whole = remote(src3, out3, send.at[1, 9], recv.at[1, 9], me, other)
            whole.start()
        spans = [pl.ds(piece * columns, columns) for piece in range(pieces)]
        everything = pl.ds(0, rows)
        first = []
        for piece, span in enumerate(spans):
            for at, dx in enumerate((2, 1, 3, 0)):
                chip = lax.rem(x + dx, 4)
                copy = remote(
                    src.at[chip * 2 + 1 - core, everything, span],
                    arrived.at[at, everything, span],
                    send.at[piece, at],
                    recv.at[piece, at],
                    partner,
                    wsh,
                )
                copy.start()
                first.append(copy)
        for block4 in blocks:
            block4.along_z(me, wsh)
        if has_extra:
            arrived2, swapped2 = refs[8:]
            give2 = remote(src2.at[1 - core], arrived2, send.at[0, 8], recv.at[0, 8], partner, wsh)
            give2.start()
        second = []
        for piece, span in enumerate(spans):
            for at, dx in enumerate((2, 1, 3)):
                chip = lax.rem(x + dx, 4)
                first[piece * 4 + at].wait_recv()
                summed[at, :, span] = (
                    src[chip * 2 + core, :, span].astype(F32) + arrived[at, :, span].astype(F32)
                ).astype(BF)
                copy = remote(
                    summed.at[at, everything, span],
                    landed.at[at, everything, span],
                    send.at[piece, 4 + at],
                    recv.at[piece, 4 + at],
                    shifted(me, 0, 0, dx, 0),
                    wsh,
                )
                copy.start()
                second.append(copy)
            first[piece * 4 + 3].wait_recv()
            total[:, span] = src[x * 2 + core, :, span].astype(F32) + arrived[3, :, span].astype(F32)
        if has_extra:
            give2.wait()
            swapped2[0] = (src2[core].astype(F32) + arrived2[...].astype(F32)).astype(BF)
            swap2 = remote(swapped2.at[0], swapped2.at[1], send.at[1, 8], recv.at[1, 8], me, other)
            swap2.start()
        swaps = []
        for piece, span in enumerate(spans):
            for at in (1, 2, 0):
                second[piece * 3 + at].wait_recv()
            swapped[0, :, span] = (
                total[:, span]
                + landed[0, :, span].astype(F32)
                + landed[1, :, span].astype(F32)
                + landed[2, :, span].astype(F32)
            ).astype(BF)
            swap = remote(
                swapped.at[0, everything, span],
                swapped.at[1, everything, span],
                send.at[piece, 7],
                recv.at[piece, 7],
                me,
                other,
            )
            swap.start()
            swaps.append(swap)
        for block4 in blocks:
            block4.along_y(me, wsh)
        for block4 in blocks:
            block4.along_row(me, wsh)
        if has_extra:
            swap2.wait()
            out2[...] = swapped2[0].astype(F32) + swapped2[1].astype(F32)
        for piece, span in enumerate(spans):
            swaps[piece].wait()
            if both:
                total[:, span] = swapped[0, :, span].astype(F32) + swapped[1, :, span].astype(F32)
            else:
                out[:, span] = swapped[0, :, span].astype(F32) + swapped[1, :, span].astype(F32)
        if both:
            keep = pltpu.make_async_copy(total, out.at[core], local)
            keep.start()
            give = remote(total, out.at[core], send.at[0, 9], recv.at[0, 9], partner, wsh)
            give.start()
            give.wait()
            keep.wait()
        for copy in first + second:
            copy.wait_send()
        for block4 in blocks:
            block4.finish()
        if has_whole:
            whole.wait()

    shapes = [jax.ShapeDtypeStruct((2,) + block if both else block, F32)]
    scratch = [
        pltpu.VMEM((4,) + block, BF),
        pltpu.VMEM((3,) + block, BF),
        pltpu.VMEM((3,) + block, BF),
        pltpu.VMEM((2,) + block, BF),
        pltpu.VMEM(block, F32),
        DMA((pieces, 10)),
        DMA((pieces, 10)),
        DMA,
    ]
    operands = [parts]
    if has_extra:
        shapes.append(jax.ShapeDtypeStruct(block, F32))
        scratch += [pltpu.VMEM(block, BF), pltpu.VMEM((2,) + block, BF)]
        operands.append(extra)
    spaces = [VMEM] * len(operands)
    if has_whole:
        shapes.append(jax.ShapeDtypeStruct(swapped_whole.shape, swapped_whole.dtype))
        operands.append(swapped_whole)
        spaces.append(ANY)
    for value in owned:
        block8 = (8,) + value.shape[1:]
        shapes.append(jax.ShapeDtypeStruct(block8, BF))
        operands.append(value)
        spaces.append(VMEM)
        scratch += Owned.scratch(value)
    return pl.pallas_call(
        body,
        out_shape=shapes,
        in_specs=spaces,
        out_specs=spaces,
        scratch_shapes=scratch,
        compiler_params=call_params(collective_id),
        name="reduce_row",
        cost_estimate=cost(40),
    )(*operands)


def reduce_chip(parts, extra, collective_id):
    _, rows, width = parts.shape
    extra_block = None if extra is None else extra.shape[1:]

    def body(*refs):
        if extra is None:
            src, out, arrived, swapped, total, send, recv = refs
        else:
            src, src2, out, out2, arrived, swapped, total, arrived2, swapped2, send, recv = refs
        me, wsh = lax.axis_index("ctx"), lax.axis_index("wsh")
        other = 1 - wsh
        core = lax.rem(me, 2)
        partner = shifted(me, 0, 0, 0, 1)
        barrier, amount = greet([(partner, wsh), (me, other)])
        pl.semaphore_wait(barrier, amount)
        give = remote(src.at[1 - core], arrived, send.at[0], recv.at[0], partner, wsh)
        give.start()
        if extra is not None:
            give2 = remote(src2.at[1 - core], arrived2, send.at[2], recv.at[2], partner, wsh)
            give2.start()
        give.wait()
        swapped[0] = (src[core].astype(F32) + arrived[...].astype(F32)).astype(BF)
        swap = remote(swapped.at[0], swapped.at[1], send.at[1], recv.at[1], me, other)
        swap.start()
        if extra is not None:
            give2.wait()
            swapped2[0] = src2[core] + arrived2[...]
            swap2 = remote(swapped2.at[0], swapped2.at[1], send.at[3], recv.at[3], me, other)
            swap2.start()
            swap2.wait()
            out2[...] = swapped2[0] + swapped2[1]
        swap.wait()
        out[...] = swapped[0].astype(F32) + swapped[1].astype(F32)

    sds = jax.ShapeDtypeStruct
    block = (rows, width)
    shapes = [sds(block, F32)]
    scratch = [pltpu.VMEM(block, BF), pltpu.VMEM((2,) + block, BF), pltpu.VMEM(block, F32)]
    operands = [parts]
    if extra is not None:
        shapes.append(sds(extra_block, F32))
        scratch += [pltpu.VMEM(extra_block, F32), pltpu.VMEM((2,) + extra_block, F32)]
        operands.append(extra)
    scratch += [DMA((4,)), DMA((4,))]
    return pl.pallas_call(
        body,
        out_shape=shapes,
        in_specs=[VMEM] * len(operands),
        out_specs=[VMEM] * len(operands),
        scratch_shapes=scratch,
        compiler_params=call_params(collective_id),
        name="reduce_chip",
        cost_estimate=cost(17),
    )(*operands)


def reduce_keys(parts, owned, collective_id):
    _, groups, _, rows, width = parts.shape

    def body(src, src4, out, out4, arrived, mid, beside, summed, landed, send, recv, *scratch4):
        block4 = Owned(src4, out4, scratch4)
        me, wsh = lax.axis_index("ctx"), lax.axis_index("wsh")
        core = lax.rem(me, 2)
        _, _, x, _ = coords(me)
        side = lax.rem(x, 2)
        partner = shifted(me, 0, 0, 0, 1)
        neighbour = me + 2 - 4 * side
        steps = COLUMN_STEPS + ((0, 0),)
        peers = [shifted(me, dz, dy, 0, 0) for dz, dy in steps]
        row_peers = [shifted(me, 0, 0, dx, dk) for dx, dk in ROW_STEPS]
        barrier, amount = greet([(peer, wsh) for peer in peers[:-1] + row_peers])
        pl.semaphore_wait(barrier, amount)
        first = []
        for at, peer in enumerate(peers):
            group = lax.div(peer, 8)
            for turn, b in enumerate((1 - side, side)):
                copy = remote(
                    src.at[1 - core, group, b],
                    arrived.at[turn, at],
                    send.at[turn, at],
                    recv.at[turn, at],
                    partner,
                    wsh,
                )
                copy.start()
                first.append(copy)
        block4.along_z(me, wsh)
        across = []
        for at, peer in enumerate(peers):
            group = lax.div(peer, 8)
            first[2 * at].wait_recv()
            mid[at] = (src[core, group, 1 - side].astype(F32) + arrived[0, at].astype(F32)).astype(BF)
            copy = remote(mid.at[at], beside.at[at], send.at[2, at], recv.at[2, at], neighbour, wsh)
            copy.start()
            across.append(copy)
        last = []
        for at, peer in enumerate(peers):
            group = lax.div(peer, 8)
            first[2 * at + 1].wait_recv()
            across[at].wait_recv()
            value = (
                src[core, group, side].astype(F32)
                + arrived[1, at].astype(F32)
                + beside[at].astype(F32)
            )
            if at == groups - 1:
                out[...] = value
            else:
                summed[at] = value.astype(BF)
                copy = remote(summed.at[at], landed.at[at], send.at[3, at], recv.at[3, at], peer, wsh)
                copy.start()
                last.append(copy)
        block4.along_y(me, wsh)
        block4.along_row(me, wsh)
        for at, copy in enumerate(last):
            copy.wait_recv()
            out[...] += landed[at].astype(F32)
        for copy in first + across + last:
            copy.wait_send()
        block4.finish()

    block = (rows, width)
    return pl.pallas_call(
        body,
        out_shape=(
            jax.ShapeDtypeStruct(block, F32),
            jax.ShapeDtypeStruct((8,) + owned.shape[1:], BF),
        ),
        in_specs=[VMEM, VMEM],
        out_specs=[VMEM, VMEM],
        scratch_shapes=[
            pltpu.VMEM((2, groups) + block, BF),
            pltpu.VMEM((groups,) + block, BF),
            pltpu.VMEM((groups,) + block, BF),
            pltpu.VMEM((groups,) + block, BF),
            pltpu.VMEM((groups,) + block, BF),
            DMA((4, groups)),
            DMA((4, groups)),
        ]
        + Owned.scratch(owned),
        compiler_params=call_params(collective_id),
        name="reduce_keys",
        cost_estimate=cost(40),
    )(parts, owned)


def exchange(arrays, collective_id):
    amount = len(arrays)

    def body(*refs):
        ins, outs = refs[:amount], refs[amount : 2 * amount]
        send, recv, local = refs[2 * amount :]
        me, wsh = lax.axis_index("ctx"), lax.axis_index("wsh")
        chip = lax.div(me, 2)

        def target(step):
            dy = lax.rem(lax.div(step, 4), 2)
            return shifted(me, lax.div(step, 8), dy, lax.rem(step, 4), 0), lax.rem(wsh + dy, 2)

        barrier, count = greet_many(32, target)
        locals_ = []
        for at in range(amount):
            copy = pltpu.make_async_copy(ins[at].at[chip], outs[at].at[chip], local.at[at])
            copy.start()
            locals_.append(copy)
        pl.semaphore_wait(barrier, count)

        def one(step, carried):
            ctx, side = target(lax.rem(step * 13, 32))
            for at in range(amount):
                remote(
                    ins[at].at[lax.div(ctx, 2)], outs[at].at[chip], send.at[at], recv.at[at], ctx, side
                ).start()
            return carried

        lax.fori_loop(1, 32, one, 0)
        for copy in locals_:
            copy.wait()
        for at in range(amount):
            rest = outs[at].at[pl.ds(0, 31)]
            done = remote(rest, rest, send.at[at], recv.at[at], me, wsh)
            done.wait_send()
            done.wait_recv()

    return pl.pallas_call(
        body,
        out_shape=[jax.ShapeDtypeStruct(a.shape, a.dtype) for a in arrays],
        in_specs=[ANY] * amount,
        out_specs=[ANY] * amount,
        scratch_shapes=[DMA((amount,)), DMA((amount,)), DMA((amount,))],
        compiler_params=call_params(collective_id),
        name="exchange",
        cost_estimate=cost(48),
    )(*arrays)


def exchange_behind(value):
    groups = []
    for core in range(2):
        for parity in range(2):
            groups.append(
                [(chip * 2 + core) * 2 + (parity + chip // 4) % 2 for chip in range(32)]
            )
    return lax.all_to_all(
        value, ("ctx", "wsh"), split_axis=0, concat_axis=0, tiled=True, axis_index_groups=groups
    )


def natural_order(plan, kv_ref, keys, values, transposed):
    def one(block, carried):
        rows = kv_ref[pl.ds(pl.multiple_of(plan[PLAN_INVERSE + block] * BLK, BLK), BLK), :]
        at = pl.ds(pl.multiple_of(block * BLK, BLK), BLK)
        keys[at, :] = rows[:, :HEAD_WIDTH]
        values[at, :] = rows[:, HEAD_WIDTH:]
        return carried

    lax.fori_loop(0, kv_ref.shape[0] // BLK, one, 0, unroll=8)
    source, turned = transposed

    def turn(chunk, carried):
        at = pl.ds(pl.multiple_of(chunk * CHUNK, CHUNK), CHUNK)
        turned[:, at] = source[at, :].T
        return carried

    lax.fori_loop(0, kv_ref.shape[0] // CHUNK, turn, 0, unroll=4)


def stacked(ref, first, second):
    rows = [ref[pl.ds(pl.multiple_of(at * BLK, BLK), BLK), :] for at in (first, second)]
    return jnp.concatenate(
        [rows[0][:, :HEAD_WIDTH], rows[0][:, HEAD_WIDTH:], rows[1][:, :HEAD_WIDTH], rows[1][:, HEAD_WIDTH:]],
        axis=0,
    )


def unstacked(ref, first, second, value):
    for at, begin in ((first, 0), (second, 2 * BLK)):
        ref[pl.ds(pl.multiple_of(at * BLK, BLK), BLK), :] = jnp.concatenate(
            [value[begin : begin + BLK], value[begin + BLK : begin + 2 * BLK]], axis=1
        )


PLAN_BOUNDS, PLAN_INVERSE, PLAN_BLOCKS, PLAN_SIZE = 16, 64, 192, 256


def start_of(lengths, position):
    begin = lengths[0] * 0
    start = position * 0
    for at in range(lengths.shape[0]):
        start = jnp.where(begin <= position, begin, start)
        begin = begin + lengths[at]
    return start


def make_plan(block_order, lengths, base, plan):
    def place(at, carried):
        plan[PLAN_INVERSE + block_order[at]] = at
        return carried

    lax.fori_loop(0, block_order.shape[0], place, 0, unroll=8)

    def rank(at, carried):
        mine = block_order[base + at]
        before = jnp.int32(0)
        for other in range(16):
            before = before + jnp.where(block_order[base + other] < mine, 1, 0)
        plan[before] = at
        plan[PLAN_BLOCKS + before] = mine
        return carried

    lax.fori_loop(0, 16, rank, 0)

    def bound(step, carried):
        one, two = plan[PLAN_BLOCKS + 2 * step], plan[PLAN_BLOCKS + 2 * step + 1]
        low = lax.div(start_of(lengths, one * BLK), CHUNK)
        high = lax.div(two * BLK, CHUNK) + 1
        last = start_of(lengths, two * BLK + BLK - 1)
        inner_low = jnp.minimum(jnp.maximum(lax.div(last + CHUNK - 1, CHUNK), low), high)
        inner_high = jnp.minimum(jnp.maximum(lax.div(one * BLK + 1, CHUNK), inner_low), high)
        for at, value in enumerate((low, inner_low, inner_high, high)):
            plan[PLAN_BOUNDS + 4 * step + at] = value
        return carried

    lax.fori_loop(0, 8, bound, 0)


def strips_of(plan, lengths, step):
    lane = lax.broadcasted_iota(jnp.int32, (1, 4 * BLK), 1)
    block = jnp.where(lane < 2 * BLK, plan[PLAN_BLOCKS + 2 * step], plan[PLAN_BLOCKS + 2 * step + 1])
    position = block * BLK + lax.rem(lane, BLK)
    return position, start_of(lengths, position)


def three_loops(step, plan, chunk, state):
    low, inner_low, inner_high, high = [plan[PLAN_BOUNDS + 4 * step + at] for at in range(4)]
    state = lax.fori_loop(low, inner_low, functools.partial(chunk, True), state)
    state = lax.fori_loop(inner_low, inner_high, functools.partial(chunk, False), state)
    return lax.fori_loop(inner_high, high, functools.partial(chunk, True), state)


def kept(scores, at, q_pos, q_start):
    k_pos = at + lax.broadcasted_iota(jnp.int32, scores.shape, 0)
    return jnp.where((k_pos <= q_pos) & (k_pos >= q_start), scores, MASKED)


SCORE_SCALE = 1.0 / math.sqrt(HEAD_WIDTH)
TWO_SCALE = SCORE_SCALE / math.log(2.0)


def forward_kernel(block_order, lengths, group, q_ref, kv_ref, out_ref, lse_ref, plan, keys, values, values_t, acc):
    step = pl.program_id(0)

    @pl.when(step == 0)
    def _():
        make_plan(block_order, lengths, group[0] * 16, plan)
        natural_order(plan, kv_ref, keys, values, (values, values_t))

    first, second = plan[2 * step], plan[2 * step + 1]
    q_t = stacked(q_ref, first, second).astype(F32).T.astype(BF)
    q_pos, q_start = strips_of(plan, lengths, step)
    width = 4 * BLK
    acc[...] = jnp.zeros_like(acc)

    def chunk(masked, index, total):
        at = pl.multiple_of(index * CHUNK, CHUNK)
        scores = matmul(keys[pl.ds(at, CHUNK), :], q_t)
        if masked:
            scores = kept(scores, at, q_pos, q_start)
        probs = jnp.exp2(scores * TWO_SCALE)
        acc[...] += matmul(values_t[:, pl.ds(at, CHUNK)], probs.astype(BF))
        return total + jnp.sum(probs, axis=0, keepdims=True)

    total = three_loops(step, plan, chunk, jnp.zeros((1, width), F32))
    lse_ref[0] = jnp.log2(total)
    unstacked(out_ref, first, second, (acc[...] / total).T.astype(BF))


def attend(block_order, lengths, group, queries, kv):
    rows = queries.shape[0]
    steps = rows // (2 * BLK)
    everything = pl.BlockSpec(queries.shape, lambda i, *_: (0, 0))
    strip = pl.BlockSpec((1, 1, 4 * BLK), lambda i, *_: (i, 0, 0))
    sds = jax.ShapeDtypeStruct
    return pl.pallas_call(
        forward_kernel,
        out_shape=(
            sds(queries.shape, BF),
            sds((steps, 1, 4 * BLK), F32),
            sds((PLAN_SIZE,), jnp.int32),
        ),
        grid_spec=pltpu.PrefetchScalarGridSpec(
            num_scalar_prefetch=3,
            grid=(steps,),
            in_specs=[everything, pl.BlockSpec(kv.shape, lambda i, *_: (0, 0))],
            out_specs=[everything, strip, pl.BlockSpec(memory_space=pltpu.SMEM)],
            scratch_shapes=[
                pltpu.VMEM((kv.shape[0], HEAD_WIDTH), BF),
                pltpu.VMEM((kv.shape[0], HEAD_WIDTH), BF),
                pltpu.VMEM((HEAD_WIDTH, kv.shape[0]), BF),
                pltpu.VMEM((HEAD_WIDTH, 4 * BLK), F32),
            ],
        ),
        compiler_params=pltpu.CompilerParams(vmem_limit_bytes=ROOM),
        name="attend",
        cost_estimate=cost(17),
    )(block_order, lengths, group, queries, kv)


def backward_kernel(plan, lengths, q_ref, heads_ref, da_ref, wo_ref, kv_ref, lse_ref, dq_ref, dkv_ref, keys, values, keys_t, d_keys, d_values, acc):
    step = pl.program_id(0)

    @pl.when(step == 0)
    def _():
        natural_order(plan, kv_ref, keys, values, (keys, keys_t))
        d_keys[...] = jnp.zeros_like(d_keys)
        d_values[...] = jnp.zeros_like(d_values)

    first, second = plan[2 * step], plan[2 * step + 1]
    q = stacked(q_ref, first, second)
    d_rows = matmul(
        jnp.concatenate(
            [da_ref[pl.ds(pl.multiple_of(at * BLK, BLK), BLK), :] for at in (first, second)], axis=0
        ),
        wo_ref[...],
    )
    d_out = jnp.concatenate(
        [
            d_rows[begin : begin + BLK, head : head + HEAD_WIDTH]
            for begin in (0, BLK)
            for head in (0, HEAD_WIDTH)
        ],
        axis=0,
    ).astype(BF)
    q_t = q.astype(F32).T.astype(BF)
    d_out_wide = d_out.astype(F32).T
    d_out_t = d_out_wide.astype(BF)
    q_pos, q_start = strips_of(plan, lengths, step)
    lse = lse_ref[0]
    dots = jnp.sum(d_out_wide * stacked(heads_ref, first, second).astype(F32).T, axis=0, keepdims=True)
    acc[...] = jnp.zeros_like(acc)

    def chunk(masked, index, carried):
        at = pl.multiple_of(index * CHUNK, CHUNK)
        here = pl.ds(at, CHUNK)
        scores = matmul(keys[here, :], q_t)
        if masked:
            scores = kept(scores, at, q_pos, q_start)
        probs = jnp.exp2(scores * TWO_SCALE - lse)
        d_probs = matmul(values[here, :], d_out_t)
        d_scores = (probs * (d_probs - dots)).astype(BF)
        d_values[here, :] += matmul(probs.astype(BF), d_out)
        d_keys[here, :] += matmul(d_scores, q)
        acc[...] += matmul(keys_t[:, here], d_scores)
        return carried

    three_loops(step, plan, chunk, 0)
    unstacked(dq_ref, first, second, (acc[...] * SCORE_SCALE).T)

    @pl.when(step == pl.num_programs(0) - 1)
    def _():
        def one(block, carried):
            dealt = plan[PLAN_INVERSE + block]
            group, inside = dealt // 16, dealt % 16
            half, rest = inside // 8, inside % 8
            at = pl.ds(pl.multiple_of(block * BLK, BLK), BLK)
            to = pl.ds(pl.multiple_of(rest * BLK, BLK), BLK)
            dkv_ref[half, group, 0, to, :] = (d_keys[at, :] * SCORE_SCALE).astype(BF)
            dkv_ref[half, group, 1, to, :] = d_values[at, :].astype(BF)
            return carried

        lax.fori_loop(0, kv_ref.shape[0] // BLK, one, 0, unroll=4)


def attend_back(plan, lengths, queries, heads, d_attn, wo_t, kv, lse):
    rows = queries.shape[0]
    total = kv.shape[0]
    steps = rows // (2 * BLK)
    everything = pl.BlockSpec(queries.shape, lambda i, *_: (0, 0))
    strip = pl.BlockSpec((1, 1, 4 * BLK), lambda i, *_: (i, 0, 0))
    sds = jax.ShapeDtypeStruct
    dkv_shape = (2, total // rows, 2, rows // 2, HEAD_WIDTH)
    return pl.pallas_call(
        backward_kernel,
        out_shape=(sds(queries.shape, F32), sds(dkv_shape, BF)),
        grid_spec=pltpu.PrefetchScalarGridSpec(
            num_scalar_prefetch=2,
            grid=(steps,),
            in_specs=[
                everything,
                everything,
                pl.BlockSpec(d_attn.shape, lambda i, *_: (0, 0)),
                pl.BlockSpec((wo_t.shape[0], queries.shape[1]), lambda i, *_: (0, 0)),
                pl.BlockSpec(kv.shape, lambda i, *_: (0, 0)),
                strip,
            ],
            out_specs=[everything, pl.BlockSpec(dkv_shape, lambda i, *_: (0, 0, 0, 0, 0))],
            scratch_shapes=[
                pltpu.VMEM((total, HEAD_WIDTH), BF),
                pltpu.VMEM((total, HEAD_WIDTH), BF),
                pltpu.VMEM((HEAD_WIDTH, total), BF),
                pltpu.VMEM((total, HEAD_WIDTH), F32),
                pltpu.VMEM((total, HEAD_WIDTH), F32),
                pltpu.VMEM((HEAD_WIDTH, 4 * BLK), F32),
            ],
        ),
        compiler_params=pltpu.CompilerParams(vmem_limit_bytes=ROOM),
        name="attend_back",
        cost_estimate=cost(24),
    )(plan, lengths, queries, heads, d_attn, wo_t, kv, lse)


def expert_kernel(side, x_ref, cot_ref, gate_ref, g_own, u_own, d_own, g_other, u_other, u_rest, d_other, y_ref, dx_ref, a_ref, dg_ref, du_ref, dy_ref, gate_w, up_w, down_w, gate_f, up_f, down_f, sems):
    half = g_other.shape[1]
    own_copies, other_copies = [], []
    for at, (own, other, whole, stage, columns) in enumerate(
        (
            (g_own, g_other, gate_w, gate_f, True),
            (u_own, u_other, up_w, up_f, True),
            (d_own, d_other, down_w, down_f, False),
        )
    ):
        span = pl.ds(half, half)
        target = whole.at[pl.ds(0, whole.shape[0]), span] if columns else whole.at[span]
        own_copies.append(pltpu.make_async_copy(own.at[side[0]], stage, sems.at[at, 0]))
        if at == 1:
            cut = u_other.shape[0]
            parts = ((u_other, pl.ds(0, cut)), (u_rest, pl.ds(cut, u_rest.shape[0])))
            for side_at, (part, place) in enumerate(parts):
                other_copies.append(
                    pltpu.make_async_copy(part, whole.at[place, span], sems.at[at, 1 + side_at])
                )
        else:
            other_copies.append(pltpu.make_async_copy(other, target, sems.at[at, 1]))

    @pl.when(pl.program_id(0) == 0)
    def _():
        for copy in own_copies + other_copies:
            copy.start()
        own_copies[0].wait()
        gate_w[:, :half] = gate_f[...].astype(BF)
        own_copies[1].wait()
        up_w[:, :half] = up_f[...].astype(BF)
        own_copies[2].wait()
        down_w[:half, :] = down_f[...].astype(BF)
        for copy in other_copies:
            copy.wait()

    x = x_ref[...]
    gate_pre = matmul(x, gate_w[...])
    up_pre = matmul(x, up_w[...])
    sigma = 1.0 / (1.0 + jnp.exp(-gate_pre))
    silu = gate_pre * sigma
    activated = (silu * up_pre).astype(BF)
    a_ref[...] = activated
    gates = gate_ref[:, 0:1].astype(F32) + gate_ref[:, 64:65].astype(F32)
    cot = cot_ref[...].astype(F32)
    out = matmul(activated, down_w[...])
    y_ref[...] = (out * gates).astype(BF)
    dots = jnp.sum(out * cot, axis=1, keepdims=True)
    high = dots.astype(BF).astype(F32)
    lane = lax.broadcasted_iota(jnp.int32, (dots.shape[0], 128), 1)
    dx_ref[:, y_ref.shape[1] :] = jnp.where(lane < 64, high, dots - high).astype(BF)
    d_pairs = (cot * gates).astype(BF)
    dy_ref[...] = d_pairs
    d_act = times_transposed(d_pairs, down_w[...])
    d_gate = (d_act * up_pre * sigma * (1.0 + gate_pre * (1.0 - sigma))).astype(BF)
    d_up = (d_act * silu).astype(BF)
    dg_ref[...] = d_gate
    du_ref[...] = d_up
    dx_ref[:, : y_ref.shape[1]] = (times_transposed(d_gate, gate_w[...]) + times_transposed(d_up, up_w[...])).astype(BF)


def run_expert(side, rows_in, cot, gates, own, other):
    count, width = rows_in.shape
    half = other[0].shape[1]
    tile = 256
    sds = jax.ShapeDtypeStruct

    def by_rows(columns):
        return pl.BlockSpec((tile, columns), lambda i, side: (i, 0))

    return pl.pallas_call(
        expert_kernel,
        out_shape=(
            sds((count, width), BF),
            sds((count, width + 128), BF),
            sds((count, 2 * half), BF),
            sds((count, 2 * half), BF),
            sds((count, 2 * half), BF),
            sds((count, width), BF),
        ),
        grid_spec=pltpu.PrefetchScalarGridSpec(
            num_scalar_prefetch=1,
            grid=(count // tile,),
            in_specs=[by_rows(width), by_rows(width), by_rows(128)] + [ANY] * 7,
            out_specs=[
                by_rows(width),
                by_rows(width + 128),
                by_rows(2 * half),
                by_rows(2 * half),
                by_rows(2 * half),
                by_rows(width),
            ],
            scratch_shapes=[
                pltpu.VMEM((width, 2 * half), BF),
                pltpu.VMEM((width, 2 * half), BF),
                pltpu.VMEM((2 * half, width), BF),
                pltpu.VMEM((width, half), F32),
                pltpu.VMEM((width, half), F32),
                pltpu.VMEM((half, width), F32),
                DMA((3, 3)),
            ],
        ),
        compiler_params=pltpu.CompilerParams(vmem_limit_bytes=ROOM),
        name="run_expert",
        cost_estimate=cost(25),
    )(side, rows_in, cot, gates, *own, *other)


def expert_grads_kernel(side, x_ref, dy_ref, a_ref, dg_ref, du_ref, gate_ref, up_ref, down_ref, gate_out, up_out, down_out, a_t):
    half = gate_ref.shape[-1]

    @pl.when(pl.program_id(0) == 0)
    def _():
        a_t[...] = a_ref[...].T

    x_t = x_ref[...].T
    for grad_ref, own, other in ((dg_ref, gate_ref, gate_out), (du_ref, up_ref, up_out)):
        value = matmul(x_t, grad_ref[...])
        own[0] = value[:, :half]
        other[...] = value[:, half:].astype(BF)
    value = matmul(a_t[...], dy_ref[...])
    down_ref[0] = value[:half]
    down_out[...] = value[half:].astype(BF)


def expert_grads(side, rows_in, d_pairs, activated, d_gate, d_up):
    count, width = rows_in.shape
    whole = activated.shape[1]
    half = whole // 2
    tile = 256
    sds = jax.ShapeDtypeStruct
    columns = pl.BlockSpec((count, tile), lambda i, side: (0, i))
    full = pl.BlockSpec((count, whole), lambda i, side: (0, 0))
    own_rows = pl.BlockSpec((1, tile, half), lambda i, side: (side[0], i, 0))
    other_rows = pl.BlockSpec((tile, half), lambda i, side: (i, 0))
    return pl.pallas_call(
        expert_grads_kernel,
        out_shape=(
            sds((2, width, half), F32),
            sds((2, width, half), F32),
            sds((2, half, width), F32),
            sds((width, half), BF),
            sds((width, half), BF),
            sds((half, width), BF),
        ),
        grid_spec=pltpu.PrefetchScalarGridSpec(
            num_scalar_prefetch=1,
            grid=(width // tile,),
            in_specs=[columns, columns, full, full, full],
            out_specs=[
                own_rows,
                own_rows,
                pl.BlockSpec((1, half, tile), lambda i, side: (side[0], 0, i)),
                other_rows,
                other_rows,
                pl.BlockSpec((half, tile), lambda i, side: (0, i)),
            ],
            scratch_shapes=[pltpu.VMEM((whole, count), BF)],
        ),
        compiler_params=pltpu.CompilerParams(vmem_limit_bytes=ROOM),
        name="expert_grads",
        cost_estimate=cost(12),
    )(side, rows_in, d_pairs, activated, d_gate, d_up)


def place_kernel(side, *refs):
    for at in range(3):
        refs[6 + at][0] = refs[at][...].astype(F32)


def place_other(side, arrived, placed):
    tile = 256
    width, half = arrived[0].shape
    rows_in = pl.BlockSpec((tile, half), lambda i, side: (i, 0))
    rows_out = pl.BlockSpec((1, tile, half), lambda i, side: (1 - side[0], i, 0))
    return pl.pallas_call(
        place_kernel,
        out_shape=[jax.ShapeDtypeStruct(value.shape, F32) for value in placed],
        grid_spec=pltpu.PrefetchScalarGridSpec(
            num_scalar_prefetch=1,
            grid=(width // tile,),
            in_specs=[rows_in, rows_in, pl.BlockSpec((half, tile), lambda i, side: (0, i))] + [ANY] * 3,
            out_specs=[
                rows_out,
                rows_out,
                pl.BlockSpec((1, half, tile), lambda i, side: (1 - side[0], 0, i)),
            ],
        ),
        input_output_aliases={4: 0, 5: 1, 6: 2},
        compiler_params=pltpu.CompilerParams(vmem_limit_bytes=ROOM),
        name="place_other",
        cost_estimate=cost(5),
    )(side, *arrived, *placed)


def project_kernel(block_order, lengths, group, t_ref, w_ref, side_ref, flag_ref, freq_ref, ga_ref, gq_ref, gk_ref, h_ref, q_ref, kv_ref, qp_ref, kp_ref, cos_ref, sin_ref):
    tile = t_ref.shape[0]
    row = lax.broadcasted_iota(jnp.int32, (tile, HEAD_WIDTH), 0)
    lane = lax.broadcasted_iota(jnp.int32, (tile, HEAD_WIDTH), 1)
    first_block = group[0] * 16 + pl.program_id(0) * (tile // BLK)
    position = row * 0
    for at in range(tile // BLK):
        inside = block_order[first_block + at] * BLK + row - at * BLK
        position = jnp.where(row >= at * BLK, inside, position)
    angles = (position - start_of(lengths, position)).astype(F32) * freq_ref[...]
    cosine = jnp.cos(angles)
    sine_tab = jnp.where(lane < HEAD_WIDTH // 2, -1.0, 1.0) * jnp.sin(angles)
    cos_ref[...] = cosine
    sin_ref[...] = sine_tab
    rows = t_ref[...].astype(F32)
    inverse = lax.rsqrt(jnp.mean(rows * rows, axis=1, keepdims=True) + EPSILON)
    hidden = (rows * inverse * ga_ref[...]).astype(BF)
    h_ref[...] = hidden
    qkv = matmul(hidden, w_ref[...])
    own = qkv[:, 2 * HEAD_WIDTH :]
    other = matmul(hidden, side_ref[...])
    first = flag_ref[0:1, :] > 0.5

    def turned(value, gain):
        root = lax.rsqrt(jnp.mean(value * value, axis=1, keepdims=True) + EPSILON)
        value = value * root * gain
        return (value * cosine + pltpu.roll(value, HEAD_WIDTH // 2, 1) * sine_tab).astype(BF)

    for head in range(2):
        span = slice(head * HEAD_WIDTH, (head + 1) * HEAD_WIDTH)
        q_ref[:, span] = turned(qkv[:, span], gq_ref[...])
    qp_ref[...] = qkv[:, : 2 * HEAD_WIDTH]
    keys = jnp.where(first, own, other)
    kp_ref[...] = keys
    kv_ref[:, :HEAD_WIDTH] = turned(keys, gk_ref[...])
    kv_ref[:, HEAD_WIDTH:] = jnp.where(first, other, own).astype(BF)


def project(block_order, lengths, group, tokens, weights, side, first, frequency, gain, gain_query, gain_key):
    rows, width = tokens.shape
    tile = 256
    sds = jax.ShapeDtypeStruct

    def by_rows(columns):
        return pl.BlockSpec((tile, columns), lambda i, *_: (i, 0))

    def whole(value):
        return pl.BlockSpec(value.shape, lambda i, *_: (0, 0))

    return pl.pallas_call(
        project_kernel,
        out_shape=(
            sds((rows, width), BF),
            sds((rows, 256), BF),
            sds((rows, 256), BF),
            sds((rows, 256), F32),
            sds((rows, 128), F32),
            sds((rows, 128), F32),
            sds((rows, 128), F32),
        ),
        grid_spec=pltpu.PrefetchScalarGridSpec(
            num_scalar_prefetch=3,
            grid=(rows // tile,),
            in_specs=[
                by_rows(width),
                whole(weights),
                whole(side),
                whole(first),
                whole(frequency),
                whole(gain),
                whole(gain_query),
                whole(gain_key),
            ],
            out_specs=[
                by_rows(width),
                by_rows(256),
                by_rows(256),
                by_rows(256),
                by_rows(128),
                by_rows(128),
                by_rows(128),
            ],
        ),
        compiler_params=pltpu.CompilerParams(vmem_limit_bytes=ROOM),
        name="project",
        cost_estimate=cost(8),
    )(block_order, lengths, group, tokens, weights, side, first, frequency, gain, gain_query, gain_key)


def project_back_kernel(dq_ref, ds_ref, qp_ref, kp_ref, cos_ref, sin_ref, h_ref, w_ref, side_ref, gq_ref, gk_ref, flag_ref, part_ref, late_ref, side_w, total, gains):
    step = pl.program_id(0)
    cosine, sine_tab = cos_ref[...], sin_ref[...]
    key, first, own = flag_ref[0:1, :], flag_ref[1:2, :], flag_ref[2:3, :]
    heads = 2 * HEAD_WIDTH

    @pl.when(step == 0)
    def _():
        gains[...] = jnp.zeros_like(gains)
        total[...] = jnp.zeros_like(total)
        side_w[...] = jnp.where(
            own > 0.5, w_ref[:, heads:].astype(F32), side_ref[...].astype(F32)
        ).astype(BF)

    def back(gradient, value, gain):
        gradient = gradient * cosine - pltpu.roll(gradient, HEAD_WIDTH // 2, 1) * sine_tab
        root = lax.rsqrt(jnp.mean(value * value, axis=1, keepdims=True) + EPSILON)
        weighted = gradient * gain
        mean_term = jnp.mean(weighted * value, axis=1, keepdims=True)
        terms = jnp.sum(gradient * value * root, axis=0, keepdims=True)
        return root * weighted - value * (root * root * root) * mean_term, terms

    columns = []
    for head in range(2):
        span = slice(head * HEAD_WIDTH, (head + 1) * HEAD_WIDTH)
        value, terms = back(dq_ref[:, span], qp_ref[:, span], gq_ref[...])
        columns.append(value.astype(BF))
        gains[0:1, :] += terms
    d_side = ds_ref[...]
    value, terms = back(d_side, kp_ref[...], gk_ref[...])
    mine = jnp.where(first == (step // 2).astype(F32), 1.0, 0.0)
    columns.append((jnp.where(key > 0.5, value, d_side) * mine).astype(BF))
    gains[1:2, :] += terms * key * mine
    d_all = jnp.concatenate(columns, axis=1)
    part_ref[...] = (
        times_transposed(d_all[:, :heads], w_ref[:, :heads])
        + times_transposed(d_all[:, heads:], side_w[...])
    ).astype(BF)
    total[...] += transposed_times(h_ref[...], d_all)

    @pl.when(step == pl.num_programs(0) - 1)
    def _():
        pieces, depth = late_ref.shape[0], h_ref.shape[1] // late_ref.shape[0]
        for at in range(3):
            value = total[:, at * HEAD_WIDTH : (at + 1) * HEAD_WIDTH].astype(BF)
            late_ref[:, at * depth : (at + 1) * depth, :] = value.reshape(pieces, depth, HEAD_WIDTH)
        late_ref[:, 3 * depth :, :] = jnp.broadcast_to(
            gains[...].astype(BF)[None], (pieces,) + gains.shape
        )


def project_back(d_queries, d_side, q_pre, k_pre, cosine, sine_tab, hidden, weights, side, gain_query, gain_key, flags):
    rows = d_queries.shape[0]
    width = hidden.shape[1]
    tile = 256
    tiles = rows // tile
    owners = 64
    sds = jax.ShapeDtypeStruct
    late = (owners, 3 * width // owners + 16, 128)

    def by_rows(columns):
        return pl.BlockSpec((tile, columns), lambda i: (i, 0))

    def whole(value):
        return pl.BlockSpec(value.shape, lambda i: (0, 0))

    half_rows = pl.BlockSpec((tile, 128), lambda i: (i % (tiles // 2), 0))
    return pl.pallas_call(
        project_back_kernel,
        grid=(tiles,),
        out_shape=(sds((rows, width), BF), sds(late, BF)),
        in_specs=[
            by_rows(256),
            half_rows,
            by_rows(256),
            by_rows(128),
            by_rows(128),
            by_rows(128),
            by_rows(width),
            whole(weights),
            whole(side),
            whole(gain_query),
            whole(gain_key),
            whole(flags),
        ],
        out_specs=[by_rows(width), pl.BlockSpec(late, lambda i: (0, 0, 0))],
        scratch_shapes=[
            pltpu.VMEM((width, 128), BF),
            pltpu.VMEM((width, 384), F32),
            pltpu.VMEM((16, 128), F32),
        ],
        compiler_params=pltpu.CompilerParams(vmem_limit_bytes=ROOM),
        name="project_back",
        cost_estimate=cost(12),
    )(
        d_queries, d_side, q_pre, k_pre, cosine, sine_tab, hidden, weights, side, gain_query, gain_key, flags
    )


def after(value, earlier):
    return lax.optimization_barrier((value, earlier))


def lanes_to(row, lanes=128):
    return jnp.pad(row, ((0, 0),) * (row.ndim - 1) + ((0, lanes - row.shape[-1]),))


def local(
    tokens,
    cotangent,
    seq_lengths,
    block_order,
    routes,
    w_query,
    key_weight,
    value_weight,
    w_out,
    gain_attn,
    gain_query,
    gain_key,
    gain_ffn,
    w_router,
    w_gate,
    w_up,
    w_down,
):
    rows = tokens.shape[0]
    width = tokens.shape[1]
    experts = w_router.shape[1]
    block_count = block_order.shape[0]
    wsh = lax.axis_index("wsh")
    me = lax.axis_index("ctx")
    core = lax.rem(me, 2)
    place = lax.rem(me, 8)
    group = lax.div(me, 8)
    row_tokens = 8 * rows

    def swap(value):
        return lax.ppermute(value, "wsh", [(0, 1), (1, 0)])

    depth = w_query.shape[0]
    q_part = to_low(w_query).reshape(depth, 8, 256).transpose(1, 0, 2)
    sides = [
        to_low(value[:, head * 128 : head * 128 + 128])
        for head in (0, 0, 1, 1)
        for value in (key_weight, value_weight)
    ]
    w_pack = jnp.concatenate([q_part, jnp.stack(sides)], axis=2)
    small = jnp.concatenate(
        [lanes_to(gain_attn[None, :]), lanes_to(gain_ffn[None, :]), jnp.zeros((6, 128), F32)], axis=0
    )
    w_all, row_rows, small_all, chip_routes, chip_cot, other_gate, other_up, other_down, w_side = gather_first(
        w_pack, tokens, small, routes.T, cotangent, (w_gate, w_up, w_down)
    )
    w_main = w_all.reshape(width, 384)
    w_side = w_side.reshape(width, 128)
    is_key = lax.rem(lax.div(me, 2), 2) == 0

    def flag(value):
        return jnp.broadcast_to(value.astype(F32).reshape(1, 1), (8, 128))

    g_attn = to_low(small_all[:, 0, :depth].reshape(width)).astype(F32)
    g_ffn = to_low(small_all[:, 1, :depth].reshape(width)).astype(F32)
    g_query = rounded(gain_query)
    g_key = rounded(gain_key)

    o_part = to_low(w_out).T.reshape(depth, 8, 256).transpose(1, 0, 2)
    r_part = jnp.broadcast_to(to_low(w_router)[None], (8, depth, experts))
    late_pack = jnp.tile(jnp.concatenate([o_part, r_part], axis=2), (8, 1, 1))
    late_pack, small_all = after(late_pack, small_all)
    late_all = lax.all_to_all(late_pack, "ctx", split_axis=0, concat_axis=0, tiled=True).reshape(width, 384)

    route_rows = chip_routes.transpose(0, 2, 1)
    hits = jnp.any(
        route_rows[:, :, :, None] == jnp.arange(experts, dtype=jnp.int32)[None, None, None, :], axis=2
    )
    before = jnp.tril(jnp.ones((rows, rows), BF), -1)
    ranks = jnp.einsum("ts,hse->hte", before, hits.astype(BF), preferred_element_type=F32).astype(jnp.int32)
    ranks = jnp.where(hits, ranks + jnp.array([0, CAP], jnp.int32)[:, None, None], -1)
    hits = hits.reshape(2 * rows, experts)
    chips = experts // 4
    chip_ids = jnp.arange(chips, dtype=jnp.int32)
    quarter = core * 2 + (wsh + chip_ids // 4 + lax.div(me, 8)) % 2

    def my_quarter(value):
        by_chip = value.reshape(2 * rows, experts).T.reshape(chips, 4, 2 * rows)
        two = lax.dynamic_slice_in_dim(by_chip, core * 2, 2, 1)
        return jnp.where((quarter % 2 == 0)[:, None], two[:, 0], two[:, 1])

    my_ranks = my_quarter(ranks)
    slots = 2 * CAP
    pick = my_ranks[:, None, :] == jnp.arange(slots, dtype=jnp.int32)[None, :, None]
    pick_low = pick.astype(BF).reshape(chips * slots, 2 * rows)
    cot_rows = matmul(pick_low, chip_cot.reshape(2 * rows, width)).astype(BF)
    half_dim = HEAD_WIDTH // 2
    frequency = jnp.power(ROPE_BASE, -2.0 * jnp.arange(half_dim, dtype=jnp.float32) / HEAD_WIDTH)
    frequency = jnp.concatenate([frequency, frequency])[None, :]
    row_rows = row_rows.reshape(row_tokens, width)
    hidden_one, queries, kv, q_pre, k_pre, cosine, sine_tab = project(
        block_order,
        seq_lengths,
        group.reshape(1),
        row_rows,
        w_main,
        w_side,
        flag(core == 0),
        frequency,
        g_attn[None, :],
        g_query[None, :],
        g_key[None, :],
    )
    kv_all = gather_keys(kv, 1).reshape(block_count * BLK, 256)
    late_all, kv_all = after(late_all, kv_all)
    wo_t = late_all[:, :256]
    wr = late_all[:, 256:]
    (cot_rows, other_gate), kv_all = after((cot_rows, other_gate), kv_all)
    gate_back = swap(other_gate)
    cot_there = exchange_behind(cot_rows.reshape(chips, slots, width)).reshape(chips * slots, width)
    heads, lse, plan = attend(block_order, seq_lengths, group.reshape(1), queries, kv_all)

    attn_parts = to_low(times_transposed(heads, wo_t)).reshape(8, rows, width)
    (gate_back, cot_there, other_up, other_down), attn_parts = after(
        (gate_back, cot_there, other_up, other_down), attn_parts
    )
    up_cut = width * 5 // 8
    attn_total, up_first = reduce_row(attn_parts, 2, True, swapped_whole=other_up[:up_cut])
    attn_total = attn_total.reshape(2 * rows, width)
    chip_stream = lax.dynamic_slice_in_dim(row_rows, (place - core) * rows, 2 * rows, 0).astype(F32)
    chip_residual = chip_stream + attn_total
    chip_inverse_two = inverse_root(chip_residual)
    chip_hidden = to_low(chip_residual * chip_inverse_two * g_ffn)
    logits = matmul(chip_hidden, wr)
    masked_logits = jnp.where(hits, logits, MASKED)
    gate_exps = jnp.where(
        hits, jnp.exp(masked_logits - jnp.max(masked_logits, axis=-1, keepdims=True)), 0.0
    )
    gates = gate_exps / jnp.sum(gate_exps, axis=-1, keepdims=True)

    def my_rows(value):
        return lax.dynamic_slice_in_dim(value, core * rows, rows, 0)

    out_rows = matmul(pick_low, chip_hidden).astype(BF).reshape(chips, slots, width)
    expert_of = jnp.repeat(4 * chip_ids + quarter, slots)
    of_expert = expert_of[:, None] == jnp.arange(experts, dtype=jnp.int32)[None, :]

    def parted(value):
        high = to_low(value)
        return high, to_low(value - high.astype(F32))

    slot_gates = [
        jnp.sum(jnp.where(of_expert, matmul(pick_low, part), 0.0), axis=1, keepdims=True)
        for part in parted(gates)
    ]
    gate_tile = to_low(
        jnp.where(jnp.arange(128)[None, :] < 64, slot_gates[0], slot_gates[1])
    ).reshape(chips, slots, 128)
    (other_down, other_up), gate_tile = after((other_down, other_up), gate_tile)
    down_back = swap(other_down)
    up_back = (up_first, swap(other_up[up_cut:]))
    arrived, gate_there = exchange([out_rows, gate_tile], 3)
    arrived = arrived.reshape(chips * slots, width)
    side = wsh.reshape(1)
    gate_there = gate_there.reshape(chips * slots, 128)
    y_rows, d_rows, activated, d_gate_pre, d_up_pre, d_pairs = run_expert(
        side, arrived, cot_there, gate_there, (w_gate, w_up, w_down), (gate_back, *up_back, down_back)
    )
    *own_grads, other_gate, other_up, other_down = expert_grads(
        side, arrived, d_pairs, activated, d_gate_pre, d_up_pre
    )
    gate_grad_back = swap(other_gate)
    d_back = exchange_behind(d_rows.reshape(chips, slots, width + 128))
    y_rows, d_back = after(y_rows, d_back)
    y_back = exchange_behind(y_rows.reshape(chips, slots, width))

    def collect(back):
        return to_low(transposed_times(pick_low, back.reshape(chips * slots, -1)))

    d_back = d_back.reshape(chips * slots, width + 128)
    d_gates_part = sum(
        transposed_times(
            pick_low, jnp.where(of_expert, d_back[:, at : at + 1], jnp.zeros((), BF))
        )
        for at in (width, width + 64)
    ).reshape(2, rows, experts)
    d_part = collect(d_back)[:, :width].reshape(2, rows, width)
    (gate_grad_back, other_up, other_down), d_part = after((gate_grad_back, other_up, other_down), d_part)
    d_hidden_moe, d_gates = reduce_chip(d_part, d_gates_part, 5)
    residual = my_rows(chip_residual)

    own_gates = my_rows(gates)
    hidden_two = my_rows(chip_hidden)
    inverse_two = my_rows(chip_inverse_two)
    d_chosen = own_gates * (d_gates - jnp.sum(own_gates * d_gates, axis=-1, keepdims=True))
    d_logits = to_low(d_chosen)
    grad_router = transposed_times(hidden_two, d_logits)
    d_hidden_two = d_hidden_moe + times_transposed(d_logits, wr)
    d_res_norm, ffn_gain_terms = norm_back(residual, inverse_two, g_ffn, d_hidden_two)
    d_residual = cotangent.astype(F32) + d_res_norm
    gain_ffn_part = jnp.sum(ffn_gain_terms, axis=0)

    other_up, d_residual = after(other_up, d_residual)
    up_grad_back = swap(other_up)
    d_attn = gather_row(to_low(d_residual), 7).reshape(row_tokens, width)
    (y_back, up_grad_back), d_attn_late = after((y_back, up_grad_back), d_attn)
    other_down, up_grad_back = after(other_down, up_grad_back)
    down_grad_back = swap(other_down)
    grad_out_t = transposed_times(d_attn, heads)
    early = jnp.concatenate(
        [
            to_low(grad_out_t[:, :128]).reshape(64, depth, 128),
            to_low(grad_out_t[:, 128:]).reshape(64, depth, 128),
            to_low(grad_router).reshape(64, depth, 128),
            jnp.pad(
                to_low(gain_ffn_part).reshape(64, 1, depth), ((0, 0), (0, 15), (0, 128 - depth))
            ),
        ],
        axis=1,
    )
    d_queries, d_kv = attend_back(
        plan, seq_lengths, queries, heads, d_attn_late, late_all, kv_all, lse
    )
    down_grad_back, d_kv = after(down_grad_back, d_kv)
    swapped_grads = (gate_grad_back, up_grad_back, down_grad_back)
    d_side, early = reduce_keys(d_kv, early, 8)
    flags = jnp.concatenate(
        [
            flag(is_key)[:1],
            flag(core)[:1],
            flag(is_key == (core == 0))[:1],
            jnp.zeros((5, 128), F32),
        ],
        axis=0,
    )
    d_hidden_parts, late = project_back(
        d_queries,
        d_side,
        q_pre,
        k_pre,
        cosine,
        sine_tab,
        hidden_one,
        w_main,
        w_side,
        g_query[None, :],
        g_key[None, :],
        flags,
    )
    d_hidden_parts = d_hidden_parts.reshape(8, rows, width)
    d_hidden_one, moe_total, late = reduce_row(
        d_hidden_parts,
        9,
        False,
        extra=collect(y_back).reshape(2, rows, width),
        owned=(late,),
    )
    out_stream = residual + moe_total
    own_stream = tokens.astype(F32)
    d_stream_norm, _ = norm_back(own_stream, inverse_root(own_stream), g_attn, d_hidden_one)
    grad_tokens = d_residual + d_stream_norm


    grad_gate, grad_up, grad_down = place_other(side, swapped_grads, own_grads)

    early, late = early.astype(F32), late.astype(F32)
    early_q = early[:, : 2 * depth].reshape(8, 2, depth, 128)
    grad_out = early_q.transpose(0, 1, 3, 2).reshape(8 * 256, depth)
    grad_router = jnp.sum(early[:, 2 * depth : 3 * depth], axis=0)
    grad_gain_ffn = jnp.sum(early[:, 3 * depth, :depth], axis=0)
    late_q = late[:, : 2 * depth].reshape(8, 2, depth, 128)
    grad_query = late_q.transpose(2, 0, 1, 3).reshape(depth, 8 * 256)
    late_kv = jnp.sum(late[:, 2 * depth : 3 * depth].reshape(2, 2, 2, depth, 128), axis=2)
    grad_key = late_kv[:, 0].transpose(1, 0, 2).reshape(depth, 256)
    grad_value = late_kv[:, 1].transpose(1, 0, 2).reshape(depth, 256)
    gain_parts = jnp.sum(late[:, 3 * depth : 3 * depth + 2], axis=0)
    gain_attn_part = (
        jnp.sum(rounded(w_query) * grad_query, axis=1)
        + jnp.sum(rounded(key_weight) * grad_key, axis=1)
        + jnp.sum(rounded(value_weight) * grad_value, axis=1)
    ) / rounded(gain_attn)
    gain_parts = lax.psum(jnp.concatenate([gain_parts, lanes_to(gain_attn_part[None, :])], axis=0), "wsh")
    return (
        out_stream,
        grad_tokens,
        grad_query,
        grad_key,
        grad_value,
        grad_out,
        gain_parts[2, :depth],
        gain_parts[0],
        gain_parts[1],
        grad_gain_ffn,
        grad_router,
        grad_gate,
        grad_up,
        grad_down,
    )


def solution(mesh):
    in_specs = (
        P("ctx", None),
        P("ctx", None),
        P(),
        P(),
        P("ctx", None),
        P("ctx", "wsh"),
        P("ctx", "wsh"),
        P("ctx", "wsh"),
        P("wsh", "ctx"),
        P("ctx"),
        P(),
        P(),
        P("ctx"),
        P("ctx", None),
        P("ctx", None, "wsh"),
        P("ctx", None, "wsh"),
        P("ctx", "wsh", None),
    )
    out_specs = (
        P("ctx", None),
        P("ctx", None),
        P("ctx", "wsh"),
        P("ctx", "wsh"),
        P("ctx", "wsh"),
        P("wsh", "ctx"),
        P("ctx"),
        P(),
        P(),
        P("ctx"),
        P("ctx", None),
        P("ctx", None, "wsh"),
        P("ctx", None, "wsh"),
        P("ctx", "wsh", None),
    )
    return jax.shard_map(local, mesh=mesh, in_specs=in_specs, out_specs=out_specs, check_vma=False)
```

```python
import functools
import math

import jax
import jax.numpy as jnp
from jax import lax
from jax.experimental import pallas as pl
from jax.experimental.pallas import tpu as pltpu
from jax.sharding import PartitionSpec as P

HEAD_WIDTH = 128
TOPK = 8
BLK = 64
MAX_SEQ_TOKENS = 4096
CAP = 12
CHUNK = 1024

EPSILON = 1e-06
ROPE_BASE = 1000000.0
MASKED = -1e30
MESH = pl.DeviceIdType.MESH
BF = jnp.bfloat16
F32 = jnp.float32


def to_low(value_rows):
    return value_rows.astype(jnp.bfloat16)


def rounded(value_rows):
    return lax.optimization_barrier(value_rows.astype(jnp.bfloat16)).astype(jnp.float32)


def matmul(left, right):
    return jnp.dot(left, right, preferred_element_type=jnp.float32)


def times_transposed(left, right):
    return lax.dot_general(
        left, right, (((1,), (1,)), ((), ())), preferred_element_type=jnp.float32
    )


def transposed_times(left, right):
    return lax.dot_general(
        left, right, (((0,), (0,)), ((), ())), preferred_element_type=jnp.float32
    )


def coords(c):
    return (
        lax.div(c, 16),
        lax.rem(lax.div(c, 8), 2),
        lax.rem(lax.div(c, 2), 4),
        lax.rem(c, 2),
    )


def index_of(z, y, x, k):
    return ((z * 2 + y) * 4 + x) * 2 + k


def shifted(me, dz, dy, dx, dk):
    z, y, x, k = coords(me)
    return index_of(lax.rem(z + dz, 4), lax.rem(y + dy, 2), lax.rem(x + dx, 4), lax.rem(k + dk, 2))


def remote(src, dst, send, recv, ctx, wsh):
    return pltpu.make_async_remote_copy(
        src_ref=src,
        dst_ref=dst,
        send_sem=send,
        recv_sem=recv,
        device_id=(ctx, wsh),
        device_id_type=MESH,
    )


def greet(targets):
    barrier = pltpu.get_barrier_semaphore()
    for ctx, wsh in targets:
        pl.semaphore_signal(barrier, inc=1, device_id=(ctx, wsh), device_id_type=MESH)
    return barrier, len(targets)


def greet_many(count, target):
    barrier = pltpu.get_barrier_semaphore()

    def one(step, carried):
        pl.semaphore_signal(barrier, inc=1, device_id=target(step), device_id_type=MESH)
        return carried

    lax.fori_loop(1, count, one, 0)
    return barrier, count - 1


ANY = pl.BlockSpec(memory_space=pl.ANY)
VMEM = pl.BlockSpec(memory_space=pltpu.VMEM)
DMA = pltpu.SemaphoreType.DMA


def cost(microseconds):
    return pl.CostEstimate(flops=0, bytes_accessed=int(microseconds * 1.2e6), transcendentals=0)


ROOM = 56 * 1024 * 1024


def call_params(collective_id):
    return pltpu.CompilerParams(
        collective_id=collective_id, has_side_effects=True, vmem_limit_bytes=ROOM
    )


def row_gather_start(src, out, me, wsh, send, recv):
    place = lax.rem(me, 8)
    copies = []
    for at, (dx, dk) in enumerate(((1, 0), (3, 0), (0, 1))):
        copy = remote(
            src, out.at[place], send.at[at], recv.at[at], shifted(me, 0, 0, dx, dk), wsh
        )
        copy.start()
        copies.append(copy)
    return copies


def row_gather_onward(out, me, wsh, copies, send, recv):
    partner = shifted(me, 0, 0, 0, 1)
    half = out.shape[1] // 2
    onward = []
    forwards = []
    for at, dx in enumerate((1, 3)):
        copies[at].wait_recv()
        from_place = lax.rem(shifted(me, 0, 0, 4 - dx, 0), 8)
        part = out.at[from_place, pl.ds(at * half, half)]
        step = remote(part, part, send.at[3 + at], recv.at[3 + at], shifted(me, 0, 0, dx, 0), wsh)
        step.start()
        onward.append(step)
        block = out.at[from_place]
        forward = remote(block, block, send.at[5 + at], recv.at[5 + at], partner, wsh)
        forward.start()
        forwards.append(forward)
    return onward, forwards


def row_gather_end(out, me, wsh, copies, onward, forwards, send, recv):
    partner = shifted(me, 0, 0, 0, 1)
    half = out.shape[1] // 2
    far = lax.rem(shifted(me, 0, 0, 2, 0), 8)
    for at in (0, 1):
        onward[at].wait_recv()
        part = out.at[far, pl.ds(at * half, half)]
        forward = remote(part, part, send.at[7 + at], recv.at[7 + at], partner, wsh)
        forward.start()
        forwards.append(forward)
    copies[2].wait_recv()
    for copy in copies + onward:
        copy.wait_send()
    for forward in forwards:
        forward.wait()


def cast_steps(steps, staging, lows, in_sems, out_sems):
    loads, stores = [], []
    for index, (src, begin, dst, to, count, at) in enumerate(steps):
        slot, span = index % 2, pl.ds(0, count)
        loads.append(
            pltpu.make_async_copy(
                src.at[pl.ds(begin, count)], staging[at].at[slot, span], in_sems.at[slot]
            )
        )
        stores.append(
            pltpu.make_async_copy(lows[at].at[slot, span], dst.at[pl.ds(to, count)], out_sems.at[slot])
        )
    loads[0].start()
    loads[1].start()
    for index, step in enumerate(steps):
        slot, count, at = index % 2, step[-2], step[-1]
        loads[index].wait()
        if index >= 2:
            stores[index - 2].wait()
        lows[at][slot, :count] = staging[at][slot, :count].astype(BF)
        stores[index].start()
        if index + 2 < len(steps):
            loads[index + 2].start()
    stores[-2].wait()
    stores[-1].wait()


def cut_steps(src, parts, rows, at):
    steps, begin = [], 0
    for part in parts:
        for to in range(0, part.shape[0], rows):
            count = min(rows, part.shape[0] - to)
            steps.append((src, begin + to, part, to, count, at))
        begin += part.shape[0]
    return steps


COLUMN_STEPS = ((1, 0), (3, 0), (0, 1), (2, 0), (1, 1), (3, 1), (2, 1))
ROW_STEPS = ((1, 0), (3, 0), (1, 1), (3, 1), (0, 1), (2, 0), (2, 1))


UP_CUT = (1280, 768)
DOWN_GRAD_CUT = (240, 144)


def gather_first(weights, gains, tokens, routes, cotangent, expert_weights):
    def body(q_in, k_in, v_in, ga_in, gf_in, t_in, r_in, c_in, *refs):
        sources, refs = refs[:3], refs[3:]
        w_out, t_out, s_out, r_out, c_out = refs[:5]
        gate_out, up_out, up_rest, down_out, side_out = refs[5:10]
        refs = refs[10:]
        wide, row_s, row_r, pair, local, col_s, col_r, tall_f, flat_f, tall_b, flat_b, in_sems, out_sems = refs[:13]
        w_in, s_in = refs[13:]
        me, wsh = lax.axis_index("ctx"), lax.axis_index("wsh")
        core = lax.rem(me, 2)
        place = lax.rem(me, 8)
        group = lax.div(me, 8)
        partner = shifted(me, 0, 0, 0, 1)
        row_peers = [shifted(me, 0, 0, dx, dk) for dx, dk in ROW_STEPS]
        col_peers = [shifted(me, dz, dy, 0, 0) for dz, dy in COLUMN_STEPS]
        barrier, amount = greet([(peer, wsh) for peer in row_peers + col_peers])
        heads = q_in.shape[1] // 8
        for at in range(8):
            w_in[at, :, :heads] = q_in[:, at * heads : (at + 1) * heads].astype(BF)
            side = (k_in, v_in)[at % 2]
            begin = at // 4 * HEAD_WIDTH
            w_in[at, :, heads:] = side[:, begin : begin + HEAD_WIDTH].astype(BF)
        s_in[...] = jnp.zeros_like(s_in)
        s_in[0:1, : ga_in.shape[1]] = ga_in[...]
        s_in[1:2, : gf_in.shape[1]] = gf_in[...]
        locals_ = [
            pltpu.make_async_copy(w_in.at[place], w_out.at[me], local.at[0]),
            pltpu.make_async_copy(s_in, s_out.at[me], local.at[1]),
            pltpu.make_async_copy(t_in, t_out.at[place], local.at[2]),
            pltpu.make_async_copy(r_in, r_out.at[core], local.at[3]),
            pltpu.make_async_copy(c_in, c_out.at[core], local.at[4]),
        ]
        for copy in locals_:
            copy.start()
        pl.semaphore_wait(barrier, amount)
        for peer in row_peers:
            remote(w_in.at[lax.rem(peer, 8)], w_out.at[me], wide.at[0], wide.at[1], peer, wsh).start()
            remote(s_in, s_out.at[me], wide.at[2], wide.at[3], peer, wsh).start()
        row_copies = row_gather_start(t_in, t_out, me, wsh, row_s, row_r)
        pair_copies = [
            remote(r_in, r_out.at[core], pair.at[0], pair.at[1], partner, wsh),
            remote(c_in, c_out.at[core], pair.at[2], pair.at[3], partner, wsh),
        ]
        for copy in pair_copies:
            copy.start()
        locals_[0].wait()
        locals_[1].wait()
        for at, out in ((0, w_out), (2, s_out)):
            rest = out.at[pl.ds(0, 7)]
            done = remote(rest, rest, wide.at[at], wide.at[at + 1], partner, wsh)
            done.wait_recv()
            done.wait_send()
        lanes = side_out.shape[2]
        depth, columns = w_out.shape[1], w_out.shape[2]

        def share(origin, at):
            blocks = pl.ds(origin * 8, 8)
            part = w_out.at[blocks, pl.ds(0, depth), pl.ds(columns - lanes, lanes)]
            give = remote(part, side_out.at[blocks], col_s.at[2, at], col_r.at[2, at], partner, wsh)
            give.start()
            return give

        mine = pl.ds(group * 8, 8)
        col_copies = []
        for at, peer in enumerate(col_peers):
            for kind, out in enumerate((w_out, s_out)):
                copy = remote(out.at[mine], out.at[mine], col_s.at[kind, at], col_r.at[kind, at], peer, wsh)
                copy.start()
                col_copies.append(copy)
        shares = [share(group, 7)]
        onward, forwards = row_gather_onward(t_out, me, wsh, row_copies, row_s, row_r)
        gate_in, up_in, down_in = [source.at[1 - wsh] for source in sources]
        buffers = ((tall_f, flat_f), (tall_b, flat_b), in_sems, out_sems)
        tall_rows, flat_rows = tall_f.shape[1], flat_f.shape[1]
        cast_steps(
            cut_steps(gate_in, (gate_out,), tall_rows, 0) + cut_steps(up_in, (up_out, up_rest), tall_rows, 0) + cut_steps(down_in, (down_out,), flat_rows, 1),
            *buffers,
        )
        row_gather_end(t_out, me, wsh, row_copies, onward, forwards, row_s, row_r)
        for at, (dz, dy) in enumerate(COLUMN_STEPS):
            col_copies[2 * at].wait_recv()
            col_copies[2 * at + 1].wait_recv()
            shares.append(share(lax.div(shifted(me, 4 - dz, 2 - dy, 0, 0), 8), at))
        for copy in pair_copies + shares:
            copy.wait()
        for copy in locals_[2:]:
            copy.wait()
        for copy in col_copies:
            copy.wait_send()

    sds = jax.ShapeDtypeStruct
    _, deep, half = expert_weights[0].shape
    depth, packed = weights[0].shape[0], weights[0].shape[1] // 8 + HEAD_WIDTH
    tall, flat = (deep // 4, half), (half // 4, deep)
    return pl.pallas_call(
        body,
        out_shape=(
            sds((64, depth, packed), BF),
            sds((8,) + tokens.shape, tokens.dtype),
            sds((64, 8, 128), F32),
            sds((2,) + routes.shape, routes.dtype),
            sds((2,) + cotangent.shape, cotangent.dtype),
        )
        + tuple(sds((count, half), BF) for count in (deep, *UP_CUT))
        + (sds((half, deep), BF), sds((64, depth, 128), BF)),
        in_specs=[VMEM] * 5 + [ANY] * 6,
        out_specs=[ANY] * 10,
        scratch_shapes=[
            DMA((4,)),
            DMA((9,)),
            DMA((9,)),
            DMA((4,)),
            DMA((5,)),
            DMA((3, 8)),
            DMA((3, 8)),
            pltpu.VMEM((2,) + tall, F32),
            pltpu.VMEM((2,) + flat, F32),
            pltpu.VMEM((2,) + tall, BF),
            pltpu.VMEM((2,) + flat, BF),
            DMA((2,)),
            DMA((2,)),
            pltpu.VMEM((8, depth, packed), BF),
            pltpu.VMEM((8, 128), F32),
        ],
        compiler_params=call_params(0),
        name="gather_first",
        cost_estimate=cost(40),
    )(*weights, *gains, tokens, routes, cotangent, *expert_weights)


def gather_row(block, swapped, collective_id):
    def body(src, src2, out, out2, row_s, row_r, pair, local):
        me, wsh = lax.axis_index("ctx"), lax.axis_index("wsh")
        barrier, amount = greet(
            [(shifted(me, 0, 0, dx, dk), wsh) for dx, dk in ((1, 0), (3, 0), (0, 1))] + [(me, 1 - wsh)]
        )
        mine = pltpu.make_async_copy(src, out.at[lax.rem(me, 8)], local)
        mine.start()
        pl.semaphore_wait(barrier, amount)
        copies = row_gather_start(src, out, me, wsh, row_s, row_r)
        cross = remote(src2, out2, pair.at[0], pair.at[1], me, 1 - wsh)
        cross.start()
        onward, forwards = row_gather_onward(out, me, wsh, copies, row_s, row_r)
        row_gather_end(out, me, wsh, copies, onward, forwards, row_s, row_r)
        mine.wait()
        cross.wait()

    return pl.pallas_call(
        body,
        out_shape=(
            jax.ShapeDtypeStruct((8,) + block.shape, block.dtype),
            jax.ShapeDtypeStruct(swapped.shape, swapped.dtype),
        ),
        in_specs=[ANY, ANY],
        out_specs=[ANY, ANY],
        scratch_shapes=[DMA((9,)), DMA((9,)), DMA((2,)), DMA],
        compiler_params=call_params(collective_id),
        name="gather_row",
        cost_estimate=cost(26),
    )(block, swapped)


def gather_keys(rows, collective_id):
    count = rows.shape[0]
    half = count // 2

    def body(src, out, send, recv, local):
        me, wsh = lax.axis_index("ctx"), lax.axis_index("wsh")
        core = lax.rem(me, 2)
        group = lax.div(me, 8)
        partner = shifted(me, 0, 0, 0, 1)
        peers = [shifted(me, dz, dy, 0, 0) for dz, dy in COLUMN_STEPS]
        barrier, amount = greet([(peer, wsh) for peer in peers + [partner]])
        mine = pltpu.make_async_copy(src, out.at[group], local)
        mine.start()
        pl.semaphore_wait(barrier, amount)
        my_half = pl.ds(pl.multiple_of(core * half, half), half)
        copies = []
        for at, peer in enumerate(peers):
            copy = remote(src.at[my_half], out.at[group, my_half], send.at[at], recv.at[at], peer, wsh)
            copy.start()
            copies.append(copy)
        forwards = []
        for at, (dz, dy) in enumerate(COLUMN_STEPS):
            copies[at].wait_recv()
            origin = lax.div(shifted(me, 4 - dz, 2 - dy, 0, 0), 8)
            part = out.at[origin, my_half]
            forward = remote(part, part, send.at[7 + at], recv.at[7 + at], partner, wsh)
            forward.start()
            forwards.append(forward)
        for copy in copies:
            copy.wait_send()
        for forward in forwards:
            forward.wait()
        mine.wait()

    return pl.pallas_call(
        body,
        out_shape=jax.ShapeDtypeStruct((8,) + rows.shape, rows.dtype),
        in_specs=[ANY],
        out_specs=ANY,
        scratch_shapes=[DMA((14,)), DMA((14,)), DMA],
        compiler_params=call_params(collective_id),
        name="gather_keys",
        cost_estimate=cost(30),
    )(rows)


class Owned:
    SCRATCH = 10

    def __init__(self, src, out, scratch):
        self.src, self.out = src, out
        self.land_z, self.sum_z, self.land_y, self.reduced, *self.sems = scratch

    @staticmethod
    def scratch(value):
        inner = value.shape[1:]
        return [
            pltpu.VMEM((3, 16) + inner, BF),
            pltpu.VMEM((16,) + inner, BF),
            pltpu.VMEM((8,) + inner, BF),
            pltpu.VMEM((8,) + inner, BF),
            DMA((3,)),
            DMA((3,)),
            DMA((1,)),
            DMA((1,)),
            DMA((7,)),
            DMA((7,)),
        ]

    def along_z(self, me, wsh):
        z, _, _, _ = coords(me)
        self.copies_z = []
        for at, dz in enumerate((1, 3, 2)):
            blocks = pl.ds(lax.rem(z + dz, 4) * 16, 16)
            copy = remote(
                self.src.at[blocks],
                self.land_z.at[at],
                self.sems[0].at[at],
                self.sems[1].at[at],
                shifted(me, dz, 0, 0, 0),
                wsh,
            )
            copy.start()
            self.copies_z.append(copy)

    def along_y(self, me, wsh):
        z, y, _, _ = coords(me)
        value = self.src[pl.ds(z * 16, 16)].astype(F32)
        for at, copy in enumerate(self.copies_z):
            copy.wait_recv()
            value = value + self.land_z[at].astype(F32)
        self.sum_z[...] = value.astype(BF)
        self.copy_y = remote(
            self.sum_z.at[pl.ds((1 - y) * 8, 8)],
            self.land_y,
            self.sems[2].at[0],
            self.sems[3].at[0],
            shifted(me, 0, 1, 0, 0),
            wsh,
        )
        self.copy_y.start()

    def along_row(self, me, wsh):
        _, y, _, _ = coords(me)
        self.copy_y.wait_recv()
        value = self.sum_z[pl.ds(y * 8, 8)].astype(F32) + self.land_y[...].astype(F32)
        self.reduced[...] = value.astype(BF)
        place = lax.rem(me, 8)
        self.copies_row = []
        for at, (dx, dk) in enumerate(ROW_STEPS):
            peer = shifted(me, 0, 0, dx, dk)
            copy = remote(
                self.reduced.at[lax.rem(peer, 8)],
                self.out.at[place],
                self.sems[4].at[at],
                self.sems[5].at[at],
                peer,
                wsh,
            )
            copy.start()
            self.copies_row.append(copy)
        self.out[place] = self.reduced[place]

    def finish(self):
        for copy in self.copies_row:
            copy.wait()
        for copy in self.copies_z + [self.copy_y]:
            copy.wait_send()


def reduce_row(parts, collective_id, both, extra=None, swapped_whole=None, owned=()):
    has_whole = swapped_whole is not None
    is_product = isinstance(parts, tuple)
    if is_product:
        rows, width = parts[0].shape[0] // 8, parts[1].shape[0]
    else:
        _, rows, width = parts.shape
    block = (rows, width)
    pieces = 4
    columns = width // pieces
    has_extra = extra is not None

    def body(*refs):
        refs = list(refs)
        if is_product:
            heads_ref, out_w = refs.pop(0), refs.pop(0)
            src = refs.pop(-1)
        else:
            src = refs.pop(0)
        if has_extra:
            pick_ref, back_ref = refs.pop(0), refs.pop(0)
        src3 = refs.pop(0) if has_whole else None
        mine_in = [refs.pop(0) for _ in owned]
        out = refs.pop(0)
        out2 = refs.pop(0) if has_extra else None
        out3 = refs.pop(0) if has_whole else None
        mine_out = [refs.pop(0) for _ in owned]
        blocks = []
        for src4, out4 in reversed(list(zip(mine_in, mine_out))):
            blocks.append(Owned(src4, out4, refs[-Owned.SCRATCH :]))
            refs = refs[: -Owned.SCRATCH]
        arrived, summed, landed, swapped, total, send, recv, local = refs[:8]
        me, wsh = lax.axis_index("ctx"), lax.axis_index("wsh")
        other = 1 - wsh
        core = lax.rem(me, 2)
        _, _, x, _ = coords(me)
        partner = shifted(me, 0, 0, 0, 1)
        peers = [shifted(me, 0, 0, dx, 0) for dx in (1, 2, 3)]
        row_peers = [shifted(me, 0, 0, dx, dk) for dx, dk in ROW_STEPS]
        col_peers = [shifted(me, dz, dy, 0, 0) for dz, dy in COLUMN_STEPS]
        greeted = row_peers + col_peers if owned else peers + [partner]
        barrier, amount = greet([(peer, wsh) for peer in greeted] + [(me, other)])
        pl.semaphore_wait(barrier, amount)
        if has_whole:
            whole = remote(
                src3, out3, send.at[1, 9], recv.at[1, 9], me, other
            )
            whole.start()
        spans = [pl.ds(piece * columns, columns) for piece in range(pieces)]
        everything = pl.ds(0, rows)
        first = []
        for piece, span in enumerate(spans):
            if is_product:
                columns_of = slice(piece * columns, (piece + 1) * columns)
                src[:, :, columns_of] = (
                    times_transposed(heads_ref[...], out_w[columns_of, : heads_ref.shape[1]])
                    .astype(BF)
                    .reshape(8, rows, columns)
                )
            for at, dx in enumerate((2, 1, 3, 0)):
                chip = lax.rem(x + dx, 4)
                copy = remote(
                    src.at[chip * 2 + 1 - core, everything, span],
                    arrived.at[at, everything, span],
                    send.at[piece, at],
                    recv.at[piece, at],
                    partner,
                    wsh,
                )
                copy.start()
                first.append(copy)
        for block4 in blocks:
            block4.along_z(me, wsh)
        if has_extra:
            arrived2, swapped2, src2 = refs[8:]
            src2[...] = matmul(pick_ref[...], back_ref[...]).astype(BF).reshape(src2.shape)
            give2 = remote(src2.at[1 - core], arrived2, send.at[0, 8], recv.at[0, 8], partner, wsh)
            give2.start()
        second = []
        for piece, span in enumerate(spans):
            for at, dx in enumerate((2, 1, 3)):
                chip = lax.rem(x + dx, 4)
                first[piece * 4 + at].wait_recv()
                summed[at, :, span] = (
                    src[chip * 2 + core, :, span].astype(F32) + arrived[at, :, span].astype(F32)
                ).astype(BF)
                copy = remote(
                    summed.at[at, everything, span],
                    landed.at[at, everything, span],
                    send.at[piece, 4 + at],
                    recv.at[piece, 4 + at],
                    shifted(me, 0, 0, dx, 0),
                    wsh,
                )
                copy.start()
                second.append(copy)
            first[piece * 4 + 3].wait_recv()
            total[:, span] = src[x * 2 + core, :, span].astype(F32) + arrived[3, :, span].astype(F32)
        if has_extra:
            give2.wait()
            swapped2[0] = (src2[core].astype(F32) + arrived2[...].astype(F32)).astype(BF)
            swap2 = remote(swapped2.at[0], swapped2.at[1], send.at[1, 8], recv.at[1, 8], me, other)
            swap2.start()
        swaps = []
        for piece, span in enumerate(spans):
            for at in (1, 2, 0):
                second[piece * 3 + at].wait_recv()
            swapped[0, :, span] = (
                total[:, span]
                + landed[0, :, span].astype(F32)
                + landed[1, :, span].astype(F32)
                + landed[2, :, span].astype(F32)
            ).astype(BF)
            swap = remote(
                swapped.at[0, everything, span],
                swapped.at[1, everything, span],
                send.at[piece, 7],
                recv.at[piece, 7],
                me,
                other,
            )
            swap.start()
            swaps.append(swap)
            if piece == pieces - 2:
                for block4 in blocks:
                    block4.along_y(me, wsh)
        for block4 in blocks:
            block4.along_row(me, wsh)
        if has_extra:
            swap2.wait()
            out2[...] = swapped2[0].astype(F32) + swapped2[1].astype(F32)
        for piece, span in enumerate(spans):
            swaps[piece].wait()
            if both:
                total[:, span] = swapped[0, :, span].astype(F32) + swapped[1, :, span].astype(F32)
            else:
                out[:, span] = swapped[0, :, span].astype(F32) + swapped[1, :, span].astype(F32)
        if both:
            keep = pltpu.make_async_copy(total, out.at[core], local)
            keep.start()
            give = remote(total, out.at[core], send.at[0, 9], recv.at[0, 9], partner, wsh)
            give.start()
            give.wait()
            keep.wait()
        for copy in first + second:
            copy.wait_send()
        for block4 in blocks:
            block4.finish()
        if has_whole:
            whole.wait()

    shapes = [jax.ShapeDtypeStruct((2,) + block if both else block, F32)]
    scratch = [
        pltpu.VMEM((4,) + block, BF),
        pltpu.VMEM((3,) + block, BF),
        pltpu.VMEM((3,) + block, BF),
        pltpu.VMEM((2,) + block, BF),
        pltpu.VMEM(block, F32),
        DMA((pieces, 10)),
        DMA((pieces, 10)),
        DMA,
    ]
    operands = list(parts) if is_product else [parts]
    out_spaces = [VMEM]
    if has_extra:
        shapes.append(jax.ShapeDtypeStruct(block, F32))
        scratch += [pltpu.VMEM(block, BF), pltpu.VMEM((2,) + block, BF), pltpu.VMEM((2,) + block, BF)]
        operands += list(extra)
        out_spaces.append(VMEM)
    spaces = [VMEM] * len(operands)
    if has_whole:
        shapes.append(jax.ShapeDtypeStruct(swapped_whole.shape, swapped_whole.dtype))
        operands.append(swapped_whole)
        spaces.append(ANY)
        out_spaces.append(ANY)
    for value in owned:
        block8 = (8,) + value.shape[1:]
        shapes.append(jax.ShapeDtypeStruct(block8, BF))
        operands.append(value)
        spaces.append(VMEM)
        out_spaces.append(VMEM)
        scratch += Owned.scratch(value)
    if is_product:
        scratch.append(pltpu.VMEM((8,) + block, BF))
    return pl.pallas_call(
        body,
        out_shape=shapes,
        in_specs=spaces,
        out_specs=out_spaces,
        scratch_shapes=scratch,
        compiler_params=call_params(collective_id),
        name="reduce_row",
        cost_estimate=cost(1),
    )(*operands)


def reduce_chip(pick, back, of_expert, width, collective_id):
    rows = pick.shape[0] // 2
    lanes = of_expert.shape[1]

    def body(pick_ref, back_ref, of_ref, out, out2, src, src2, arrived, swapped, arrived2, swapped2, send, recv):
        me, wsh = lax.axis_index("ctx"), lax.axis_index("wsh")
        other = 1 - wsh
        core = lax.rem(me, 2)
        partner = shifted(me, 0, 0, 0, 1)
        barrier, amount = greet([(partner, wsh), (me, other)])
        src[...] = matmul(pick_ref[...], back_ref[:, :width]).astype(BF).reshape(src.shape)
        parts = [back_ref[:, at : at + 1] * of_ref[...] for at in (width, width + 64)]
        src2[...] = (matmul(pick_ref[...], parts[0]) + matmul(pick_ref[...], parts[1])).reshape(src2.shape)
        pl.semaphore_wait(barrier, amount)
        give = remote(src.at[1 - core], arrived, send.at[0], recv.at[0], partner, wsh)
        give.start()
        give2 = remote(src2.at[1 - core], arrived2, send.at[2], recv.at[2], partner, wsh)
        give2.start()
        give.wait()
        swapped[0] = (src[core].astype(F32) + arrived[...].astype(F32)).astype(BF)
        swap = remote(swapped.at[0], swapped.at[1], send.at[1], recv.at[1], me, other)
        swap.start()
        give2.wait()
        swapped2[0] = src2[core] + arrived2[...]
        swap2 = remote(swapped2.at[0], swapped2.at[1], send.at[3], recv.at[3], me, other)
        swap2.start()
        swap2.wait()
        out2[...] = swapped2[0] + swapped2[1]
        swap.wait()
        out[...] = swapped[0].astype(F32) + swapped[1].astype(F32)

    sds = jax.ShapeDtypeStruct
    block, block2 = (rows, width), (rows, lanes)
    return pl.pallas_call(
        body,
        out_shape=(sds(block, F32), sds(block2, F32)),
        in_specs=[VMEM] * 3,
        out_specs=[VMEM] * 2,
        scratch_shapes=[
            pltpu.VMEM((2,) + block, BF),
            pltpu.VMEM((2,) + block2, F32),
            pltpu.VMEM(block, BF),
            pltpu.VMEM((2,) + block, BF),
            pltpu.VMEM(block2, F32),
            pltpu.VMEM((2,) + block2, F32),
            DMA((4,)),
            DMA((4,)),
        ],
        compiler_params=call_params(collective_id),
        name="reduce_chip",
        cost_estimate=cost(17),
    )(pick, back, of_expert)


def reduce_keys(parts, owned, swapped, collective_id):
    _, groups, _, rows, width = parts.shape

    def body(src, src4, src5, out, out4, out5, arrived, mid, beside, summed, landed, send, recv, pair, *scratch4):
        block4 = Owned(src4, out4, scratch4)
        me, wsh = lax.axis_index("ctx"), lax.axis_index("wsh")
        core = lax.rem(me, 2)
        _, _, x, _ = coords(me)
        side = lax.rem(x, 2)
        partner = shifted(me, 0, 0, 0, 1)
        neighbour = me + 2 - 4 * side
        steps = COLUMN_STEPS + ((0, 0),)
        peers = [shifted(me, dz, dy, 0, 0) for dz, dy in steps]
        row_peers = [shifted(me, 0, 0, dx, dk) for dx, dk in ROW_STEPS]
        barrier, amount = greet([(peer, wsh) for peer in peers[:-1] + row_peers] + [(me, 1 - wsh)])
        pl.semaphore_wait(barrier, amount)
        first = []
        for at, peer in enumerate(peers):
            group = lax.div(peer, 8)
            for turn, b in enumerate((1 - side, side)):
                copy = remote(
                    src.at[1 - core, group, b],
                    arrived.at[turn, at],
                    send.at[turn, at],
                    recv.at[turn, at],
                    partner,
                    wsh,
                )
                copy.start()
                first.append(copy)
        block4.along_z(me, wsh)
        cross = remote(src5, out5, pair.at[0], pair.at[1], me, 1 - wsh)
        cross.start()
        across = []
        for at, peer in enumerate(peers):
            group = lax.div(peer, 8)
            first[2 * at].wait_recv()
            mid[at] = (src[core, group, 1 - side].astype(F32) + arrived[0, at].astype(F32)).astype(BF)
            copy = remote(mid.at[at], beside.at[at], send.at[2, at], recv.at[2, at], neighbour, wsh)
            copy.start()
            across.append(copy)
        last = []
        for at, peer in enumerate(peers):
            group = lax.div(peer, 8)
            first[2 * at + 1].wait_recv()
            across[at].wait_recv()
            value = (
                src[core, group, side].astype(F32)
                + arrived[1, at].astype(F32)
                + beside[at].astype(F32)
            )
            if at == groups - 1:
                out[...] = value
            else:
                summed[at] = value.astype(BF)
                copy = remote(summed.at[at], landed.at[at], send.at[3, at], recv.at[3, at], peer, wsh)
                copy.start()
                last.append(copy)
            if at == 5:
                block4.along_y(me, wsh)
        block4.along_row(me, wsh)
        for at, copy in enumerate(last):
            copy.wait_recv()
            out[...] += landed[at].astype(F32)
        for copy in first + across + last:
            copy.wait_send()
        block4.finish()
        cross.wait()

    block = (rows, width)
    return pl.pallas_call(
        body,
        out_shape=(
            jax.ShapeDtypeStruct(block, F32),
            jax.ShapeDtypeStruct((8,) + owned.shape[1:], BF),
            jax.ShapeDtypeStruct(swapped.shape, swapped.dtype),
        ),
        in_specs=[VMEM, VMEM, ANY],
        out_specs=[VMEM, VMEM, ANY],
        scratch_shapes=[
            pltpu.VMEM((2, groups) + block, BF),
            pltpu.VMEM((groups,) + block, BF),
            pltpu.VMEM((groups,) + block, BF),
            pltpu.VMEM((groups,) + block, BF),
            pltpu.VMEM((groups,) + block, BF),
            DMA((4, groups)),
            DMA((4, groups)),
            DMA((2,)),
        ]
        + Owned.scratch(owned),
        compiler_params=call_params(collective_id),
        name="reduce_keys",
        cost_estimate=cost(40),
    )(parts, owned, swapped)


def exchange(arrays, collective_id):
    amount = len(arrays)

    def body(*refs):
        ins, outs = refs[:amount], refs[amount : 2 * amount]
        send, recv, local = refs[2 * amount :]
        me, wsh = lax.axis_index("ctx"), lax.axis_index("wsh")
        chip = lax.div(me, 2)

        def target(step):
            dy = lax.rem(lax.div(step, 4), 2)
            return shifted(me, lax.div(step, 8), dy, lax.rem(step, 4), 0), lax.rem(wsh + dy, 2)

        barrier, count = greet_many(32, target)
        locals_ = []
        for at in range(amount):
            copy = pltpu.make_async_copy(ins[at].at[chip], outs[at].at[chip], local.at[at])
            copy.start()
            locals_.append(copy)
        pl.semaphore_wait(barrier, count)

        def one(step, carried):
            ctx, side = target(lax.rem(step * 13, 32))
            for at in range(amount):
                remote(
                    ins[at].at[lax.div(ctx, 2)], outs[at].at[chip], send.at[at], recv.at[at], ctx, side
                ).start()
            return carried

        lax.fori_loop(1, 32, one, 0)
        for copy in locals_:
            copy.wait()
        for at in range(amount):
            rest = outs[at].at[pl.ds(0, 31)]
            done = remote(rest, rest, send.at[at], recv.at[at], me, wsh)
            done.wait_send()
            done.wait_recv()

    return pl.pallas_call(
        body,
        out_shape=[jax.ShapeDtypeStruct(a.shape, a.dtype) for a in arrays],
        in_specs=[ANY] * amount,
        out_specs=[ANY] * amount,
        scratch_shapes=[DMA((amount,)), DMA((amount,)), DMA((amount,))],
        compiler_params=call_params(collective_id),
        name="exchange",
        cost_estimate=cost(48),
    )(*arrays)


def exchange_behind(value):
    groups = []
    for core in range(2):
        for parity in range(2):
            groups.append(
                [(chip * 2 + core) * 2 + (parity + chip // 4) % 2 for chip in range(32)]
            )
    return lax.all_to_all(
        value, ("ctx", "wsh"), split_axis=0, concat_axis=0, tiled=True, axis_index_groups=groups
    )


def natural_order(plan, kv_ref, keys, values, transposed):
    def one(block, carried):
        rows = kv_ref[pl.ds(pl.multiple_of(plan[PLAN_INVERSE + block] * BLK, BLK), BLK), :]
        at = pl.ds(pl.multiple_of(block * BLK, BLK), BLK)
        keys[at, :] = rows[:, :HEAD_WIDTH]
        values[at, :] = rows[:, HEAD_WIDTH:]
        return carried

    lax.fori_loop(0, kv_ref.shape[0] // BLK, one, 0, unroll=8)
    source, turned = transposed

    def turn(chunk, carried):
        at = pl.ds(pl.multiple_of(chunk * CHUNK, CHUNK), CHUNK)
        turned[:, at] = source[at, :].T
        return carried

    lax.fori_loop(0, kv_ref.shape[0] // CHUNK, turn, 0, unroll=4)


def stacked(ref, first, second):
    rows = [ref[pl.ds(pl.multiple_of(at * BLK, BLK), BLK), :] for at in (first, second)]
    return jnp.concatenate(
        [rows[0][:, :HEAD_WIDTH], rows[0][:, HEAD_WIDTH:], rows[1][:, :HEAD_WIDTH], rows[1][:, HEAD_WIDTH:]],
        axis=0,
    )


def unstacked(ref, first, second, value):
    for at, begin in ((first, 0), (second, 2 * BLK)):
        ref[pl.ds(pl.multiple_of(at * BLK, BLK), BLK), :] = jnp.concatenate(
            [value[begin : begin + BLK], value[begin + BLK : begin + 2 * BLK]], axis=1
        )


PLAN_BOUNDS, PLAN_INVERSE, PLAN_BLOCKS, PLAN_SIZE = 16, 64, 192, 256


def start_of(lengths, position):
    begin = lengths[0] * 0
    start = position * 0
    for at in range(lengths.shape[0]):
        start = jnp.where(begin <= position, begin, start)
        begin = begin + lengths[at]
    return start


def make_plan(block_order, lengths, base, plan):
    def place(at, carried):
        plan[PLAN_INVERSE + block_order[at]] = at
        return carried

    lax.fori_loop(0, block_order.shape[0], place, 0, unroll=8)

    def rank(at, carried):
        mine = block_order[base + at]
        before = jnp.int32(0)
        for other in range(16):
            before = before + jnp.where(block_order[base + other] < mine, 1, 0)
        plan[before] = at
        plan[PLAN_BLOCKS + before] = mine
        return carried

    lax.fori_loop(0, 16, rank, 0)

    def bound(step, carried):
        one, two = plan[PLAN_BLOCKS + 2 * step], plan[PLAN_BLOCKS + 2 * step + 1]
        low = lax.div(start_of(lengths, one * BLK), CHUNK)
        high = lax.div(two * BLK, CHUNK) + 1
        last = start_of(lengths, two * BLK + BLK - 1)
        inner_low = jnp.minimum(jnp.maximum(lax.div(last + CHUNK - 1, CHUNK), low), high)
        inner_high = jnp.minimum(jnp.maximum(lax.div(one * BLK + 1, CHUNK), inner_low), high)
        for at, value in enumerate((low, inner_low, inner_high, high)):
            plan[PLAN_BOUNDS + 4 * step + at] = value
        return carried

    lax.fori_loop(0, 8, bound, 0)


def strips_of(plan, lengths, step):
    lane = lax.broadcasted_iota(jnp.int32, (1, 4 * BLK), 1)
    block = jnp.where(lane < 2 * BLK, plan[PLAN_BLOCKS + 2 * step], plan[PLAN_BLOCKS + 2 * step + 1])
    position = block * BLK + lax.rem(lane, BLK)
    return position, start_of(lengths, position)


def three_loops(step, plan, chunk, state):
    low, inner_low, inner_high, high = [plan[PLAN_BOUNDS + 4 * step + at] for at in range(4)]
    state = lax.fori_loop(low, inner_low, functools.partial(chunk, True), state)
    state = lax.fori_loop(inner_low, inner_high, functools.partial(chunk, False), state)
    return lax.fori_loop(inner_high, high, functools.partial(chunk, True), state)


def kept(scores, at, q_pos, q_start):
    k_pos = at + lax.broadcasted_iota(jnp.int32, scores.shape, 0)
    return jnp.where((k_pos <= q_pos) & (k_pos >= q_start), scores, MASKED)


SCORE_SCALE = 1.0 / math.sqrt(HEAD_WIDTH)
TWO_SCALE = SCORE_SCALE / math.log(2.0)


def forward_kernel(block_order, lengths, group, q_ref, kv_ref, out_ref, lse_ref, plan, keys, values, values_t, acc):
    step = pl.program_id(0)

    @pl.when(step == 0)
    def _():
        make_plan(block_order, lengths, group[0] * 16, plan)
        natural_order(plan, kv_ref, keys, values, (values, values_t))

    first, second = plan[2 * step], plan[2 * step + 1]
    q_t = stacked(q_ref, first, second).astype(F32).T.astype(BF)
    q_pos, q_start = strips_of(plan, lengths, step)
    width = 4 * BLK
    acc[...] = jnp.zeros_like(acc)

    def chunk(masked, index, total):
        at = pl.multiple_of(index * CHUNK, CHUNK)
        scores = matmul(keys[pl.ds(at, CHUNK), :], q_t)
        if masked:
            scores = kept(scores, at, q_pos, q_start)
        probs = jnp.exp2(scores * TWO_SCALE)
        acc[...] += matmul(values_t[:, pl.ds(at, CHUNK)], probs.astype(BF))
        return total + jnp.sum(probs, axis=0, keepdims=True)

    total = three_loops(step, plan, chunk, jnp.zeros((1, width), F32))
    lse_ref[0] = jnp.log2(total)
    unstacked(out_ref, first, second, (acc[...] / total).T.astype(BF))


def attend(block_order, lengths, group, queries, kv):
    rows = queries.shape[0]
    steps = rows // (2 * BLK)
    everything = pl.BlockSpec(queries.shape, lambda i, *_: (0, 0))
    strip = pl.BlockSpec((1, 1, 4 * BLK), lambda i, *_: (i, 0, 0))
    sds = jax.ShapeDtypeStruct
    return pl.pallas_call(
        forward_kernel,
        out_shape=(
            sds(queries.shape, BF),
            sds((steps, 1, 4 * BLK), F32),
            sds((PLAN_SIZE,), jnp.int32),
        ),
        grid_spec=pltpu.PrefetchScalarGridSpec(
            num_scalar_prefetch=3,
            grid=(steps,),
            in_specs=[everything, pl.BlockSpec(kv.shape, lambda i, *_: (0, 0))],
            out_specs=[everything, strip, pl.BlockSpec(memory_space=pltpu.SMEM)],
            scratch_shapes=[
                pltpu.VMEM((kv.shape[0], HEAD_WIDTH), BF),
                pltpu.VMEM((kv.shape[0], HEAD_WIDTH), BF),
                pltpu.VMEM((HEAD_WIDTH, kv.shape[0]), BF),
                pltpu.VMEM((HEAD_WIDTH, 4 * BLK), F32),
            ],
        ),
        compiler_params=pltpu.CompilerParams(vmem_limit_bytes=ROOM),
        name="attend",
        cost_estimate=cost(17),
    )(block_order, lengths, group, queries, kv)


def backward_kernel(plan, lengths, q_ref, heads_ref, da_ref, wo_ref, kv_ref, lse_ref, part_ref, dq_ref, dkv_ref, early_ref, keys, values, keys_t, d_keys, d_values, acc):
    step = pl.program_id(0)

    @pl.when(step == 0)
    def _():
        natural_order(plan, kv_ref, keys, values, (keys, keys_t))
        d_keys[...] = jnp.zeros_like(d_keys)
        d_values[...] = jnp.zeros_like(d_values)

    first, second = plan[2 * step], plan[2 * step + 1]
    q = stacked(q_ref, first, second)
    d_rows = matmul(
        jnp.concatenate(
            [da_ref[pl.ds(pl.multiple_of(at * BLK, BLK), BLK), :] for at in (first, second)], axis=0
        ),
        wo_ref[...],
    )
    d_out = jnp.concatenate(
        [
            d_rows[begin : begin + BLK, head : head + HEAD_WIDTH]
            for begin in (0, BLK)
            for head in (0, HEAD_WIDTH)
        ],
        axis=0,
    ).astype(BF)
    q_t = q.astype(F32).T.astype(BF)
    d_out_wide = d_out.astype(F32).T
    d_out_t = d_out_wide.astype(BF)
    q_pos, q_start = strips_of(plan, lengths, step)
    lse = lse_ref[0]
    dots = jnp.sum(d_out_wide * stacked(heads_ref, first, second).astype(F32).T, axis=0, keepdims=True)
    acc[...] = jnp.zeros_like(acc)

    def chunk(masked, index, carried):
        at = pl.multiple_of(index * CHUNK, CHUNK)
        here = pl.ds(at, CHUNK)
        scores = matmul(keys[here, :], q_t)
        if masked:
            scores = kept(scores, at, q_pos, q_start)
        probs = jnp.exp2(scores * TWO_SCALE - lse)
        d_probs = matmul(values[here, :], d_out_t)
        d_scores = (probs * (d_probs - dots)).astype(BF)
        d_values[here, :] += matmul(probs.astype(BF), d_out)
        d_keys[here, :] += matmul(d_scores, q)
        acc[...] += matmul(keys_t[:, here], d_scores)
        return carried

    three_loops(step, plan, chunk, 0)
    unstacked(dq_ref, first, second, (acc[...] * SCORE_SCALE).T)

    @pl.when(step == pl.num_programs(0) - 1)
    def _():
        def one(block, carried):
            dealt = plan[PLAN_INVERSE + block]
            group, inside = dealt // 16, dealt % 16
            half, rest = inside // 8, inside % 8
            at = pl.ds(pl.multiple_of(block * BLK, BLK), BLK)
            to = pl.ds(pl.multiple_of(rest * BLK, BLK), BLK)
            dkv_ref[half, group, 0, to, :] = (d_keys[at, :] * SCORE_SCALE).astype(BF)
            dkv_ref[half, group, 1, to, :] = d_values[at, :].astype(BF)
            return carried

        lax.fori_loop(0, kv_ref.shape[0] // BLK, one, 0, unroll=4)
        owners = early_ref.shape[0]
        depth = da_ref.shape[1] // owners
        span = 256
        for at in range(da_ref.shape[1] // span):
            value = transposed_times(da_ref[:, at * span : (at + 1) * span], heads_ref[...])
            some = slice(at * span // depth, (at + 1) * span // depth)
            for head in range(2):
                early_ref[some, head * depth : (head + 1) * depth, :] = (
                    value[:, head * HEAD_WIDTH : (head + 1) * HEAD_WIDTH]
                    .astype(BF)
                    .reshape(span // depth, depth, HEAD_WIDTH)
                )
        early_ref[:, 2 * depth :, :] = part_ref[...]


def attend_back(plan, lengths, queries, heads, d_attn, wo_t, kv, lse, part):
    rows = queries.shape[0]
    total = kv.shape[0]
    steps = rows // (2 * BLK)
    everything = pl.BlockSpec(queries.shape, lambda i, *_: (0, 0))
    strip = pl.BlockSpec((1, 1, 4 * BLK), lambda i, *_: (i, 0, 0))
    sds = jax.ShapeDtypeStruct
    owners = part.shape[0]
    early_shape = (owners, part.shape[1] + 2 * d_attn.shape[1] // owners, HEAD_WIDTH)
    dkv_shape = (2, total // rows, 2, rows // 2, HEAD_WIDTH)
    return pl.pallas_call(
        backward_kernel,
        out_shape=(sds(queries.shape, F32), sds(dkv_shape, BF), sds(early_shape, BF)),
        grid_spec=pltpu.PrefetchScalarGridSpec(
            num_scalar_prefetch=2,
            grid=(steps,),
            in_specs=[
                everything,
                everything,
                pl.BlockSpec(d_attn.shape, lambda i, *_: (0, 0)),
                pl.BlockSpec((wo_t.shape[0], queries.shape[1]), lambda i, *_: (0, 0)),
                pl.BlockSpec(kv.shape, lambda i, *_: (0, 0)),
                strip,
                pl.BlockSpec(part.shape, lambda i, *_: (0, 0, 0)),
            ],
            out_specs=[
                everything,
                pl.BlockSpec(dkv_shape, lambda i, *_: (0, 0, 0, 0, 0)),
                pl.BlockSpec(early_shape, lambda i, *_: (0, 0, 0)),
            ],
            scratch_shapes=[
                pltpu.VMEM((total, HEAD_WIDTH), BF),
                pltpu.VMEM((total, HEAD_WIDTH), BF),
                pltpu.VMEM((HEAD_WIDTH, total), BF),
                pltpu.VMEM((total, HEAD_WIDTH), F32),
                pltpu.VMEM((total, HEAD_WIDTH), F32),
                pltpu.VMEM((HEAD_WIDTH, 4 * BLK), F32),
            ],
        ),
        compiler_params=pltpu.CompilerParams(vmem_limit_bytes=ROOM),
        name="attend_back",
        cost_estimate=cost(24),
    )(plan, lengths, queries, heads, d_attn, wo_t, kv, lse, part)


def expert_kernel(side, x_ref, cot_ref, gate_ref, g_own, u_own, d_own, g_other, u_other, u_rest, d_other, y_ref, dx_ref, a_ref, dg_ref, du_ref, dy_ref, gate_w, up_w, down_w, gate_f, up_f, down_f, sems):
    half = gate_f.shape[1]
    own_copies, other_copies = [], []
    for at, (own, others, whole, stage) in enumerate(
        (
            (g_own, (g_other,), gate_w, gate_f),
            (u_own, (u_other, u_rest), up_w, up_f),
            (d_own, (d_other,), down_w, down_f),
        )
    ):
        own_copies.append(pltpu.make_async_copy(own.at[side[0]], stage, sems.at[at, 0]))
        begin = 0
        for which, part in enumerate(others):
            count = part.shape[0]
            if at < 2:
                target = whole.at[pl.ds(begin, count), pl.ds(half, half)]
            else:
                target = whole.at[pl.ds(half, half)]
            other_copies.append(pltpu.make_async_copy(part, target, sems.at[at, 1 + which]))
            begin += count

    @pl.when(pl.program_id(0) == 0)
    def _():
        for copy in own_copies + other_copies:
            copy.start()
        own_copies[0].wait()
        gate_w[:, :half] = gate_f[...].astype(BF)
        own_copies[1].wait()
        up_w[:, :half] = up_f[...].astype(BF)
        own_copies[2].wait()
        down_w[:half, :] = down_f[...].astype(BF)
        for copy in other_copies:
            copy.wait()

    x = x_ref[...]
    gate_pre = matmul(x, gate_w[...])
    up_pre = matmul(x, up_w[...])
    sigma = 1.0 / (1.0 + jnp.exp(-gate_pre))
    silu = gate_pre * sigma
    activated = (silu * up_pre).astype(BF)
    a_ref[...] = activated
    gates = gate_ref[:, 0:1].astype(F32) + gate_ref[:, 64:65].astype(F32)
    cot = cot_ref[...].astype(F32)
    out = matmul(activated, down_w[...])
    y_ref[...] = (out * gates).astype(BF)
    dots = jnp.sum(out * cot, axis=1, keepdims=True)
    high = dots.astype(BF).astype(F32)
    lane = lax.broadcasted_iota(jnp.int32, (dots.shape[0], 128), 1)
    dx_ref[:, y_ref.shape[1] :] = jnp.where(lane < 64, high, dots - high).astype(BF)
    d_pairs = (cot * gates).astype(BF)
    dy_ref[...] = d_pairs
    d_act = times_transposed(d_pairs, down_w[...])
    d_gate = (d_act * up_pre * sigma * (1.0 + gate_pre * (1.0 - sigma))).astype(BF)
    d_up = (d_act * silu).astype(BF)
    dg_ref[...] = d_gate
    du_ref[...] = d_up
    dx_ref[:, : y_ref.shape[1]] = (times_transposed(d_gate, gate_w[...]) + times_transposed(d_up, up_w[...])).astype(BF)


def run_expert(side, rows_in, cot, gates, own, other):
    count, width = rows_in.shape
    half = own[0].shape[2]
    tile = 256
    sds = jax.ShapeDtypeStruct

    def by_rows(columns):
        return pl.BlockSpec((tile, columns), lambda i, side: (i, 0))

    return pl.pallas_call(
        expert_kernel,
        out_shape=(
            sds((count, width), BF),
            sds((count, width + 128), BF),
            sds((count, 2 * half), BF),
            sds((count, 2 * half), BF),
            sds((count, 2 * half), BF),
            sds((count, width), BF),
        ),
        grid_spec=pltpu.PrefetchScalarGridSpec(
            num_scalar_prefetch=1,
            grid=(count // tile,),
            in_specs=[by_rows(width), by_rows(width), by_rows(128)] + [ANY] * 7,
            out_specs=[
                by_rows(width),
                by_rows(width + 128),
                by_rows(2 * half),
                by_rows(2 * half),
                by_rows(2 * half),
                by_rows(width),
            ],
            scratch_shapes=[
                pltpu.VMEM((width, 2 * half), BF),
                pltpu.VMEM((width, 2 * half), BF),
                pltpu.VMEM((2 * half, width), BF),
                pltpu.VMEM((width, half), F32),
                pltpu.VMEM((width, half), F32),
                pltpu.VMEM((half, width), F32),
                DMA((3, 3)),
            ],
        ),
        compiler_params=pltpu.CompilerParams(vmem_limit_bytes=ROOM),
        name="run_expert",
        cost_estimate=cost(25),
    )(side, rows_in, cot, gates, *own, *other)


def expert_grads_kernel(side, x_ref, dy_ref, a_ref, dg_ref, du_ref, gate_ref, up_ref, down_ref, gate_out, up_out, up_rest, down_out, down_rest, a_t):
    half = gate_ref.shape[-1]
    step = pl.program_id(0)
    turn_at = up_out.shape[0]

    @pl.when(step == 0)
    def _():
        a_t[...] = a_ref[...].T

    x_t = x_ref[...].T
    value = matmul(x_t, dg_ref[...])
    gate_ref[0] = value[:, :half]
    gate_out[...] = value[:, half:].astype(BF)
    value = matmul(x_t, du_ref[...])
    up_ref[0] = value[:, :half]
    low = value[:, half:].astype(BF)

    @pl.when(step < UP_CUT[0] // turn_at)
    def _():
        up_out[...] = low

    @pl.when(step >= UP_CUT[0] // turn_at)
    def _():
        up_rest[...] = low

    value = matmul(a_t[...], dy_ref[...])
    down_ref[0] = value[:half]
    cut = half + down_out.shape[0]
    down_out[...] = value[half:cut].astype(BF)
    down_rest[...] = value[cut:].astype(BF)


def expert_grads(side, rows_in, d_pairs, activated, d_gate, d_up):
    count, width = rows_in.shape
    whole = activated.shape[1]
    half = whole // 2
    tile = 256
    first = UP_CUT[0] // tile
    sds = jax.ShapeDtypeStruct
    columns = pl.BlockSpec((count, tile), lambda i, side: (0, i))
    full = pl.BlockSpec((count, whole), lambda i, side: (0, 0))
    own_rows = pl.BlockSpec((1, tile, half), lambda i, side: (side[0], i, 0))
    return pl.pallas_call(
        expert_grads_kernel,
        out_shape=(
            sds((2, width, half), F32),
            sds((2, width, half), F32),
            sds((2, half, width), F32),
            sds((width, half), BF),
            sds((UP_CUT[0], half), BF),
            sds((UP_CUT[1], half), BF),
            sds((DOWN_GRAD_CUT[0], width), BF),
            sds((DOWN_GRAD_CUT[1], width), BF),
        ),
        grid_spec=pltpu.PrefetchScalarGridSpec(
            num_scalar_prefetch=1,
            grid=(width // tile,),
            in_specs=[columns, columns, full, full, full],
            out_specs=[
                own_rows,
                own_rows,
                pl.BlockSpec((1, half, tile), lambda i, side: (side[0], 0, i)),
                pl.BlockSpec((tile, half), lambda i, side: (i, 0)),
                pl.BlockSpec((tile, half), lambda i, side: (jnp.minimum(i, first - 1), 0)),
                pl.BlockSpec((tile, half), lambda i, side: (jnp.maximum(i - first, 0), 0)),
                pl.BlockSpec((DOWN_GRAD_CUT[0], tile), lambda i, side: (0, i)),
                pl.BlockSpec((DOWN_GRAD_CUT[1], tile), lambda i, side: (0, i)),
            ],
            scratch_shapes=[pltpu.VMEM((whole, count), BF)],
        ),
        compiler_params=pltpu.CompilerParams(vmem_limit_bytes=ROOM),
        name="expert_grads",
        cost_estimate=cost(12),
    )(side, rows_in, d_pairs, activated, d_gate, d_up)


def route_kernel(where, routes_ref, cot_ref, pick_ref, turned_ref, of_ref, hits_ref, rows_ref):
    slots, rows = pick_ref.shape[0], routes_ref.shape[2]
    experts = of_ref.shape[1]
    slot = lax.broadcasted_iota(jnp.int32, (slots, experts), 0)
    lane = lax.broadcasted_iota(jnp.int32, (slots, experts), 1)
    chip = lax.div(slot, 2 * CAP)
    side = lax.rem(where[1] + lax.div(chip, 4) + where[2], 2)
    of_expert = (lane == 4 * chip + 2 * where[0] + side).astype(F32).astype(BF)
    of_ref[...] = of_expert
    expert = lax.broadcasted_iota(jnp.int32, (experts, rows), 0)
    before = (
        lax.broadcasted_iota(jnp.int32, (rows, rows), 0) < lax.broadcasted_iota(jnp.int32, (rows, rows), 1)
    ).astype(F32).astype(BF)
    hits, ranks = [], []
    for half in range(2):
        hit = jnp.zeros((experts, rows), F32)
        for choice in range(TOPK):
            hit = hit + (routes_ref[half, choice : choice + 1, :] == expert).astype(F32)
        rank = matmul(hit.astype(BF), before) + half * CAP
        hits.append(hit)
        ranks.append(jnp.where(hit > 0.5, rank, -1.0))
    hits_ref[...] = jnp.concatenate(hits, axis=1).T
    mine = matmul(of_expert, jnp.concatenate(ranks, axis=1).astype(BF))
    wanted = lax.rem(lax.broadcasted_iota(jnp.int32, mine.shape, 0), 2 * CAP).astype(F32)
    pick = (mine == wanted).astype(F32)
    pick_low = pick.astype(BF)
    pick_ref[...] = pick_low
    turned_ref[...] = pick.T.astype(BF)
    rows_ref[...] = matmul(pick_low, cot_ref[...]).astype(BF)


def route(where, routes, cotangent, experts):
    rows, width = cotangent.shape
    slots = experts // 4 * 2 * CAP
    sds = jax.ShapeDtypeStruct
    return pl.pallas_call(
        route_kernel,
        out_shape=(
            sds((slots, rows), BF),
            sds((rows, slots), BF),
            sds((slots, experts), BF),
            sds((rows, experts), F32),
            sds((slots, width), BF),
        ),
        in_specs=[pl.BlockSpec(memory_space=pltpu.SMEM), VMEM, VMEM],
        out_specs=[VMEM] * 5,
        compiler_params=pltpu.CompilerParams(vmem_limit_bytes=ROOM),
        name="route",
        cost_estimate=cost(5),
    )(where, routes, cotangent)


def middle_kernel(chip, t_ref, attn_ref, gain_ref, wr_ref, hits_ref, pick_ref, of_ref, res_ref, h_ref, inv_ref, gates_ref, rows_ref, tile_ref):
    residual = t_ref[...].astype(F32) + attn_ref[...]
    res_ref[...] = residual
    inverse = lax.rsqrt(jnp.mean(residual * residual, axis=1, keepdims=True) + EPSILON)
    inv_ref[...] = jnp.broadcast_to(inverse, inv_ref.shape)
    hidden = (residual * inverse * gain_ref[...]).astype(BF)
    h_ref[...] = hidden
    pick = pick_ref[...]
    rows_ref[...] = matmul(pick, hidden).astype(BF)
    hit = hits_ref[...] > 0.5
    logits = jnp.where(hit, matmul(hidden, wr_ref[...]), MASKED)
    exps = jnp.where(hit, jnp.exp(logits - jnp.max(logits, axis=1, keepdims=True)), 0.0)
    gates = exps / jnp.sum(exps, axis=1, keepdims=True)
    gates_ref[...] = gates
    high = gates.astype(BF)
    chosen = [
        jnp.sum(matmul(pick, part) * of_ref[...].astype(F32), axis=1, keepdims=True)
        for part in (high, (gates - high.astype(F32)).astype(BF))
    ]
    lane = lax.broadcasted_iota(jnp.int32, tile_ref.shape, 1)
    tile_ref[...] = jnp.where(lane < 64, chosen[0], chosen[1]).astype(BF)


def middle(chip, row_rows, attn_total, gain, late_all, hits, pick, of_expert):
    rows, width = attn_total.shape
    slots, experts = of_expert.shape
    sds = jax.ShapeDtypeStruct

    def whole(value):
        return pl.BlockSpec(value.shape, lambda i, chip: (0, 0))

    def out(*shape):
        return pl.BlockSpec(shape, lambda i, chip: (0, 0))

    shapes = (
        sds((rows, width), F32),
        sds((rows, width), BF),
        sds((rows, 128), F32),
        sds((rows, experts), F32),
        sds((slots, width), BF),
        sds((slots, 128), BF),
    )
    return pl.pallas_call(
        middle_kernel,
        out_shape=shapes,
        grid_spec=pltpu.PrefetchScalarGridSpec(
            num_scalar_prefetch=1,
            grid=(1,),
            in_specs=[
                pl.BlockSpec((rows, width), lambda i, chip: (chip[0], 0)),
                whole(attn_total),
                whole(gain),
                pl.BlockSpec((width, experts), lambda i, chip: (0, 2)),
                whole(hits),
                whole(pick),
                whole(of_expert),
            ],
            out_specs=[out(*value.shape) for value in shapes],
        ),
        compiler_params=pltpu.CompilerParams(vmem_limit_bytes=ROOM),
        name="middle",
        cost_estimate=cost(1),
    )(chip, row_rows, attn_total, gain, late_all, hits, pick, of_expert)


def turn_kernel(core, moe_ref, dg_ref, gates_ref, h_ref, res_ref, inv_ref, wr_ref, gain_ref, cot_ref, d_ref, low_ref, part_ref):
    gates = gates_ref[...]
    d_gates = dg_ref[...]
    d_logits = (gates * (d_gates - jnp.sum(gates * d_gates, axis=1, keepdims=True))).astype(BF)
    hidden = h_ref[...]
    gradient = moe_ref[...] + times_transposed(d_logits, wr_ref[...])
    residual, inverse = res_ref[...], inv_ref[:, 0:1]
    weighted = gradient * gain_ref[...]
    mean_term = jnp.mean(weighted * residual, axis=1, keepdims=True)
    back = inverse * weighted - residual * (inverse * inverse * inverse) * mean_term
    value = cot_ref[...].astype(F32) + back
    d_ref[...] = value
    low_ref[...] = value.astype(BF)
    owners, rows, _ = part_ref.shape
    depth = hidden.shape[1] // owners
    grad_router = transposed_times(hidden, d_logits).astype(BF)
    part_ref[:, :depth, :] = grad_router.reshape(owners, depth, grad_router.shape[1])
    terms = jnp.sum(gradient * residual * inverse, axis=0, keepdims=True)
    wide = jnp.broadcast_to(terms, (8, terms.shape[1]))
    by_owner = jnp.concatenate(
        [wide[:1, owner * depth : (owner + 1) * depth] for owner in range(owners)], axis=0
    )
    by_owner = jnp.concatenate([by_owner, jnp.zeros((owners, 128 - depth), F32)], axis=1)
    part_ref[:, depth:, :] = jnp.broadcast_to(
        by_owner[:, None, :], (owners, rows - depth, 128)
    ).astype(BF)


def turn(core, d_moe, d_gates, gates, hidden, residual, inverse, late_all, gain, cotangent):
    rows, width = d_moe.shape
    experts = gates.shape[1]
    owners = 64
    sds = jax.ShapeDtypeStruct

    def mine(columns):
        return pl.BlockSpec((rows, columns), lambda i, core: (core[0], 0))

    def whole(*shape):
        return pl.BlockSpec(shape, lambda i, core: (0,) * len(shape))

    parts = (owners, width // owners + 16, 128)
    return pl.pallas_call(
        turn_kernel,
        out_shape=(sds((rows, width), F32), sds((rows, width), BF), sds(parts, BF)),
        grid_spec=pltpu.PrefetchScalarGridSpec(
            num_scalar_prefetch=1,
            grid=(1,),
            in_specs=[
                whole(rows, width),
                whole(rows, experts),
                mine(experts),
                mine(width),
                mine(width),
                mine(128),
                pl.BlockSpec((width, experts), lambda i, core: (0, 2)),
                whole(1, width),
                whole(rows, width),
            ],
            out_specs=[whole(rows, width), whole(rows, width), whole(*parts)],
        ),
        compiler_params=pltpu.CompilerParams(vmem_limit_bytes=ROOM),
        name="turn",
        cost_estimate=cost(6),
    )(core, d_moe, d_gates, gates, hidden, residual, inverse, late_all, gain, cotangent)


def last_kernel(side, g_in, u_in, u_rest, d_in, d_rest, *refs):
    (t_ref, dh_ref, dr_ref, moe_ref, res_ref, ga_ref, late_ref, early_ref, wq_ref, wk_ref, wv_ref), refs = refs[3:14], refs[14:]
    g_out, u_out, d_out, out_ref, gt_ref, gq_ref, gk_ref, gv_ref, go_ref, gr_ref, gains_ref, ffn_ref = refs[:12]
    keys, router, gains, ffn, dots = refs[12:]
    step = pl.program_id(0)
    g_out[0] = g_in[...].astype(F32)
    u_out[0] = jnp.where(step < UP_CUT[0] // u_in.shape[0], u_in[...], u_rest[...]).astype(F32)
    d_out[0, : d_in.shape[0]] = d_in[...].astype(F32)
    d_out[0, d_in.shape[0] :] = d_rest[...].astype(F32)
    rows = t_ref[...].astype(F32)
    out_ref[...] = res_ref[...] + moe_ref[...]
    inverse = lax.rsqrt(jnp.mean(rows * rows, axis=1, keepdims=True) + EPSILON)
    weighted = dh_ref[...] * ga_ref[...]
    mean_term = jnp.mean(weighted * rows, axis=1, keepdims=True)
    gt_ref[...] = dr_ref[...] + (
        inverse * weighted - rows * (inverse * inverse * inverse) * mean_term
    )

    @pl.when(step == 0)
    def _():
        for ref in (keys, router, gains, ffn, dots):
            ref[...] = jnp.zeros_like(ref)

    depth = gq_ref.shape[0]
    late, early = late_ref[0].astype(F32), early_ref[0].astype(F32)
    query = jnp.concatenate([late[:depth], late[depth : 2 * depth]], axis=1)
    gq_ref[...] = query
    low_q = wq_ref[...].astype(BF).astype(F32)
    dots[...] += jnp.sum(low_q * query, axis=1, keepdims=True)
    keys[lax.div(step, 2)] += late[2 * depth : 3 * depth]
    gains[...] += late[3 * depth :]
    router[...] += early[2 * depth : 3 * depth]
    ffn[...] += early[3 * depth : 3 * depth + 8]
    go_ref[...] = jnp.concatenate([early[:depth], early[depth : 2 * depth]], axis=1)

    @pl.when(step == pl.num_programs(0) - 1)
    def _():
        gk_ref[...] = jnp.concatenate([keys[0], keys[2]], axis=1)
        gv_ref[...] = jnp.concatenate([keys[1], keys[3]], axis=1)
        gr_ref[...] = router[...]
        ffn_ref[...] = ffn[...]
        total = (
            dots[:, 0:1]
            + jnp.sum(wk_ref[...].astype(BF).astype(F32) * gk_ref[...], axis=1, keepdims=True)
            + jnp.sum(wv_ref[...].astype(BF).astype(F32) * gv_ref[...], axis=1, keepdims=True)
        )
        blank = jnp.zeros((128 - depth, 128), F32)
        square = jnp.concatenate([jnp.broadcast_to(total, (depth, 128)), blank], axis=0).T
        row = lax.broadcasted_iota(jnp.int32, gains_ref.shape, 0)
        gains_ref[...] = jnp.where(row < 2, gains[:8], square[:8])


def last(side, arrived, placed, tokens, d_hidden, d_residual, moe, residual, gain, late, early, weights):
    width, half = arrived[0].shape
    rows = tokens.shape[0]
    steps = 8
    tile, strip = width // steps, rows // steps
    depth = weights[0].shape[0]
    sds = jax.ShapeDtypeStruct

    def whole(*shape):
        return pl.BlockSpec(shape, lambda i, side: (0,) * len(shape))

    first = UP_CUT[0] // tile
    rows_out = pl.BlockSpec((1, tile, half), lambda i, side: (1 - side[0], i, 0))
    columns_out = pl.BlockSpec((1, half, tile), lambda i, side: (1 - side[0], 0, i))
    strips = pl.BlockSpec((strip, width), lambda i, side: (i, 0))
    mine = pl.BlockSpec((strip, width), lambda i, side: (side[1] * steps + i, 0))
    place = pl.BlockSpec((1,) + late.shape[1:], lambda i, side: (i, 0, 0))
    query = pl.BlockSpec((depth, weights[0].shape[1] // steps), lambda i, side: (0, i))
    narrow = (depth, weights[1].shape[1])
    return pl.pallas_call(
        last_kernel,
        out_shape=[sds(value.shape, F32) for value in placed]
        + [
            sds((rows, width), F32),
            sds((rows, width), F32),
            sds(weights[0].shape, F32),
            sds(narrow, F32),
            sds(narrow, F32),
            sds(weights[0].shape, F32),
            sds((depth, 128), F32),
            sds((8, 128), F32),
            sds((8, 128), F32),
        ],
        grid_spec=pltpu.PrefetchScalarGridSpec(
            num_scalar_prefetch=1,
            grid=(steps,),
            in_specs=[
                pl.BlockSpec((tile, half), lambda i, side: (i, 0)),
                pl.BlockSpec((tile, half), lambda i, side: (jnp.minimum(i, first - 1), 0)),
                pl.BlockSpec((tile, half), lambda i, side: (jnp.maximum(i - first, 0), 0)),
                pl.BlockSpec((DOWN_GRAD_CUT[0], tile), lambda i, side: (0, i)),
                pl.BlockSpec((DOWN_GRAD_CUT[1], tile), lambda i, side: (0, i)),
            ]
            + [ANY] * 3
            + [
                strips,
                strips,
                strips,
                strips,
                mine,
                whole(1, width),
                place,
                place,
                query,
                whole(*narrow),
                whole(*narrow),
            ],
            out_specs=[
                rows_out,
                rows_out,
                columns_out,
                strips,
                strips,
                query,
                whole(*narrow),
                whole(*narrow),
                query,
                whole(depth, 128),
                whole(8, 128),
                whole(8, 128),
            ],
            scratch_shapes=[
                pltpu.VMEM((4, depth, 128), F32),
                pltpu.VMEM((depth, 128), F32),
                pltpu.VMEM((16, 128), F32),
                pltpu.VMEM((8, 128), F32),
                pltpu.VMEM((depth, 128), F32),
            ],
        ),
        input_output_aliases={6: 0, 7: 1, 8: 2},
        compiler_params=pltpu.CompilerParams(vmem_limit_bytes=ROOM),
        name="last",
        cost_estimate=cost(9),
    )(side, *arrived, *placed, tokens, d_hidden, d_residual, moe, residual, gain, late, early, *weights)


def project_kernel(block_order, lengths, group, t_ref, w_ref, side_ref, flag_ref, freq_ref, ga_ref, gq_ref, gk_ref, h_ref, q_ref, kv_ref, qp_ref, kp_ref, cos_ref, sin_ref):
    tile = t_ref.shape[0]
    row = lax.broadcasted_iota(jnp.int32, (tile, HEAD_WIDTH), 0)
    lane = lax.broadcasted_iota(jnp.int32, (tile, HEAD_WIDTH), 1)
    first_block = group[0] * 16 + pl.program_id(0) * (tile // BLK)
    position = row * 0
    for at in range(tile // BLK):
        inside = block_order[first_block + at] * BLK + row - at * BLK
        position = jnp.where(row >= at * BLK, inside, position)
    angles = (position - start_of(lengths, position)).astype(F32) * freq_ref[...]
    cosine = jnp.cos(angles)
    sine_tab = jnp.where(lane < HEAD_WIDTH // 2, -1.0, 1.0) * jnp.sin(angles)
    cos_ref[...] = cosine
    sin_ref[...] = sine_tab
    rows = t_ref[...].astype(F32)
    inverse = lax.rsqrt(jnp.mean(rows * rows, axis=1, keepdims=True) + EPSILON)
    hidden = (rows * inverse * ga_ref[...]).astype(BF)
    h_ref[...] = hidden
    qkv = matmul(hidden, w_ref[...])
    own = qkv[:, 2 * HEAD_WIDTH :]
    other = matmul(hidden, side_ref[...])
    first = flag_ref[0:1, :] > 0.5

    def turned(value, gain):
        root = lax.rsqrt(jnp.mean(value * value, axis=1, keepdims=True) + EPSILON)
        value = value * root * gain
        return (value * cosine + pltpu.roll(value, HEAD_WIDTH // 2, 1) * sine_tab).astype(BF)

    for head in range(2):
        span = slice(head * HEAD_WIDTH, (head + 1) * HEAD_WIDTH)
        q_ref[:, span] = turned(qkv[:, span], gq_ref[...])
    qp_ref[...] = qkv[:, : 2 * HEAD_WIDTH]
    keys = jnp.where(first, own, other)
    kp_ref[...] = keys
    kv_ref[:, :HEAD_WIDTH] = turned(keys, gk_ref[...])
    kv_ref[:, HEAD_WIDTH:] = jnp.where(first, other, own).astype(BF)


def project(block_order, lengths, group, tokens, weights, side, first, frequency, gain, gain_query, gain_key):
    rows, width = tokens.shape
    tile = 256
    sds = jax.ShapeDtypeStruct

    def by_rows(columns):
        return pl.BlockSpec((tile, columns), lambda i, *_: (i, 0))

    def whole(value):
        return pl.BlockSpec(value.shape, lambda i, *_: (0, 0))

    return pl.pallas_call(
        project_kernel,
        out_shape=(
            sds((rows, width), BF),
            sds((rows, 256), BF),
            sds((rows, 256), BF),
            sds((rows, 256), F32),
            sds((rows, 128), F32),
            sds((rows, 128), F32),
            sds((rows, 128), F32),
        ),
        grid_spec=pltpu.PrefetchScalarGridSpec(
            num_scalar_prefetch=3,
            grid=(rows // tile,),
            in_specs=[
                by_rows(width),
                whole(weights),
                whole(side),
                whole(first),
                whole(frequency),
                whole(gain),
                whole(gain_query),
                whole(gain_key),
            ],
            out_specs=[
                by_rows(width),
                by_rows(256),
                by_rows(256),
                by_rows(256),
                by_rows(128),
                by_rows(128),
                by_rows(128),
            ],
        ),
        compiler_params=pltpu.CompilerParams(vmem_limit_bytes=ROOM),
        name="project",
        cost_estimate=cost(8),
    )(block_order, lengths, group, tokens, weights, side, first, frequency, gain, gain_query, gain_key)


def project_back_kernel(dq_ref, ds_ref, qp_ref, kp_ref, cos_ref, sin_ref, h_ref, w_ref, side_ref, gq_ref, gk_ref, flag_ref, part_ref, late_ref, side_w, total, gains):
    step = pl.program_id(0)
    cosine, sine_tab = cos_ref[...], sin_ref[...]
    key, first, own = flag_ref[0:1, :], flag_ref[1:2, :], flag_ref[2:3, :]
    heads = 2 * HEAD_WIDTH

    @pl.when(step == 0)
    def _():
        gains[...] = jnp.zeros_like(gains)
        total[...] = jnp.zeros_like(total)
        side_w[...] = jnp.where(
            own > 0.5, w_ref[:, heads:].astype(F32), side_ref[...].astype(F32)
        ).astype(BF)

    def back(gradient, value, gain):
        gradient = gradient * cosine - pltpu.roll(gradient, HEAD_WIDTH // 2, 1) * sine_tab
        root = lax.rsqrt(jnp.mean(value * value, axis=1, keepdims=True) + EPSILON)
        weighted = gradient * gain
        mean_term = jnp.mean(weighted * value, axis=1, keepdims=True)
        terms = jnp.sum(gradient * value * root, axis=0, keepdims=True)
        return root * weighted - value * (root * root * root) * mean_term, terms

    columns = []
    for head in range(2):
        span = slice(head * HEAD_WIDTH, (head + 1) * HEAD_WIDTH)
        value, terms = back(dq_ref[:, span], qp_ref[:, span], gq_ref[...])
        columns.append(value.astype(BF))
        gains[0:1, :] += terms
    d_side = ds_ref[...]
    value, terms = back(d_side, kp_ref[...], gk_ref[...])
    mine = jnp.where(first == (step // 2).astype(F32), 1.0, 0.0)
    columns.append((jnp.where(key > 0.5, value, d_side) * mine).astype(BF))
    gains[1:2, :] += terms * key * mine
    d_all = jnp.concatenate(columns, axis=1)
    part_ref[...] = (
        times_transposed(d_all[:, :heads], w_ref[:, :heads])
        + times_transposed(d_all[:, heads:], side_w[...])
    ).astype(BF)
    total[...] += transposed_times(h_ref[...], d_all)

    @pl.when(step == pl.num_programs(0) - 1)
    def _():
        pieces, depth = late_ref.shape[0], h_ref.shape[1] // late_ref.shape[0]
        for at in range(3):
            value = total[:, at * HEAD_WIDTH : (at + 1) * HEAD_WIDTH].astype(BF)
            late_ref[:, at * depth : (at + 1) * depth, :] = value.reshape(pieces, depth, HEAD_WIDTH)
        late_ref[:, 3 * depth :, :] = jnp.broadcast_to(
            gains[...].astype(BF)[None], (pieces,) + gains.shape
        )


def project_back(d_queries, d_side, q_pre, k_pre, cosine, sine_tab, hidden, weights, side, gain_query, gain_key, flags):
    rows = d_queries.shape[0]
    width = hidden.shape[1]
    tile = 256
    tiles = rows // tile
    owners = 64
    sds = jax.ShapeDtypeStruct
    late = (owners, 3 * width // owners + 16, 128)

    def by_rows(columns):
        return pl.BlockSpec((tile, columns), lambda i: (i, 0))

    def whole(value):
        return pl.BlockSpec(value.shape, lambda i: (0, 0))

    half_rows = pl.BlockSpec((tile, 128), lambda i: (i % (tiles // 2), 0))
    return pl.pallas_call(
        project_back_kernel,
        grid=(tiles,),
        out_shape=(sds((rows, width), BF), sds(late, BF)),
        in_specs=[
            by_rows(256),
            half_rows,
            by_rows(256),
            by_rows(128),
            by_rows(128),
            by_rows(128),
            by_rows(width),
            whole(weights),
            whole(side),
            whole(gain_query),
            whole(gain_key),
            whole(flags),
        ],
        out_specs=[by_rows(width), pl.BlockSpec(late, lambda i: (0, 0, 0))],
        scratch_shapes=[
            pltpu.VMEM((width, 128), BF),
            pltpu.VMEM((width, 384), F32),
            pltpu.VMEM((16, 128), F32),
        ],
        compiler_params=pltpu.CompilerParams(vmem_limit_bytes=ROOM),
        name="project_back",
        cost_estimate=cost(12),
    )(
        d_queries, d_side, q_pre, k_pre, cosine, sine_tab, hidden, weights, side, gain_query, gain_key, flags
    )


def after(value, earlier):
    return lax.optimization_barrier((value, earlier))


def lanes_to(row, lanes=128):
    return jnp.pad(row, ((0, 0),) * (row.ndim - 1) + ((0, lanes - row.shape[-1]),))


def local(
    tokens,
    cotangent,
    seq_lengths,
    block_order,
    routes,
    w_query,
    key_weight,
    value_weight,
    w_out,
    gain_attn,
    gain_query,
    gain_key,
    gain_ffn,
    w_router,
    w_gate,
    w_up,
    w_down,
):
    rows = tokens.shape[0]
    width = tokens.shape[1]
    experts = w_router.shape[1]
    block_count = block_order.shape[0]
    wsh = lax.axis_index("wsh")
    me = lax.axis_index("ctx")
    core = lax.rem(me, 2)
    place = lax.rem(me, 8)
    group = lax.div(me, 8)
    row_tokens = 8 * rows

    def swap(value):
        return lax.ppermute(value, "wsh", [(0, 1), (1, 0)])

    depth = w_query.shape[0]
    (
        w_all,
        row_rows,
        small_all,
        chip_routes,
        chip_cot,
        other_gate,
        up_first,
        other_up,
        other_down,
        w_side,
    ) = gather_first(
        (w_query, key_weight, value_weight),
        (gain_attn[None, :], gain_ffn[None, :]),
        tokens,
        routes.T,
        cotangent,
        (w_gate, w_up, w_down),
    )
    w_main = w_all.reshape(width, 384)
    w_side = w_side.reshape(width, 128)
    is_key = lax.rem(lax.div(me, 2), 2) == 0

    def flag(value):
        return jnp.broadcast_to(value.astype(F32).reshape(1, 1), (8, 128))

    g_attn = to_low(small_all[:, 0, :depth].reshape(width)).astype(F32)
    g_ffn = to_low(small_all[:, 1, :depth].reshape(width)).astype(F32)
    g_query = rounded(gain_query)
    g_key = rounded(gain_key)

    o_part = to_low(w_out).T.reshape(depth, 8, 256).transpose(1, 0, 2)
    r_part = jnp.broadcast_to(to_low(w_router)[None], (8, depth, experts))
    late_pack = jnp.tile(jnp.concatenate([o_part, r_part], axis=2), (8, 1, 1))
    late_pack, small_all = after(late_pack, small_all)
    late_all = lax.all_to_all(late_pack, "ctx", split_axis=0, concat_axis=0, tiled=True).reshape(width, 384)

    chips = experts // 4
    slots = 2 * CAP
    y_half = lax.rem(lax.div(me, 8), 2)
    pick_low, pick_turned, of_expert, hits, cot_rows = route(
        jnp.stack([core, wsh, y_half]), chip_routes, chip_cot.reshape(2 * rows, width), experts
    )

    half_dim = HEAD_WIDTH // 2
    frequency = jnp.power(ROPE_BASE, -2.0 * jnp.arange(half_dim, dtype=jnp.float32) / HEAD_WIDTH)
    frequency = jnp.concatenate([frequency, frequency])[None, :]
    row_rows = row_rows.reshape(row_tokens, width)
    hidden_one, queries, kv, q_pre, k_pre, cosine, sine_tab = project(
        block_order,
        seq_lengths,
        group.reshape(1),
        row_rows,
        w_main,
        w_side,
        flag(core == 0),
        frequency,
        g_attn[None, :],
        g_query[None, :],
        g_key[None, :],
    )
    kv_all = gather_keys(kv, 1).reshape(block_count * BLK, 256)
    late_all, kv_all = after(late_all, kv_all)
    (cot_rows, other_gate), kv_all = after((cot_rows, other_gate), kv_all)
    gate_back = swap(other_gate)
    cot_there = exchange_behind(cot_rows.reshape(chips, slots, width)).reshape(chips * slots, width)
    heads, lse, plan = attend(block_order, seq_lengths, group.reshape(1), queries, kv_all)

    (other_up, other_down), heads = after((other_up, other_down), heads)
    attn_total, up_first = reduce_row((heads, late_all), 2, True, swapped_whole=up_first)
    residual, hidden_two, inverse_two, gates, out_rows, gate_tile = middle(
        lax.div(place, 2).reshape(1),
        row_rows,
        attn_total.reshape(2 * rows, width),
        g_ffn[None, :],
        late_all,
        hits,
        pick_low,
        of_expert,
    )

    out_rows = out_rows.reshape(chips, slots, width)
    gate_tile = gate_tile.reshape(chips, slots, 128)
    (gate_back, cot_there, other_down, other_up), gate_tile = after(
        (gate_back, cot_there, other_down, other_up), gate_tile
    )
    down_back = swap(other_down)
    up_back = (up_first, swap(other_up))
    arrived, gate_there = exchange([out_rows, gate_tile], 3)
    arrived = arrived.reshape(chips * slots, width)
    side = wsh.reshape(1)
    gate_there = gate_there.reshape(chips * slots, 128)
    y_rows, d_rows, activated, d_gate_pre, d_up_pre, d_pairs = run_expert(
        side, arrived, cot_there, gate_there, (w_gate, w_up, w_down), (gate_back, *up_back, down_back)
    )
    *own_grads, other_gate, up_first, other_up, other_down, down_rest = expert_grads(
        side, arrived, d_pairs, activated, d_gate_pre, d_up_pre
    )
    gate_grad_back = swap(other_gate)
    d_back = exchange_behind(d_rows.reshape(chips, slots, width + 128))
    y_rows, _ = after(y_rows, (d_back, gate_grad_back))
    y_back = exchange_behind(y_rows.reshape(chips, slots, width))

    d_back = d_back.reshape(chips * slots, width + 128)
    (gate_grad_back, other_up, other_down), d_back = after((gate_grad_back, other_up, other_down), d_back)
    d_hidden_moe, d_gates = reduce_chip(pick_turned, d_back, of_expert, width, 5)
    d_residual, d_residual_low, part = turn(
        core.reshape(1),
        d_hidden_moe,
        d_gates,
        gates,
        hidden_two,
        residual,
        inverse_two,
        late_all,
        g_ffn[None, :],
        cotangent,
    )

    d_attn, up_first = gather_row(d_residual_low, up_first, 7)
    d_attn = d_attn.reshape(row_tokens, width)
    (y_back, other_up, other_down), d_attn_late = after((y_back, other_up, other_down), d_attn)
    up_grad_back = swap(other_up)
    down_grad_back = swap(other_down)
    d_queries, d_kv, early = attend_back(
        plan, seq_lengths, queries, heads, d_attn_late, late_all, kv_all, lse, part
    )
    (up_grad_back, down_grad_back), d_kv = after((up_grad_back, down_grad_back), d_kv)
    d_side, early, down_rest = reduce_keys(d_kv, early, down_rest, 8)
    swapped_grads = (gate_grad_back, up_first, up_grad_back, down_grad_back, down_rest)
    flags = jnp.concatenate(
        [
            flag(is_key)[:1],
            flag(core)[:1],
            flag(is_key == (core == 0))[:1],
            jnp.zeros((5, 128), F32),
        ],
        axis=0,
    )
    d_hidden_parts, late = project_back(
        d_queries,
        d_side,
        q_pre,
        k_pre,
        cosine,
        sine_tab,
        hidden_one,
        w_main,
        w_side,
        g_query[None, :],
        g_key[None, :],
        flags,
    )
    d_hidden_parts = d_hidden_parts.reshape(8, rows, width)
    d_hidden_one, moe_total, late = reduce_row(
        d_hidden_parts,
        9,
        False,
        extra=(pick_turned, y_back.reshape(chips * slots, width)),
        owned=(late,),
    )
    (
        grad_gate,
        grad_up,
        grad_down,
        out_stream,
        grad_tokens,
        grad_query,
        grad_key,
        grad_value,
        grad_out_t,
        grad_router,
        gain_parts,
        grad_gain_ffn,
    ) = last(
        jnp.stack([wsh, core]),
        swapped_grads,
        own_grads,
        tokens,
        d_hidden_one,
        d_residual,
        moe_total,
        residual,
        g_attn[None, :],
        late,
        early,
        (w_query, key_weight, value_weight),
    )
    gain_parts = lax.psum(gain_parts, "wsh")
    return (
        out_stream,
        grad_tokens,
        grad_query,
        grad_key,
        grad_value,
        grad_out_t.T,
        gain_parts[2, :depth] / rounded(gain_attn),
        gain_parts[0],
        gain_parts[1],
        grad_gain_ffn[0, :depth],
        grad_router,
        grad_gate,
        grad_up,
        grad_down,
    )


def solution(mesh):
    in_specs = (
        P("ctx", None),
        P("ctx", None),
        P(),
        P(),
        P("ctx", None),
        P("ctx", "wsh"),
        P("ctx", "wsh"),
        P("ctx", "wsh"),
        P("wsh", "ctx"),
        P("ctx"),
        P(),
        P(),
        P("ctx"),
        P("ctx", None),
        P("ctx", None, "wsh"),
        P("ctx", None, "wsh"),
        P("ctx", "wsh", None),
    )
    out_specs = (
        P("ctx", None),
        P("ctx", None),
        P("ctx", "wsh"),
        P("ctx", "wsh"),
        P("ctx", "wsh"),
        P("wsh", "ctx"),
        P("ctx"),
        P(),
        P(),
        P("ctx"),
        P("ctx", None),
        P("ctx", None, "wsh"),
        P("ctx", None, "wsh"),
        P("ctx", "wsh", None),
    )
    return jax.shard_map(local, mesh=mesh, in_specs=in_specs, out_specs=out_specs, check_vma=False)
```

```python
import functools
import math

import jax
import jax.numpy as jnp
from jax import lax
from jax.experimental import pallas as pl
from jax.experimental.pallas import tpu as pltpu
from jax.sharding import PartitionSpec as P

HEAD_WIDTH = 128
TOPK = 8
BLK = 64
MAX_SEQ_TOKENS = 4096
CAP = 12
CHUNK = 1024

EPSILON = 1e-06
ROPE_BASE = 1000000.0
MASKED = -1e30
MESH = pl.DeviceIdType.MESH
BF = jnp.bfloat16
F32 = jnp.float32


def to_low(value_rows):
    return value_rows.astype(jnp.bfloat16)


def rounded(value_rows):
    return lax.optimization_barrier(value_rows.astype(jnp.bfloat16)).astype(jnp.float32)


def matmul(left, right):
    return jnp.dot(left, right, preferred_element_type=jnp.float32)


def times_transposed(left, right):
    return lax.dot_general(
        left, right, (((1,), (1,)), ((), ())), preferred_element_type=jnp.float32
    )


def transposed_times(left, right):
    return lax.dot_general(
        left, right, (((0,), (0,)), ((), ())), preferred_element_type=jnp.float32
    )


def coords(c):
    return (
        lax.div(c, 16),
        lax.rem(lax.div(c, 8), 2),
        lax.rem(lax.div(c, 2), 4),
        lax.rem(c, 2),
    )


def index_of(z, y, x, k):
    return ((z * 2 + y) * 4 + x) * 2 + k


def shifted(me, dz, dy, dx, dk):
    z, y, x, k = coords(me)
    return index_of(lax.rem(z + dz, 4), lax.rem(y + dy, 2), lax.rem(x + dx, 4), lax.rem(k + dk, 2))


def remote(src, dst, send, recv, ctx, wsh):
    return pltpu.make_async_remote_copy(
        src_ref=src,
        dst_ref=dst,
        send_sem=send,
        recv_sem=recv,
        device_id=(ctx, wsh),
        device_id_type=MESH,
    )


def greet(targets):
    barrier = pltpu.get_barrier_semaphore()
    for ctx, wsh in targets:
        pl.semaphore_signal(barrier, inc=1, device_id=(ctx, wsh), device_id_type=MESH)
    return barrier, len(targets)


def greet_many(count, target):
    barrier = pltpu.get_barrier_semaphore()

    def one(step, carried):
        pl.semaphore_signal(barrier, inc=1, device_id=target(step), device_id_type=MESH)
        return carried

    lax.fori_loop(1, count, one, 0)
    return barrier, count - 1


ANY = pl.BlockSpec(memory_space=pl.ANY)
VMEM = pl.BlockSpec(memory_space=pltpu.VMEM)
DMA = pltpu.SemaphoreType.DMA


def cost(microseconds):
    return pl.CostEstimate(flops=0, bytes_accessed=int(microseconds * 1.2e6), transcendentals=0)


ROOM = 56 * 1024 * 1024


def call_params(collective_id):
    return pltpu.CompilerParams(
        collective_id=collective_id, has_side_effects=True, vmem_limit_bytes=ROOM
    )


def row_gather_start(src, out, me, wsh, send, recv):
    place = lax.rem(me, 8)
    copies = []
    for at, (dx, dk) in enumerate(((1, 0), (3, 0), (0, 1))):
        copy = remote(
            src, out.at[place], send.at[at], recv.at[at], shifted(me, 0, 0, dx, dk), wsh
        )
        copy.start()
        copies.append(copy)
    return copies


def row_gather_onward(out, me, wsh, copies, send, recv):
    partner = shifted(me, 0, 0, 0, 1)
    half = out.shape[1] // 2
    onward = []
    forwards = []
    for at, dx in enumerate((1, 3)):
        copies[at].wait_recv()
        from_place = lax.rem(shifted(me, 0, 0, 4 - dx, 0), 8)
        part = out.at[from_place, pl.ds(at * half, half)]
        step = remote(part, part, send.at[3 + at], recv.at[3 + at], shifted(me, 0, 0, dx, 0), wsh)
        step.start()
        onward.append(step)
        block = out.at[from_place]
        forward = remote(block, block, send.at[5 + at], recv.at[5 + at], partner, wsh)
        forward.start()
        forwards.append(forward)
    return onward, forwards


def row_gather_end(out, me, wsh, copies, onward, forwards, send, recv):
    partner = shifted(me, 0, 0, 0, 1)
    half = out.shape[1] // 2
    far = lax.rem(shifted(me, 0, 0, 2, 0), 8)
    for at in (0, 1):
        onward[at].wait_recv()
        part = out.at[far, pl.ds(at * half, half)]
        forward = remote(part, part, send.at[7 + at], recv.at[7 + at], partner, wsh)
        forward.start()
        forwards.append(forward)
    copies[2].wait_recv()
    for copy in copies + onward:
        copy.wait_send()
    for forward in forwards:
        forward.wait()


def cast_steps(steps, staging, lows, in_sems, out_sems):
    loads, stores = [], []
    for index, (src, begin, dst, to, count, at) in enumerate(steps):
        slot, span = index % 2, pl.ds(0, count)
        loads.append(
            pltpu.make_async_copy(
                src.at[pl.ds(begin, count)], staging[at].at[slot, span], in_sems.at[slot]
            )
        )
        stores.append(
            pltpu.make_async_copy(lows[at].at[slot, span], dst.at[pl.ds(to, count)], out_sems.at[slot])
        )
    loads[0].start()
    loads[1].start()
    for index, step in enumerate(steps):
        slot, count, at = index % 2, step[-2], step[-1]
        loads[index].wait()
        if index >= 2:
            stores[index - 2].wait()
        lows[at][slot, :count] = staging[at][slot, :count].astype(BF)
        stores[index].start()
        if index + 2 < len(steps):
            loads[index + 2].start()
    stores[-2].wait()
    stores[-1].wait()


def cut_steps(src, parts, rows, at):
    steps, begin = [], 0
    for part in parts:
        for to in range(0, part.shape[0], rows):
            count = min(rows, part.shape[0] - to)
            steps.append((src, begin + to, part, to, count, at))
        begin += part.shape[0]
    return steps


COLUMN_STEPS = ((1, 0), (3, 0), (0, 1), (2, 0), (1, 1), (3, 1), (2, 1))
ROW_STEPS = ((1, 0), (3, 0), (1, 1), (3, 1), (0, 1), (2, 0), (2, 1))


UP_CUT = (1280, 768)
DOWN_GRAD_CUT = (240, 144)


def gather_first(weights, gains, tokens, routes, cotangent, expert_weights):
    def body(q_in, k_in, v_in, ga_in, gf_in, t_in, r_in, c_in, *refs):
        sources, refs = refs[:3], refs[3:]
        w_out, t_out, s_out, r_out, c_out = refs[:5]
        gate_out, up_out, up_rest, down_out, side_out = refs[5:10]
        refs = refs[10:]
        wide, row_s, row_r, pair, local, col_s, col_r, tall_f, flat_f, tall_b, flat_b, in_sems, out_sems = refs[:13]
        w_in, s_in = refs[13:]
        me, wsh = lax.axis_index("ctx"), lax.axis_index("wsh")
        core = lax.rem(me, 2)
        place = lax.rem(me, 8)
        group = lax.div(me, 8)
        partner = shifted(me, 0, 0, 0, 1)
        row_peers = [shifted(me, 0, 0, dx, dk) for dx, dk in ROW_STEPS]
        col_peers = [shifted(me, dz, dy, 0, 0) for dz, dy in COLUMN_STEPS]
        barrier, amount = greet([(peer, wsh) for peer in row_peers + col_peers])
        heads = q_in.shape[1] // 8
        for at in range(8):
            w_in[at, :, :heads] = q_in[:, at * heads : (at + 1) * heads].astype(BF)
            side = (k_in, v_in)[at % 2]
            begin = at // 4 * HEAD_WIDTH
            w_in[at, :, heads:] = side[:, begin : begin + HEAD_WIDTH].astype(BF)
        s_in[...] = jnp.zeros_like(s_in)
        s_in[0:1, : ga_in.shape[1]] = ga_in[...]
        s_in[1:2, : gf_in.shape[1]] = gf_in[...]
        locals_ = [
            pltpu.make_async_copy(w_in.at[place], w_out.at[me], local.at[0]),
            pltpu.make_async_copy(s_in, s_out.at[me], local.at[1]),
            pltpu.make_async_copy(t_in, t_out.at[place], local.at[2]),
            pltpu.make_async_copy(r_in, r_out.at[core], local.at[3]),
            pltpu.make_async_copy(c_in, c_out.at[core], local.at[4]),
        ]
        for copy in locals_:
            copy.start()
        pl.semaphore_wait(barrier, amount)
        for peer in row_peers:
            remote(w_in.at[lax.rem(peer, 8)], w_out.at[me], wide.at[0], wide.at[1], peer, wsh).start()
            remote(s_in, s_out.at[me], wide.at[2], wide.at[3], peer, wsh).start()
        row_copies = row_gather_start(t_in, t_out, me, wsh, row_s, row_r)
        pair_copies = [
            remote(r_in, r_out.at[core], pair.at[0], pair.at[1], partner, wsh),
            remote(c_in, c_out.at[core], pair.at[2], pair.at[3], partner, wsh),
        ]
        for copy in pair_copies:
            copy.start()
        locals_[0].wait()
        locals_[1].wait()
        for at, out in ((0, w_out), (2, s_out)):
            rest = out.at[pl.ds(0, 7)]
            done = remote(rest, rest, wide.at[at], wide.at[at + 1], partner, wsh)
            done.wait_recv()
            done.wait_send()
        lanes = side_out.shape[2]
        depth, columns = w_out.shape[1], w_out.shape[2]

        def share(origin, at):
            blocks = pl.ds(origin * 8, 8)
            part = w_out.at[blocks, pl.ds(0, depth), pl.ds(columns - lanes, lanes)]
            give = remote(part, side_out.at[blocks], col_s.at[2, at], col_r.at[2, at], partner, wsh)
            give.start()
            return give

        mine = pl.ds(group * 8, 8)
        col_copies = []
        for at, peer in enumerate(col_peers):
            for kind, out in enumerate((w_out, s_out)):
                copy = remote(out.at[mine], out.at[mine], col_s.at[kind, at], col_r.at[kind, at], peer, wsh)
                copy.start()
                col_copies.append(copy)
        shares = [share(group, 7)]
        onward, forwards = row_gather_onward(t_out, me, wsh, row_copies, row_s, row_r)
        gate_in, up_in, down_in = [source.at[1 - wsh] for source in sources]
        buffers = ((tall_f, flat_f), (tall_b, flat_b), in_sems, out_sems)
        tall_rows, flat_rows = tall_f.shape[1], flat_f.shape[1]
        cast_steps(
            cut_steps(gate_in, (gate_out,), tall_rows, 0) + cut_steps(up_in, (up_out, up_rest), tall_rows, 0) + cut_steps(down_in, (down_out,), flat_rows, 1),
            *buffers,
        )
        row_gather_end(t_out, me, wsh, row_copies, onward, forwards, row_s, row_r)
        for at, (dz, dy) in enumerate(COLUMN_STEPS):
            col_copies[2 * at].wait_recv()
            col_copies[2 * at + 1].wait_recv()
            shares.append(share(lax.div(shifted(me, 4 - dz, 2 - dy, 0, 0), 8), at))
        for copy in pair_copies + shares:
            copy.wait()
        for copy in locals_[2:]:
            copy.wait()
        for copy in col_copies:
            copy.wait_send()

    sds = jax.ShapeDtypeStruct
    _, deep, half = expert_weights[0].shape
    depth, packed = weights[0].shape[0], weights[0].shape[1] // 8 + HEAD_WIDTH
    tall, flat = (deep // 4, half), (half // 4, deep)
    return pl.pallas_call(
        body,
        out_shape=(
            sds((64, depth, packed), BF),
            sds((8,) + tokens.shape, tokens.dtype),
            sds((64, 8, 128), F32),
            sds((2,) + routes.shape, routes.dtype),
            sds((2,) + cotangent.shape, cotangent.dtype),
        )
        + tuple(sds((count, half), BF) for count in (deep, *UP_CUT))
        + (sds((half, deep), BF), sds((64, depth, 128), BF)),
        in_specs=[VMEM] * 5 + [ANY] * 6,
        out_specs=[ANY] * 10,
        scratch_shapes=[
            DMA((4,)),
            DMA((9,)),
            DMA((9,)),
            DMA((4,)),
            DMA((5,)),
            DMA((3, 8)),
            DMA((3, 8)),
            pltpu.VMEM((2,) + tall, F32),
            pltpu.VMEM((2,) + flat, F32),
            pltpu.VMEM((2,) + tall, BF),
            pltpu.VMEM((2,) + flat, BF),
            DMA((2,)),
            DMA((2,)),
            pltpu.VMEM((8, depth, packed), BF),
            pltpu.VMEM((8, 128), F32),
        ],
        compiler_params=call_params(0),
        name="gather_first",
        cost_estimate=cost(40),
    )(*weights, *gains, tokens, routes, cotangent, *expert_weights)


def gather_row(block, swapped, collective_id):
    def body(src, src2, out, out2, row_s, row_r, pair, local):
        me, wsh = lax.axis_index("ctx"), lax.axis_index("wsh")
        barrier, amount = greet(
            [(shifted(me, 0, 0, dx, dk), wsh) for dx, dk in ((1, 0), (3, 0), (0, 1))] + [(me, 1 - wsh)]
        )
        mine = pltpu.make_async_copy(src, out.at[lax.rem(me, 8)], local)
        mine.start()
        pl.semaphore_wait(barrier, amount)
        copies = row_gather_start(src, out, me, wsh, row_s, row_r)
        cross = remote(src2, out2, pair.at[0], pair.at[1], me, 1 - wsh)
        cross.start()
        onward, forwards = row_gather_onward(out, me, wsh, copies, row_s, row_r)
        row_gather_end(out, me, wsh, copies, onward, forwards, row_s, row_r)
        mine.wait()
        cross.wait()

    return pl.pallas_call(
        body,
        out_shape=(
            jax.ShapeDtypeStruct((8,) + block.shape, block.dtype),
            jax.ShapeDtypeStruct(swapped.shape, swapped.dtype),
        ),
        in_specs=[ANY, ANY],
        out_specs=[ANY, ANY],
        scratch_shapes=[DMA((9,)), DMA((9,)), DMA((2,)), DMA],
        compiler_params=call_params(collective_id),
        name="gather_row",
        cost_estimate=cost(26),
    )(block, swapped)


def gather_keys(rows, collective_id):
    count = rows.shape[0]
    half = count // 2

    def body(src, out, send, recv, local):
        me, wsh = lax.axis_index("ctx"), lax.axis_index("wsh")
        core = lax.rem(me, 2)
        group = lax.div(me, 8)
        partner = shifted(me, 0, 0, 0, 1)
        across = shifted(me, 0, 1, 0, 0)
        steps = (1, 3, 2)
        peers = [shifted(me, dz, 0, 0, 0) for dz in steps]
        barrier, amount = greet([(peer, wsh) for peer in peers + [across, partner]])
        mine = pltpu.make_async_copy(src, out.at[group], local)
        mine.start()
        pl.semaphore_wait(barrier, amount)
        my_half = pl.ds(pl.multiple_of(core * half, half), half)
        copies = []
        for at, peer in enumerate([across] + peers):
            copy = remote(src.at[my_half], out.at[group, my_half], send.at[at], recv.at[at], peer, wsh)
            copy.start()
            copies.append(copy)
        forwards = []

        def hand_on(origin, at):
            part = out.at[origin, my_half]
            forward = remote(part, part, send.at[7 + at], recv.at[7 + at], partner, wsh)
            forward.start()
            forwards.append(forward)

        copies[0].wait_recv()
        beside = lax.div(across, 8)
        for at, peer in enumerate(peers):
            part = out.at[beside, my_half]
            copy = remote(part, part, send.at[4 + at], recv.at[4 + at], peer, wsh)
            copy.start()
            copies.append(copy)
        hand_on(beside, 0)
        for dy in range(2):
            for at, dz in enumerate(steps):
                copies[1 + 3 * dy + at].wait_recv()
                hand_on(lax.div(shifted(me, 4 - dz, dy, 0, 0), 8), 1 + 3 * dy + at)
        for copy in copies:
            copy.wait_send()
        for forward in forwards:
            forward.wait()
        mine.wait()

    return pl.pallas_call(
        body,
        out_shape=jax.ShapeDtypeStruct((8,) + rows.shape, rows.dtype),
        in_specs=[ANY],
        out_specs=ANY,
        scratch_shapes=[DMA((14,)), DMA((14,)), DMA],
        compiler_params=call_params(collective_id),
        name="gather_keys",
        cost_estimate=cost(30),
    )(rows)


class Owned:
    SCRATCH = 10

    def __init__(self, src, out, scratch):
        self.src, self.out = src, out
        self.land_z, self.sum_z, self.land_y, self.reduced, *self.sems = scratch

    @staticmethod
    def scratch(value):
        inner = value.shape[1:]
        return [
            pltpu.VMEM((3, 16) + inner, BF),
            pltpu.VMEM((16,) + inner, BF),
            pltpu.VMEM((8,) + inner, BF),
            pltpu.VMEM((8,) + inner, BF),
            DMA((3,)),
            DMA((3,)),
            DMA((1,)),
            DMA((1,)),
            DMA((7,)),
            DMA((7,)),
        ]

    def along_z(self, me, wsh):
        z, _, _, _ = coords(me)
        self.copies_z = []
        for at, dz in enumerate((1, 3, 2)):
            blocks = pl.ds(lax.rem(z + dz, 4) * 16, 16)
            copy = remote(
                self.src.at[blocks],
                self.land_z.at[at],
                self.sems[0].at[at],
                self.sems[1].at[at],
                shifted(me, dz, 0, 0, 0),
                wsh,
            )
            copy.start()
            self.copies_z.append(copy)

    def along_y(self, me, wsh):
        z, y, _, _ = coords(me)
        value = self.src[pl.ds(z * 16, 16)].astype(F32)
        for at, copy in enumerate(self.copies_z):
            copy.wait_recv()
            value = value + self.land_z[at].astype(F32)
        self.sum_z[...] = value.astype(BF)
        self.copy_y = remote(
            self.sum_z.at[pl.ds((1 - y) * 8, 8)],
            self.land_y,
            self.sems[2].at[0],
            self.sems[3].at[0],
            shifted(me, 0, 1, 0, 0),
            wsh,
        )
        self.copy_y.start()

    def along_row(self, me, wsh):
        _, y, _, _ = coords(me)
        self.copy_y.wait_recv()
        value = self.sum_z[pl.ds(y * 8, 8)].astype(F32) + self.land_y[...].astype(F32)
        self.reduced[...] = value.astype(BF)
        place = lax.rem(me, 8)
        self.copies_row = []
        for at, (dx, dk) in enumerate(ROW_STEPS):
            peer = shifted(me, 0, 0, dx, dk)
            copy = remote(
                self.reduced.at[lax.rem(peer, 8)],
                self.out.at[place],
                self.sems[4].at[at],
                self.sems[5].at[at],
                peer,
                wsh,
            )
            copy.start()
            self.copies_row.append(copy)
        self.out[place] = self.reduced[place]

    def finish(self):
        for copy in self.copies_row:
            copy.wait()
        for copy in self.copies_z + [self.copy_y]:
            copy.wait_send()


def reduce_row(parts, collective_id, both, extra=None, swapped_whole=None, owned=()):
    has_whole = swapped_whole is not None
    is_product = isinstance(parts, tuple)
    if is_product:
        rows, width = parts[0].shape[0] // 8, parts[1].shape[0]
    else:
        _, rows, width = parts.shape
    block = (rows, width)
    pieces = 4
    columns = width // pieces
    has_extra = extra is not None

    def body(*refs):
        refs = list(refs)
        if is_product:
            heads_ref, out_w = refs.pop(0), refs.pop(0)
            src = refs.pop(-1)
        else:
            src = refs.pop(0)
        if has_extra:
            pick_ref, back_ref = refs.pop(0), refs.pop(0)
        src3 = refs.pop(0) if has_whole else None
        mine_in = [refs.pop(0) for _ in owned]
        out = refs.pop(0)
        out2 = refs.pop(0) if has_extra else None
        out3 = refs.pop(0) if has_whole else None
        mine_out = [refs.pop(0) for _ in owned]
        blocks = []
        for src4, out4 in reversed(list(zip(mine_in, mine_out))):
            blocks.append(Owned(src4, out4, refs[-Owned.SCRATCH :]))
            refs = refs[: -Owned.SCRATCH]
        arrived, summed, landed, swapped, total, send, recv, local = refs[:8]
        me, wsh = lax.axis_index("ctx"), lax.axis_index("wsh")
        other = 1 - wsh
        core = lax.rem(me, 2)
        _, _, x, _ = coords(me)
        partner = shifted(me, 0, 0, 0, 1)
        peers = [shifted(me, 0, 0, dx, 0) for dx in (1, 2, 3)]
        row_peers = [shifted(me, 0, 0, dx, dk) for dx, dk in ROW_STEPS]
        col_peers = [shifted(me, dz, dy, 0, 0) for dz, dy in COLUMN_STEPS]
        greeted = row_peers + col_peers if owned else peers + [partner]
        barrier, amount = greet([(peer, wsh) for peer in greeted] + [(me, other)])
        pl.semaphore_wait(barrier, amount)
        if has_whole:
            whole = remote(
                src3, out3, send.at[1, 9], recv.at[1, 9], me, other
            )
            whole.start()
        spans = [pl.ds(piece * columns, columns) for piece in range(pieces)]
        everything = pl.ds(0, rows)
        first = []
        for piece, span in enumerate(spans):
            if is_product:
                columns_of = slice(piece * columns, (piece + 1) * columns)
                src[:, :, columns_of] = (
                    times_transposed(heads_ref[...], out_w[columns_of, : heads_ref.shape[1]])
                    .astype(BF)
                    .reshape(8, rows, columns)
                )
            for at, dx in enumerate((2, 1, 3, 0)):
                chip = lax.rem(x + dx, 4)
                copy = remote(
                    src.at[chip * 2 + 1 - core, everything, span],
                    arrived.at[at, everything, span],
                    send.at[piece, at],
                    recv.at[piece, at],
                    partner,
                    wsh,
                )
                copy.start()
                first.append(copy)
        for block4 in blocks:
            block4.along_z(me, wsh)
        if has_extra:
            arrived2, swapped2, src2 = refs[8:]
            src2[...] = matmul(pick_ref[...], back_ref[...]).astype(BF).reshape(src2.shape)
            give2 = remote(src2.at[1 - core], arrived2, send.at[0, 8], recv.at[0, 8], partner, wsh)
            give2.start()
        second = []
        for piece, span in enumerate(spans):
            for at, dx in enumerate((2, 1, 3)):
                chip = lax.rem(x + dx, 4)
                first[piece * 4 + at].wait_recv()
                summed[at, :, span] = (
                    src[chip * 2 + core, :, span].astype(F32) + arrived[at, :, span].astype(F32)
                ).astype(BF)
                copy = remote(
                    summed.at[at, everything, span],
                    landed.at[at, everything, span],
                    send.at[piece, 4 + at],
                    recv.at[piece, 4 + at],
                    shifted(me, 0, 0, dx, 0),
                    wsh,
                )
                copy.start()
                second.append(copy)
            first[piece * 4 + 3].wait_recv()
            total[:, span] = src[x * 2 + core, :, span].astype(F32) + arrived[3, :, span].astype(F32)
        if has_extra:
            give2.wait()
            swapped2[0] = (src2[core].astype(F32) + arrived2[...].astype(F32)).astype(BF)
            swap2 = remote(swapped2.at[0], swapped2.at[1], send.at[1, 8], recv.at[1, 8], me, other)
            swap2.start()
        swaps = []
        for piece, span in enumerate(spans):
            for at in (1, 2, 0):
                second[piece * 3 + at].wait_recv()
            swapped[0, :, span] = (
                total[:, span]
                + landed[0, :, span].astype(F32)
                + landed[1, :, span].astype(F32)
                + landed[2, :, span].astype(F32)
            ).astype(BF)
            swap = remote(
                swapped.at[0, everything, span],
                swapped.at[1, everything, span],
                send.at[piece, 7],
                recv.at[piece, 7],
                me,
                other,
            )
            swap.start()
            swaps.append(swap)
            if piece == pieces - 2:
                for block4 in blocks:
                    block4.along_y(me, wsh)
        for block4 in blocks:
            block4.along_row(me, wsh)
        if has_extra:
            swap2.wait()
            out2[...] = swapped2[0].astype(F32) + swapped2[1].astype(F32)
        for piece, span in enumerate(spans):
            swaps[piece].wait()
            if both:
                total[:, span] = swapped[0, :, span].astype(F32) + swapped[1, :, span].astype(F32)
            else:
                out[:, span] = swapped[0, :, span].astype(F32) + swapped[1, :, span].astype(F32)
        if both:
            keep = pltpu.make_async_copy(total, out.at[core], local)
            keep.start()
            give = remote(total, out.at[core], send.at[0, 9], recv.at[0, 9], partner, wsh)
            give.start()
            give.wait()
            keep.wait()
        for copy in first + second:
            copy.wait_send()
        for block4 in blocks:
            block4.finish()
        if has_whole:
            whole.wait()

    shapes = [jax.ShapeDtypeStruct((2,) + block if both else block, F32)]
    scratch = [
        pltpu.VMEM((4,) + block, BF),
        pltpu.VMEM((3,) + block, BF),
        pltpu.VMEM((3,) + block, BF),
        pltpu.VMEM((2,) + block, BF),
        pltpu.VMEM(block, F32),
        DMA((pieces, 10)),
        DMA((pieces, 10)),
        DMA,
    ]
    operands = list(parts) if is_product else [parts]
    out_spaces = [VMEM]
    if has_extra:
        shapes.append(jax.ShapeDtypeStruct(block, F32))
        scratch += [pltpu.VMEM(block, BF), pltpu.VMEM((2,) + block, BF), pltpu.VMEM((2,) + block, BF)]
        operands += list(extra)
        out_spaces.append(VMEM)
    spaces = [VMEM] * len(operands)
    if has_whole:
        shapes.append(jax.ShapeDtypeStruct(swapped_whole.shape, swapped_whole.dtype))
        operands.append(swapped_whole)
        spaces.append(ANY)
        out_spaces.append(ANY)
    for value in owned:
        block8 = (8,) + value.shape[1:]
        shapes.append(jax.ShapeDtypeStruct(block8, BF))
        operands.append(value)
        spaces.append(VMEM)
        out_spaces.append(VMEM)
        scratch += Owned.scratch(value)
    if is_product:
        scratch.append(pltpu.VMEM((8,) + block, BF))
    return pl.pallas_call(
        body,
        out_shape=shapes,
        in_specs=spaces,
        out_specs=out_spaces,
        scratch_shapes=scratch,
        compiler_params=call_params(collective_id),
        name="reduce_row",
        cost_estimate=cost(1),
    )(*operands)


def reduce_chip(pick, back, of_expert, width, collective_id):
    rows = pick.shape[0] // 2
    lanes = of_expert.shape[1]

    def body(pick_ref, back_ref, of_ref, out, out2, src, src2, arrived, swapped, arrived2, swapped2, send, recv):
        me, wsh = lax.axis_index("ctx"), lax.axis_index("wsh")
        other = 1 - wsh
        core = lax.rem(me, 2)
        partner = shifted(me, 0, 0, 0, 1)
        barrier, amount = greet([(partner, wsh), (me, other)])
        src[...] = matmul(pick_ref[...], back_ref[:, :width]).astype(BF).reshape(src.shape)
        parts = [back_ref[:, at : at + 1] * of_ref[...] for at in (width, width + 64)]
        src2[...] = (matmul(pick_ref[...], parts[0]) + matmul(pick_ref[...], parts[1])).reshape(src2.shape)
        pl.semaphore_wait(barrier, amount)
        give = remote(src.at[1 - core], arrived, send.at[0], recv.at[0], partner, wsh)
        give.start()
        give2 = remote(src2.at[1 - core], arrived2, send.at[2], recv.at[2], partner, wsh)
        give2.start()
        give.wait()
        swapped[0] = (src[core].astype(F32) + arrived[...].astype(F32)).astype(BF)
        swap = remote(swapped.at[0], swapped.at[1], send.at[1], recv.at[1], me, other)
        swap.start()
        give2.wait()
        swapped2[0] = src2[core] + arrived2[...]
        swap2 = remote(swapped2.at[0], swapped2.at[1], send.at[3], recv.at[3], me, other)
        swap2.start()
        swap2.wait()
        out2[...] = swapped2[0] + swapped2[1]
        swap.wait()
        out[...] = swapped[0].astype(F32) + swapped[1].astype(F32)

    sds = jax.ShapeDtypeStruct
    block, block2 = (rows, width), (rows, lanes)
    return pl.pallas_call(
        body,
        out_shape=(sds(block, F32), sds(block2, F32)),
        in_specs=[VMEM] * 3,
        out_specs=[VMEM] * 2,
        scratch_shapes=[
            pltpu.VMEM((2,) + block, BF),
            pltpu.VMEM((2,) + block2, F32),
            pltpu.VMEM(block, BF),
            pltpu.VMEM((2,) + block, BF),
            pltpu.VMEM(block2, F32),
            pltpu.VMEM((2,) + block2, F32),
            DMA((4,)),
            DMA((4,)),
        ],
        compiler_params=call_params(collective_id),
        name="reduce_chip",
        cost_estimate=cost(17),
    )(pick, back, of_expert)


def reduce_keys(parts, owned, swapped, collective_id):
    _, groups, _, rows, width = parts.shape

    def body(src, src4, src5, out, out4, out5, arrived, mid, beside, summed, landed, send, recv, pair, *scratch4):
        block4 = Owned(src4, out4, scratch4)
        me, wsh = lax.axis_index("ctx"), lax.axis_index("wsh")
        core = lax.rem(me, 2)
        _, _, x, _ = coords(me)
        side = lax.rem(x, 2)
        partner = shifted(me, 0, 0, 0, 1)
        neighbour = me + 2 - 4 * side
        steps = COLUMN_STEPS + ((0, 0),)
        peers = [shifted(me, dz, dy, 0, 0) for dz, dy in steps]
        row_peers = [shifted(me, 0, 0, dx, dk) for dx, dk in ROW_STEPS]
        barrier, amount = greet([(peer, wsh) for peer in peers[:-1] + row_peers] + [(me, 1 - wsh)])
        pl.semaphore_wait(barrier, amount)
        first = []
        for at, peer in enumerate(peers):
            group = lax.div(peer, 8)
            for turn, b in enumerate((1 - side, side)):
                copy = remote(
                    src.at[1 - core, group, b],
                    arrived.at[turn, at],
                    send.at[turn, at],
                    recv.at[turn, at],
                    partner,
                    wsh,
                )
                copy.start()
                first.append(copy)
        block4.along_z(me, wsh)
        cross = remote(src5, out5, pair.at[0], pair.at[1], me, 1 - wsh)
        cross.start()
        across = []
        for at, peer in enumerate(peers):
            group = lax.div(peer, 8)
            first[2 * at].wait_recv()
            mid[at] = (src[core, group, 1 - side].astype(F32) + arrived[0, at].astype(F32)).astype(BF)
            copy = remote(mid.at[at], beside.at[at], send.at[2, at], recv.at[2, at], neighbour, wsh)
            copy.start()
            across.append(copy)
        last = []
        for at, peer in enumerate(peers):
            group = lax.div(peer, 8)
            first[2 * at + 1].wait_recv()
            across[at].wait_recv()
            value = (
                src[core, group, side].astype(F32)
                + arrived[1, at].astype(F32)
                + beside[at].astype(F32)
            )
            if at == groups - 1:
                out[...] = value
            else:
                summed[at] = value.astype(BF)
                copy = remote(summed.at[at], landed.at[at], send.at[3, at], recv.at[3, at], peer, wsh)
                copy.start()
                last.append(copy)
            if at == 5:
                block4.along_y(me, wsh)
        block4.along_row(me, wsh)
        for at, copy in enumerate(last):
            copy.wait_recv()
            out[...] += landed[at].astype(F32)
        for copy in first + across + last:
            copy.wait_send()
        block4.finish()
        cross.wait()

    block = (rows, width)
    return pl.pallas_call(
        body,
        out_shape=(
            jax.ShapeDtypeStruct(block, F32),
            jax.ShapeDtypeStruct((8,) + owned.shape[1:], BF),
            jax.ShapeDtypeStruct(swapped.shape, swapped.dtype),
        ),
        in_specs=[VMEM, VMEM, ANY],
        out_specs=[VMEM, VMEM, ANY],
        scratch_shapes=[
            pltpu.VMEM((2, groups) + block, BF),
            pltpu.VMEM((groups,) + block, BF),
            pltpu.VMEM((groups,) + block, BF),
            pltpu.VMEM((groups,) + block, BF),
            pltpu.VMEM((groups,) + block, BF),
            DMA((4, groups)),
            DMA((4, groups)),
            DMA((2,)),
        ]
        + Owned.scratch(owned),
        compiler_params=call_params(collective_id),
        name="reduce_keys",
        cost_estimate=cost(40),
    )(parts, owned, swapped)


def exchange(arrays, collective_id):
    amount = len(arrays)

    def body(*refs):
        ins, outs = refs[:amount], refs[amount : 2 * amount]
        send, recv, local = refs[2 * amount :]
        me, wsh = lax.axis_index("ctx"), lax.axis_index("wsh")
        chip = lax.div(me, 2)

        def target(step):
            dy = lax.rem(lax.div(step, 4), 2)
            return shifted(me, lax.div(step, 8), dy, lax.rem(step, 4), 0), lax.rem(wsh + dy, 2)

        barrier, count = greet_many(32, target)
        locals_ = []
        for at in range(amount):
            copy = pltpu.make_async_copy(ins[at].at[chip], outs[at].at[chip], local.at[at])
            copy.start()
            locals_.append(copy)
        pl.semaphore_wait(barrier, count)

        def one(step, carried):
            ctx, side = target(lax.rem(step * 27, 32))
            for at in range(amount):
                remote(
                    ins[at].at[lax.div(ctx, 2)], outs[at].at[chip], send.at[at], recv.at[at], ctx, side
                ).start()
            return carried

        lax.fori_loop(1, 32, one, 0)
        for copy in locals_:
            copy.wait()
        for at in range(amount):
            rest = outs[at].at[pl.ds(0, 31)]
            done = remote(rest, rest, send.at[at], recv.at[at], me, wsh)
            done.wait_send()
            done.wait_recv()

    return pl.pallas_call(
        body,
        out_shape=[jax.ShapeDtypeStruct(a.shape, a.dtype) for a in arrays],
        in_specs=[ANY] * amount,
        out_specs=[ANY] * amount,
        scratch_shapes=[DMA((amount,)), DMA((amount,)), DMA((amount,))],
        compiler_params=call_params(collective_id),
        name="exchange",
        cost_estimate=cost(48),
    )(*arrays)


def exchange_behind(value):
    groups = []
    for core in range(2):
        for parity in range(2):
            groups.append(
                [(chip * 2 + core) * 2 + (parity + chip // 4) % 2 for chip in range(32)]
            )
    return lax.all_to_all(
        value, ("ctx", "wsh"), split_axis=0, concat_axis=0, tiled=True, axis_index_groups=groups
    )


def natural_order(plan, kv_ref, keys, values, transposed):
    def one(block, carried):
        rows = kv_ref[pl.ds(pl.multiple_of(plan[PLAN_INVERSE + block] * BLK, BLK), BLK), :]
        at = pl.ds(pl.multiple_of(block * BLK, BLK), BLK)
        keys[at, :] = rows[:, :HEAD_WIDTH]
        values[at, :] = rows[:, HEAD_WIDTH:]
        return carried

    lax.fori_loop(0, kv_ref.shape[0] // BLK, one, 0, unroll=8)
    source, turned = transposed

    def turn(chunk, carried):
        at = pl.ds(pl.multiple_of(chunk * CHUNK, CHUNK), CHUNK)
        turned[:, at] = source[at, :].T
        return carried

    lax.fori_loop(0, kv_ref.shape[0] // CHUNK, turn, 0, unroll=4)


def stacked(ref, first, second):
    rows = [ref[pl.ds(pl.multiple_of(at * BLK, BLK), BLK), :] for at in (first, second)]
    return jnp.concatenate(
        [rows[0][:, :HEAD_WIDTH], rows[0][:, HEAD_WIDTH:], rows[1][:, :HEAD_WIDTH], rows[1][:, HEAD_WIDTH:]],
        axis=0,
    )


def unstacked(ref, first, second, value):
    for at, begin in ((first, 0), (second, 2 * BLK)):
        ref[pl.ds(pl.multiple_of(at * BLK, BLK), BLK), :] = jnp.concatenate(
            [value[begin : begin + BLK], value[begin + BLK : begin + 2 * BLK]], axis=1
        )


PLAN_BOUNDS, PLAN_INVERSE, PLAN_BLOCKS, PLAN_SIZE = 16, 64, 192, 256


def start_of(lengths, position):
    begin = lengths[0] * 0
    start = position * 0
    for at in range(lengths.shape[0]):
        start = jnp.where(begin <= position, begin, start)
        begin = begin + lengths[at]
    return start


def make_plan(block_order, lengths, base, plan):
    def place(at, carried):
        plan[PLAN_INVERSE + block_order[at]] = at
        return carried

    lax.fori_loop(0, block_order.shape[0], place, 0, unroll=8)

    def rank(at, carried):
        mine = block_order[base + at]
        before = jnp.int32(0)
        for other in range(16):
            before = before + jnp.where(block_order[base + other] < mine, 1, 0)
        plan[before] = at
        plan[PLAN_BLOCKS + before] = mine
        return carried

    lax.fori_loop(0, 16, rank, 0)

    def bound(step, carried):
        one, two = plan[PLAN_BLOCKS + 2 * step], plan[PLAN_BLOCKS + 2 * step + 1]
        low = lax.div(start_of(lengths, one * BLK), CHUNK)
        high = lax.div(two * BLK, CHUNK) + 1
        last = start_of(lengths, two * BLK + BLK - 1)
        inner_low = jnp.minimum(jnp.maximum(lax.div(last + CHUNK - 1, CHUNK), low), high)
        inner_high = jnp.minimum(jnp.maximum(lax.div(one * BLK + 1, CHUNK), inner_low), high)
        for at, value in enumerate((low, inner_low, inner_high, high)):
            plan[PLAN_BOUNDS + 4 * step + at] = value
        return carried

    lax.fori_loop(0, 8, bound, 0)


def strips_of(plan, lengths, step):
    lane = lax.broadcasted_iota(jnp.int32, (1, 4 * BLK), 1)
    block = jnp.where(lane < 2 * BLK, plan[PLAN_BLOCKS + 2 * step], plan[PLAN_BLOCKS + 2 * step + 1])
    position = block * BLK + lax.rem(lane, BLK)
    return position, start_of(lengths, position)


def three_loops(step, plan, chunk, state):
    low, inner_low, inner_high, high = [plan[PLAN_BOUNDS + 4 * step + at] for at in range(4)]
    state = lax.fori_loop(low, inner_low, functools.partial(chunk, True), state)
    state = lax.fori_loop(inner_low, inner_high, functools.partial(chunk, False), state)
    return lax.fori_loop(inner_high, high, functools.partial(chunk, True), state)


def kept(scores, at, q_pos, q_start):
    k_pos = at + lax.broadcasted_iota(jnp.int32, scores.shape, 0)
    return jnp.where((k_pos <= q_pos) & (k_pos >= q_start), scores, MASKED)


SCORE_SCALE = 1.0 / math.sqrt(HEAD_WIDTH)
TWO_SCALE = SCORE_SCALE / math.log(2.0)


def forward_kernel(block_order, lengths, group, q_ref, kv_ref, out_ref, lse_ref, plan, keys, values, values_t, acc):
    step = pl.program_id(0)

    @pl.when(step == 0)
    def _():
        make_plan(block_order, lengths, group[0] * 16, plan)
        natural_order(plan, kv_ref, keys, values, (values, values_t))

    first, second = plan[2 * step], plan[2 * step + 1]
    q_t = stacked(q_ref, first, second).astype(F32).T.astype(BF)
    q_pos, q_start = strips_of(plan, lengths, step)
    width = 4 * BLK
    acc[...] = jnp.zeros_like(acc)

    def chunk(masked, index, total):
        at = pl.multiple_of(index * CHUNK, CHUNK)
        scores = matmul(keys[pl.ds(at, CHUNK), :], q_t)
        if masked:
            scores = kept(scores, at, q_pos, q_start)
        probs = jnp.exp2(scores * TWO_SCALE)
        acc[...] += matmul(values_t[:, pl.ds(at, CHUNK)], probs.astype(BF))
        return total + jnp.sum(probs, axis=0, keepdims=True)

    total = three_loops(step, plan, chunk, jnp.zeros((1, width), F32))
    lse_ref[0] = jnp.log2(total)
    unstacked(out_ref, first, second, (acc[...] / total).T.astype(BF))


def attend(block_order, lengths, group, queries, kv):
    rows = queries.shape[0]
    steps = rows // (2 * BLK)
    everything = pl.BlockSpec(queries.shape, lambda i, *_: (0, 0))
    strip = pl.BlockSpec((1, 1, 4 * BLK), lambda i, *_: (i, 0, 0))
    sds = jax.ShapeDtypeStruct
    return pl.pallas_call(
        forward_kernel,
        out_shape=(
            sds(queries.shape, BF),
            sds((steps, 1, 4 * BLK), F32),
            sds((PLAN_SIZE,), jnp.int32),
        ),
        grid_spec=pltpu.PrefetchScalarGridSpec(
            num_scalar_prefetch=3,
            grid=(steps,),
            in_specs=[everything, pl.BlockSpec(kv.shape, lambda i, *_: (0, 0))],
            out_specs=[everything, strip, pl.BlockSpec(memory_space=pltpu.SMEM)],
            scratch_shapes=[
                pltpu.VMEM((kv.shape[0], HEAD_WIDTH), BF),
                pltpu.VMEM((kv.shape[0], HEAD_WIDTH), BF),
                pltpu.VMEM((HEAD_WIDTH, kv.shape[0]), BF),
                pltpu.VMEM((HEAD_WIDTH, 4 * BLK), F32),
            ],
        ),
        compiler_params=pltpu.CompilerParams(vmem_limit_bytes=ROOM),
        name="attend",
        cost_estimate=cost(17),
    )(block_order, lengths, group, queries, kv)


def backward_kernel(plan, lengths, q_ref, heads_ref, da_ref, wo_ref, kv_ref, lse_ref, part_ref, dq_ref, dkv_ref, early_ref, keys, values, keys_t, d_keys, d_values, acc):
    step = pl.program_id(0)

    @pl.when(step == 0)
    def _():
        natural_order(plan, kv_ref, keys, values, (keys, keys_t))
        d_keys[...] = jnp.zeros_like(d_keys)
        d_values[...] = jnp.zeros_like(d_values)

    first, second = plan[2 * step], plan[2 * step + 1]
    q = stacked(q_ref, first, second)
    d_rows = matmul(
        jnp.concatenate(
            [da_ref[pl.ds(pl.multiple_of(at * BLK, BLK), BLK), :] for at in (first, second)], axis=0
        ),
        wo_ref[...],
    )
    d_out = jnp.concatenate(
        [
            d_rows[begin : begin + BLK, head : head + HEAD_WIDTH]
            for begin in (0, BLK)
            for head in (0, HEAD_WIDTH)
        ],
        axis=0,
    ).astype(BF)
    q_t = q.astype(F32).T.astype(BF)
    d_out_wide = d_out.astype(F32).T
    d_out_t = d_out_wide.astype(BF)
    q_pos, q_start = strips_of(plan, lengths, step)
    lse = lse_ref[0]
    dots = jnp.sum(d_out_wide * stacked(heads_ref, first, second).astype(F32).T, axis=0, keepdims=True)
    acc[...] = jnp.zeros_like(acc)

    def chunk(masked, index, carried):
        at = pl.multiple_of(index * CHUNK, CHUNK)
        here = pl.ds(at, CHUNK)
        scores = matmul(keys[here, :], q_t)
        if masked:
            scores = kept(scores, at, q_pos, q_start)
        probs = jnp.exp2(scores * TWO_SCALE - lse)
        d_probs = matmul(values[here, :], d_out_t)
        d_scores = (probs * (d_probs - dots)).astype(BF)
        d_values[here, :] += matmul(probs.astype(BF), d_out)
        d_keys[here, :] += matmul(d_scores, q)
        acc[...] += matmul(keys_t[:, here], d_scores)
        return carried

    three_loops(step, plan, chunk, 0)
    unstacked(dq_ref, first, second, (acc[...] * SCORE_SCALE).T)

    @pl.when(step == pl.num_programs(0) - 1)
    def _():
        def one(block, carried):
            dealt = plan[PLAN_INVERSE + block]
            group, inside = dealt // 16, dealt % 16
            half, rest = inside // 8, inside % 8
            at = pl.ds(pl.multiple_of(block * BLK, BLK), BLK)
            to = pl.ds(pl.multiple_of(rest * BLK, BLK), BLK)
            dkv_ref[half, group, 0, to, :] = (d_keys[at, :] * SCORE_SCALE).astype(BF)
            dkv_ref[half, group, 1, to, :] = d_values[at, :].astype(BF)
            return carried

        lax.fori_loop(0, kv_ref.shape[0] // BLK, one, 0, unroll=4)
        owners = early_ref.shape[0]
        depth = da_ref.shape[1] // owners
        span = 256
        for at in range(da_ref.shape[1] // span):
            value = transposed_times(da_ref[:, at * span : (at + 1) * span], heads_ref[...])
            some = slice(at * span // depth, (at + 1) * span // depth)
            for head in range(2):
                early_ref[some, head * depth : (head + 1) * depth, :] = (
                    value[:, head * HEAD_WIDTH : (head + 1) * HEAD_WIDTH]
                    .astype(BF)
                    .reshape(span // depth, depth, HEAD_WIDTH)
                )
        early_ref[:, 2 * depth :, :] = part_ref[...]


def attend_back(plan, lengths, queries, heads, d_attn, wo_t, kv, lse, part):
    rows = queries.shape[0]
    total = kv.shape[0]
    steps = rows // (2 * BLK)
    everything = pl.BlockSpec(queries.shape, lambda i, *_: (0, 0))
    strip = pl.BlockSpec((1, 1, 4 * BLK), lambda i, *_: (i, 0, 0))
    sds = jax.ShapeDtypeStruct
    owners = part.shape[0]
    early_shape = (owners, part.shape[1] + 2 * d_attn.shape[1] // owners, HEAD_WIDTH)
    dkv_shape = (2, total // rows, 2, rows // 2, HEAD_WIDTH)
    return pl.pallas_call(
        backward_kernel,
        out_shape=(sds(queries.shape, F32), sds(dkv_shape, BF), sds(early_shape, BF)),
        grid_spec=pltpu.PrefetchScalarGridSpec(
            num_scalar_prefetch=2,
            grid=(steps,),
            in_specs=[
                everything,
                everything,
                pl.BlockSpec(d_attn.shape, lambda i, *_: (0, 0)),
                pl.BlockSpec((wo_t.shape[0], queries.shape[1]), lambda i, *_: (0, 0)),
                pl.BlockSpec(kv.shape, lambda i, *_: (0, 0)),
                strip,
                pl.BlockSpec(part.shape, lambda i, *_: (0, 0, 0)),
            ],
            out_specs=[
                everything,
                pl.BlockSpec(dkv_shape, lambda i, *_: (0, 0, 0, 0, 0)),
                pl.BlockSpec(early_shape, lambda i, *_: (0, 0, 0)),
            ],
            scratch_shapes=[
                pltpu.VMEM((total, HEAD_WIDTH), BF),
                pltpu.VMEM((total, HEAD_WIDTH), BF),
                pltpu.VMEM((HEAD_WIDTH, total), BF),
                pltpu.VMEM((total, HEAD_WIDTH), F32),
                pltpu.VMEM((total, HEAD_WIDTH), F32),
                pltpu.VMEM((HEAD_WIDTH, 4 * BLK), F32),
            ],
        ),
        compiler_params=pltpu.CompilerParams(vmem_limit_bytes=ROOM),
        name="attend_back",
        cost_estimate=cost(24),
    )(plan, lengths, queries, heads, d_attn, wo_t, kv, lse, part)


def expert_kernel(side, x_ref, cot_ref, gate_ref, g_own, u_own, d_own, g_other, u_other, u_rest, d_other, y_ref, dx_ref, a_ref, dg_ref, du_ref, dy_ref, gate_w, up_w, down_w, gate_f, up_f, down_f, sems):
    half = gate_f.shape[1]
    own_copies, other_copies = [], []
    for at, (own, others, whole, stage) in enumerate(
        (
            (g_own, (g_other,), gate_w, gate_f),
            (u_own, (u_other, u_rest), up_w, up_f),
            (d_own, (d_other,), down_w, down_f),
        )
    ):
        own_copies.append(pltpu.make_async_copy(own.at[side[0]], stage, sems.at[at, 0]))
        begin = 0
        other_copies.append([])
        for which, part in enumerate(others):
            count = part.shape[0]
            if at < 2:
                target = whole.at[pl.ds(begin, count), pl.ds(half, half)]
            else:
                target = whole.at[pl.ds(half, half)]
            other_copies[at].append(pltpu.make_async_copy(part, target, sems.at[at, 1 + which]))
            begin += count

    @pl.when(pl.program_id(0) == 0)
    def _():
        for which in range(3):
            own_copies[which].start()
            for copy in other_copies[which]:
                copy.start()

    def ready(which, fill):
        @pl.when(pl.program_id(0) == 0)
        def _():
            own_copies[which].wait()
            fill()
            for copy in other_copies[which]:
                copy.wait()

    def fill_gate():
        gate_w[:, :half] = gate_f[...].astype(BF)

    def fill_up():
        up_w[:, :half] = up_f[...].astype(BF)

    def fill_down():
        down_w[:half, :] = down_f[...].astype(BF)

    x = x_ref[...]
    ready(0, fill_gate)
    gate_pre = matmul(x, gate_w[...])
    ready(1, fill_up)
    up_pre = matmul(x, up_w[...])
    ready(2, fill_down)
    sigma = 1.0 / (1.0 + jnp.exp(-gate_pre))
    silu = gate_pre * sigma
    activated = (silu * up_pre).astype(BF)
    a_ref[...] = activated
    gates = gate_ref[:, 0:1].astype(F32) + gate_ref[:, 64:65].astype(F32)
    cot = cot_ref[...].astype(F32)
    out = matmul(activated, down_w[...])
    y_ref[...] = (out * gates).astype(BF)
    dots = jnp.sum(out * cot, axis=1, keepdims=True)
    high = dots.astype(BF).astype(F32)
    lane = lax.broadcasted_iota(jnp.int32, (dots.shape[0], 128), 1)
    dx_ref[:, y_ref.shape[1] :] = jnp.where(lane < 64, high, dots - high).astype(BF)
    d_pairs = (cot * gates).astype(BF)
    dy_ref[...] = d_pairs
    d_act = times_transposed(d_pairs, down_w[...])
    d_gate = (d_act * up_pre * sigma * (1.0 + gate_pre * (1.0 - sigma))).astype(BF)
    d_up = (d_act * silu).astype(BF)
    dg_ref[...] = d_gate
    du_ref[...] = d_up
    dx_ref[:, : y_ref.shape[1]] = (times_transposed(d_gate, gate_w[...]) + times_transposed(d_up, up_w[...])).astype(BF)


def run_expert(side, rows_in, cot, gates, own, other):
    count, width = rows_in.shape
    half = own[0].shape[2]
    tile = 256
    sds = jax.ShapeDtypeStruct

    def by_rows(columns):
        return pl.BlockSpec((tile, columns), lambda i, side: (i, 0))

    return pl.pallas_call(
        expert_kernel,
        out_shape=(
            sds((count, width), BF),
            sds((count, width + 128), BF),
            sds((count, 2 * half), BF),
            sds((count, 2 * half), BF),
            sds((count, 2 * half), BF),
            sds((count, width), BF),
        ),
        grid_spec=pltpu.PrefetchScalarGridSpec(
            num_scalar_prefetch=1,
            grid=(count // tile,),
            in_specs=[by_rows(width), by_rows(width), by_rows(128)] + [ANY] * 7,
            out_specs=[
                by_rows(width),
                by_rows(width + 128),
                by_rows(2 * half),
                by_rows(2 * half),
                by_rows(2 * half),
                by_rows(width),
            ],
            scratch_shapes=[
                pltpu.VMEM((width, 2 * half), BF),
                pltpu.VMEM((width, 2 * half), BF),
                pltpu.VMEM((2 * half, width), BF),
                pltpu.VMEM((width, half), F32),
                pltpu.VMEM((width, half), F32),
                pltpu.VMEM((half, width), F32),
                DMA((3, 3)),
            ],
        ),
        compiler_params=pltpu.CompilerParams(vmem_limit_bytes=ROOM),
        name="run_expert",
        cost_estimate=cost(25),
    )(side, rows_in, cot, gates, *own, *other)


def gate_grads_kernel(side, x_ref, dg_ref, gate_ref, gate_out):
    half = gate_ref.shape[-1]
    value = matmul(x_ref[...].T, dg_ref[...])
    gate_ref[0] = value[:, :half]
    gate_out[...] = value[:, half:].astype(BF)


def gate_grads(side, rows_in, d_gate):
    count, width = rows_in.shape
    whole = d_gate.shape[1]
    half = whole // 2
    tile = 1024
    sds = jax.ShapeDtypeStruct
    return pl.pallas_call(
        gate_grads_kernel,
        out_shape=(sds((2, width, half), F32), sds((width, half), BF)),
        grid_spec=pltpu.PrefetchScalarGridSpec(
            num_scalar_prefetch=1,
            grid=(width // tile,),
            in_specs=[
                pl.BlockSpec((count, tile), lambda i, side: (0, i)),
                pl.BlockSpec((count, whole), lambda i, side: (0, 0)),
            ],
            out_specs=[
                pl.BlockSpec((1, tile, half), lambda i, side: (side[0], i, 0)),
                pl.BlockSpec((tile, half), lambda i, side: (i, 0)),
            ],
        ),
        compiler_params=pltpu.CompilerParams(vmem_limit_bytes=ROOM),
        name="gate_grads",
        cost_estimate=cost(5),
    )(side, rows_in, d_gate)


def expert_grads_kernel(side, x_ref, dy_ref, a_ref, du_ref, up_ref, down_ref, up_out, up_rest, down_out, down_rest, a_t):
    half = up_ref.shape[-1]
    step = pl.program_id(0)
    turn_at = up_out.shape[0]

    @pl.when(step == 0)
    def _():
        a_t[...] = a_ref[...].T

    value = matmul(x_ref[...].T, du_ref[...])
    up_ref[0] = value[:, :half]
    low = value[:, half:].astype(BF)

    @pl.when(step < UP_CUT[0] // turn_at)
    def _():
        up_out[...] = low

    @pl.when(step >= UP_CUT[0] // turn_at)
    def _():
        up_rest[...] = low

    value = matmul(a_t[...], dy_ref[...])
    down_ref[0] = value[:half]
    cut = half + down_out.shape[0]
    down_out[...] = value[half:cut].astype(BF)
    down_rest[...] = value[cut:].astype(BF)


def expert_grads(side, rows_in, d_pairs, activated, d_up):
    count, width = rows_in.shape
    whole = activated.shape[1]
    half = whole // 2
    tile = 256
    first = UP_CUT[0] // tile
    sds = jax.ShapeDtypeStruct
    columns = pl.BlockSpec((count, tile), lambda i, side: (0, i))
    full = pl.BlockSpec((count, whole), lambda i, side: (0, 0))
    return pl.pallas_call(
        expert_grads_kernel,
        out_shape=(
            sds((2, width, half), F32),
            sds((2, half, width), F32),
            sds((UP_CUT[0], half), BF),
            sds((UP_CUT[1], half), BF),
            sds((DOWN_GRAD_CUT[0], width), BF),
            sds((DOWN_GRAD_CUT[1], width), BF),
        ),
        grid_spec=pltpu.PrefetchScalarGridSpec(
            num_scalar_prefetch=1,
            grid=(width // tile,),
            in_specs=[columns, columns, full, full],
            out_specs=[
                pl.BlockSpec((1, tile, half), lambda i, side: (side[0], i, 0)),
                pl.BlockSpec((1, half, tile), lambda i, side: (side[0], 0, i)),
                pl.BlockSpec((tile, half), lambda i, side: (jnp.minimum(i, first - 1), 0)),
                pl.BlockSpec((tile, half), lambda i, side: (jnp.maximum(i - first, 0), 0)),
                pl.BlockSpec((DOWN_GRAD_CUT[0], tile), lambda i, side: (0, i)),
                pl.BlockSpec((DOWN_GRAD_CUT[1], tile), lambda i, side: (0, i)),
            ],
            scratch_shapes=[pltpu.VMEM((whole, count), BF)],
        ),
        compiler_params=pltpu.CompilerParams(vmem_limit_bytes=ROOM),
        name="expert_grads",
        cost_estimate=cost(10),
    )(side, rows_in, d_pairs, activated, d_up)


def route_kernel(where, routes_ref, cot_ref, pick_ref, turned_ref, of_ref, hits_ref, rows_ref):
    slots, rows = pick_ref.shape[0], routes_ref.shape[2]
    experts = of_ref.shape[1]
    slot = lax.broadcasted_iota(jnp.int32, (slots, experts), 0)
    lane = lax.broadcasted_iota(jnp.int32, (slots, experts), 1)
    chip = lax.div(slot, 2 * CAP)
    side = lax.rem(where[1] + lax.div(chip, 4) + where[2], 2)
    of_expert = (lane == 4 * chip + 2 * where[0] + side).astype(F32).astype(BF)
    of_ref[...] = of_expert
    expert = lax.broadcasted_iota(jnp.int32, (experts, rows), 0)
    before = (
        lax.broadcasted_iota(jnp.int32, (rows, rows), 0) < lax.broadcasted_iota(jnp.int32, (rows, rows), 1)
    ).astype(F32).astype(BF)
    hits, ranks = [], []
    for half in range(2):
        hit = jnp.zeros((experts, rows), F32)
        for choice in range(TOPK):
            hit = hit + (routes_ref[half, choice : choice + 1, :] == expert).astype(F32)
        rank = matmul(hit.astype(BF), before) + half * CAP
        hits.append(hit)
        ranks.append(jnp.where(hit > 0.5, rank, -1.0))
    hits_ref[...] = jnp.concatenate(hits, axis=1).T
    mine = matmul(of_expert, jnp.concatenate(ranks, axis=1).astype(BF))
    wanted = lax.rem(lax.broadcasted_iota(jnp.int32, mine.shape, 0), 2 * CAP).astype(F32)
    pick = (mine == wanted).astype(F32)
    pick_low = pick.astype(BF)
    pick_ref[...] = pick_low
    turned_ref[...] = pick.T.astype(BF)
    rows_ref[...] = matmul(pick_low, cot_ref[...]).astype(BF)


def route(where, routes, cotangent, experts):
    rows, width = cotangent.shape
    slots = experts // 4 * 2 * CAP
    sds = jax.ShapeDtypeStruct
    return pl.pallas_call(
        route_kernel,
        out_shape=(
            sds((slots, rows), BF),
            sds((rows, slots), BF),
            sds((slots, experts), BF),
            sds((rows, experts), F32),
            sds((slots, width), BF),
        ),
        in_specs=[pl.BlockSpec(memory_space=pltpu.SMEM), VMEM, VMEM],
        out_specs=[VMEM] * 5,
        compiler_params=pltpu.CompilerParams(vmem_limit_bytes=ROOM),
        name="route",
        cost_estimate=cost(5),
    )(where, routes, cotangent)


def middle_kernel(chip, t_ref, attn_ref, gain_ref, wr_ref, hits_ref, pick_ref, of_ref, res_ref, h_ref, inv_ref, gates_ref, rows_ref, tile_ref):
    residual = t_ref[...].astype(F32) + attn_ref[...]
    res_ref[...] = residual
    inverse = lax.rsqrt(jnp.mean(residual * residual, axis=1, keepdims=True) + EPSILON)
    inv_ref[...] = jnp.broadcast_to(inverse, inv_ref.shape)
    hidden = (residual * inverse * gain_ref[...]).astype(BF)
    h_ref[...] = hidden
    pick = pick_ref[...]
    rows_ref[...] = matmul(pick, hidden).astype(BF)
    hit = hits_ref[...] > 0.5
    logits = jnp.where(hit, matmul(hidden, wr_ref[...]), MASKED)
    exps = jnp.where(hit, jnp.exp(logits - jnp.max(logits, axis=1, keepdims=True)), 0.0)
    gates = exps / jnp.sum(exps, axis=1, keepdims=True)
    gates_ref[...] = gates
    high = gates.astype(BF)
    chosen = [
        jnp.sum(matmul(pick, part) * of_ref[...].astype(F32), axis=1, keepdims=True)
        for part in (high, (gates - high.astype(F32)).astype(BF))
    ]
    lane = lax.broadcasted_iota(jnp.int32, tile_ref.shape, 1)
    tile_ref[...] = jnp.where(lane < 64, chosen[0], chosen[1]).astype(BF)


def middle(chip, row_rows, attn_total, gain, late_all, hits, pick, of_expert):
    rows, width = attn_total.shape
    slots, experts = of_expert.shape
    sds = jax.ShapeDtypeStruct

    def whole(value):
        return pl.BlockSpec(value.shape, lambda i, chip: (0, 0))

    def out(*shape):
        return pl.BlockSpec(shape, lambda i, chip: (0, 0))

    shapes = (
        sds((rows, width), F32),
        sds((rows, width), BF),
        sds((rows, 128), F32),
        sds((rows, experts), F32),
        sds((slots, width), BF),
        sds((slots, 128), BF),
    )
    return pl.pallas_call(
        middle_kernel,
        out_shape=shapes,
        grid_spec=pltpu.PrefetchScalarGridSpec(
            num_scalar_prefetch=1,
            grid=(1,),
            in_specs=[
                pl.BlockSpec((rows, width), lambda i, chip: (chip[0], 0)),
                whole(attn_total),
                whole(gain),
                pl.BlockSpec((width, experts), lambda i, chip: (0, 2)),
                whole(hits),
                whole(pick),
                whole(of_expert),
            ],
            out_specs=[out(*value.shape) for value in shapes],
        ),
        compiler_params=pltpu.CompilerParams(vmem_limit_bytes=ROOM),
        name="middle",
        cost_estimate=cost(1),
    )(chip, row_rows, attn_total, gain, late_all, hits, pick, of_expert)


def turn_kernel(core, moe_ref, dg_ref, gates_ref, h_ref, res_ref, inv_ref, wr_ref, gain_ref, cot_ref, d_ref, low_ref, part_ref):
    gates = gates_ref[...]
    d_gates = dg_ref[...]
    d_logits = (gates * (d_gates - jnp.sum(gates * d_gates, axis=1, keepdims=True))).astype(BF)
    hidden = h_ref[...]
    gradient = moe_ref[...] + times_transposed(d_logits, wr_ref[...])
    residual, inverse = res_ref[...], inv_ref[:, 0:1]
    weighted = gradient * gain_ref[...]
    mean_term = jnp.mean(weighted * residual, axis=1, keepdims=True)
    back = inverse * weighted - residual * (inverse * inverse * inverse) * mean_term
    value = cot_ref[...].astype(F32) + back
    d_ref[...] = value
    low_ref[...] = value.astype(BF)
    owners, rows, _ = part_ref.shape
    depth = hidden.shape[1] // owners
    grad_router = transposed_times(hidden, d_logits).astype(BF)
    part_ref[:, :depth, :] = grad_router.reshape(owners, depth, grad_router.shape[1])
    terms = jnp.sum(gradient * residual * inverse, axis=0, keepdims=True)
    wide = jnp.broadcast_to(terms, (8, terms.shape[1]))
    by_owner = jnp.concatenate(
        [wide[:1, owner * depth : (owner + 1) * depth] for owner in range(owners)], axis=0
    )
    by_owner = jnp.concatenate([by_owner, jnp.zeros((owners, 128 - depth), F32)], axis=1)
    part_ref[:, depth:, :] = jnp.broadcast_to(
        by_owner[:, None, :], (owners, rows - depth, 128)
    ).astype(BF)


def turn(core, d_moe, d_gates, gates, hidden, residual, inverse, late_all, gain, cotangent):
    rows, width = d_moe.shape
    experts = gates.shape[1]
    owners = 64
    sds = jax.ShapeDtypeStruct

    def mine(columns):
        return pl.BlockSpec((rows, columns), lambda i, core: (core[0], 0))

    def whole(*shape):
        return pl.BlockSpec(shape, lambda i, core: (0,) * len(shape))

    parts = (owners, width // owners + 16, 128)
    return pl.pallas_call(
        turn_kernel,
        out_shape=(sds((rows, width), F32), sds((rows, width), BF), sds(parts, BF)),
        grid_spec=pltpu.PrefetchScalarGridSpec(
            num_scalar_prefetch=1,
            grid=(1,),
            in_specs=[
                whole(rows, width),
                whole(rows, experts),
                mine(experts),
                mine(width),
                mine(width),
                mine(128),
                pl.BlockSpec((width, experts), lambda i, core: (0, 2)),
                whole(1, width),
                whole(rows, width),
            ],
            out_specs=[whole(rows, width), whole(rows, width), whole(*parts)],
        ),
        compiler_params=pltpu.CompilerParams(vmem_limit_bytes=ROOM),
        name="turn",
        cost_estimate=cost(6),
    )(core, d_moe, d_gates, gates, hidden, residual, inverse, late_all, gain, cotangent)


def last_kernel(side, g_in, u_in, u_rest, d_in, d_rest, *refs):
    (t_ref, dh_ref, dr_ref, moe_ref, res_ref, ga_ref, late_ref, early_ref, wq_ref, wk_ref, wv_ref), refs = refs[3:14], refs[14:]
    g_out, u_out, d_out, out_ref, gt_ref, gq_ref, gk_ref, gv_ref, go_ref, gr_ref, gains_ref, ffn_ref = refs[:12]
    keys, router, gains, ffn, dots = refs[12:]
    step = pl.program_id(0)
    g_out[0] = g_in[...].astype(F32)
    u_out[0] = jnp.where(step < UP_CUT[0] // u_in.shape[0], u_in[...], u_rest[...]).astype(F32)
    d_out[0, : d_in.shape[0]] = d_in[...].astype(F32)
    d_out[0, d_in.shape[0] :] = d_rest[...].astype(F32)
    rows = t_ref[...].astype(F32)
    out_ref[...] = res_ref[...] + moe_ref[...]
    inverse = lax.rsqrt(jnp.mean(rows * rows, axis=1, keepdims=True) + EPSILON)
    weighted = dh_ref[...] * ga_ref[...]
    mean_term = jnp.mean(weighted * rows, axis=1, keepdims=True)
    gt_ref[...] = dr_ref[...] + (
        inverse * weighted - rows * (inverse * inverse * inverse) * mean_term
    )

    @pl.when(step == 0)
    def _():
        for ref in (keys, router, gains, ffn, dots):
            ref[...] = jnp.zeros_like(ref)

    depth = gq_ref.shape[0]
    late, early = late_ref[0].astype(F32), early_ref[0].astype(F32)
    query = jnp.concatenate([late[:depth], late[depth : 2 * depth]], axis=1)
    gq_ref[...] = query
    low_q = wq_ref[...].astype(BF).astype(F32)
    dots[...] += jnp.sum(low_q * query, axis=1, keepdims=True)
    keys[lax.div(step, 2)] += late[2 * depth : 3 * depth]
    gains[...] += late[3 * depth :]
    router[...] += early[2 * depth : 3 * depth]
    ffn[...] += early[3 * depth : 3 * depth + 8]
    go_ref[...] = jnp.concatenate([early[:depth], early[depth : 2 * depth]], axis=1)

    @pl.when(step == pl.num_programs(0) - 1)
    def _():
        gk_ref[...] = jnp.concatenate([keys[0], keys[2]], axis=1)
        gv_ref[...] = jnp.concatenate([keys[1], keys[3]], axis=1)
        gr_ref[...] = router[...]
        ffn_ref[...] = ffn[...]
        total = (
            dots[:, 0:1]
            + jnp.sum(wk_ref[...].astype(BF).astype(F32) * gk_ref[...], axis=1, keepdims=True)
            + jnp.sum(wv_ref[...].astype(BF).astype(F32) * gv_ref[...], axis=1, keepdims=True)
        )
        blank = jnp.zeros((128 - depth, 128), F32)
        square = jnp.concatenate([jnp.broadcast_to(total, (depth, 128)), blank], axis=0).T
        row = lax.broadcasted_iota(jnp.int32, gains_ref.shape, 0)
        gains_ref[...] = jnp.where(row < 2, gains[:8], square[:8])


def last(side, arrived, placed, tokens, d_hidden, d_residual, moe, residual, gain, late, early, weights):
    width, half = arrived[0].shape
    rows = tokens.shape[0]
    steps = 8
    tile, strip = width // steps, rows // steps
    depth = weights[0].shape[0]
    sds = jax.ShapeDtypeStruct

    def whole(*shape):
        return pl.BlockSpec(shape, lambda i, side: (0,) * len(shape))

    first = UP_CUT[0] // tile
    rows_out = pl.BlockSpec((1, tile, half), lambda i, side: (1 - side[0], i, 0))
    columns_out = pl.BlockSpec((1, half, tile), lambda i, side: (1 - side[0], 0, i))
    strips = pl.BlockSpec((strip, width), lambda i, side: (i, 0))
    mine = pl.BlockSpec((strip, width), lambda i, side: (side[1] * steps + i, 0))
    place = pl.BlockSpec((1,) + late.shape[1:], lambda i, side: (i, 0, 0))
    query = pl.BlockSpec((depth, weights[0].shape[1] // steps), lambda i, side: (0, i))
    narrow = (depth, weights[1].shape[1])
    return pl.pallas_call(
        last_kernel,
        out_shape=[sds(value.shape, F32) for value in placed]
        + [
            sds((rows, width), F32),
            sds((rows, width), F32),
            sds(weights[0].shape, F32),
            sds(narrow, F32),
            sds(narrow, F32),
            sds(weights[0].shape, F32),
            sds((depth, 128), F32),
            sds((8, 128), F32),
            sds((8, 128), F32),
        ],
        grid_spec=pltpu.PrefetchScalarGridSpec(
            num_scalar_prefetch=1,
            grid=(steps,),
            in_specs=[
                pl.BlockSpec((tile, half), lambda i, side: (i, 0)),
                pl.BlockSpec((tile, half), lambda i, side: (jnp.minimum(i, first - 1), 0)),
                pl.BlockSpec((tile, half), lambda i, side: (jnp.maximum(i - first, 0), 0)),
                pl.BlockSpec((DOWN_GRAD_CUT[0], tile), lambda i, side: (0, i)),
                pl.BlockSpec((DOWN_GRAD_CUT[1], tile), lambda i, side: (0, i)),
            ]
            + [ANY] * 3
            + [
                strips,
                strips,
                strips,
                strips,
                mine,
                whole(1, width),
                place,
                place,
                query,
                whole(*narrow),
                whole(*narrow),
            ],
            out_specs=[
                rows_out,
                rows_out,
                columns_out,
                strips,
                strips,
                query,
                whole(*narrow),
                whole(*narrow),
                query,
                whole(depth, 128),
                whole(8, 128),
                whole(8, 128),
            ],
            scratch_shapes=[
                pltpu.VMEM((4, depth, 128), F32),
                pltpu.VMEM((depth, 128), F32),
                pltpu.VMEM((16, 128), F32),
                pltpu.VMEM((8, 128), F32),
                pltpu.VMEM((depth, 128), F32),
            ],
        ),
        input_output_aliases={6: 0, 7: 1, 8: 2},
        compiler_params=pltpu.CompilerParams(vmem_limit_bytes=ROOM),
        name="last",
        cost_estimate=cost(9),
    )(side, *arrived, *placed, tokens, d_hidden, d_residual, moe, residual, gain, late, early, *weights)


def project_kernel(block_order, lengths, group, t_ref, w_ref, side_ref, flag_ref, freq_ref, ga_ref, gq_ref, gk_ref, h_ref, q_ref, kv_ref, qp_ref, kp_ref, cos_ref, sin_ref):
    tile = t_ref.shape[0]
    row = lax.broadcasted_iota(jnp.int32, (tile, HEAD_WIDTH), 0)
    lane = lax.broadcasted_iota(jnp.int32, (tile, HEAD_WIDTH), 1)
    first_block = group[0] * 16 + pl.program_id(0) * (tile // BLK)
    position = row * 0
    for at in range(tile // BLK):
        inside = block_order[first_block + at] * BLK + row - at * BLK
        position = jnp.where(row >= at * BLK, inside, position)
    angles = (position - start_of(lengths, position)).astype(F32) * freq_ref[...]
    cosine = jnp.cos(angles)
    sine_tab = jnp.where(lane < HEAD_WIDTH // 2, -1.0, 1.0) * jnp.sin(angles)
    cos_ref[...] = cosine
    sin_ref[...] = sine_tab
    rows = t_ref[...].astype(F32)
    inverse = lax.rsqrt(jnp.mean(rows * rows, axis=1, keepdims=True) + EPSILON)
    hidden = (rows * inverse * ga_ref[...]).astype(BF)
    h_ref[...] = hidden
    qkv = matmul(hidden, w_ref[...])
    own = qkv[:, 2 * HEAD_WIDTH :]
    other = matmul(hidden, side_ref[...])
    first = flag_ref[0:1, :] > 0.5

    def turned(value, gain):
        root = lax.rsqrt(jnp.mean(value * value, axis=1, keepdims=True) + EPSILON)
        value = value * root * gain
        return (value * cosine + pltpu.roll(value, HEAD_WIDTH // 2, 1) * sine_tab).astype(BF)

    for head in range(2):
        span = slice(head * HEAD_WIDTH, (head + 1) * HEAD_WIDTH)
        q_ref[:, span] = turned(qkv[:, span], gq_ref[...])
    qp_ref[...] = qkv[:, : 2 * HEAD_WIDTH]
    keys = jnp.where(first, own, other)
    kp_ref[...] = keys
    kv_ref[:, :HEAD_WIDTH] = turned(keys, gk_ref[...])
    kv_ref[:, HEAD_WIDTH:] = jnp.where(first, other, own).astype(BF)


def project(block_order, lengths, group, tokens, weights, side, first, frequency, gain, gain_query, gain_key):
    rows, width = tokens.shape
    tile = 256
    sds = jax.ShapeDtypeStruct

    def by_rows(columns):
        return pl.BlockSpec((tile, columns), lambda i, *_: (i, 0))

    def whole(value):
        return pl.BlockSpec(value.shape, lambda i, *_: (0, 0))

    return pl.pallas_call(
        project_kernel,
        out_shape=(
            sds((rows, width), BF),
            sds((rows, 256), BF),
            sds((rows, 256), BF),
            sds((rows, 256), F32),
            sds((rows, 128), F32),
            sds((rows, 128), F32),
            sds((rows, 128), F32),
        ),
        grid_spec=pltpu.PrefetchScalarGridSpec(
            num_scalar_prefetch=3,
            grid=(rows // tile,),
            in_specs=[
                by_rows(width),
                whole(weights),
                whole(side),
                whole(first),
                whole(frequency),
                whole(gain),
                whole(gain_query),
                whole(gain_key),
            ],
            out_specs=[
                by_rows(width),
                by_rows(256),
                by_rows(256),
                by_rows(256),
                by_rows(128),
                by_rows(128),
                by_rows(128),
            ],
        ),
        compiler_params=pltpu.CompilerParams(vmem_limit_bytes=ROOM),
        name="project",
        cost_estimate=cost(8),
    )(block_order, lengths, group, tokens, weights, side, first, frequency, gain, gain_query, gain_key)


def project_back_kernel(dq_ref, ds_ref, qp_ref, kp_ref, cos_ref, sin_ref, h_ref, w_ref, side_ref, gq_ref, gk_ref, flag_ref, part_ref, late_ref, side_w, total, gains):
    step = pl.program_id(0)
    cosine, sine_tab = cos_ref[...], sin_ref[...]
    key, first, own = flag_ref[0:1, :], flag_ref[1:2, :], flag_ref[2:3, :]
    heads = 2 * HEAD_WIDTH

    @pl.when(step == 0)
    def _():
        gains[...] = jnp.zeros_like(gains)
        total[...] = jnp.zeros_like(total)
        side_w[...] = jnp.where(
            own > 0.5, w_ref[:, heads:].astype(F32), side_ref[...].astype(F32)
        ).astype(BF)

    def back(gradient, value, gain):
        gradient = gradient * cosine - pltpu.roll(gradient, HEAD_WIDTH // 2, 1) * sine_tab
        root = lax.rsqrt(jnp.mean(value * value, axis=1, keepdims=True) + EPSILON)
        weighted = gradient * gain
        mean_term = jnp.mean(weighted * value, axis=1, keepdims=True)
        terms = jnp.sum(gradient * value * root, axis=0, keepdims=True)
        return root * weighted - value * (root * root * root) * mean_term, terms

    columns = []
    for head in range(2):
        span = slice(head * HEAD_WIDTH, (head + 1) * HEAD_WIDTH)
        value, terms = back(dq_ref[:, span], qp_ref[:, span], gq_ref[...])
        columns.append(value.astype(BF))
        gains[0:1, :] += terms
    d_side = ds_ref[...]
    value, terms = back(d_side, kp_ref[...], gk_ref[...])
    mine = jnp.where(first == (step // 2).astype(F32), 1.0, 0.0)
    columns.append((jnp.where(key > 0.5, value, d_side) * mine).astype(BF))
    gains[1:2, :] += terms * key * mine
    d_all = jnp.concatenate(columns, axis=1)
    part_ref[...] = (
        times_transposed(d_all[:, :heads], w_ref[:, :heads])
        + times_transposed(d_all[:, heads:], side_w[...])
    ).astype(BF)
    total[...] += transposed_times(h_ref[...], d_all)

    @pl.when(step == pl.num_programs(0) - 1)
    def _():
        pieces, depth = late_ref.shape[0], h_ref.shape[1] // late_ref.shape[0]
        for at in range(3):
            value = total[:, at * HEAD_WIDTH : (at + 1) * HEAD_WIDTH].astype(BF)
            late_ref[:, at * depth : (at + 1) * depth, :] = value.reshape(pieces, depth, HEAD_WIDTH)
        late_ref[:, 3 * depth :, :] = jnp.broadcast_to(
            gains[...].astype(BF)[None], (pieces,) + gains.shape
        )


def project_back(d_queries, d_side, q_pre, k_pre, cosine, sine_tab, hidden, weights, side, gain_query, gain_key, flags):
    rows = d_queries.shape[0]
    width = hidden.shape[1]
    tile = 256
    tiles = rows // tile
    owners = 64
    sds = jax.ShapeDtypeStruct
    late = (owners, 3 * width // owners + 16, 128)

    def by_rows(columns):
        return pl.BlockSpec((tile, columns), lambda i: (i, 0))

    def whole(value):
        return pl.BlockSpec(value.shape, lambda i: (0, 0))

    half_rows = pl.BlockSpec((tile, 128), lambda i: (i % (tiles // 2), 0))
    return pl.pallas_call(
        project_back_kernel,
        grid=(tiles,),
        out_shape=(sds((rows, width), BF), sds(late, BF)),
        in_specs=[
            by_rows(256),
            half_rows,
            by_rows(256),
            by_rows(128),
            by_rows(128),
            by_rows(128),
            by_rows(width),
            whole(weights),
            whole(side),
            whole(gain_query),
            whole(gain_key),
            whole(flags),
        ],
        out_specs=[by_rows(width), pl.BlockSpec(late, lambda i: (0, 0, 0))],
        scratch_shapes=[
            pltpu.VMEM((width, 128), BF),
            pltpu.VMEM((width, 384), F32),
            pltpu.VMEM((16, 128), F32),
        ],
        compiler_params=pltpu.CompilerParams(vmem_limit_bytes=ROOM),
        name="project_back",
        cost_estimate=cost(12),
    )(
        d_queries, d_side, q_pre, k_pre, cosine, sine_tab, hidden, weights, side, gain_query, gain_key, flags
    )


def after(value, earlier):
    return lax.optimization_barrier((value, earlier))


def lanes_to(row, lanes=128):
    return jnp.pad(row, ((0, 0),) * (row.ndim - 1) + ((0, lanes - row.shape[-1]),))


def local(
    tokens,
    cotangent,
    seq_lengths,
    block_order,
    routes,
    w_query,
    key_weight,
    value_weight,
    w_out,
    gain_attn,
    gain_query,
    gain_key,
    gain_ffn,
    w_router,
    w_gate,
    w_up,
    w_down,
):
    rows = tokens.shape[0]
    width = tokens.shape[1]
    experts = w_router.shape[1]
    block_count = block_order.shape[0]
    wsh = lax.axis_index("wsh")
    me = lax.axis_index("ctx")
    core = lax.rem(me, 2)
    place = lax.rem(me, 8)
    group = lax.div(me, 8)
    row_tokens = 8 * rows

    def swap(value):
        return lax.ppermute(value, "wsh", [(0, 1), (1, 0)])

    depth = w_query.shape[0]
    (
        w_all,
        row_rows,
        small_all,
        chip_routes,
        chip_cot,
        other_gate,
        up_first,
        other_up,
        other_down,
        w_side,
    ) = gather_first(
        (w_query, key_weight, value_weight),
        (gain_attn[None, :], gain_ffn[None, :]),
        tokens,
        routes.T,
        cotangent,
        (w_gate, w_up, w_down),
    )
    w_main = w_all.reshape(width, 384)
    w_side = w_side.reshape(width, 128)
    is_key = lax.rem(lax.div(me, 2), 2) == 0

    def flag(value):
        return jnp.broadcast_to(value.astype(F32).reshape(1, 1), (8, 128))

    g_attn = to_low(small_all[:, 0, :depth].reshape(width)).astype(F32)
    g_ffn = to_low(small_all[:, 1, :depth].reshape(width)).astype(F32)
    g_query = rounded(gain_query)
    g_key = rounded(gain_key)

    o_part = to_low(w_out).T.reshape(depth, 8, 256).transpose(1, 0, 2)
    r_part = jnp.broadcast_to(to_low(w_router)[None], (8, depth, experts))
    late_pack = jnp.tile(jnp.concatenate([o_part, r_part], axis=2), (8, 1, 1))
    late_pack, small_all = after(late_pack, small_all)
    late_all = lax.all_to_all(late_pack, "ctx", split_axis=0, concat_axis=0, tiled=True).reshape(width, 384)

    chips = experts // 4
    slots = 2 * CAP
    y_half = lax.rem(lax.div(me, 8), 2)
    pick_low, pick_turned, of_expert, hits, cot_rows = route(
        jnp.stack([core, wsh, y_half]), chip_routes, chip_cot.reshape(2 * rows, width), experts
    )

    half_dim = HEAD_WIDTH // 2
    frequency = jnp.power(ROPE_BASE, -2.0 * jnp.arange(half_dim, dtype=jnp.float32) / HEAD_WIDTH)
    frequency = jnp.concatenate([frequency, frequency])[None, :]
    row_rows = row_rows.reshape(row_tokens, width)
    hidden_one, queries, kv, q_pre, k_pre, cosine, sine_tab = project(
        block_order,
        seq_lengths,
        group.reshape(1),
        row_rows,
        w_main,
        w_side,
        flag(core == 0),
        frequency,
        g_attn[None, :],
        g_query[None, :],
        g_key[None, :],
    )
    kv_all = gather_keys(kv, 1).reshape(block_count * BLK, 256)
    late_all, kv_all = after(late_all, kv_all)
    (cot_rows, other_gate), kv_all = after((cot_rows, other_gate), kv_all)
    gate_back = swap(other_gate)
    cot_there = exchange_behind(cot_rows.reshape(chips, slots, width)).reshape(chips * slots, width)
    heads, lse, plan = attend(block_order, seq_lengths, group.reshape(1), queries, kv_all)

    (other_up, other_down), heads = after((other_up, other_down), heads)
    attn_total, up_first = reduce_row((heads, late_all), 2, True, swapped_whole=up_first)
    residual, hidden_two, inverse_two, gates, out_rows, gate_tile = middle(
        lax.div(place, 2).reshape(1),
        row_rows,
        attn_total.reshape(2 * rows, width),
        g_ffn[None, :],
        late_all,
        hits,
        pick_low,
        of_expert,
    )

    out_rows = out_rows.reshape(chips, slots, width)
    gate_tile = gate_tile.reshape(chips, slots, 128)
    (gate_back, cot_there, other_down, other_up), gate_tile = after(
        (gate_back, cot_there, other_down, other_up), gate_tile
    )
    down_back = swap(other_down)
    up_back = (up_first, swap(other_up))
    arrived, gate_there = exchange([out_rows, gate_tile], 3)
    arrived = arrived.reshape(chips * slots, width)
    side = wsh.reshape(1)
    gate_there = gate_there.reshape(chips * slots, 128)
    y_rows, d_rows, activated, d_gate_pre, d_up_pre, d_pairs = run_expert(
        side, arrived, cot_there, gate_there, (w_gate, w_up, w_down), (gate_back, *up_back, down_back)
    )
    own_gate, other_gate = gate_grads(side, arrived, d_gate_pre)
    activated, other_gate = after(activated, other_gate)
    own_up, own_down, up_first, other_up, other_down, down_rest = expert_grads(
        side, arrived, d_pairs, activated, d_up_pre
    )
    own_grads = (own_gate, own_up, own_down)
    gate_grad_back = swap(other_gate)
    d_back = exchange_behind(d_rows.reshape(chips, slots, width + 128))
    d_back = d_back.reshape(chips * slots, width + 128)
    (gate_grad_back, other_up, other_down, down_rest), d_back = after(
        (gate_grad_back, other_up, other_down, down_rest), d_back
    )
    d_hidden_moe, d_gates = reduce_chip(pick_turned, d_back, of_expert, width, 5)
    d_residual, d_residual_low, part = turn(
        core.reshape(1),
        d_hidden_moe,
        d_gates,
        gates,
        hidden_two,
        residual,
        inverse_two,
        late_all,
        g_ffn[None, :],
        cotangent,
    )

    d_attn, up_first = gather_row(d_residual_low, up_first, 7)
    d_attn = d_attn.reshape(row_tokens, width)
    (y_rows, other_up, other_down), d_attn_late = after((y_rows, other_up, other_down), d_attn)
    y_back = exchange_behind(y_rows.reshape(chips, slots, width))
    up_grad_back = swap(other_up)
    down_grad_back = swap(other_down)
    d_queries, d_kv, early = attend_back(
        plan, seq_lengths, queries, heads, d_attn_late, late_all, kv_all, lse, part
    )
    (y_back, up_grad_back, down_grad_back), d_kv = after((y_back, up_grad_back, down_grad_back), d_kv)
    d_side, early, down_rest = reduce_keys(d_kv, early, down_rest, 8)
    swapped_grads = (gate_grad_back, up_first, up_grad_back, down_grad_back, down_rest)
    flags = jnp.concatenate(
        [
            flag(is_key)[:1],
            flag(core)[:1],
            flag(is_key == (core == 0))[:1],
            jnp.zeros((5, 128), F32),
        ],
        axis=0,
    )
    d_hidden_parts, late = project_back(
        d_queries,
        d_side,
        q_pre,
        k_pre,
        cosine,
        sine_tab,
        hidden_one,
        w_main,
        w_side,
        g_query[None, :],
        g_key[None, :],
        flags,
    )
    d_hidden_parts = d_hidden_parts.reshape(8, rows, width)
    d_hidden_one, moe_total, late = reduce_row(
        d_hidden_parts,
        9,
        False,
        extra=(pick_turned, y_back.reshape(chips * slots, width)),
        owned=(late,),
    )
    (
        grad_gate,
        grad_up,
        grad_down,
        out_stream,
        grad_tokens,
        grad_query,
        grad_key,
        grad_value,
        grad_out_t,
        grad_router,
        gain_parts,
        grad_gain_ffn,
    ) = last(
        jnp.stack([wsh, core]),
        swapped_grads,
        own_grads,
        tokens,
        d_hidden_one,
        d_residual,
        moe_total,
        residual,
        g_attn[None, :],
        late,
        early,
        (w_query, key_weight, value_weight),
    )
    gain_parts = lax.psum(gain_parts, "wsh")
    return (
        out_stream,
        grad_tokens,
        grad_query,
        grad_key,
        grad_value,
        grad_out_t.T,
        gain_parts[2, :depth] / rounded(gain_attn),
        gain_parts[0],
        gain_parts[1],
        grad_gain_ffn[0, :depth],
        grad_router,
        grad_gate,
        grad_up,
        grad_down,
    )


def solution(mesh):
    in_specs = (
        P("ctx", None),
        P("ctx", None),
        P(),
        P(),
        P("ctx", None),
        P("ctx", "wsh"),
        P("ctx", "wsh"),
        P("ctx", "wsh"),
        P("wsh", "ctx"),
        P("ctx"),
        P(),
        P(),
        P("ctx"),
        P("ctx", None),
        P("ctx", None, "wsh"),
        P("ctx", None, "wsh"),
        P("ctx", "wsh", None),
    )
    out_specs = (
        P("ctx", None),
        P("ctx", None),
        P("ctx", "wsh"),
        P("ctx", "wsh"),
        P("ctx", "wsh"),
        P("wsh", "ctx"),
        P("ctx"),
        P(),
        P(),
        P("ctx"),
        P("ctx", None),
        P("ctx", None, "wsh"),
        P("ctx", None, "wsh"),
        P("ctx", "wsh", None),
    )
    return jax.shard_map(local, mesh=mesh, in_specs=in_specs, out_specs=out_specs, check_vma=False)
```

```python
import functools
import math

import jax
import jax.numpy as jnp
from jax import lax
from jax.experimental import pallas as pl
from jax.experimental.pallas import tpu as pltpu
from jax.sharding import PartitionSpec as P

HEAD_WIDTH = 128
TOPK = 8
BLK = 64
MAX_SEQ_TOKENS = 4096
CAP = 12
CHUNK = 1024

EPSILON = 1e-06
ROPE_BASE = 1000000.0
MASKED = -1e30
MESH = pl.DeviceIdType.MESH
BF = jnp.bfloat16
F32 = jnp.float32


def to_low(value_rows):
    return value_rows.astype(jnp.bfloat16)


def rounded(value_rows):
    return lax.optimization_barrier(value_rows.astype(jnp.bfloat16)).astype(jnp.float32)


def matmul(left, right):
    return jnp.dot(left, right, preferred_element_type=jnp.float32)


def times_transposed(left, right):
    return lax.dot_general(
        left, right, (((1,), (1,)), ((), ())), preferred_element_type=jnp.float32
    )


def transposed_times(left, right):
    return lax.dot_general(
        left, right, (((0,), (0,)), ((), ())), preferred_element_type=jnp.float32
    )


def coords(c):
    return (
        lax.div(c, 16),
        lax.rem(lax.div(c, 8), 2),
        lax.rem(lax.div(c, 2), 4),
        lax.rem(c, 2),
    )


def index_of(z, y, x, k):
    return ((z * 2 + y) * 4 + x) * 2 + k


def shifted(me, dz, dy, dx, dk):
    z, y, x, k = coords(me)
    return index_of(lax.rem(z + dz, 4), lax.rem(y + dy, 2), lax.rem(x + dx, 4), lax.rem(k + dk, 2))


def remote(src, dst, send, recv, ctx, wsh):
    return pltpu.make_async_remote_copy(
        src_ref=src,
        dst_ref=dst,
        send_sem=send,
        recv_sem=recv,
        device_id=(ctx, wsh),
        device_id_type=MESH,
    )


def greet(targets):
    barrier = pltpu.get_barrier_semaphore()
    for ctx, wsh in targets:
        pl.semaphore_signal(barrier, inc=1, device_id=(ctx, wsh), device_id_type=MESH)
    return barrier, len(targets)


def greet_many(count, target):
    barrier = pltpu.get_barrier_semaphore()

    def one(step, carried):
        pl.semaphore_signal(barrier, inc=1, device_id=target(step), device_id_type=MESH)
        return carried

    lax.fori_loop(1, count, one, 0)
    return barrier, count - 1


ANY = pl.BlockSpec(memory_space=pl.ANY)
VMEM = pl.BlockSpec(memory_space=pltpu.VMEM)
DMA = pltpu.SemaphoreType.DMA


def cost(microseconds):
    return pl.CostEstimate(flops=0, bytes_accessed=int(microseconds * 1.2e6), transcendentals=0)


ROOM = 56 * 1024 * 1024


def call_params(collective_id):
    return pltpu.CompilerParams(
        collective_id=collective_id, has_side_effects=True, vmem_limit_bytes=ROOM
    )


def row_gather_start(src, out, me, wsh, send, recv):
    place = lax.rem(me, 8)
    copies = []
    for at, (dx, dk) in enumerate(((1, 0), (3, 0), (0, 1))):
        copy = remote(
            src, out.at[place], send.at[at], recv.at[at], shifted(me, 0, 0, dx, dk), wsh
        )
        copy.start()
        copies.append(copy)
    return copies


def row_gather_onward(out, me, wsh, copies, send, recv):
    partner = shifted(me, 0, 0, 0, 1)
    half = out.shape[1] // 2
    onward = []
    forwards = []
    for at, dx in enumerate((1, 3)):
        copies[at].wait_recv()
        from_place = lax.rem(shifted(me, 0, 0, 4 - dx, 0), 8)
        part = out.at[from_place, pl.ds(at * half, half)]
        step = remote(part, part, send.at[3 + at], recv.at[3 + at], shifted(me, 0, 0, dx, 0), wsh)
        step.start()
        onward.append(step)
        block = out.at[from_place]
        forward = remote(block, block, send.at[5 + at], recv.at[5 + at], partner, wsh)
        forward.start()
        forwards.append(forward)
    return onward, forwards


def row_gather_end(out, me, wsh, copies, onward, forwards, send, recv):
    partner = shifted(me, 0, 0, 0, 1)
    half = out.shape[1] // 2
    far = lax.rem(shifted(me, 0, 0, 2, 0), 8)
    for at in (0, 1):
        onward[at].wait_recv()
        part = out.at[far, pl.ds(at * half, half)]
        forward = remote(part, part, send.at[7 + at], recv.at[7 + at], partner, wsh)
        forward.start()
        forwards.append(forward)
    copies[2].wait_recv()
    for copy in copies + onward:
        copy.wait_send()
    for forward in forwards:
        forward.wait()


def cast_steps(steps, staging, lows, in_sems, out_sems):
    loads, stores = [], []
    for index, (src, begin, dst, to, count, at) in enumerate(steps):
        slot, span = index % 2, pl.ds(0, count)
        loads.append(
            pltpu.make_async_copy(
                src.at[pl.ds(begin, count)], staging[at].at[slot, span], in_sems.at[slot]
            )
        )
        stores.append(
            pltpu.make_async_copy(lows[at].at[slot, span], dst.at[pl.ds(to, count)], out_sems.at[slot])
        )
    loads[0].start()
    loads[1].start()
    for index, step in enumerate(steps):
        slot, count, at = index % 2, step[-2], step[-1]
        loads[index].wait()
        if index >= 2:
            stores[index - 2].wait()
        lows[at][slot, :count] = staging[at][slot, :count].astype(BF)
        stores[index].start()
        if index + 2 < len(steps):
            loads[index + 2].start()
    stores[-2].wait()
    stores[-1].wait()


def cut_steps(src, parts, rows, at):
    steps, begin = [], 0
    for part in parts:
        for to in range(0, part.shape[0], rows):
            count = min(rows, part.shape[0] - to)
            steps.append((src, begin + to, part, to, count, at))
        begin += part.shape[0]
    return steps


COLUMN_STEPS = ((1, 0), (3, 0), (0, 1), (2, 0), (1, 1), (3, 1), (2, 1))
ROW_STEPS = ((1, 0), (3, 0), (1, 1), (3, 1), (0, 1), (2, 0), (2, 1))


UP_CUT = (1280, 768)
DOWN_GRAD_CUT = (240, 144)


def gather_first(weights, out_weight, router, gains, tokens, routes, cotangent, expert_weights):
    def body(q_in, k_in, v_in, o_in, ro_in, ga_in, gf_in, t_in, r_in, c_in, *refs):
        sources, refs = refs[:3], refs[3:]
        w_out, t_out, s_out, r_out, c_out = refs[:5]
        gate_out, up_out, up_rest, down_out, side_out, late_out = refs[5:11]
        refs = refs[11:]
        wide, row_s, row_r, pair, local, col_s, col_r, tall_f, flat_f, tall_b, flat_b, in_sems, out_sems = refs[:13]
        w_in, s_in, late_in, late_sem = refs[13:]
        me, wsh = lax.axis_index("ctx"), lax.axis_index("wsh")
        core = lax.rem(me, 2)
        place = lax.rem(me, 8)
        group = lax.div(me, 8)
        partner = shifted(me, 0, 0, 0, 1)
        row_peers = [shifted(me, 0, 0, dx, dk) for dx, dk in ROW_STEPS]
        col_peers = [shifted(me, dz, dy, 0, 0) for dz, dy in COLUMN_STEPS]
        barrier, amount = greet([(peer, wsh) for peer in row_peers + col_peers])
        heads = q_in.shape[1] // 8
        for at in range(8):
            w_in[at, :, :heads] = q_in[:, at * heads : (at + 1) * heads].astype(BF)
            side = (k_in, v_in)[at % 2]
            begin = at // 4 * HEAD_WIDTH
            w_in[at, :, heads:] = side[:, begin : begin + HEAD_WIDTH].astype(BF)
            late_in[at, :, :heads] = o_in[:, at * heads : (at + 1) * heads].astype(BF)
            late_in[at, :, heads:] = ro_in[...].astype(BF)
        s_in[...] = jnp.zeros_like(s_in)
        s_in[0:1, : ga_in.shape[1]] = ga_in[...]
        s_in[1:2, : gf_in.shape[1]] = gf_in[...]
        locals_ = [
            pltpu.make_async_copy(w_in.at[place], w_out.at[me], local.at[0]),
            pltpu.make_async_copy(s_in, s_out.at[me], local.at[1]),
            pltpu.make_async_copy(t_in, t_out.at[place], local.at[2]),
            pltpu.make_async_copy(r_in, r_out.at[core], local.at[3]),
            pltpu.make_async_copy(c_in, c_out.at[core], local.at[4]),
        ]
        for copy in locals_:
            copy.start()
        late_copies = [
            pltpu.make_async_copy(late_in, late_out.at[pl.ds(at * 8, 8)], late_sem.at[at]) for at in range(8)
        ]
        pl.semaphore_wait(barrier, amount)
        for peer in row_peers:
            remote(w_in.at[lax.rem(peer, 8)], w_out.at[me], wide.at[0], wide.at[1], peer, wsh).start()
            remote(s_in, s_out.at[me], wide.at[2], wide.at[3], peer, wsh).start()
        row_copies = row_gather_start(t_in, t_out, me, wsh, row_s, row_r)
        pair_copies = [
            remote(r_in, r_out.at[core], pair.at[0], pair.at[1], partner, wsh),
            remote(c_in, c_out.at[core], pair.at[2], pair.at[3], partner, wsh),
        ]
        for copy in pair_copies:
            copy.start()
        locals_[0].wait()
        locals_[1].wait()
        for at, out in ((0, w_out), (2, s_out)):
            rest = out.at[pl.ds(0, 7)]
            done = remote(rest, rest, wide.at[at], wide.at[at + 1], partner, wsh)
            done.wait_recv()
            done.wait_send()
        lanes = side_out.shape[2]
        depth, columns = w_out.shape[1], w_out.shape[2]

        def share(origin, at):
            blocks = pl.ds(origin * 8, 8)
            part = w_out.at[blocks, pl.ds(0, depth), pl.ds(columns - lanes, lanes)]
            give = remote(part, side_out.at[blocks], col_s.at[2, at], col_r.at[2, at], partner, wsh)
            give.start()
            return give

        mine = pl.ds(group * 8, 8)
        col_copies = []
        for at, peer in enumerate(col_peers):
            for kind, out in enumerate((w_out, s_out)):
                copy = remote(out.at[mine], out.at[mine], col_s.at[kind, at], col_r.at[kind, at], peer, wsh)
                copy.start()
                col_copies.append(copy)
        shares = [share(group, 7)]
        onward, forwards = row_gather_onward(t_out, me, wsh, row_copies, row_s, row_r)
        for copy in late_copies:
            copy.start()
        gate_in, up_in, down_in = [source.at[1 - wsh] for source in sources]
        buffers = ((tall_f, flat_f), (tall_b, flat_b), in_sems, out_sems)
        tall_rows, flat_rows = tall_f.shape[1], flat_f.shape[1]
        cast_steps(
            cut_steps(gate_in, (gate_out,), tall_rows, 0) + cut_steps(up_in, (up_out, up_rest), tall_rows, 0) + cut_steps(down_in, (down_out,), flat_rows, 1),
            *buffers,
        )
        row_gather_end(t_out, me, wsh, row_copies, onward, forwards, row_s, row_r)
        for at, (dz, dy) in enumerate(COLUMN_STEPS):
            col_copies[2 * at].wait_recv()
            col_copies[2 * at + 1].wait_recv()
            shares.append(share(lax.div(shifted(me, 4 - dz, 2 - dy, 0, 0), 8), at))
        for copy in pair_copies + shares + late_copies:
            copy.wait()
        for copy in locals_[2:]:
            copy.wait()
        for copy in col_copies:
            copy.wait_send()

    sds = jax.ShapeDtypeStruct
    _, deep, half = expert_weights[0].shape
    depth, packed = weights[0].shape[0], weights[0].shape[1] // 8 + HEAD_WIDTH
    tall, flat = (deep // 4, half), (half // 4, deep)
    return pl.pallas_call(
        body,
        out_shape=(
            sds((64, depth, packed), BF),
            sds((8,) + tokens.shape, tokens.dtype),
            sds((64, 8, 128), F32),
            sds((2,) + routes.shape, routes.dtype),
            sds((2,) + cotangent.shape, cotangent.dtype),
        )
        + tuple(sds((count, half), BF) for count in (deep, *UP_CUT))
        + (
            sds((half, deep), BF),
            sds((64, depth, 128), BF),
            sds((64, depth, out_weight.shape[1] // 8 + router.shape[1]), BF),
        ),
        in_specs=[VMEM] * 7 + [ANY] * 6,
        out_specs=[ANY] * 11,
        scratch_shapes=[
            DMA((4,)),
            DMA((9,)),
            DMA((9,)),
            DMA((4,)),
            DMA((5,)),
            DMA((3, 8)),
            DMA((3, 8)),
            pltpu.VMEM((2,) + tall, F32),
            pltpu.VMEM((2,) + flat, F32),
            pltpu.VMEM((2,) + tall, BF),
            pltpu.VMEM((2,) + flat, BF),
            DMA((2,)),
            DMA((2,)),
            pltpu.VMEM((8, depth, packed), BF),
            pltpu.VMEM((8, 128), F32),
            pltpu.VMEM((8, depth, out_weight.shape[1] // 8 + router.shape[1]), BF),
            DMA((8,)),
        ],
        compiler_params=call_params(0),
        name="gather_first",
        cost_estimate=cost(40),
    )(*weights, out_weight, router, *gains, tokens, routes, cotangent, *expert_weights)


def gather_row(block, swapped, collective_id):
    def body(src, src2, out, out2, row_s, row_r, pair, local):
        me, wsh = lax.axis_index("ctx"), lax.axis_index("wsh")
        barrier, amount = greet(
            [(shifted(me, 0, 0, dx, dk), wsh) for dx, dk in ((1, 0), (3, 0), (0, 1))] + [(me, 1 - wsh)]
        )
        mine = pltpu.make_async_copy(src, out.at[lax.rem(me, 8)], local)
        mine.start()
        pl.semaphore_wait(barrier, amount)
        copies = row_gather_start(src, out, me, wsh, row_s, row_r)
        cross = remote(src2, out2, pair.at[0], pair.at[1], me, 1 - wsh)
        cross.start()
        onward, forwards = row_gather_onward(out, me, wsh, copies, row_s, row_r)
        row_gather_end(out, me, wsh, copies, onward, forwards, row_s, row_r)
        mine.wait()
        cross.wait()

    return pl.pallas_call(
        body,
        out_shape=(
            jax.ShapeDtypeStruct((8,) + block.shape, block.dtype),
            jax.ShapeDtypeStruct(swapped.shape, swapped.dtype),
        ),
        in_specs=[ANY, ANY],
        out_specs=[ANY, ANY],
        scratch_shapes=[DMA((9,)), DMA((9,)), DMA((2,)), DMA],
        compiler_params=call_params(collective_id),
        name="gather_row",
        cost_estimate=cost(26),
    )(block, swapped)


def gather_keys(rows, routes, cotangent, experts, collective_id):
    chip_rows, deep = cotangent.shape
    slots = experts // 4 * 2 * CAP
    count = rows.shape[0]
    half = count // 2

    def body(src, routes_ref, cot_ref, out, pick_ref, turned_ref, of_ref, hits_ref, rows_out, send, recv, local, rows_ref, rows_sem):
        me, wsh = lax.axis_index("ctx"), lax.axis_index("wsh")
        core = lax.rem(me, 2)
        group = lax.div(me, 8)
        partner = shifted(me, 0, 0, 0, 1)
        across = shifted(me, 0, 1, 0, 0)
        steps = (1, 3, 2)
        peers = [shifted(me, dz, 0, 0, 0) for dz in steps]
        barrier, amount = greet([(peer, wsh) for peer in peers + [across, partner]])
        mine = pltpu.make_async_copy(src, out.at[group], local)
        mine.start()
        pl.semaphore_wait(barrier, amount)
        my_half = pl.ds(pl.multiple_of(core * half, half), half)
        copies = []
        for at, peer in enumerate([across] + peers):
            copy = remote(src.at[my_half], out.at[group, my_half], send.at[at], recv.at[at], peer, wsh)
            copy.start()
            copies.append(copy)
        forwards = []

        def hand_on(origin, at):
            part = out.at[origin, my_half]
            forward = remote(part, part, send.at[7 + at], recv.at[7 + at], partner, wsh)
            forward.start()
            forwards.append(forward)

        copies[0].wait_recv()
        beside = lax.div(across, 8)
        for at, peer in enumerate(peers):
            part = out.at[beside, my_half]
            copy = remote(part, part, send.at[4 + at], recv.at[4 + at], peer, wsh)
            copy.start()
            copies.append(copy)
        hand_on(beside, 0)
        route_rows((core, wsh, lax.rem(group, 2)), routes_ref, cot_ref, pick_ref, turned_ref, of_ref, hits_ref, rows_ref)
        rows_copy = pltpu.make_async_copy(rows_ref, rows_out, rows_sem)
        rows_copy.start()
        for dy in range(2):
            for at, dz in enumerate(steps):
                copies[1 + 3 * dy + at].wait_recv()
                hand_on(lax.div(shifted(me, 4 - dz, dy, 0, 0), 8), 1 + 3 * dy + at)
        for copy in copies:
            copy.wait_send()
        for forward in forwards:
            forward.wait()
        mine.wait()
        rows_copy.wait()

    sds = jax.ShapeDtypeStruct
    return pl.pallas_call(
        body,
        out_shape=(
            sds((8,) + rows.shape, rows.dtype),
            sds((slots, chip_rows), BF),
            sds((chip_rows, slots), BF),
            sds((slots, experts), BF),
            sds((chip_rows, experts), F32),
            sds((slots, deep), BF),
        ),
        in_specs=[ANY, VMEM, VMEM],
        out_specs=[ANY, VMEM, VMEM, VMEM, VMEM, ANY],
        scratch_shapes=[DMA((14,)), DMA((14,)), DMA, pltpu.VMEM((slots, deep), BF), DMA],
        compiler_params=call_params(collective_id),
        name="gather_keys",
        cost_estimate=cost(30),
    )(rows, routes, cotangent)


class Staged:
    def __init__(self, sources, buffers, sems):
        self.copies = [
            pltpu.make_async_copy(src, buffer, sems.at[at])
            for at, (src, buffer) in enumerate(zip(sources, buffers))
        ]
        for copy in self.copies:
            copy.start()

    def ready(self, *which):
        for at in which:
            self.copies[at].wait()

    @staticmethod
    def scratch(values):
        return [pltpu.VMEM(value.shape, value.dtype) for value in values] + [DMA((len(values),))]


class Owned:
    SCRATCH = 10

    def __init__(self, src, out, scratch):
        self.src, self.out = src, out
        self.land_z, self.sum_z, self.land_y, self.reduced, *self.sems = scratch

    @staticmethod
    def scratch(value):
        inner = value.shape[1:]
        return [
            pltpu.VMEM((3, 16) + inner, BF),
            pltpu.VMEM((16,) + inner, BF),
            pltpu.VMEM((8,) + inner, BF),
            pltpu.VMEM((8,) + inner, BF),
            DMA((3,)),
            DMA((3,)),
            DMA((1,)),
            DMA((1,)),
            DMA((7,)),
            DMA((7,)),
        ]

    def along_z(self, me, wsh):
        z, _, _, _ = coords(me)
        self.copies_z = []
        for at, dz in enumerate((1, 3, 2)):
            blocks = pl.ds(lax.rem(z + dz, 4) * 16, 16)
            copy = remote(
                self.src.at[blocks],
                self.land_z.at[at],
                self.sems[0].at[at],
                self.sems[1].at[at],
                shifted(me, dz, 0, 0, 0),
                wsh,
            )
            copy.start()
            self.copies_z.append(copy)

    def along_y(self, me, wsh):
        z, y, _, _ = coords(me)
        value = self.src[pl.ds(z * 16, 16)].astype(F32)
        for at, copy in enumerate(self.copies_z):
            copy.wait_recv()
            value = value + self.land_z[at].astype(F32)
        self.sum_z[...] = value.astype(BF)
        self.copy_y = remote(
            self.sum_z.at[pl.ds((1 - y) * 8, 8)],
            self.land_y,
            self.sems[2].at[0],
            self.sems[3].at[0],
            shifted(me, 0, 1, 0, 0),
            wsh,
        )
        self.copy_y.start()

    def along_row(self, me, wsh):
        _, y, _, _ = coords(me)
        self.copy_y.wait_recv()
        value = self.sum_z[pl.ds(y * 8, 8)].astype(F32) + self.land_y[...].astype(F32)
        self.reduced[...] = value.astype(BF)
        place = lax.rem(me, 8)
        self.copies_row = []
        for at, (dx, dk) in enumerate(ROW_STEPS):
            peer = shifted(me, 0, 0, dx, dk)
            copy = remote(
                self.reduced.at[lax.rem(peer, 8)],
                self.out.at[place],
                self.sems[4].at[at],
                self.sems[5].at[at],
                peer,
                wsh,
            )
            copy.start()
            self.copies_row.append(copy)
        self.out[place] = self.reduced[place]

    def finish(self):
        for copy in self.copies_row:
            copy.wait()
        for copy in self.copies_z + [self.copy_y]:
            copy.wait_send()


def reduce_row(parts, collective_id, both, extra=None, swapped_whole=None, owned=()):
    has_whole = swapped_whole is not None
    is_product = isinstance(parts, tuple)
    if is_product:
        rows, width = parts[0].shape[0] // 8, parts[1].shape[0]
    else:
        _, rows, width = parts.shape
    block = (rows, width)
    pieces = 4
    columns = width // pieces
    has_extra = extra is not None

    def body(*refs):
        refs = list(refs)
        stage_sems = refs.pop(-1)
        buffers = [refs.pop(-1) for _ in staged_values][::-1]
        sources = [refs.pop(0) for _ in staged_values[: len(staged_values) - len(owned)]]
        held = list(buffers)
        if is_product:
            heads_ref, out_w = held.pop(0), held.pop(0)
            src = refs.pop(-1)
        else:
            src = held.pop(0)
        if has_extra:
            pick_ref, back_ref = held.pop(0), held.pop(0)
        src3 = refs.pop(0) if has_whole else None
        sources += [refs.pop(0) for _ in owned]
        mine_in = held
        staged = Staged(sources, buffers, stage_sems)
        out = refs.pop(0)
        out2 = refs.pop(0) if has_extra else None
        out3 = refs.pop(0) if has_whole else None
        mine_out = [refs.pop(0) for _ in owned]
        blocks = []
        for src4, out4 in reversed(list(zip(mine_in, mine_out))):
            blocks.append(Owned(src4, out4, refs[-Owned.SCRATCH :]))
            refs = refs[: -Owned.SCRATCH]
        arrived, summed, landed, swapped, total, send, recv, local = refs[:8]
        me, wsh = lax.axis_index("ctx"), lax.axis_index("wsh")
        other = 1 - wsh
        core = lax.rem(me, 2)
        _, _, x, _ = coords(me)
        partner = shifted(me, 0, 0, 0, 1)
        peers = [shifted(me, 0, 0, dx, 0) for dx in (1, 2, 3)]
        row_peers = [shifted(me, 0, 0, dx, dk) for dx, dk in ROW_STEPS]
        col_peers = [shifted(me, dz, dy, 0, 0) for dz, dy in COLUMN_STEPS]
        greeted = row_peers + col_peers if owned else peers + [partner]
        barrier, amount = greet([(peer, wsh) for peer in greeted] + [(me, other)])
        pl.semaphore_wait(barrier, amount)
        staged.ready(*range(2 if is_product else 1))
        if has_whole:
            whole = remote(
                src3, out3, send.at[1, 9], recv.at[1, 9], me, other
            )
            whole.start()
        spans = [pl.ds(piece * columns, columns) for piece in range(pieces)]
        everything = pl.ds(0, rows)
        first = []
        for piece, span in enumerate(spans):
            if is_product:
                columns_of = slice(piece * columns, (piece + 1) * columns)
                src[:, :, columns_of] = (
                    times_transposed(heads_ref[...], out_w[columns_of, : heads_ref.shape[1]])
                    .astype(BF)
                    .reshape(8, rows, columns)
                )
            for at, dx in enumerate((2, 1, 3, 0)):
                chip = lax.rem(x + dx, 4)
                copy = remote(
                    src.at[chip * 2 + 1 - core, everything, span],
                    arrived.at[at, everything, span],
                    send.at[piece, at],
                    recv.at[piece, at],
                    partner,
                    wsh,
                )
                copy.start()
                first.append(copy)
        staged.ready(*range(len(staged_values) - len(owned), len(staged_values)))
        for block4 in blocks:
            block4.along_z(me, wsh)
        if has_extra:
            staged.ready(1, 2)
            arrived2, swapped2, src2 = refs[8:]
            src2[...] = matmul(pick_ref[...], back_ref[...]).astype(BF).reshape(src2.shape)
            give2 = remote(src2.at[1 - core], arrived2, send.at[0, 8], recv.at[0, 8], partner, wsh)
            give2.start()
        second = []
        for piece, span in enumerate(spans):
            for at, dx in enumerate((2, 1, 3)):
                chip = lax.rem(x + dx, 4)
                first[piece * 4 + at].wait_recv()
                summed[at, :, span] = (
                    src[chip * 2 + core, :, span].astype(F32) + arrived[at, :, span].astype(F32)
                ).astype(BF)
                copy = remote(
                    summed.at[at, everything, span],
                    landed.at[at, everything, span],
                    send.at[piece, 4 + at],
                    recv.at[piece, 4 + at],
                    shifted(me, 0, 0, dx, 0),
                    wsh,
                )
                copy.start()
                second.append(copy)
            first[piece * 4 + 3].wait_recv()
            total[:, span] = src[x * 2 + core, :, span].astype(F32) + arrived[3, :, span].astype(F32)
        if has_extra:
            give2.wait()
            swapped2[0] = (src2[core].astype(F32) + arrived2[...].astype(F32)).astype(BF)
            swap2 = remote(swapped2.at[0], swapped2.at[1], send.at[1, 8], recv.at[1, 8], me, other)
            swap2.start()
        swaps = []
        for piece, span in enumerate(spans):
            for at in (1, 2, 0):
                second[piece * 3 + at].wait_recv()
            swapped[0, :, span] = (
                total[:, span]
                + landed[0, :, span].astype(F32)
                + landed[1, :, span].astype(F32)
                + landed[2, :, span].astype(F32)
            ).astype(BF)
            swap = remote(
                swapped.at[0, everything, span],
                swapped.at[1, everything, span],
                send.at[piece, 7],
                recv.at[piece, 7],
                me,
                other,
            )
            swap.start()
            swaps.append(swap)
            if piece == pieces - 2:
                for block4 in blocks:
                    block4.along_y(me, wsh)
        for block4 in blocks:
            block4.along_row(me, wsh)
        if has_extra:
            swap2.wait()
            out2[...] = swapped2[0].astype(F32) + swapped2[1].astype(F32)
        for piece, span in enumerate(spans):
            swaps[piece].wait()
            if both:
                total[:, span] = swapped[0, :, span].astype(F32) + swapped[1, :, span].astype(F32)
            else:
                out[:, span] = swapped[0, :, span].astype(F32) + swapped[1, :, span].astype(F32)
        if both:
            keep = pltpu.make_async_copy(total, out.at[core], local)
            keep.start()
            give = remote(total, out.at[core], send.at[0, 9], recv.at[0, 9], partner, wsh)
            give.start()
            give.wait()
            keep.wait()
        for copy in first + second:
            copy.wait_send()
        for block4 in blocks:
            block4.finish()
        if has_whole:
            whole.wait()

    shapes = [jax.ShapeDtypeStruct((2,) + block if both else block, F32)]
    scratch = [
        pltpu.VMEM((4,) + block, BF),
        pltpu.VMEM((3,) + block, BF),
        pltpu.VMEM((3,) + block, BF),
        pltpu.VMEM((2,) + block, BF),
        pltpu.VMEM(block, F32),
        DMA((pieces, 10)),
        DMA((pieces, 10)),
        DMA,
    ]
    operands = list(parts) if is_product else [parts]
    out_spaces = [VMEM]
    if has_extra:
        shapes.append(jax.ShapeDtypeStruct(block, F32))
        scratch += [pltpu.VMEM(block, BF), pltpu.VMEM((2,) + block, BF), pltpu.VMEM((2,) + block, BF)]
        operands += list(extra)
        out_spaces.append(VMEM)
    spaces = [ANY] * len(operands)
    staged_values = list(operands) + list(owned)
    if has_whole:
        shapes.append(jax.ShapeDtypeStruct(swapped_whole.shape, swapped_whole.dtype))
        operands.append(swapped_whole)
        spaces.append(ANY)
        out_spaces.append(ANY)
    for value in owned:
        block8 = (8,) + value.shape[1:]
        shapes.append(jax.ShapeDtypeStruct(block8, BF))
        operands.append(value)
        spaces.append(ANY)
        out_spaces.append(VMEM)
        scratch += Owned.scratch(value)
    if is_product:
        scratch.append(pltpu.VMEM((8,) + block, BF))
    scratch += Staged.scratch(staged_values)
    return pl.pallas_call(
        body,
        out_shape=shapes,
        in_specs=spaces,
        out_specs=out_spaces,
        scratch_shapes=scratch,
        compiler_params=call_params(collective_id),
        name="reduce_row",
        cost_estimate=cost(1),
    )(*operands)


def reduce_chip(pick, back, of_expert, width, collective_id):
    rows = pick.shape[0] // 2
    lanes = of_expert.shape[1]

    def body(pick_in, back_in, of_in, out, out2, src, src2, arrived, swapped, arrived2, swapped2, send, recv, pick_ref, back_ref, of_ref, sems):
        staged = Staged((pick_in, back_in, of_in), (pick_ref, back_ref, of_ref), sems)
        me, wsh = lax.axis_index("ctx"), lax.axis_index("wsh")
        other = 1 - wsh
        core = lax.rem(me, 2)
        partner = shifted(me, 0, 0, 0, 1)
        barrier, amount = greet([(partner, wsh), (me, other)])
        staged.ready(0, 1, 2)
        src[...] = matmul(pick_ref[...], back_ref[:, :width]).astype(BF).reshape(src.shape)
        parts = [back_ref[:, at : at + 1] * of_ref[...] for at in (width, width + 64)]
        src2[...] = (matmul(pick_ref[...], parts[0]) + matmul(pick_ref[...], parts[1])).reshape(src2.shape)
        pl.semaphore_wait(barrier, amount)
        give = remote(src.at[1 - core], arrived, send.at[0], recv.at[0], partner, wsh)
        give.start()
        give2 = remote(src2.at[1 - core], arrived2, send.at[2], recv.at[2], partner, wsh)
        give2.start()
        give.wait()
        swapped[0] = (src[core].astype(F32) + arrived[...].astype(F32)).astype(BF)
        swap = remote(swapped.at[0], swapped.at[1], send.at[1], recv.at[1], me, other)
        swap.start()
        give2.wait()
        swapped2[0] = src2[core] + arrived2[...]
        swap2 = remote(swapped2.at[0], swapped2.at[1], send.at[3], recv.at[3], me, other)
        swap2.start()
        swap2.wait()
        out2[...] = swapped2[0] + swapped2[1]
        swap.wait()
        out[...] = swapped[0].astype(F32) + swapped[1].astype(F32)

    sds = jax.ShapeDtypeStruct
    block, block2 = (rows, width), (rows, lanes)
    return pl.pallas_call(
        body,
        out_shape=(sds(block, F32), sds(block2, F32)),
        in_specs=[ANY] * 3,
        out_specs=[VMEM] * 2,
        scratch_shapes=[
            pltpu.VMEM((2,) + block, BF),
            pltpu.VMEM((2,) + block2, F32),
            pltpu.VMEM(block, BF),
            pltpu.VMEM((2,) + block, BF),
            pltpu.VMEM(block2, F32),
            pltpu.VMEM((2,) + block2, F32),
            DMA((4,)),
            DMA((4,)),
        ]
        + Staged.scratch((pick, back, of_expert)),
        compiler_params=call_params(collective_id),
        name="reduce_chip",
        cost_estimate=cost(17),
    )(pick, back, of_expert)


def reduce_keys(parts, owned, swapped, collective_id):
    _, groups, _, rows, width = parts.shape

    def body(src_in, src4_in, src5, out, out4, out5, arrived, mid, beside, summed, landed, send, recv, pair, *scratch4):
        src, src4, sems = scratch4[-3:]
        staged = Staged((src_in, src4_in), (src, src4), sems)
        block4 = Owned(src4, out4, scratch4[:-3])
        me, wsh = lax.axis_index("ctx"), lax.axis_index("wsh")
        core = lax.rem(me, 2)
        _, _, x, _ = coords(me)
        side = lax.rem(x, 2)
        partner = shifted(me, 0, 0, 0, 1)
        neighbour = me + 2 - 4 * side
        steps = COLUMN_STEPS + ((0, 0),)
        peers = [shifted(me, dz, dy, 0, 0) for dz, dy in steps]
        row_peers = [shifted(me, 0, 0, dx, dk) for dx, dk in ROW_STEPS]
        barrier, amount = greet([(peer, wsh) for peer in peers[:-1] + row_peers] + [(me, 1 - wsh)])
        pl.semaphore_wait(barrier, amount)
        staged.ready(0, 1)
        first = []
        for at, peer in enumerate(peers):
            group = lax.div(peer, 8)
            for turn, b in enumerate((1 - side, side)):
                copy = remote(
                    src.at[1 - core, group, b],
                    arrived.at[turn, at],
                    send.at[turn, at],
                    recv.at[turn, at],
                    partner,
                    wsh,
                )
                copy.start()
                first.append(copy)
        block4.along_z(me, wsh)
        cross = remote(src5, out5, pair.at[0], pair.at[1], me, 1 - wsh)
        cross.start()
        across = []
        for at, peer in enumerate(peers):
            group = lax.div(peer, 8)
            first[2 * at].wait_recv()
            mid[at] = (src[core, group, 1 - side].astype(F32) + arrived[0, at].astype(F32)).astype(BF)
            copy = remote(mid.at[at], beside.at[at], send.at[2, at], recv.at[2, at], neighbour, wsh)
            copy.start()
            across.append(copy)
        last = []
        for at, peer in enumerate(peers):
            group = lax.div(peer, 8)
            first[2 * at + 1].wait_recv()
            across[at].wait_recv()
            value = (
                src[core, group, side].astype(F32)
                + arrived[1, at].astype(F32)
                + beside[at].astype(F32)
            )
            if at == groups - 1:
                out[...] = value
            else:
                summed[at] = value.astype(BF)
                copy = remote(summed.at[at], landed.at[at], send.at[3, at], recv.at[3, at], peer, wsh)
                copy.start()
                last.append(copy)
            if at == 5:
                block4.along_y(me, wsh)
        block4.along_row(me, wsh)
        for at, copy in enumerate(last):
            copy.wait_recv()
            out[...] += landed[at].astype(F32)
        for copy in first + across + last:
            copy.wait_send()
        block4.finish()
        cross.wait()

    block = (rows, width)
    return pl.pallas_call(
        body,
        out_shape=(
            jax.ShapeDtypeStruct(block, F32),
            jax.ShapeDtypeStruct((8,) + owned.shape[1:], BF),
            jax.ShapeDtypeStruct(swapped.shape, swapped.dtype),
        ),
        in_specs=[ANY, ANY, ANY],
        out_specs=[VMEM, VMEM, ANY],
        scratch_shapes=[
            pltpu.VMEM((2, groups) + block, BF),
            pltpu.VMEM((groups,) + block, BF),
            pltpu.VMEM((groups,) + block, BF),
            pltpu.VMEM((groups,) + block, BF),
            pltpu.VMEM((groups,) + block, BF),
            DMA((4, groups)),
            DMA((4, groups)),
            DMA((2,)),
        ]
        + Owned.scratch(owned)
        + Staged.scratch((parts, owned)),
        compiler_params=call_params(collective_id),
        name="reduce_keys",
        cost_estimate=cost(40),
    )(parts, owned, swapped)


def exchange(arrays, collective_id):
    amount = len(arrays)

    def body(*refs):
        ins, outs = refs[:amount], refs[amount : 2 * amount]
        send, recv, local = refs[2 * amount :]
        me, wsh = lax.axis_index("ctx"), lax.axis_index("wsh")
        chip = lax.div(me, 2)

        def target(step):
            dy = lax.rem(lax.div(step, 4), 2)
            return shifted(me, lax.div(step, 8), dy, lax.rem(step, 4), 0), lax.rem(wsh + dy, 2)

        barrier, count = greet_many(32, target)
        locals_ = []
        for at in range(amount):
            copy = pltpu.make_async_copy(ins[at].at[chip], outs[at].at[chip], local.at[at])
            copy.start()
            locals_.append(copy)
        pl.semaphore_wait(barrier, count)

        def one(step, carried):
            ctx, side = target(lax.rem(step * 27, 32))
            for at in range(amount):
                remote(
                    ins[at].at[lax.div(ctx, 2)], outs[at].at[chip], send.at[at], recv.at[at], ctx, side
                ).start()
            return carried

        lax.fori_loop(1, 32, one, 0)
        for copy in locals_:
            copy.wait()
        for at in range(amount):
            rest = outs[at].at[pl.ds(0, 31)]
            done = remote(rest, rest, send.at[at], recv.at[at], me, wsh)
            done.wait_send()
            done.wait_recv()

    return pl.pallas_call(
        body,
        out_shape=[jax.ShapeDtypeStruct(a.shape, a.dtype) for a in arrays],
        in_specs=[ANY] * amount,
        out_specs=[ANY] * amount,
        scratch_shapes=[DMA((amount,)), DMA((amount,)), DMA((amount,))],
        compiler_params=call_params(collective_id),
        name="exchange",
        cost_estimate=cost(48),
    )(*arrays)


def exchange_behind(value):
    groups = []
    for core in range(2):
        for parity in range(2):
            groups.append(
                [(chip * 2 + core) * 2 + (parity + chip // 4) % 2 for chip in range(32)]
            )
    return lax.all_to_all(
        value, ("ctx", "wsh"), split_axis=0, concat_axis=0, tiled=True, axis_index_groups=groups
    )


def natural_order(plan, kv_ref, keys, values, transposed):
    def one(block, carried):
        rows = kv_ref[pl.ds(pl.multiple_of(plan[PLAN_INVERSE + block] * BLK, BLK), BLK), :]
        at = pl.ds(pl.multiple_of(block * BLK, BLK), BLK)
        keys[at, :] = rows[:, :HEAD_WIDTH]
        values[at, :] = rows[:, HEAD_WIDTH:]
        return carried

    lax.fori_loop(0, kv_ref.shape[0] // BLK, one, 0, unroll=8)
    source, turned = transposed

    def turn(chunk, carried):
        at = pl.ds(pl.multiple_of(chunk * CHUNK, CHUNK), CHUNK)
        turned[:, at] = source[at, :].T
        return carried

    lax.fori_loop(0, kv_ref.shape[0] // CHUNK, turn, 0, unroll=4)


def stacked(ref, first, second):
    rows = [ref[pl.ds(pl.multiple_of(at * BLK, BLK), BLK), :] for at in (first, second)]
    return jnp.concatenate(
        [rows[0][:, :HEAD_WIDTH], rows[0][:, HEAD_WIDTH:], rows[1][:, :HEAD_WIDTH], rows[1][:, HEAD_WIDTH:]],
        axis=0,
    )


def unstacked(ref, first, second, value):
    for at, begin in ((first, 0), (second, 2 * BLK)):
        ref[pl.ds(pl.multiple_of(at * BLK, BLK), BLK), :] = jnp.concatenate(
            [value[begin : begin + BLK], value[begin + BLK : begin + 2 * BLK]], axis=1
        )


PLAN_BOUNDS, PLAN_INVERSE, PLAN_BLOCKS, PLAN_SIZE = 16, 64, 192, 256


def start_of(lengths, position):
    begin = lengths[0] * 0
    start = position * 0
    for at in range(lengths.shape[0]):
        start = jnp.where(begin <= position, begin, start)
        begin = begin + lengths[at]
    return start


def make_plan(block_order, lengths, base, plan):
    def place(at, carried):
        plan[PLAN_INVERSE + block_order[at]] = at
        return carried

    lax.fori_loop(0, block_order.shape[0], place, 0, unroll=8)

    def rank(at, carried):
        mine = block_order[base + at]
        before = jnp.int32(0)
        for other in range(16):
            before = before + jnp.where(block_order[base + other] < mine, 1, 0)
        plan[before] = at
        plan[PLAN_BLOCKS + before] = mine
        return carried

    lax.fori_loop(0, 16, rank, 0)

    def bound(step, carried):
        one, two = plan[PLAN_BLOCKS + 2 * step], plan[PLAN_BLOCKS + 2 * step + 1]
        low = lax.div(start_of(lengths, one * BLK), CHUNK)
        high = lax.div(two * BLK, CHUNK) + 1
        last = start_of(lengths, two * BLK + BLK - 1)
        inner_low = jnp.minimum(jnp.maximum(lax.div(last + CHUNK - 1, CHUNK), low), high)
        inner_high = jnp.minimum(jnp.maximum(lax.div(one * BLK + 1, CHUNK), inner_low), high)
        for at, value in enumerate((low, inner_low, inner_high, high)):
            plan[PLAN_BOUNDS + 4 * step + at] = value
        return carried

    lax.fori_loop(0, 8, bound, 0)


def strips_of(plan, lengths, step):
    lane = lax.broadcasted_iota(jnp.int32, (1, 4 * BLK), 1)
    block = jnp.where(lane < 2 * BLK, plan[PLAN_BLOCKS + 2 * step], plan[PLAN_BLOCKS + 2 * step + 1])
    position = block * BLK + lax.rem(lane, BLK)
    return position, start_of(lengths, position)


def three_loops(step, plan, chunk, state):
    low, inner_low, inner_high, high = [plan[PLAN_BOUNDS + 4 * step + at] for at in range(4)]
    state = lax.fori_loop(low, inner_low, functools.partial(chunk, True), state)
    state = lax.fori_loop(inner_low, inner_high, functools.partial(chunk, False), state)
    return lax.fori_loop(inner_high, high, functools.partial(chunk, True), state)


def kept(scores, at, q_pos, q_start):
    k_pos = at + lax.broadcasted_iota(jnp.int32, scores.shape, 0)
    return jnp.where((k_pos <= q_pos) & (k_pos >= q_start), scores, MASKED)


SCORE_SCALE = 1.0 / math.sqrt(HEAD_WIDTH)
TWO_SCALE = SCORE_SCALE / math.log(2.0)


def forward_kernel(block_order, lengths, group, q_ref, kv_ref, out_ref, lse_ref, plan, keys, values, values_t, acc):
    step = pl.program_id(0)

    @pl.when(step == 0)
    def _():
        make_plan(block_order, lengths, group[0] * 16, plan)
        natural_order(plan, kv_ref, keys, values, (values, values_t))

    first, second = plan[2 * step], plan[2 * step + 1]
    q_t = stacked(q_ref, first, second).astype(F32).T.astype(BF)
    q_pos, q_start = strips_of(plan, lengths, step)
    width = 4 * BLK
    acc[...] = jnp.zeros_like(acc)

    def chunk(masked, index, total):
        at = pl.multiple_of(index * CHUNK, CHUNK)
        scores = matmul(keys[pl.ds(at, CHUNK), :], q_t)
        if masked:
            scores = kept(scores, at, q_pos, q_start)
        probs = jnp.exp2(scores * TWO_SCALE)
        acc[...] += matmul(values_t[:, pl.ds(at, CHUNK)], probs.astype(BF))
        return total + jnp.sum(probs, axis=0, keepdims=True)

    total = three_loops(step, plan, chunk, jnp.zeros((1, width), F32))
    lse_ref[0] = jnp.log2(total)
    unstacked(out_ref, first, second, (acc[...] / total).T.astype(BF))


def attend(block_order, lengths, group, queries, kv):
    rows = queries.shape[0]
    steps = rows // (2 * BLK)
    everything = pl.BlockSpec(queries.shape, lambda i, *_: (0, 0))
    strip = pl.BlockSpec((1, 1, 4 * BLK), lambda i, *_: (i, 0, 0))
    sds = jax.ShapeDtypeStruct
    return pl.pallas_call(
        forward_kernel,
        out_shape=(
            sds(queries.shape, BF),
            sds((steps, 1, 4 * BLK), F32),
            sds((PLAN_SIZE,), jnp.int32),
        ),
        grid_spec=pltpu.PrefetchScalarGridSpec(
            num_scalar_prefetch=3,
            grid=(steps,),
            in_specs=[everything, pl.BlockSpec(kv.shape, lambda i, *_: (0, 0))],
            out_specs=[everything, strip, pl.BlockSpec(memory_space=pltpu.SMEM)],
            scratch_shapes=[
                pltpu.VMEM((kv.shape[0], HEAD_WIDTH), BF),
                pltpu.VMEM((kv.shape[0], HEAD_WIDTH), BF),
                pltpu.VMEM((HEAD_WIDTH, kv.shape[0]), BF),
                pltpu.VMEM((HEAD_WIDTH, 4 * BLK), F32),
            ],
        ),
        compiler_params=pltpu.CompilerParams(vmem_limit_bytes=ROOM),
        name="attend",
        cost_estimate=cost(17),
    )(block_order, lengths, group, queries, kv)


def backward_kernel(plan, lengths, q_ref, heads_ref, da_in, wo_ref, kv_ref, lse_ref, part_ref, dq_ref, dkv_out, early_ref, keys, values, keys_t, d_keys, d_values, acc, da_ref, dkv_ref, sems):
    step = pl.program_id(0)
    load = pltpu.make_async_copy(da_in, da_ref, sems.at[0])
    store = pltpu.make_async_copy(dkv_ref, dkv_out, sems.at[1])

    @pl.when(step == 0)
    def _():
        load.start()
        natural_order(plan, kv_ref, keys, values, (keys, keys_t))
        d_keys[...] = jnp.zeros_like(d_keys)
        d_values[...] = jnp.zeros_like(d_values)
        load.wait()

    first, second = plan[2 * step], plan[2 * step + 1]
    q = stacked(q_ref, first, second)
    d_rows = matmul(
        jnp.concatenate(
            [da_ref[pl.ds(pl.multiple_of(at * BLK, BLK), BLK), :] for at in (first, second)], axis=0
        ),
        wo_ref[...],
    )
    d_out = jnp.concatenate(
        [
            d_rows[begin : begin + BLK, head : head + HEAD_WIDTH]
            for begin in (0, BLK)
            for head in (0, HEAD_WIDTH)
        ],
        axis=0,
    ).astype(BF)
    q_t = q.astype(F32).T.astype(BF)
    d_out_wide = d_out.astype(F32).T
    d_out_t = d_out_wide.astype(BF)
    q_pos, q_start = strips_of(plan, lengths, step)
    lse = lse_ref[0]
    dots = jnp.sum(d_out_wide * stacked(heads_ref, first, second).astype(F32).T, axis=0, keepdims=True)
    acc[...] = jnp.zeros_like(acc)

    def chunk(masked, index, carried):
        at = pl.multiple_of(index * CHUNK, CHUNK)
        here = pl.ds(at, CHUNK)
        scores = matmul(keys[here, :], q_t)
        if masked:
            scores = kept(scores, at, q_pos, q_start)
        probs = jnp.exp2(scores * TWO_SCALE - lse)
        d_probs = matmul(values[here, :], d_out_t)
        d_scores = (probs * (d_probs - dots)).astype(BF)
        d_values[here, :] += matmul(probs.astype(BF), d_out)
        d_keys[here, :] += matmul(d_scores, q)
        acc[...] += matmul(keys_t[:, here], d_scores)
        return carried

    three_loops(step, plan, chunk, 0)
    unstacked(dq_ref, first, second, (acc[...] * SCORE_SCALE).T)

    @pl.when(step == pl.num_programs(0) - 1)
    def _():
        def one(block, carried):
            dealt = plan[PLAN_INVERSE + block]
            group, inside = dealt // 16, dealt % 16
            half, rest = inside // 8, inside % 8
            at = pl.ds(pl.multiple_of(block * BLK, BLK), BLK)
            to = pl.ds(pl.multiple_of(rest * BLK, BLK), BLK)
            dkv_ref[half, group, 0, to, :] = (d_keys[at, :] * SCORE_SCALE).astype(BF)
            dkv_ref[half, group, 1, to, :] = d_values[at, :].astype(BF)
            return carried

        lax.fori_loop(0, kv_ref.shape[0] // BLK, one, 0, unroll=4)
        store.start()
        owners = early_ref.shape[0]
        depth = da_ref.shape[1] // owners
        span = 256
        for at in range(da_ref.shape[1] // span):
            value = transposed_times(da_ref[:, at * span : (at + 1) * span], heads_ref[...])
            some = slice(at * span // depth, (at + 1) * span // depth)
            for head in range(2):
                early_ref[some, head * depth : (head + 1) * depth, :] = (
                    value[:, head * HEAD_WIDTH : (head + 1) * HEAD_WIDTH]
                    .astype(BF)
                    .reshape(span // depth, depth, HEAD_WIDTH)
                )
        early_ref[:, 2 * depth :, :] = part_ref[...]
        store.wait()


def attend_back(plan, lengths, queries, heads, d_attn, wo_t, kv, lse, part):
    rows = queries.shape[0]
    total = kv.shape[0]
    steps = rows // (2 * BLK)
    everything = pl.BlockSpec(queries.shape, lambda i, *_: (0, 0))
    strip = pl.BlockSpec((1, 1, 4 * BLK), lambda i, *_: (i, 0, 0))
    sds = jax.ShapeDtypeStruct
    owners = part.shape[0]
    early_shape = (owners, part.shape[1] + 2 * d_attn.shape[1] // owners, HEAD_WIDTH)
    dkv_shape = (2, total // rows, 2, rows // 2, HEAD_WIDTH)
    return pl.pallas_call(
        backward_kernel,
        out_shape=(sds(queries.shape, F32), sds(dkv_shape, BF), sds(early_shape, BF)),
        grid_spec=pltpu.PrefetchScalarGridSpec(
            num_scalar_prefetch=2,
            grid=(steps,),
            in_specs=[
                everything,
                everything,
                ANY,
                pl.BlockSpec((wo_t.shape[0], queries.shape[1]), lambda i, *_: (0, 0)),
                pl.BlockSpec(kv.shape, lambda i, *_: (0, 0)),
                strip,
                pl.BlockSpec(part.shape, lambda i, *_: (0, 0, 0)),
            ],
            out_specs=[
                everything,
                ANY,
                pl.BlockSpec(early_shape, lambda i, *_: (0, 0, 0)),
            ],
            scratch_shapes=[
                pltpu.VMEM((total, HEAD_WIDTH), BF),
                pltpu.VMEM((total, HEAD_WIDTH), BF),
                pltpu.VMEM((HEAD_WIDTH, total), BF),
                pltpu.VMEM((total, HEAD_WIDTH), F32),
                pltpu.VMEM((total, HEAD_WIDTH), F32),
                pltpu.VMEM((HEAD_WIDTH, 4 * BLK), F32),
                pltpu.VMEM(d_attn.shape, BF),
                pltpu.VMEM(dkv_shape, BF),
                DMA((2,)),
            ],
        ),
        compiler_params=pltpu.CompilerParams(vmem_limit_bytes=ROOM),
        name="attend_back",
        cost_estimate=cost(24),
    )(plan, lengths, queries, heads, d_attn, wo_t, kv, lse, part)


def expert_kernel(side, x_ref, cot_ref, gate_ref, g_own, u_own, d_own, g_other, u_other, u_rest, d_other, y_ref, dx_ref, a_ref, dg_ref, du_ref, dy_ref, gate_w, up_w, down_w, gate_f, up_f, down_f, sems):
    half = gate_f.shape[1]
    own_copies, other_copies = [], []
    for at, (own, others, whole, stage) in enumerate(
        (
            (g_own, (g_other,), gate_w, gate_f),
            (u_own, (u_other, u_rest), up_w, up_f),
            (d_own, (d_other,), down_w, down_f),
        )
    ):
        own_copies.append(pltpu.make_async_copy(own.at[side[0]], stage, sems.at[at, 0]))
        begin = 0
        other_copies.append([])
        for which, part in enumerate(others):
            count = part.shape[0]
            if at < 2:
                target = whole.at[pl.ds(begin, count), pl.ds(half, half)]
            else:
                target = whole.at[pl.ds(half, half)]
            other_copies[at].append(pltpu.make_async_copy(part, target, sems.at[at, 1 + which]))
            begin += count

    @pl.when(pl.program_id(0) == 0)
    def _():
        for which in range(3):
            own_copies[which].start()
            for copy in other_copies[which]:
                copy.start()

    def ready(which, fill):
        @pl.when(pl.program_id(0) == 0)
        def _():
            own_copies[which].wait()
            fill()
            for copy in other_copies[which]:
                copy.wait()

    def fill_gate():
        gate_w[:, :half] = gate_f[...].astype(BF)

    def fill_up():
        up_w[:, :half] = up_f[...].astype(BF)

    def fill_down():
        down_w[:half, :] = down_f[...].astype(BF)

    x = x_ref[...]
    ready(0, fill_gate)
    gate_pre = matmul(x, gate_w[...])
    ready(1, fill_up)
    up_pre = matmul(x, up_w[...])
    ready(2, fill_down)
    sigma = 1.0 / (1.0 + jnp.exp(-gate_pre))
    silu = gate_pre * sigma
    activated = (silu * up_pre).astype(BF)
    a_ref[...] = activated
    gates = gate_ref[:, 0:1].astype(F32) + gate_ref[:, 64:65].astype(F32)
    cot = cot_ref[...].astype(F32)
    out = matmul(activated, down_w[...])
    y_ref[...] = (out * gates).astype(BF)
    dots = jnp.sum(out * cot, axis=1, keepdims=True)
    high = dots.astype(BF).astype(F32)
    lane = lax.broadcasted_iota(jnp.int32, (dots.shape[0], 128), 1)
    dx_ref[:, y_ref.shape[1] :] = jnp.where(lane < 64, high, dots - high).astype(BF)
    d_pairs = (cot * gates).astype(BF)
    dy_ref[...] = d_pairs
    d_act = times_transposed(d_pairs, down_w[...])
    d_gate = (d_act * up_pre * sigma * (1.0 + gate_pre * (1.0 - sigma))).astype(BF)
    d_up = (d_act * silu).astype(BF)
    dg_ref[...] = d_gate
    du_ref[...] = d_up
    dx_ref[:, : y_ref.shape[1]] = (times_transposed(d_gate, gate_w[...]) + times_transposed(d_up, up_w[...])).astype(BF)


def run_expert(side, rows_in, cot, gates, own, other):
    count, width = rows_in.shape
    half = own[0].shape[2]
    tile = 256
    sds = jax.ShapeDtypeStruct

    def by_rows(columns):
        return pl.BlockSpec((tile, columns), lambda i, side: (i, 0))

    return pl.pallas_call(
        expert_kernel,
        out_shape=(
            sds((count, width), BF),
            sds((count, width + 128), BF),
            sds((count, 2 * half), BF),
            sds((count, 2 * half), BF),
            sds((count, 2 * half), BF),
            sds((count, width), BF),
        ),
        grid_spec=pltpu.PrefetchScalarGridSpec(
            num_scalar_prefetch=1,
            grid=(count // tile,),
            in_specs=[by_rows(width), by_rows(width), by_rows(128)] + [ANY] * 7,
            out_specs=[
                by_rows(width),
                by_rows(width + 128),
                by_rows(2 * half),
                by_rows(2 * half),
                by_rows(2 * half),
                by_rows(width),
            ],
            scratch_shapes=[
                pltpu.VMEM((width, 2 * half), BF),
                pltpu.VMEM((width, 2 * half), BF),
                pltpu.VMEM((2 * half, width), BF),
                pltpu.VMEM((width, half), F32),
                pltpu.VMEM((width, half), F32),
                pltpu.VMEM((half, width), F32),
                DMA((3, 3)),
            ],
        ),
        compiler_params=pltpu.CompilerParams(vmem_limit_bytes=ROOM),
        name="run_expert",
        cost_estimate=cost(25),
    )(side, rows_in, cot, gates, *own, *other)


def gate_grads_kernel(side, x_ref, dg_ref, gate_ref, gate_out):
    half = gate_ref.shape[-1]
    value = matmul(x_ref[...].T, dg_ref[...])
    gate_ref[0] = value[:, :half]
    gate_out[...] = value[:, half:].astype(BF)


def gate_grads(side, rows_in, d_gate):
    count, width = rows_in.shape
    whole = d_gate.shape[1]
    half = whole // 2
    tile = 1024
    sds = jax.ShapeDtypeStruct
    return pl.pallas_call(
        gate_grads_kernel,
        out_shape=(sds((2, width, half), F32), sds((width, half), BF)),
        grid_spec=pltpu.PrefetchScalarGridSpec(
            num_scalar_prefetch=1,
            grid=(width // tile,),
            in_specs=[
                pl.BlockSpec((count, tile), lambda i, side: (0, i)),
                pl.BlockSpec((count, whole), lambda i, side: (0, 0)),
            ],
            out_specs=[
                pl.BlockSpec((1, tile, half), lambda i, side: (side[0], i, 0)),
                pl.BlockSpec((tile, half), lambda i, side: (i, 0)),
            ],
        ),
        compiler_params=pltpu.CompilerParams(vmem_limit_bytes=ROOM),
        name="gate_grads",
        cost_estimate=cost(5),
    )(side, rows_in, d_gate)


def expert_grads_kernel(side, x_ref, dy_ref, a_ref, du_ref, up_ref, down_ref, up_out, up_rest, down_out, down_rest, a_t):
    half = up_ref.shape[-1]
    step = pl.program_id(0)
    turn_at = up_out.shape[0]

    @pl.when(step == 0)
    def _():
        a_t[...] = a_ref[...].T

    value = matmul(x_ref[...].T, du_ref[...])
    up_ref[0] = value[:, :half]
    low = value[:, half:].astype(BF)

    @pl.when(step < UP_CUT[0] // turn_at)
    def _():
        up_out[...] = low

    @pl.when(step >= UP_CUT[0] // turn_at)
    def _():
        up_rest[...] = low

    value = matmul(a_t[...], dy_ref[...])
    down_ref[0] = value[:half]
    cut = half + down_out.shape[0]
    down_out[...] = value[half:cut].astype(BF)
    down_rest[...] = value[cut:].astype(BF)


def expert_grads(side, rows_in, d_pairs, activated, d_up):
    count, width = rows_in.shape
    whole = activated.shape[1]
    half = whole // 2
    tile = 256
    first = UP_CUT[0] // tile
    sds = jax.ShapeDtypeStruct
    columns = pl.BlockSpec((count, tile), lambda i, side: (0, i))
    full = pl.BlockSpec((count, whole), lambda i, side: (0, 0))
    return pl.pallas_call(
        expert_grads_kernel,
        out_shape=(
            sds((2, width, half), F32),
            sds((2, half, width), F32),
            sds((UP_CUT[0], half), BF),
            sds((UP_CUT[1], half), BF),
            sds((DOWN_GRAD_CUT[0], width), BF),
            sds((DOWN_GRAD_CUT[1], width), BF),
        ),
        grid_spec=pltpu.PrefetchScalarGridSpec(
            num_scalar_prefetch=1,
            grid=(width // tile,),
            in_specs=[columns, columns, full, full],
            out_specs=[
                pl.BlockSpec((1, tile, half), lambda i, side: (side[0], i, 0)),
                pl.BlockSpec((1, half, tile), lambda i, side: (side[0], 0, i)),
                pl.BlockSpec((tile, half), lambda i, side: (jnp.minimum(i, first - 1), 0)),
                pl.BlockSpec((tile, half), lambda i, side: (jnp.maximum(i - first, 0), 0)),
                pl.BlockSpec((DOWN_GRAD_CUT[0], tile), lambda i, side: (0, i)),
                pl.BlockSpec((DOWN_GRAD_CUT[1], tile), lambda i, side: (0, i)),
            ],
            scratch_shapes=[pltpu.VMEM((whole, count), BF)],
        ),
        compiler_params=pltpu.CompilerParams(vmem_limit_bytes=ROOM),
        name="expert_grads",
        cost_estimate=cost(10),
    )(side, rows_in, d_pairs, activated, d_up)


def route_rows(where, routes_ref, cot_ref, pick_ref, turned_ref, of_ref, hits_ref, rows_ref):
    slots, rows = pick_ref.shape[0], routes_ref.shape[2]
    experts = of_ref.shape[1]
    slot = lax.broadcasted_iota(jnp.int32, (slots, experts), 0)
    lane = lax.broadcasted_iota(jnp.int32, (slots, experts), 1)
    chip = lax.div(slot, 2 * CAP)
    side = lax.rem(where[1] + lax.div(chip, 4) + where[2], 2)
    of_expert = (lane == 4 * chip + 2 * where[0] + side).astype(F32).astype(BF)
    of_ref[...] = of_expert
    expert = lax.broadcasted_iota(jnp.int32, (experts, rows), 0)
    before = (
        lax.broadcasted_iota(jnp.int32, (rows, rows), 0) < lax.broadcasted_iota(jnp.int32, (rows, rows), 1)
    ).astype(F32).astype(BF)
    hits, ranks = [], []
    for half in range(2):
        hit = jnp.zeros((experts, rows), F32)
        for choice in range(TOPK):
            hit = hit + (routes_ref[half, choice : choice + 1, :] == expert).astype(F32)
        rank = matmul(hit.astype(BF), before) + half * CAP
        hits.append(hit)
        ranks.append(jnp.where(hit > 0.5, rank, -1.0))
    hits_ref[...] = jnp.concatenate(hits, axis=1).T
    mine = matmul(of_expert, jnp.concatenate(ranks, axis=1).astype(BF))
    wanted = lax.rem(lax.broadcasted_iota(jnp.int32, mine.shape, 0), 2 * CAP).astype(F32)
    pick = (mine == wanted).astype(F32)
    pick_low = pick.astype(BF)
    pick_ref[...] = pick_low
    turned_ref[...] = pick.T.astype(BF)
    rows_ref[...] = matmul(pick_low, cot_ref[...]).astype(BF)


def middle_kernel(chip, t_ref, attn_ref, gain_ref, wr_ref, hits_ref, pick_ref, of_ref, res_ref, h_ref, inv_ref, gates_ref, rows_ref, tile_ref):
    residual = t_ref[...].astype(F32) + attn_ref[...]
    res_ref[...] = residual
    inverse = lax.rsqrt(jnp.mean(residual * residual, axis=1, keepdims=True) + EPSILON)
    inv_ref[...] = jnp.broadcast_to(inverse, inv_ref.shape)
    hidden = (residual * inverse * gain_ref[...]).astype(BF)
    h_ref[...] = hidden
    pick = pick_ref[...]
    rows_ref[...] = matmul(pick, hidden).astype(BF)
    hit = hits_ref[...] > 0.5
    logits = jnp.where(hit, matmul(hidden, wr_ref[...]), MASKED)
    exps = jnp.where(hit, jnp.exp(logits - jnp.max(logits, axis=1, keepdims=True)), 0.0)
    gates = exps / jnp.sum(exps, axis=1, keepdims=True)
    gates_ref[...] = gates
    high = gates.astype(BF)
    chosen = [
        jnp.sum(matmul(pick, part) * of_ref[...].astype(F32), axis=1, keepdims=True)
        for part in (high, (gates - high.astype(F32)).astype(BF))
    ]
    lane = lax.broadcasted_iota(jnp.int32, tile_ref.shape, 1)
    tile_ref[...] = jnp.where(lane < 64, chosen[0], chosen[1]).astype(BF)


def middle(chip, row_rows, attn_total, gain, late_all, hits, pick, of_expert):
    rows, width = attn_total.shape
    slots, experts = of_expert.shape
    sds = jax.ShapeDtypeStruct

    def whole(value):
        return pl.BlockSpec(value.shape, lambda i, chip: (0, 0))

    def out(*shape):
        return pl.BlockSpec(shape, lambda i, chip: (0, 0))

    shapes = (
        sds((rows, width), F32),
        sds((rows, width), BF),
        sds((rows, 128), F32),
        sds((rows, experts), F32),
        sds((slots, width), BF),
        sds((slots, 128), BF),
    )
    return pl.pallas_call(
        middle_kernel,
        out_shape=shapes,
        grid_spec=pltpu.PrefetchScalarGridSpec(
            num_scalar_prefetch=1,
            grid=(1,),
            in_specs=[
                pl.BlockSpec((rows, width), lambda i, chip: (chip[0], 0)),
                whole(attn_total),
                whole(gain),
                pl.BlockSpec((width, experts), lambda i, chip: (0, 2)),
                whole(hits),
                whole(pick),
                whole(of_expert),
            ],
            out_specs=[out(*value.shape) for value in shapes],
        ),
        compiler_params=pltpu.CompilerParams(vmem_limit_bytes=ROOM),
        name="middle",
        cost_estimate=cost(1),
    )(chip, row_rows, attn_total, gain, late_all, hits, pick, of_expert)


def turn_kernel(core, moe_ref, dg_ref, gates_ref, h_ref, res_ref, inv_ref, wr_ref, gain_ref, cot_ref, d_ref, low_ref, part_ref):
    gates = gates_ref[...]
    d_gates = dg_ref[...]
    d_logits = (gates * (d_gates - jnp.sum(gates * d_gates, axis=1, keepdims=True))).astype(BF)
    hidden = h_ref[...]
    gradient = moe_ref[...] + times_transposed(d_logits, wr_ref[...])
    residual, inverse = res_ref[...], inv_ref[:, 0:1]
    weighted = gradient * gain_ref[...]
    mean_term = jnp.mean(weighted * residual, axis=1, keepdims=True)
    back = inverse * weighted - residual * (inverse * inverse * inverse) * mean_term
    value = cot_ref[...].astype(F32) + back
    d_ref[...] = value
    low_ref[...] = value.astype(BF)
    owners, rows, _ = part_ref.shape
    depth = hidden.shape[1] // owners
    grad_router = transposed_times(hidden, d_logits).astype(BF)
    part_ref[:, :depth, :] = grad_router.reshape(owners, depth, grad_router.shape[1])
    terms = jnp.sum(gradient * residual * inverse, axis=0, keepdims=True)
    wide = jnp.broadcast_to(terms, (8, terms.shape[1]))
    by_owner = jnp.concatenate(
        [wide[:1, owner * depth : (owner + 1) * depth] for owner in range(owners)], axis=0
    )
    by_owner = jnp.concatenate([by_owner, jnp.zeros((owners, 128 - depth), F32)], axis=1)
    part_ref[:, depth:, :] = jnp.broadcast_to(
        by_owner[:, None, :], (owners, rows - depth, 128)
    ).astype(BF)


def turn(core, d_moe, d_gates, gates, hidden, residual, inverse, late_all, gain, cotangent):
    rows, width = d_moe.shape
    experts = gates.shape[1]
    owners = 64
    sds = jax.ShapeDtypeStruct

    def mine(columns):
        return pl.BlockSpec((rows, columns), lambda i, core: (core[0], 0))

    def whole(*shape):
        return pl.BlockSpec(shape, lambda i, core: (0,) * len(shape))

    parts = (owners, width // owners + 16, 128)
    return pl.pallas_call(
        turn_kernel,
        out_shape=(sds((rows, width), F32), sds((rows, width), BF), sds(parts, BF)),
        grid_spec=pltpu.PrefetchScalarGridSpec(
            num_scalar_prefetch=1,
            grid=(1,),
            in_specs=[
                whole(rows, width),
                whole(rows, experts),
                mine(experts),
                mine(width),
                mine(width),
                mine(128),
                pl.BlockSpec((width, experts), lambda i, core: (0, 2)),
                whole(1, width),
                whole(rows, width),
            ],
            out_specs=[whole(rows, width), whole(rows, width), whole(*parts)],
        ),
        compiler_params=pltpu.CompilerParams(vmem_limit_bytes=ROOM),
        name="turn",
        cost_estimate=cost(6),
    )(core, d_moe, d_gates, gates, hidden, residual, inverse, late_all, gain, cotangent)


def last_kernel(side, g_in, u_in, u_rest, d_in, d_rest, *refs):
    (t_ref, dh_ref, dr_ref, moe_ref, res_ref, ga_ref, late_ref, early_ref, wq_ref, wk_ref, wv_ref), refs = refs[3:14], refs[14:]
    g_out, u_out, d_out, out_ref, gt_ref, gq_ref, gk_ref, gv_ref, go_ref, gr_ref, gains_ref, ffn_ref = refs[:12]
    keys, router, gains, ffn, dots = refs[12:]
    step = pl.program_id(0)
    g_out[0] = g_in[...].astype(F32)
    u_out[0] = jnp.where(step < UP_CUT[0] // u_in.shape[0], u_in[...], u_rest[...]).astype(F32)
    d_out[0] = jnp.where(step < DOWN_GRAD_CUT[0] // d_in.shape[0], d_in[...], d_rest[...]).astype(F32)
    rows = t_ref[...].astype(F32)
    out_ref[...] = res_ref[...] + moe_ref[...]
    inverse = lax.rsqrt(jnp.mean(rows * rows, axis=1, keepdims=True) + EPSILON)
    weighted = dh_ref[...] * ga_ref[...]
    mean_term = jnp.mean(weighted * rows, axis=1, keepdims=True)
    gt_ref[...] = dr_ref[...] + (
        inverse * weighted - rows * (inverse * inverse * inverse) * mean_term
    )

    @pl.when(step == 0)
    def _():
        for ref in (keys, router, gains, ffn, dots):
            ref[...] = jnp.zeros_like(ref)

    depth = gq_ref.shape[0]
    late, early = late_ref[0].astype(F32), early_ref[0].astype(F32)
    query = jnp.concatenate([late[:depth], late[depth : 2 * depth]], axis=1)
    gq_ref[...] = query
    low_q = wq_ref[...].astype(BF).astype(F32)
    dots[...] += jnp.sum(low_q * query, axis=1, keepdims=True)
    keys[lax.div(step, 2)] += late[2 * depth : 3 * depth]
    gains[...] += late[3 * depth :]
    router[...] += early[2 * depth : 3 * depth]
    ffn[...] += early[3 * depth : 3 * depth + 8]
    go_ref[...] = jnp.concatenate([early[:depth], early[depth : 2 * depth]], axis=1)

    @pl.when(step == pl.num_programs(0) - 1)
    def _():
        gk_ref[...] = jnp.concatenate([keys[0], keys[2]], axis=1)
        gv_ref[...] = jnp.concatenate([keys[1], keys[3]], axis=1)
        gr_ref[...] = router[...]
        ffn_ref[...] = ffn[...]
        total = (
            dots[:, 0:1]
            + jnp.sum(wk_ref[...].astype(BF).astype(F32) * gk_ref[...], axis=1, keepdims=True)
            + jnp.sum(wv_ref[...].astype(BF).astype(F32) * gv_ref[...], axis=1, keepdims=True)
        )
        blank = jnp.zeros((128 - depth, 128), F32)
        square = jnp.concatenate([jnp.broadcast_to(total, (depth, 128)), blank], axis=0).T
        row = lax.broadcasted_iota(jnp.int32, gains_ref.shape, 0)
        gains_ref[...] = jnp.where(row < 2, gains[:8], square[:8])


def last(side, arrived, placed, tokens, d_hidden, d_residual, moe, residual, gain, late, early, weights):
    width, half = arrived[0].shape
    rows = tokens.shape[0]
    steps = 8
    tile, strip = width // steps, rows // steps
    depth = weights[0].shape[0]
    sds = jax.ShapeDtypeStruct

    def whole(*shape):
        return pl.BlockSpec(shape, lambda i, side: (0,) * len(shape))

    first = UP_CUT[0] // tile
    rows_out = pl.BlockSpec((1, tile, half), lambda i, side: (1 - side[0], i, 0))
    short = half // steps
    short_first = DOWN_GRAD_CUT[0] // short
    short_out = pl.BlockSpec((1, short, width), lambda i, side: (1 - side[0], i, 0))
    strips = pl.BlockSpec((strip, width), lambda i, side: (i, 0))
    mine = pl.BlockSpec((strip, width), lambda i, side: (side[1] * steps + i, 0))
    place = pl.BlockSpec((1,) + late.shape[1:], lambda i, side: (i, 0, 0))
    query = pl.BlockSpec((depth, weights[0].shape[1] // steps), lambda i, side: (0, i))
    narrow = (depth, weights[1].shape[1])
    return pl.pallas_call(
        last_kernel,
        out_shape=[sds(value.shape, F32) for value in placed]
        + [
            sds((rows, width), F32),
            sds((rows, width), F32),
            sds(weights[0].shape, F32),
            sds(narrow, F32),
            sds(narrow, F32),
            sds(weights[0].shape, F32),
            sds((depth, 128), F32),
            sds((8, 128), F32),
            sds((8, 128), F32),
        ],
        grid_spec=pltpu.PrefetchScalarGridSpec(
            num_scalar_prefetch=1,
            grid=(steps,),
            in_specs=[
                pl.BlockSpec((tile, half), lambda i, side: (i, 0)),
                pl.BlockSpec((tile, half), lambda i, side: (jnp.minimum(i, first - 1), 0)),
                pl.BlockSpec((tile, half), lambda i, side: (jnp.maximum(i - first, 0), 0)),
                pl.BlockSpec((short, width), lambda i, side: (jnp.minimum(i, short_first - 1), 0)),
                pl.BlockSpec((short, width), lambda i, side: (jnp.maximum(i - short_first, 0), 0)),
            ]
            + [ANY] * 3
            + [
                strips,
                strips,
                strips,
                strips,
                mine,
                whole(1, width),
                place,
                place,
                query,
                whole(*narrow),
                whole(*narrow),
            ],
            out_specs=[
                rows_out,
                rows_out,
                short_out,
                strips,
                strips,
                query,
                whole(*narrow),
                whole(*narrow),
                query,
                whole(depth, 128),
                whole(8, 128),
                whole(8, 128),
            ],
            scratch_shapes=[
                pltpu.VMEM((4, depth, 128), F32),
                pltpu.VMEM((depth, 128), F32),
                pltpu.VMEM((16, 128), F32),
                pltpu.VMEM((8, 128), F32),
                pltpu.VMEM((depth, 128), F32),
            ],
        ),
        input_output_aliases={6: 0, 7: 1, 8: 2},
        compiler_params=pltpu.CompilerParams(vmem_limit_bytes=ROOM),
        name="last",
        cost_estimate=cost(9),
    )(side, *arrived, *placed, tokens, d_hidden, d_residual, moe, residual, gain, late, early, *weights)


def project_kernel(block_order, lengths, group, t_ref, w_ref, side_ref, flag_ref, freq_ref, ga_ref, gq_ref, gk_ref, h_ref, q_ref, kv_ref, qp_ref, kp_ref, cos_ref, sin_ref):
    tile = t_ref.shape[0]
    row = lax.broadcasted_iota(jnp.int32, (tile, HEAD_WIDTH), 0)
    lane = lax.broadcasted_iota(jnp.int32, (tile, HEAD_WIDTH), 1)
    first_block = group[0] * 16 + pl.program_id(0) * (tile // BLK)
    position = row * 0
    for at in range(tile // BLK):
        inside = block_order[first_block + at] * BLK + row - at * BLK
        position = jnp.where(row >= at * BLK, inside, position)
    angles = (position - start_of(lengths, position)).astype(F32) * freq_ref[...]
    cosine = jnp.cos(angles)
    sine_tab = jnp.where(lane < HEAD_WIDTH // 2, -1.0, 1.0) * jnp.sin(angles)
    cos_ref[...] = cosine
    sin_ref[...] = sine_tab
    rows = t_ref[...].astype(F32)
    inverse = lax.rsqrt(jnp.mean(rows * rows, axis=1, keepdims=True) + EPSILON)
    hidden = (rows * inverse * ga_ref[...]).astype(BF)
    h_ref[...] = hidden
    qkv = matmul(hidden, w_ref[...])
    own = qkv[:, 2 * HEAD_WIDTH :]
    other = matmul(hidden, side_ref[...])
    first = flag_ref[0:1, :] > 0.5

    def turned(value, gain):
        root = lax.rsqrt(jnp.mean(value * value, axis=1, keepdims=True) + EPSILON)
        value = value * root * gain
        return (value * cosine + pltpu.roll(value, HEAD_WIDTH // 2, 1) * sine_tab).astype(BF)

    for head in range(2):
        span = slice(head * HEAD_WIDTH, (head + 1) * HEAD_WIDTH)
        q_ref[:, span] = turned(qkv[:, span], gq_ref[...])
    qp_ref[...] = qkv[:, : 2 * HEAD_WIDTH]
    keys = jnp.where(first, own, other)
    kp_ref[...] = keys
    kv_ref[:, :HEAD_WIDTH] = turned(keys, gk_ref[...])
    kv_ref[:, HEAD_WIDTH:] = jnp.where(first, other, own).astype(BF)


def project(block_order, lengths, group, tokens, weights, side, first, frequency, gain, gain_query, gain_key):
    rows, width = tokens.shape
    tile = 256
    sds = jax.ShapeDtypeStruct

    def by_rows(columns):
        return pl.BlockSpec((tile, columns), lambda i, *_: (i, 0))

    def whole(value):
        return pl.BlockSpec(value.shape, lambda i, *_: (0, 0))

    return pl.pallas_call(
        project_kernel,
        out_shape=(
            sds((rows, width), BF),
            sds((rows, 256), BF),
            sds((rows, 256), BF),
            sds((rows, 256), F32),
            sds((rows, 128), F32),
            sds((rows, 128), F32),
            sds((rows, 128), F32),
        ),
        grid_spec=pltpu.PrefetchScalarGridSpec(
            num_scalar_prefetch=3,
            grid=(rows // tile,),
            in_specs=[
                by_rows(width),
                whole(weights),
                whole(side),
                whole(first),
                whole(frequency),
                whole(gain),
                whole(gain_query),
                whole(gain_key),
            ],
            out_specs=[
                by_rows(width),
                by_rows(256),
                by_rows(256),
                by_rows(256),
                by_rows(128),
                by_rows(128),
                by_rows(128),
            ],
        ),
        compiler_params=pltpu.CompilerParams(vmem_limit_bytes=ROOM),
        name="project",
        cost_estimate=cost(8),
    )(block_order, lengths, group, tokens, weights, side, first, frequency, gain, gain_query, gain_key)


def project_back_kernel(dq_ref, ds_ref, qp_ref, kp_ref, cos_ref, sin_ref, h_ref, w_ref, side_ref, gq_ref, gk_ref, flag_ref, part_ref, late_ref, side_w, total, gains):
    step = pl.program_id(0)
    cosine, sine_tab = cos_ref[...], sin_ref[...]
    key, first, own = flag_ref[0:1, :], flag_ref[1:2, :], flag_ref[2:3, :]
    heads = 2 * HEAD_WIDTH

    @pl.when(step == 0)
    def _():
        gains[...] = jnp.zeros_like(gains)
        total[...] = jnp.zeros_like(total)
        side_w[...] = jnp.where(
            own > 0.5, w_ref[:, heads:].astype(F32), side_ref[...].astype(F32)
        ).astype(BF)

    def back(gradient, value, gain):
        gradient = gradient * cosine - pltpu.roll(gradient, HEAD_WIDTH // 2, 1) * sine_tab
        root = lax.rsqrt(jnp.mean(value * value, axis=1, keepdims=True) + EPSILON)
        weighted = gradient * gain
        mean_term = jnp.mean(weighted * value, axis=1, keepdims=True)
        terms = jnp.sum(gradient * value * root, axis=0, keepdims=True)
        return root * weighted - value * (root * root * root) * mean_term, terms

    columns = []
    for head in range(2):
        span = slice(head * HEAD_WIDTH, (head + 1) * HEAD_WIDTH)
        value, terms = back(dq_ref[:, span], qp_ref[:, span], gq_ref[...])
        columns.append(value.astype(BF))
        gains[0:1, :] += terms
    d_side = ds_ref[...]
    value, terms = back(d_side, kp_ref[...], gk_ref[...])
    mine = jnp.where(first == (step // 2).astype(F32), 1.0, 0.0)
    columns.append((jnp.where(key > 0.5, value, d_side) * mine).astype(BF))
    gains[1:2, :] += terms * key * mine
    d_all = jnp.concatenate(columns, axis=1)
    part_ref[...] = (
        times_transposed(d_all[:, :heads], w_ref[:, :heads])
        + times_transposed(d_all[:, heads:], side_w[...])
    ).astype(BF)
    total[...] += transposed_times(h_ref[...], d_all)

    @pl.when(step == pl.num_programs(0) - 1)
    def _():
        pieces, depth = late_ref.shape[0], h_ref.shape[1] // late_ref.shape[0]
        for at in range(3):
            value = total[:, at * HEAD_WIDTH : (at + 1) * HEAD_WIDTH].astype(BF)
            late_ref[:, at * depth : (at + 1) * depth, :] = value.reshape(pieces, depth, HEAD_WIDTH)
        late_ref[:, 3 * depth :, :] = jnp.broadcast_to(
            gains[...].astype(BF)[None], (pieces,) + gains.shape
        )


def project_back(d_queries, d_side, q_pre, k_pre, cosine, sine_tab, hidden, weights, side, gain_query, gain_key, flags):
    rows = d_queries.shape[0]
    width = hidden.shape[1]
    tile = 256
    tiles = rows // tile
    owners = 64
    sds = jax.ShapeDtypeStruct
    late = (owners, 3 * width // owners + 16, 128)

    def by_rows(columns):
        return pl.BlockSpec((tile, columns), lambda i: (i, 0))

    def whole(value):
        return pl.BlockSpec(value.shape, lambda i: (0, 0))

    half_rows = pl.BlockSpec((tile, 128), lambda i: (i % (tiles // 2), 0))
    return pl.pallas_call(
        project_back_kernel,
        grid=(tiles,),
        out_shape=(sds((rows, width), BF), sds(late, BF)),
        in_specs=[
            by_rows(256),
            half_rows,
            by_rows(256),
            by_rows(128),
            by_rows(128),
            by_rows(128),
            by_rows(width),
            whole(weights),
            whole(side),
            whole(gain_query),
            whole(gain_key),
            whole(flags),
        ],
        out_specs=[by_rows(width), pl.BlockSpec(late, lambda i: (0, 0, 0))],
        scratch_shapes=[
            pltpu.VMEM((width, 128), BF),
            pltpu.VMEM((width, 384), F32),
            pltpu.VMEM((16, 128), F32),
        ],
        compiler_params=pltpu.CompilerParams(vmem_limit_bytes=ROOM),
        name="project_back",
        cost_estimate=cost(12),
    )(
        d_queries, d_side, q_pre, k_pre, cosine, sine_tab, hidden, weights, side, gain_query, gain_key, flags
    )


def after(value, earlier):
    return lax.optimization_barrier((value, earlier))


def lanes_to(row, lanes=128):
    return jnp.pad(row, ((0, 0),) * (row.ndim - 1) + ((0, lanes - row.shape[-1]),))


def local(
    tokens,
    cotangent,
    seq_lengths,
    block_order,
    routes,
    w_query,
    key_weight,
    value_weight,
    w_out,
    gain_attn,
    gain_query,
    gain_key,
    gain_ffn,
    w_router,
    w_gate,
    w_up,
    w_down,
):
    rows = tokens.shape[0]
    width = tokens.shape[1]
    experts = w_router.shape[1]
    block_count = block_order.shape[0]
    wsh = lax.axis_index("wsh")
    me = lax.axis_index("ctx")
    core = lax.rem(me, 2)
    place = lax.rem(me, 8)
    group = lax.div(me, 8)
    row_tokens = 8 * rows

    def swap(value):
        return lax.ppermute(value, "wsh", [(0, 1), (1, 0)])

    depth = w_query.shape[0]
    (
        w_all,
        row_rows,
        small_all,
        chip_routes,
        chip_cot,
        other_gate,
        up_first,
        other_up,
        other_down,
        w_side,
        late_pack,
    ) = gather_first(
        (w_query, key_weight, value_weight),
        w_out.T,
        w_router,
        (gain_attn[None, :], gain_ffn[None, :]),
        tokens,
        routes.T,
        cotangent,
        (w_gate, w_up, w_down),
    )
    w_main = w_all.reshape(width, 384)
    w_side = w_side.reshape(width, 128)
    is_key = lax.rem(lax.div(me, 2), 2) == 0

    def flag(value):
        return jnp.broadcast_to(value.astype(F32).reshape(1, 1), (8, 128))

    g_attn = to_low(small_all[:, 0, :depth].reshape(width)).astype(F32)
    g_ffn = to_low(small_all[:, 1, :depth].reshape(width)).astype(F32)
    g_query = rounded(gain_query)
    g_key = rounded(gain_key)

    late_all = lax.all_to_all(late_pack, "ctx", split_axis=0, concat_axis=0, tiled=True).reshape(width, 384)

    chips = experts // 4
    slots = 2 * CAP

    half_dim = HEAD_WIDTH // 2
    frequency = jnp.power(ROPE_BASE, -2.0 * jnp.arange(half_dim, dtype=jnp.float32) / HEAD_WIDTH)
    frequency = jnp.concatenate([frequency, frequency])[None, :]
    row_rows = row_rows.reshape(row_tokens, width)
    hidden_one, queries, kv, q_pre, k_pre, cosine, sine_tab = project(
        block_order,
        seq_lengths,
        group.reshape(1),
        row_rows,
        w_main,
        w_side,
        flag(core == 0),
        frequency,
        g_attn[None, :],
        g_query[None, :],
        g_key[None, :],
    )
    kv_all, pick_low, pick_turned, of_expert, hits, cot_rows = gather_keys(
        kv, chip_routes, chip_cot.reshape(2 * rows, width), experts, 1
    )
    kv_all = kv_all.reshape(block_count * BLK, 256)
    late_all, kv_all = after(late_all, kv_all)
    (cot_rows, other_gate), kv_all = after((cot_rows, other_gate), kv_all)
    gate_back = swap(other_gate)
    cot_there = exchange_behind(cot_rows.reshape(chips, slots, width)).reshape(chips * slots, width)
    heads, lse, plan = attend(block_order, seq_lengths, group.reshape(1), queries, kv_all)

    (other_up, other_down), heads = after((other_up, other_down), heads)
    attn_total, up_first = reduce_row((heads, late_all), 2, True, swapped_whole=up_first)
    residual, hidden_two, inverse_two, gates, out_rows, gate_tile = middle(
        lax.div(place, 2).reshape(1),
        row_rows,
        attn_total.reshape(2 * rows, width),
        g_ffn[None, :],
        late_all,
        hits,
        pick_low,
        of_expert,
    )

    out_rows = out_rows.reshape(chips, slots, width)
    gate_tile = gate_tile.reshape(chips, slots, 128)
    (gate_back, cot_there, other_down, other_up), gate_tile = after(
        (gate_back, cot_there, other_down, other_up), gate_tile
    )
    down_back = swap(other_down)
    up_back = (up_first, swap(other_up))
    arrived, gate_there = exchange([out_rows, gate_tile], 3)
    arrived = arrived.reshape(chips * slots, width)
    side = wsh.reshape(1)
    gate_there = gate_there.reshape(chips * slots, 128)
    y_rows, d_rows, activated, d_gate_pre, d_up_pre, d_pairs = run_expert(
        side, arrived, cot_there, gate_there, (w_gate, w_up, w_down), (gate_back, *up_back, down_back)
    )
    own_gate, other_gate = gate_grads(side, arrived, d_gate_pre)
    activated, other_gate = after(activated, other_gate)
    own_up, own_down, up_first, other_up, other_down, down_rest = expert_grads(
        side, arrived, d_pairs, activated, d_up_pre
    )
    own_grads = (own_gate, own_up, own_down)
    gate_grad_back = swap(other_gate)
    d_back = exchange_behind(d_rows.reshape(chips, slots, width + 128))
    d_back = d_back.reshape(chips * slots, width + 128)
    (gate_grad_back, other_up, other_down, down_rest), d_back = after(
        (gate_grad_back, other_up, other_down, down_rest), d_back
    )
    d_hidden_moe, d_gates = reduce_chip(pick_turned, d_back, of_expert, width, 5)
    d_residual, d_residual_low, part = turn(
        core.reshape(1),
        d_hidden_moe,
        d_gates,
        gates,
        hidden_two,
        residual,
        inverse_two,
        late_all,
        g_ffn[None, :],
        cotangent,
    )

    d_attn, up_first = gather_row(d_residual_low, up_first, 7)
    d_attn = d_attn.reshape(row_tokens, width)
    (y_rows, other_up, other_down), d_attn_late = after((y_rows, other_up, other_down), d_attn)
    y_back = exchange_behind(y_rows.reshape(chips, slots, width))
    up_grad_back = swap(other_up)
    down_grad_back = swap(other_down)
    d_queries, d_kv, early = attend_back(
        plan, seq_lengths, queries, heads, d_attn_late, late_all, kv_all, lse, part
    )
    (y_back, up_grad_back, down_grad_back), d_kv = after((y_back, up_grad_back, down_grad_back), d_kv)
    d_side, early, down_rest = reduce_keys(d_kv, early, down_rest, 8)
    swapped_grads = (gate_grad_back, up_first, up_grad_back, down_grad_back, down_rest)
    flags = jnp.concatenate(
        [
            flag(is_key)[:1],
            flag(core)[:1],
            flag(is_key == (core == 0))[:1],
            jnp.zeros((5, 128), F32),
        ],
        axis=0,
    )
    d_hidden_parts, late = project_back(
        d_queries,
        d_side,
        q_pre,
        k_pre,
        cosine,
        sine_tab,
        hidden_one,
        w_main,
        w_side,
        g_query[None, :],
        g_key[None, :],
        flags,
    )
    d_hidden_parts = d_hidden_parts.reshape(8, rows, width)
    d_hidden_one, moe_total, late = reduce_row(
        d_hidden_parts,
        9,
        False,
        extra=(pick_turned, y_back.reshape(chips * slots, width)),
        owned=(late,),
    )
    (
        grad_gate,
        grad_up,
        grad_down,
        out_stream,
        grad_tokens,
        grad_query,
        grad_key,
        grad_value,
        grad_out_t,
        grad_router,
        gain_parts,
        grad_gain_ffn,
    ) = last(
        jnp.stack([wsh, core]),
        swapped_grads,
        own_grads,
        tokens,
        d_hidden_one,
        d_residual,
        moe_total,
        residual,
        g_attn[None, :],
        late,
        early,
        (w_query, key_weight, value_weight),
    )
    gain_parts = lax.psum(gain_parts, "wsh")
    return (
        out_stream,
        grad_tokens,
        grad_query,
        grad_key,
        grad_value,
        grad_out_t.T,
        gain_parts[2, :depth] / rounded(gain_attn),
        gain_parts[0],
        gain_parts[1],
        grad_gain_ffn[0, :depth],
        grad_router,
        grad_gate,
        grad_up,
        grad_down,
    )


def solution(mesh):
    in_specs = (
        P("ctx", None),
        P("ctx", None),
        P(),
        P(),
        P("ctx", None),
        P("ctx", "wsh"),
        P("ctx", "wsh"),
        P("ctx", "wsh"),
        P("wsh", "ctx"),
        P("ctx"),
        P(),
        P(),
        P("ctx"),
        P("ctx", None),
        P("ctx", None, "wsh"),
        P("ctx", None, "wsh"),
        P("ctx", "wsh", None),
    )
    out_specs = (
        P("ctx", None),
        P("ctx", None),
        P("ctx", "wsh"),
        P("ctx", "wsh"),
        P("ctx", "wsh"),
        P("wsh", "ctx"),
        P("ctx"),
        P(),
        P(),
        P("ctx"),
        P("ctx", None),
        P("ctx", None, "wsh"),
        P("ctx", None, "wsh"),
        P("ctx", "wsh", None),
    )
    return jax.shard_map(local, mesh=mesh, in_specs=in_specs, out_specs=out_specs, check_vma=False)
```

```python
import functools
import math

import jax
import jax.numpy as jnp
from jax import lax
from jax.experimental import pallas as pl
from jax.experimental.pallas import tpu as pltpu
from jax.sharding import PartitionSpec as P

HEAD_WIDTH = 128
TOPK = 8
BLK = 64
MAX_SEQ_TOKENS = 4096
CAP = 12
CHUNK = 1024

EPSILON = 1e-06
ROPE_BASE = 1000000.0
MASKED = -1e30
MESH = pl.DeviceIdType.MESH
BF = jnp.bfloat16
F32 = jnp.float32


def to_low(value_rows):
    return value_rows.astype(jnp.bfloat16)


def rounded(value_rows):
    return lax.optimization_barrier(value_rows.astype(jnp.bfloat16)).astype(jnp.float32)


def matmul(left, right):
    return jnp.dot(left, right, preferred_element_type=jnp.float32)


def times_transposed(left, right):
    return lax.dot_general(
        left, right, (((1,), (1,)), ((), ())), preferred_element_type=jnp.float32
    )


def transposed_times(left, right):
    return lax.dot_general(
        left, right, (((0,), (0,)), ((), ())), preferred_element_type=jnp.float32
    )


def coords(c):
    return (
        lax.div(c, 16),
        lax.rem(lax.div(c, 8), 2),
        lax.rem(lax.div(c, 2), 4),
        lax.rem(c, 2),
    )


def index_of(z, y, x, k):
    return ((z * 2 + y) * 4 + x) * 2 + k


def shifted(me, dz, dy, dx, dk):
    z, y, x, k = coords(me)
    return index_of(lax.rem(z + dz, 4), lax.rem(y + dy, 2), lax.rem(x + dx, 4), lax.rem(k + dk, 2))


def remote(src, dst, send, recv, ctx, wsh):
    return pltpu.make_async_remote_copy(
        src_ref=src,
        dst_ref=dst,
        send_sem=send,
        recv_sem=recv,
        device_id=(ctx, wsh),
        device_id_type=MESH,
    )


def greet(targets):
    barrier = pltpu.get_barrier_semaphore()
    for ctx, wsh in targets:
        pl.semaphore_signal(barrier, inc=1, device_id=(ctx, wsh), device_id_type=MESH)
    return barrier, len(targets)


def greet_many(count, target):
    barrier = pltpu.get_barrier_semaphore()

    def one(step, carried):
        pl.semaphore_signal(barrier, inc=1, device_id=target(step), device_id_type=MESH)
        return carried

    lax.fori_loop(1, count, one, 0)
    return barrier, count - 1


ANY = pl.BlockSpec(memory_space=pl.ANY)
VMEM = pl.BlockSpec(memory_space=pltpu.VMEM)
DMA = pltpu.SemaphoreType.DMA


def cost(microseconds):
    return pl.CostEstimate(flops=0, bytes_accessed=int(microseconds * 1.2e6), transcendentals=0)


ROOM = 56 * 1024 * 1024


def call_params(collective_id):
    return pltpu.CompilerParams(
        collective_id=collective_id, has_side_effects=True, vmem_limit_bytes=ROOM
    )


def row_gather_start(src, out, me, wsh, send, recv):
    place = lax.rem(me, 8)
    copies = []
    for at, (dx, dk) in enumerate(((1, 0), (3, 0), (0, 1))):
        copy = remote(
            src, out.at[place], send.at[at], recv.at[at], shifted(me, 0, 0, dx, dk), wsh
        )
        copy.start()
        copies.append(copy)
    return copies


def row_gather_onward(out, me, wsh, copies, send, recv):
    partner = shifted(me, 0, 0, 0, 1)
    half = out.shape[1] // 2
    onward = []
    forwards = []
    for at, dx in enumerate((1, 3)):
        copies[at].wait_recv()
        from_place = lax.rem(shifted(me, 0, 0, 4 - dx, 0), 8)
        part = out.at[from_place, pl.ds(at * half, half)]
        step = remote(part, part, send.at[3 + at], recv.at[3 + at], shifted(me, 0, 0, dx, 0), wsh)
        step.start()
        onward.append(step)
        block = out.at[from_place]
        forward = remote(block, block, send.at[5 + at], recv.at[5 + at], partner, wsh)
        forward.start()
        forwards.append(forward)
    return onward, forwards


def row_gather_end(out, me, wsh, copies, onward, forwards, send, recv):
    partner = shifted(me, 0, 0, 0, 1)
    half = out.shape[1] // 2
    far = lax.rem(shifted(me, 0, 0, 2, 0), 8)
    for at in (0, 1):
        onward[at].wait_recv()
        part = out.at[far, pl.ds(at * half, half)]
        forward = remote(part, part, send.at[7 + at], recv.at[7 + at], partner, wsh)
        forward.start()
        forwards.append(forward)
    copies[2].wait_recv()
    for copy in copies + onward:
        copy.wait_send()
    for forward in forwards:
        forward.wait()


def cast_steps(steps, staging, lows, in_sems, out_sems):
    loads, stores = [], []
    for index, (src, begin, dst, to, count, at) in enumerate(steps):
        slot, span = index % 2, pl.ds(0, count)
        loads.append(
            pltpu.make_async_copy(
                src.at[pl.ds(begin, count)], staging[at].at[slot, span], in_sems.at[slot]
            )
        )
        stores.append(
            pltpu.make_async_copy(lows[at].at[slot, span], dst.at[pl.ds(to, count)], out_sems.at[slot])
        )
    loads[0].start()
    loads[1].start()
    for index, step in enumerate(steps):
        slot, count, at = index % 2, step[-2], step[-1]
        loads[index].wait()
        if index >= 2:
            stores[index - 2].wait()
        lows[at][slot, :count] = staging[at][slot, :count].astype(BF)
        stores[index].start()
        if index + 2 < len(steps):
            loads[index + 2].start()
    stores[-2].wait()
    stores[-1].wait()


def cut_steps(src, parts, rows, at):
    steps, begin = [], 0
    for part in parts:
        for to in range(0, part.shape[0], rows):
            count = min(rows, part.shape[0] - to)
            steps.append((src, begin + to, part, to, count, at))
        begin += part.shape[0]
    return steps


COLUMN_STEPS = ((1, 0), (3, 0), (0, 1), (2, 0), (1, 1), (3, 1), (2, 1))
ROW_STEPS = ((1, 0), (3, 0), (1, 1), (3, 1), (0, 1), (2, 0), (2, 1))


UP_CUT = (1280, 768)
UP_GRAD_CUT = (768, 1280)
DOWN_GRAD_CUT = (240, 144)


def gather_first(weights, out_weight, router, gains, tokens, routes, cotangent, expert_weights):
    def body(q_in, k_in, v_in, o_in, ro_in, ga_in, gf_in, t_in, r_in, c_in, *refs):
        sources, refs = refs[:3], refs[3:]
        w_out, t_out, s_out, r_out, c_out = refs[:5]
        gate_out, up_out, up_rest, down_out, side_out, late_out = refs[5:11]
        refs = refs[11:]
        wide, row_s, row_r, pair, local, col_s, col_r, tall_f, flat_f, tall_b, flat_b, in_sems, out_sems = refs[:13]
        w_in, s_in, late_in, late_sem = refs[13:]
        me, wsh = lax.axis_index("ctx"), lax.axis_index("wsh")
        core = lax.rem(me, 2)
        place = lax.rem(me, 8)
        group = lax.div(me, 8)
        partner = shifted(me, 0, 0, 0, 1)
        row_peers = [shifted(me, 0, 0, dx, dk) for dx, dk in ROW_STEPS]
        col_peers = [shifted(me, dz, dy, 0, 0) for dz, dy in COLUMN_STEPS]
        barrier, amount = greet([(peer, wsh) for peer in row_peers + col_peers])
        heads = q_in.shape[1] // 8
        for at in range(8):
            w_in[at, :, :heads] = q_in[:, at * heads : (at + 1) * heads].astype(BF)
            side = (k_in, v_in)[at % 2]
            begin = at // 4 * HEAD_WIDTH
            w_in[at, :, heads:] = side[:, begin : begin + HEAD_WIDTH].astype(BF)
            late_in[at, :, :heads] = o_in[:, at * heads : (at + 1) * heads].astype(BF)
            late_in[at, :, heads:] = ro_in[...].astype(BF)
        s_in[...] = jnp.zeros_like(s_in)
        s_in[0:1, : ga_in.shape[1]] = ga_in[...]
        s_in[1:2, : gf_in.shape[1]] = gf_in[...]
        locals_ = [
            pltpu.make_async_copy(w_in.at[place], w_out.at[me], local.at[0]),
            pltpu.make_async_copy(s_in, s_out.at[me], local.at[1]),
            pltpu.make_async_copy(t_in, t_out.at[place], local.at[2]),
            pltpu.make_async_copy(r_in, r_out.at[core], local.at[3]),
            pltpu.make_async_copy(c_in, c_out.at[core], local.at[4]),
        ]
        for copy in locals_:
            copy.start()
        late_copies = [
            pltpu.make_async_copy(late_in, late_out.at[pl.ds(at * 8, 8)], late_sem.at[at]) for at in range(8)
        ]
        pl.semaphore_wait(barrier, amount)
        for peer in row_peers:
            remote(w_in.at[lax.rem(peer, 8)], w_out.at[me], wide.at[0], wide.at[1], peer, wsh).start()
            remote(s_in, s_out.at[me], wide.at[2], wide.at[3], peer, wsh).start()
        row_copies = row_gather_start(t_in, t_out, me, wsh, row_s, row_r)
        pair_copies = [
            remote(r_in, r_out.at[core], pair.at[0], pair.at[1], partner, wsh),
            remote(c_in, c_out.at[core], pair.at[2], pair.at[3], partner, wsh),
        ]
        for copy in pair_copies:
            copy.start()
        locals_[0].wait()
        locals_[1].wait()
        for at, out in ((0, w_out), (2, s_out)):
            rest = out.at[pl.ds(0, 7)]
            done = remote(rest, rest, wide.at[at], wide.at[at + 1], partner, wsh)
            done.wait_recv()
            done.wait_send()
        lanes = side_out.shape[2]
        depth, columns = w_out.shape[1], w_out.shape[2]

        def share(origin, at):
            blocks = pl.ds(origin * 8, 8)
            part = w_out.at[blocks, pl.ds(0, depth), pl.ds(columns - lanes, lanes)]
            give = remote(part, side_out.at[blocks], col_s.at[2, at], col_r.at[2, at], partner, wsh)
            give.start()
            return give

        mine = pl.ds(group * 8, 8)
        col_copies = []
        for at, peer in enumerate(col_peers):
            for kind, out in enumerate((w_out, s_out)):
                copy = remote(out.at[mine], out.at[mine], col_s.at[kind, at], col_r.at[kind, at], peer, wsh)
                copy.start()
                col_copies.append(copy)
        shares = [share(group, 7)]
        onward, forwards = row_gather_onward(t_out, me, wsh, row_copies, row_s, row_r)
        for copy in late_copies:
            copy.start()
        gate_in, up_in, down_in = [source.at[1 - wsh] for source in sources]
        buffers = ((tall_f, flat_f), (tall_b, flat_b), in_sems, out_sems)
        tall_rows, flat_rows = tall_f.shape[1], flat_f.shape[1]
        cast_steps(
            cut_steps(gate_in, (gate_out,), tall_rows, 0) + cut_steps(up_in, (up_out, up_rest), tall_rows, 0) + cut_steps(down_in, (down_out,), flat_rows, 1),
            *buffers,
        )
        row_gather_end(t_out, me, wsh, row_copies, onward, forwards, row_s, row_r)
        for at, (dz, dy) in enumerate(COLUMN_STEPS):
            col_copies[2 * at].wait_recv()
            col_copies[2 * at + 1].wait_recv()
            shares.append(share(lax.div(shifted(me, 4 - dz, 2 - dy, 0, 0), 8), at))
        for copy in pair_copies + shares + late_copies:
            copy.wait()
        for copy in locals_[2:]:
            copy.wait()
        for copy in col_copies:
            copy.wait_send()

    sds = jax.ShapeDtypeStruct
    _, deep, half = expert_weights[0].shape
    depth, packed = weights[0].shape[0], weights[0].shape[1] // 8 + HEAD_WIDTH
    tall, flat = (deep // 4, half), (half // 4, deep)
    return pl.pallas_call(
        body,
        out_shape=(
            sds((64, depth, packed), BF),
            sds((8,) + tokens.shape, tokens.dtype),
            sds((64, 8, 128), F32),
            sds((2,) + routes.shape, routes.dtype),
            sds((2,) + cotangent.shape, cotangent.dtype),
        )
        + tuple(sds((count, half), BF) for count in (deep, *UP_CUT))
        + (
            sds((half, deep), BF),
            sds((64, depth, 128), BF),
            sds((64, depth, out_weight.shape[1] // 8 + router.shape[1]), BF),
        ),
        in_specs=[VMEM] * 7 + [ANY] * 6,
        out_specs=[ANY] * 11,
        scratch_shapes=[
            DMA((4,)),
            DMA((9,)),
            DMA((9,)),
            DMA((4,)),
            DMA((5,)),
            DMA((3, 8)),
            DMA((3, 8)),
            pltpu.VMEM((2,) + tall, F32),
            pltpu.VMEM((2,) + flat, F32),
            pltpu.VMEM((2,) + tall, BF),
            pltpu.VMEM((2,) + flat, BF),
            DMA((2,)),
            DMA((2,)),
            pltpu.VMEM((8, depth, packed), BF),
            pltpu.VMEM((8, 128), F32),
            pltpu.VMEM((8, depth, out_weight.shape[1] // 8 + router.shape[1]), BF),
            DMA((8,)),
        ],
        compiler_params=call_params(0),
        name="gather_first",
        cost_estimate=cost(40),
    )(*weights, out_weight, router, *gains, tokens, routes, cotangent, *expert_weights)


def gather_row(block, swapped, collective_id):
    def body(src, src2, out, out2, row_s, row_r, pair, local):
        me, wsh = lax.axis_index("ctx"), lax.axis_index("wsh")
        barrier, amount = greet(
            [(shifted(me, 0, 0, dx, dk), wsh) for dx, dk in ((1, 0), (3, 0), (0, 1))] + [(me, 1 - wsh)]
        )
        mine = pltpu.make_async_copy(src, out.at[lax.rem(me, 8)], local)
        mine.start()
        pl.semaphore_wait(barrier, amount)
        copies = row_gather_start(src, out, me, wsh, row_s, row_r)
        cross = remote(src2, out2, pair.at[0], pair.at[1], me, 1 - wsh)
        cross.start()
        onward, forwards = row_gather_onward(out, me, wsh, copies, row_s, row_r)
        row_gather_end(out, me, wsh, copies, onward, forwards, row_s, row_r)
        mine.wait()
        cross.wait()

    return pl.pallas_call(
        body,
        out_shape=(
            jax.ShapeDtypeStruct((8,) + block.shape, block.dtype),
            jax.ShapeDtypeStruct(swapped.shape, swapped.dtype),
        ),
        in_specs=[ANY, ANY],
        out_specs=[ANY, ANY],
        scratch_shapes=[DMA((9,)), DMA((9,)), DMA((2,)), DMA],
        compiler_params=call_params(collective_id),
        name="gather_row",
        cost_estimate=cost(26),
    )(block, swapped)


def gather_keys(rows, routes, cotangent, experts, collective_id):
    chip_rows, deep = cotangent.shape
    slots = experts // 4 * 2 * CAP
    count = rows.shape[0]
    half = count // 2

    def body(src, routes_ref, cot_ref, out, pick_ref, turned_ref, of_ref, hits_ref, rows_out, send, recv, local, rows_ref, rows_sem):
        me, wsh = lax.axis_index("ctx"), lax.axis_index("wsh")
        core = lax.rem(me, 2)
        group = lax.div(me, 8)
        partner = shifted(me, 0, 0, 0, 1)
        across = shifted(me, 0, 1, 0, 0)
        steps = (1, 3, 2)
        peers = [shifted(me, dz, 0, 0, 0) for dz in steps]
        barrier, amount = greet([(peer, wsh) for peer in peers + [across, partner]])
        mine = pltpu.make_async_copy(src, out.at[group], local)
        mine.start()
        pl.semaphore_wait(barrier, amount)
        my_half = pl.ds(pl.multiple_of(core * half, half), half)
        copies = []
        for at, peer in enumerate([across] + peers):
            copy = remote(src.at[my_half], out.at[group, my_half], send.at[at], recv.at[at], peer, wsh)
            copy.start()
            copies.append(copy)
        forwards = []

        def hand_on(origin, at):
            part = out.at[origin, my_half]
            forward = remote(part, part, send.at[7 + at], recv.at[7 + at], partner, wsh)
            forward.start()
            forwards.append(forward)

        copies[0].wait_recv()
        beside = lax.div(across, 8)
        for at, peer in enumerate(peers):
            part = out.at[beside, my_half]
            copy = remote(part, part, send.at[4 + at], recv.at[4 + at], peer, wsh)
            copy.start()
            copies.append(copy)
        hand_on(beside, 0)
        route_rows((core, wsh, lax.rem(group, 2)), routes_ref, cot_ref, pick_ref, turned_ref, of_ref, hits_ref, rows_ref)
        rows_copy = pltpu.make_async_copy(rows_ref, rows_out, rows_sem)
        rows_copy.start()
        for dy in range(2):
            for at, dz in enumerate(steps):
                copies[1 + 3 * dy + at].wait_recv()
                hand_on(lax.div(shifted(me, 4 - dz, dy, 0, 0), 8), 1 + 3 * dy + at)
        for copy in copies:
            copy.wait_send()
        for forward in forwards:
            forward.wait()
        mine.wait()
        rows_copy.wait()

    sds = jax.ShapeDtypeStruct
    return pl.pallas_call(
        body,
        out_shape=(
            sds((8,) + rows.shape, rows.dtype),
            sds((slots, chip_rows), BF),
            sds((chip_rows, slots), BF),
            sds((slots, experts), BF),
            sds((chip_rows, experts), F32),
            sds((slots, deep), BF),
        ),
        in_specs=[ANY, VMEM, VMEM],
        out_specs=[ANY, VMEM, VMEM, VMEM, VMEM, ANY],
        scratch_shapes=[DMA((14,)), DMA((14,)), DMA, pltpu.VMEM((slots, deep), BF), DMA],
        compiler_params=call_params(collective_id),
        name="gather_keys",
        cost_estimate=cost(30),
    )(rows, routes, cotangent)


class Staged:
    def __init__(self, sources, buffers, sems):
        self.copies = [
            pltpu.make_async_copy(src, buffer, sems.at[at])
            for at, (src, buffer) in enumerate(zip(sources, buffers))
        ]
        for copy in self.copies:
            copy.start()

    def ready(self, *which):
        for at in which:
            self.copies[at].wait()

    @staticmethod
    def scratch(values):
        return [pltpu.VMEM(value.shape, value.dtype) for value in values] + [DMA((len(values),))]


class Owned:
    SCRATCH = 10

    def __init__(self, src, out, scratch):
        self.src, self.out = src, out
        self.land_z, self.sum_z, self.land_y, self.reduced, *self.sems = scratch

    @staticmethod
    def scratch(value):
        inner = value.shape[1:]
        return [
            pltpu.VMEM((3, 16) + inner, BF),
            pltpu.VMEM((16,) + inner, BF),
            pltpu.VMEM((8,) + inner, BF),
            pltpu.VMEM((8,) + inner, BF),
            DMA((3,)),
            DMA((3,)),
            DMA((1,)),
            DMA((1,)),
            DMA((7,)),
            DMA((7,)),
        ]

    def along_z(self, me, wsh):
        z, _, _, _ = coords(me)
        self.copies_z = []
        for at, dz in enumerate((1, 3, 2)):
            blocks = pl.ds(lax.rem(z + dz, 4) * 16, 16)
            copy = remote(
                self.src.at[blocks],
                self.land_z.at[at],
                self.sems[0].at[at],
                self.sems[1].at[at],
                shifted(me, dz, 0, 0, 0),
                wsh,
            )
            copy.start()
            self.copies_z.append(copy)

    def along_y(self, me, wsh):
        z, y, _, _ = coords(me)
        value = self.src[pl.ds(z * 16, 16)].astype(F32)
        for at, copy in enumerate(self.copies_z):
            copy.wait_recv()
            value = value + self.land_z[at].astype(F32)
        self.sum_z[...] = value.astype(BF)
        self.copy_y = remote(
            self.sum_z.at[pl.ds((1 - y) * 8, 8)],
            self.land_y,
            self.sems[2].at[0],
            self.sems[3].at[0],
            shifted(me, 0, 1, 0, 0),
            wsh,
        )
        self.copy_y.start()

    def along_row(self, me, wsh):
        _, y, _, _ = coords(me)
        self.copy_y.wait_recv()
        value = self.sum_z[pl.ds(y * 8, 8)].astype(F32) + self.land_y[...].astype(F32)
        self.reduced[...] = value.astype(BF)
        place = lax.rem(me, 8)
        self.copies_row = []
        for at, (dx, dk) in enumerate(ROW_STEPS):
            peer = shifted(me, 0, 0, dx, dk)
            copy = remote(
                self.reduced.at[lax.rem(peer, 8)],
                self.out.at[place],
                self.sems[4].at[at],
                self.sems[5].at[at],
                peer,
                wsh,
            )
            copy.start()
            self.copies_row.append(copy)
        self.out[place] = self.reduced[place]

    def finish(self):
        for copy in self.copies_row:
            copy.wait()
        for copy in self.copies_z + [self.copy_y]:
            copy.wait_send()


def reduce_row(parts, collective_id, closing=None, extra=None, swapped_whole=None, owned=()):
    has_whole = swapped_whole is not None
    both = closing is not None
    is_product = isinstance(parts, tuple)
    if is_product:
        rows, width = parts[0].shape[0] // 8, parts[1].shape[0]
    else:
        _, rows, width = parts.shape
    block = (rows, width)
    pieces = 4
    columns = width // pieces
    has_extra = extra is not None

    def body(*refs):
        refs = list(refs)
        stage_sems = refs.pop(-1)
        buffers = [refs.pop(-1) for _ in staged_values][::-1]
        sources = [refs.pop(0) for _ in range(len(staged_values) - len(owned) - (len(closing) if both else 0))]
        held = list(buffers)
        if is_product:
            heads_ref, out_w = held.pop(0), held.pop(0)
            if both:
                attn = refs.pop(-1)
            src = refs.pop(-1)
        else:
            src = held.pop(0)
        if has_extra:
            pick_ref, back_ref = held.pop(0), held.pop(0)
        src3 = refs.pop(0) if has_whole else None
        sources += [refs.pop(0) for _ in owned]
        if both:
            own_chip = lax.div(lax.rem(lax.axis_index("ctx"), 8), 2)
            rows_in, *others_in = [refs.pop(0) for _ in closing]
            sources += [rows_in.at[pl.ds(pl.multiple_of(own_chip * 2 * rows, 2 * rows), 2 * rows)]] + others_in
            mine_in, closing_in = held[: len(owned)], held[len(owned) :]
        else:
            mine_in = held
        staged = Staged(sources, buffers, stage_sems)
        out = [refs.pop(0) for _ in range(6)] if both else refs.pop(0)
        out2 = refs.pop(0) if has_extra else None
        out3 = refs.pop(0) if has_whole else None
        mine_out = [refs.pop(0) for _ in owned]
        blocks = []
        for src4, out4 in reversed(list(zip(mine_in, mine_out))):
            blocks.append(Owned(src4, out4, refs[-Owned.SCRATCH :]))
            refs = refs[: -Owned.SCRATCH]
        arrived, summed, landed, swapped, total, send, recv, local = refs[:8]
        me, wsh = lax.axis_index("ctx"), lax.axis_index("wsh")
        other = 1 - wsh
        core = lax.rem(me, 2)
        _, _, x, _ = coords(me)
        partner = shifted(me, 0, 0, 0, 1)
        peers = [shifted(me, 0, 0, dx, 0) for dx in (1, 2, 3)]
        row_peers = [shifted(me, 0, 0, dx, dk) for dx, dk in ROW_STEPS]
        col_peers = [shifted(me, dz, dy, 0, 0) for dz, dy in COLUMN_STEPS]
        greeted = row_peers + col_peers if owned else peers + [partner]
        barrier, amount = greet([(peer, wsh) for peer in greeted] + [(me, other)])
        pl.semaphore_wait(barrier, amount)
        staged.ready(*range(2 if is_product else 1))
        if has_whole:
            whole = remote(
                src3, out3, send.at[1, 9], recv.at[1, 9], me, other
            )
            whole.start()
        spans = [pl.ds(piece * columns, columns) for piece in range(pieces)]
        everything = pl.ds(0, rows)
        first = []
        for piece, span in enumerate(spans):
            if is_product:
                columns_of = slice(piece * columns, (piece + 1) * columns)
                src[:, :, columns_of] = (
                    times_transposed(heads_ref[...], out_w[columns_of, : heads_ref.shape[1]])
                    .astype(BF)
                    .reshape(8, rows, columns)
                )
            for at, dx in enumerate((2, 1, 3, 0)):
                chip = lax.rem(x + dx, 4)
                copy = remote(
                    src.at[chip * 2 + 1 - core, everything, span],
                    arrived.at[at, everything, span],
                    send.at[piece, at],
                    recv.at[piece, at],
                    partner,
                    wsh,
                )
                copy.start()
                first.append(copy)
        if owned:
            staged.ready(*range(len(staged_values) - len(owned), len(staged_values)))
        for block4 in blocks:
            block4.along_z(me, wsh)
        if has_extra:
            staged.ready(1, 2)
            arrived2, swapped2, src2 = refs[8:]
            src2[...] = matmul(pick_ref[...], back_ref[...]).astype(BF).reshape(src2.shape)
            give2 = remote(src2.at[1 - core], arrived2, send.at[0, 8], recv.at[0, 8], partner, wsh)
            give2.start()
        second = []
        for piece, span in enumerate(spans):
            for at, dx in enumerate((2, 1, 3)):
                chip = lax.rem(x + dx, 4)
                first[piece * 4 + at].wait_recv()
                summed[at, :, span] = (
                    src[chip * 2 + core, :, span].astype(F32) + arrived[at, :, span].astype(F32)
                ).astype(BF)
                copy = remote(
                    summed.at[at, everything, span],
                    landed.at[at, everything, span],
                    send.at[piece, 4 + at],
                    recv.at[piece, 4 + at],
                    shifted(me, 0, 0, dx, 0),
                    wsh,
                )
                copy.start()
                second.append(copy)
            first[piece * 4 + 3].wait_recv()
            total[:, span] = src[x * 2 + core, :, span].astype(F32) + arrived[3, :, span].astype(F32)
        if has_extra:
            give2.wait()
            swapped2[0] = (src2[core].astype(F32) + arrived2[...].astype(F32)).astype(BF)
            swap2 = remote(swapped2.at[0], swapped2.at[1], send.at[1, 8], recv.at[1, 8], me, other)
            swap2.start()
        swaps = []
        for piece, span in enumerate(spans):
            for at in (1, 2, 0):
                second[piece * 3 + at].wait_recv()
            swapped[0, :, span] = (
                total[:, span]
                + landed[0, :, span].astype(F32)
                + landed[1, :, span].astype(F32)
                + landed[2, :, span].astype(F32)
            ).astype(BF)
            swap = remote(
                swapped.at[0, everything, span],
                swapped.at[1, everything, span],
                send.at[piece, 7],
                recv.at[piece, 7],
                me,
                other,
            )
            swap.start()
            swaps.append(swap)
            if piece == pieces - 2:
                for block4 in blocks:
                    block4.along_y(me, wsh)
        for block4 in blocks:
            block4.along_row(me, wsh)
        if has_extra:
            swap2.wait()
            out2[...] = swapped2[0].astype(F32) + swapped2[1].astype(F32)
        for piece, span in enumerate(spans):
            swaps[piece].wait()
            if both:
                total[:, span] = swapped[0, :, span].astype(F32) + swapped[1, :, span].astype(F32)
            else:
                out[:, span] = swapped[0, :, span].astype(F32) + swapped[1, :, span].astype(F32)
        if both:
            mine = pl.ds(pl.multiple_of(core * rows, rows), rows)
            keep = pltpu.make_async_copy(total, attn.at[mine], local)
            keep.start()
            give = remote(total, attn.at[mine], send.at[0, 9], recv.at[0, 9], partner, wsh)
            give.start()
            staged.ready(*range(len(staged_values) - len(closing), len(staged_values)))
            give.wait()
            keep.wait()
            tokens_ref, gain_ref, hits_ref, pick_ref, of_ref = closing_in
            router_ref = out_w.at[pl.ds(0, width), pl.ds(heads_ref.shape[1], of_ref.shape[1])]
            middle_rows(tokens_ref, attn, gain_ref, router_ref, hits_ref, pick_ref, of_ref, *out)
        for copy in first + second:
            copy.wait_send()
        for block4 in blocks:
            block4.finish()
        if has_whole:
            whole.wait()

    if both:
        slots, experts = closing[4].shape
        shapes = [
            jax.ShapeDtypeStruct(shape, dtype)
            for shape, dtype in (
                ((2 * rows, width), F32),
                ((2 * rows, width), BF),
                ((2 * rows, 128), F32),
                ((2 * rows, experts), F32),
                ((slots, width), BF),
                ((slots, 128), BF),
            )
        ]
    else:
        shapes = [jax.ShapeDtypeStruct(block, F32)]
    scratch = [
        pltpu.VMEM((4,) + block, BF),
        pltpu.VMEM((3,) + block, BF),
        pltpu.VMEM((3,) + block, BF),
        pltpu.VMEM((2,) + block, BF),
        pltpu.VMEM(block, F32),
        DMA((pieces, 10)),
        DMA((pieces, 10)),
        DMA,
    ]
    operands = list(parts) if is_product else [parts]
    out_spaces = [VMEM] * len(shapes)
    if has_extra:
        shapes.append(jax.ShapeDtypeStruct(block, F32))
        scratch += [pltpu.VMEM(block, BF), pltpu.VMEM((2,) + block, BF), pltpu.VMEM((2,) + block, BF)]
        operands += list(extra)
        out_spaces.append(VMEM)
    spaces = [ANY] * len(operands)
    staged_values = list(operands) + list(owned)
    if has_whole:
        shapes.append(jax.ShapeDtypeStruct(swapped_whole.shape, swapped_whole.dtype))
        operands.append(swapped_whole)
        spaces.append(ANY)
        out_spaces.append(ANY)
    for value in owned:
        block8 = (8,) + value.shape[1:]
        shapes.append(jax.ShapeDtypeStruct(block8, BF))
        operands.append(value)
        spaces.append(ANY)
        out_spaces.append(VMEM)
        scratch += Owned.scratch(value)
    if is_product:
        scratch.append(pltpu.VMEM((8,) + block, BF))
    if both:
        scratch.append(pltpu.VMEM((2 * rows, width), F32))
        operands += list(closing)
        spaces += [ANY] * len(closing)
        staged_values += [jax.ShapeDtypeStruct((2 * rows, width), BF)] + list(closing[1:])
    scratch += Staged.scratch(staged_values)
    return pl.pallas_call(
        body,
        out_shape=shapes,
        in_specs=spaces,
        out_specs=out_spaces,
        scratch_shapes=scratch,
        compiler_params=call_params(collective_id),
        name="reduce_row",
        cost_estimate=cost(1),
    )(*operands)


def reduce_chip(pick, back, of_expert, gates, hidden, residual, inverse, late_all, gain, cotangent, collective_id):
    rows, width = cotangent.shape
    lanes = of_expert.shape[1]
    owners = 64

    def body(*refs):
        ins, outs, refs = refs[:10], refs[10:13], refs[13:]
        src, src2, arrived, swapped, arrived2, swapped2, send, recv = refs[:8]
        buffers, sems, moe, d_gates = refs[8:18], refs[18], refs[19], refs[20]
        me, wsh = lax.axis_index("ctx"), lax.axis_index("wsh")
        other = 1 - wsh
        core = lax.rem(me, 2)
        partner = shifted(me, 0, 0, 0, 1)
        mine = pl.ds(pl.multiple_of(core * rows, rows), rows)
        pick_in, back_in, of_in, gates_in, hidden_in, residual_in, inverse_in, late_in, gain_in, cot_in = ins
        staged = Staged(
            (pick_in, back_in, of_in)
            + tuple(ref.at[mine] for ref in (gates_in, hidden_in, residual_in, inverse_in))
            + (late_in.at[pl.ds(0, width), pl.ds(2 * HEAD_WIDTH, lanes)], gain_in, cot_in),
            buffers,
            sems,
        )
        pick_ref, back_ref, of_ref = buffers[:3]
        barrier, amount = greet([(partner, wsh), (me, other)])
        staged.ready(0, 1, 2)
        src[...] = matmul(pick_ref[...], back_ref[:, :width]).astype(BF).reshape(src.shape)
        parts = [back_ref[:, at : at + 1] * of_ref[...] for at in (width, width + 64)]
        src2[...] = (matmul(pick_ref[...], parts[0]) + matmul(pick_ref[...], parts[1])).reshape(src2.shape)
        pl.semaphore_wait(barrier, amount)
        give = remote(src.at[1 - core], arrived, send.at[0], recv.at[0], partner, wsh)
        give.start()
        give2 = remote(src2.at[1 - core], arrived2, send.at[2], recv.at[2], partner, wsh)
        give2.start()
        give.wait()
        swapped[0] = (src[core].astype(F32) + arrived[...].astype(F32)).astype(BF)
        swap = remote(swapped.at[0], swapped.at[1], send.at[1], recv.at[1], me, other)
        swap.start()
        give2.wait()
        swapped2[0] = src2[core] + arrived2[...]
        swap2 = remote(swapped2.at[0], swapped2.at[1], send.at[3], recv.at[3], me, other)
        swap2.start()
        staged.ready(*range(3, 10))
        swap2.wait()
        d_gates[...] = swapped2[0] + swapped2[1]
        swap.wait()
        moe[...] = swapped[0].astype(F32) + swapped[1].astype(F32)
        turn_rows(moe, d_gates, *buffers[3:], *outs)

    sds = jax.ShapeDtypeStruct
    block, block2 = (rows, width), (rows, lanes)
    staged_values = (
        pick,
        back,
        of_expert,
        sds((rows, gates.shape[1]), F32),
        sds(block, BF),
        sds(block, F32),
        sds((rows, inverse.shape[1]), F32),
        sds((width, lanes), BF),
        gain,
        cotangent,
    )
    return pl.pallas_call(
        body,
        out_shape=(sds(block, F32), sds(block, BF), sds((owners, width // owners + 16, 128), BF)),
        in_specs=[ANY] * 10,
        out_specs=[VMEM] * 3,
        scratch_shapes=[
            pltpu.VMEM((2,) + block, BF),
            pltpu.VMEM((2,) + block2, F32),
            pltpu.VMEM(block, BF),
            pltpu.VMEM((2,) + block, BF),
            pltpu.VMEM(block2, F32),
            pltpu.VMEM((2,) + block2, F32),
            DMA((4,)),
            DMA((4,)),
        ]
        + Staged.scratch(staged_values)
        + [pltpu.VMEM(block, F32), pltpu.VMEM(block2, F32)],
        compiler_params=call_params(collective_id),
        name="reduce_chip",
        cost_estimate=cost(17),
    )(pick, back, of_expert, gates, hidden, residual, inverse, late_all, gain, cotangent)


def reduce_keys(parts, owned, swapped, collective_id):
    _, groups, _, rows, width = parts.shape

    def body(src_in, src4_in, src5, out, out4, out5, arrived, mid, beside, summed, landed, send, recv, pair, *scratch4):
        src, src4, sems = scratch4[-3:]
        staged = Staged((src_in, src4_in), (src, src4), sems)
        block4 = Owned(src4, out4, scratch4[:-3])
        me, wsh = lax.axis_index("ctx"), lax.axis_index("wsh")
        core = lax.rem(me, 2)
        _, _, x, _ = coords(me)
        side = lax.rem(x, 2)
        partner = shifted(me, 0, 0, 0, 1)
        neighbour = me + 2 - 4 * side
        steps = COLUMN_STEPS + ((0, 0),)
        peers = [shifted(me, dz, dy, 0, 0) for dz, dy in steps]
        row_peers = [shifted(me, 0, 0, dx, dk) for dx, dk in ROW_STEPS]
        barrier, amount = greet([(peer, wsh) for peer in peers[:-1] + row_peers] + [(me, 1 - wsh)])
        pl.semaphore_wait(barrier, amount)
        staged.ready(0, 1)
        first = []
        for at, peer in enumerate(peers):
            group = lax.div(peer, 8)
            for turn, b in enumerate((1 - side, side)):
                copy = remote(
                    src.at[1 - core, group, b],
                    arrived.at[turn, at],
                    send.at[turn, at],
                    recv.at[turn, at],
                    partner,
                    wsh,
                )
                copy.start()
                first.append(copy)
        block4.along_z(me, wsh)
        cross = remote(src5, out5, pair.at[0], pair.at[1], me, 1 - wsh)
        cross.start()
        across = []
        for at, peer in enumerate(peers):
            group = lax.div(peer, 8)
            first[2 * at].wait_recv()
            mid[at] = (src[core, group, 1 - side].astype(F32) + arrived[0, at].astype(F32)).astype(BF)
            copy = remote(mid.at[at], beside.at[at], send.at[2, at], recv.at[2, at], neighbour, wsh)
            copy.start()
            across.append(copy)
        last = []
        for at, peer in enumerate(peers):
            group = lax.div(peer, 8)
            first[2 * at + 1].wait_recv()
            across[at].wait_recv()
            value = (
                src[core, group, side].astype(F32)
                + arrived[1, at].astype(F32)
                + beside[at].astype(F32)
            )
            if at == groups - 1:
                out[...] = value
            else:
                summed[at] = value.astype(BF)
                copy = remote(summed.at[at], landed.at[at], send.at[3, at], recv.at[3, at], peer, wsh)
                copy.start()
                last.append(copy)
            if at == 5:
                block4.along_y(me, wsh)
        block4.along_row(me, wsh)
        for at, copy in enumerate(last):
            copy.wait_recv()
            out[...] += landed[at].astype(F32)
        for copy in first + across + last:
            copy.wait_send()
        block4.finish()
        cross.wait()

    block = (rows, width)
    return pl.pallas_call(
        body,
        out_shape=(
            jax.ShapeDtypeStruct(block, F32),
            jax.ShapeDtypeStruct((8,) + owned.shape[1:], BF),
            jax.ShapeDtypeStruct(swapped.shape, swapped.dtype),
        ),
        in_specs=[ANY, ANY, ANY],
        out_specs=[VMEM, VMEM, ANY],
        scratch_shapes=[
            pltpu.VMEM((2, groups) + block, BF),
            pltpu.VMEM((groups,) + block, BF),
            pltpu.VMEM((groups,) + block, BF),
            pltpu.VMEM((groups,) + block, BF),
            pltpu.VMEM((groups,) + block, BF),
            DMA((4, groups)),
            DMA((4, groups)),
            DMA((2,)),
        ]
        + Owned.scratch(owned)
        + Staged.scratch((parts, owned)),
        compiler_params=call_params(collective_id),
        name="reduce_keys",
        cost_estimate=cost(40),
    )(parts, owned, swapped)


def exchange(arrays, collective_id):
    amount = len(arrays)

    def body(*refs):
        ins, outs = refs[:amount], refs[amount : 2 * amount]
        send, recv, local = refs[2 * amount :]
        me, wsh = lax.axis_index("ctx"), lax.axis_index("wsh")
        chip = lax.div(me, 2)

        def target(step):
            dy = lax.rem(lax.div(step, 4), 2)
            return shifted(me, lax.div(step, 8), dy, lax.rem(step, 4), 0), lax.rem(wsh + dy, 2)

        barrier, count = greet_many(32, target)
        locals_ = []
        for at in range(amount):
            copy = pltpu.make_async_copy(ins[at].at[chip], outs[at].at[chip], local.at[at])
            copy.start()
            locals_.append(copy)
        pl.semaphore_wait(barrier, count)

        def one(step, carried):
            ctx, side = target(lax.rem(step * 27, 32))
            for at in range(amount):
                remote(
                    ins[at].at[lax.div(ctx, 2)], outs[at].at[chip], send.at[at], recv.at[at], ctx, side
                ).start()
            return carried

        lax.fori_loop(1, 32, one, 0)
        for copy in locals_:
            copy.wait()
        for at in range(amount):
            rest = outs[at].at[pl.ds(0, 31)]
            done = remote(rest, rest, send.at[at], recv.at[at], me, wsh)
            done.wait_send()
            done.wait_recv()

    return pl.pallas_call(
        body,
        out_shape=[jax.ShapeDtypeStruct(a.shape, a.dtype) for a in arrays],
        in_specs=[ANY] * amount,
        out_specs=[ANY] * amount,
        scratch_shapes=[DMA((amount,)), DMA((amount,)), DMA((amount,))],
        compiler_params=call_params(collective_id),
        name="exchange",
        cost_estimate=cost(48),
    )(*arrays)


def exchange_behind(value):
    groups = []
    for core in range(2):
        for parity in range(2):
            groups.append(
                [(chip * 2 + core) * 2 + (parity + chip // 4) % 2 for chip in range(32)]
            )
    return lax.all_to_all(
        value, ("ctx", "wsh"), split_axis=0, concat_axis=0, tiled=True, axis_index_groups=groups
    )


def natural_order(plan, kv_ref, keys, values, transposed):
    def one(block, carried):
        rows = kv_ref[pl.ds(pl.multiple_of(plan[PLAN_INVERSE + block] * BLK, BLK), BLK), :]
        at = pl.ds(pl.multiple_of(block * BLK, BLK), BLK)
        keys[at, :] = rows[:, :HEAD_WIDTH]
        values[at, :] = rows[:, HEAD_WIDTH:]
        return carried

    lax.fori_loop(0, kv_ref.shape[0] // BLK, one, 0, unroll=8)
    source, turned = transposed

    def turn(chunk, carried):
        at = pl.ds(pl.multiple_of(chunk * CHUNK, CHUNK), CHUNK)
        turned[:, at] = source[at, :].T
        return carried

    lax.fori_loop(0, kv_ref.shape[0] // CHUNK, turn, 0, unroll=4)


def stacked(ref, first, second):
    rows = [ref[pl.ds(pl.multiple_of(at * BLK, BLK), BLK), :] for at in (first, second)]
    return jnp.concatenate(
        [rows[0][:, :HEAD_WIDTH], rows[0][:, HEAD_WIDTH:], rows[1][:, :HEAD_WIDTH], rows[1][:, HEAD_WIDTH:]],
        axis=0,
    )


def unstacked(ref, first, second, value):
    for at, begin in ((first, 0), (second, 2 * BLK)):
        ref[pl.ds(pl.multiple_of(at * BLK, BLK), BLK), :] = jnp.concatenate(
            [value[begin : begin + BLK], value[begin + BLK : begin + 2 * BLK]], axis=1
        )


PLAN_BOUNDS, PLAN_INVERSE, PLAN_BLOCKS, PLAN_SIZE = 16, 64, 192, 256


def start_of(lengths, position):
    begin = lengths[0] * 0
    start = position * 0
    for at in range(lengths.shape[0]):
        start = jnp.where(begin <= position, begin, start)
        begin = begin + lengths[at]
    return start


def make_plan(block_order, lengths, base, plan):
    def place(at, carried):
        plan[PLAN_INVERSE + block_order[at]] = at
        return carried

    lax.fori_loop(0, block_order.shape[0], place, 0, unroll=8)

    def rank(at, carried):
        mine = block_order[base + at]
        before = jnp.int32(0)
        for other in range(16):
            before = before + jnp.where(block_order[base + other] < mine, 1, 0)
        plan[before] = at
        plan[PLAN_BLOCKS + before] = mine
        return carried

    lax.fori_loop(0, 16, rank, 0)

    def bound(step, carried):
        one, two = plan[PLAN_BLOCKS + 2 * step], plan[PLAN_BLOCKS + 2 * step + 1]
        low = lax.div(start_of(lengths, one * BLK), CHUNK)
        high = lax.div(two * BLK, CHUNK) + 1
        last = start_of(lengths, two * BLK + BLK - 1)
        inner_low = jnp.minimum(jnp.maximum(lax.div(last + CHUNK - 1, CHUNK), low), high)
        inner_high = jnp.minimum(jnp.maximum(lax.div(one * BLK + 1, CHUNK), inner_low), high)
        for at, value in enumerate((low, inner_low, inner_high, high)):
            plan[PLAN_BOUNDS + 4 * step + at] = value
        return carried

    lax.fori_loop(0, 8, bound, 0)


def strips_of(plan, lengths, step):
    lane = lax.broadcasted_iota(jnp.int32, (1, 4 * BLK), 1)
    block = jnp.where(lane < 2 * BLK, plan[PLAN_BLOCKS + 2 * step], plan[PLAN_BLOCKS + 2 * step + 1])
    position = block * BLK + lax.rem(lane, BLK)
    return position, start_of(lengths, position)


def three_loops(step, plan, chunk, state):
    low, inner_low, inner_high, high = [plan[PLAN_BOUNDS + 4 * step + at] for at in range(4)]
    state = lax.fori_loop(low, inner_low, functools.partial(chunk, True), state)
    state = lax.fori_loop(inner_low, inner_high, functools.partial(chunk, False), state)
    return lax.fori_loop(inner_high, high, functools.partial(chunk, True), state)


def kept(scores, at, q_pos, q_start):
    k_pos = at + lax.broadcasted_iota(jnp.int32, scores.shape, 0)
    return jnp.where((k_pos <= q_pos) & (k_pos >= q_start), scores, MASKED)


SCORE_SCALE = 1.0 / math.sqrt(HEAD_WIDTH)
TWO_SCALE = SCORE_SCALE / math.log(2.0)


def forward_kernel(block_order, lengths, group, q_ref, kv_ref, out_ref, lse_ref, plan, keys, values, values_t, acc):
    step = pl.program_id(0)

    @pl.when(step == 0)
    def _():
        make_plan(block_order, lengths, group[0] * 16, plan)
        natural_order(plan, kv_ref, keys, values, (values, values_t))

    first, second = plan[2 * step], plan[2 * step + 1]
    q_t = stacked(q_ref, first, second).astype(F32).T.astype(BF)
    q_pos, q_start = strips_of(plan, lengths, step)
    width = 4 * BLK
    acc[...] = jnp.zeros_like(acc)

    def chunk(masked, index, total):
        at = pl.multiple_of(index * CHUNK, CHUNK)
        scores = matmul(keys[pl.ds(at, CHUNK), :], q_t)
        if masked:
            scores = kept(scores, at, q_pos, q_start)
        probs = jnp.exp2(scores * TWO_SCALE)
        acc[...] += matmul(values_t[:, pl.ds(at, CHUNK)], probs.astype(BF))
        return total + jnp.sum(probs, axis=0, keepdims=True)

    total = three_loops(step, plan, chunk, jnp.zeros((1, width), F32))
    lse_ref[0] = jnp.log2(total)
    unstacked(out_ref, first, second, (acc[...] / total).T.astype(BF))


def attend(block_order, lengths, group, queries, kv):
    rows = queries.shape[0]
    steps = rows // (2 * BLK)
    everything = pl.BlockSpec(queries.shape, lambda i, *_: (0, 0))
    strip = pl.BlockSpec((1, 1, 4 * BLK), lambda i, *_: (i, 0, 0))
    sds = jax.ShapeDtypeStruct
    return pl.pallas_call(
        forward_kernel,
        out_shape=(
            sds(queries.shape, BF),
            sds((steps, 1, 4 * BLK), F32),
            sds((PLAN_SIZE,), jnp.int32),
        ),
        grid_spec=pltpu.PrefetchScalarGridSpec(
            num_scalar_prefetch=3,
            grid=(steps,),
            in_specs=[everything, pl.BlockSpec(kv.shape, lambda i, *_: (0, 0))],
            out_specs=[everything, strip, pl.BlockSpec(memory_space=pltpu.SMEM)],
            scratch_shapes=[
                pltpu.VMEM((kv.shape[0], HEAD_WIDTH), BF),
                pltpu.VMEM((kv.shape[0], HEAD_WIDTH), BF),
                pltpu.VMEM((HEAD_WIDTH, kv.shape[0]), BF),
                pltpu.VMEM((HEAD_WIDTH, 4 * BLK), F32),
            ],
        ),
        compiler_params=pltpu.CompilerParams(vmem_limit_bytes=ROOM),
        name="attend",
        cost_estimate=cost(17),
    )(block_order, lengths, group, queries, kv)


def backward_kernel(plan, lengths, q_ref, heads_ref, da_in, wo_ref, kv_ref, lse_ref, part_ref, dq_ref, dkv_out, early_ref, keys, values, keys_t, d_keys, d_values, acc, da_ref, dkv_ref, sems):
    step = pl.program_id(0)
    load = pltpu.make_async_copy(da_in, da_ref, sems.at[0])
    store = pltpu.make_async_copy(dkv_ref, dkv_out, sems.at[1])

    @pl.when(step == 0)
    def _():
        load.start()
        natural_order(plan, kv_ref, keys, values, (keys, keys_t))
        d_keys[...] = jnp.zeros_like(d_keys)
        d_values[...] = jnp.zeros_like(d_values)
        load.wait()

    first, second = plan[2 * step], plan[2 * step + 1]
    q = stacked(q_ref, first, second)
    d_rows = matmul(
        jnp.concatenate(
            [da_ref[pl.ds(pl.multiple_of(at * BLK, BLK), BLK), :] for at in (first, second)], axis=0
        ),
        wo_ref[...],
    )
    d_out = jnp.concatenate(
        [
            d_rows[begin : begin + BLK, head : head + HEAD_WIDTH]
            for begin in (0, BLK)
            for head in (0, HEAD_WIDTH)
        ],
        axis=0,
    ).astype(BF)
    q_t = q.astype(F32).T.astype(BF)
    d_out_wide = d_out.astype(F32).T
    d_out_t = d_out_wide.astype(BF)
    q_pos, q_start = strips_of(plan, lengths, step)
    lse = lse_ref[0]
    dots = jnp.sum(d_out_wide * stacked(heads_ref, first, second).astype(F32).T, axis=0, keepdims=True)
    acc[...] = jnp.zeros_like(acc)

    def chunk(masked, index, carried):
        at = pl.multiple_of(index * CHUNK, CHUNK)
        here = pl.ds(at, CHUNK)
        scores = matmul(keys[here, :], q_t)
        if masked:
            scores = kept(scores, at, q_pos, q_start)
        probs = jnp.exp2(scores * TWO_SCALE - lse)
        d_probs = matmul(values[here, :], d_out_t)
        d_scores = (probs * (d_probs - dots)).astype(BF)
        d_values[here, :] += matmul(probs.astype(BF), d_out)
        d_keys[here, :] += matmul(d_scores, q)
        acc[...] += matmul(keys_t[:, here], d_scores)
        return carried

    three_loops(step, plan, chunk, 0)
    unstacked(dq_ref, first, second, (acc[...] * SCORE_SCALE).T)

    @pl.when(step == pl.num_programs(0) - 1)
    def _():
        def one(block, carried):
            dealt = plan[PLAN_INVERSE + block]
            group, inside = dealt // 16, dealt % 16
            half, rest = inside // 8, inside % 8
            at = pl.ds(pl.multiple_of(block * BLK, BLK), BLK)
            to = pl.ds(pl.multiple_of(rest * BLK, BLK), BLK)
            dkv_ref[half, group, 0, to, :] = (d_keys[at, :] * SCORE_SCALE).astype(BF)
            dkv_ref[half, group, 1, to, :] = d_values[at, :].astype(BF)
            return carried

        lax.fori_loop(0, kv_ref.shape[0] // BLK, one, 0, unroll=4)
        store.start()
        owners = early_ref.shape[0]
        depth = da_ref.shape[1] // owners
        span = 256
        for at in range(da_ref.shape[1] // span):
            value = transposed_times(da_ref[:, at * span : (at + 1) * span], heads_ref[...])
            some = slice(at * span // depth, (at + 1) * span // depth)
            for head in range(2):
                early_ref[some, head * depth : (head + 1) * depth, :] = (
                    value[:, head * HEAD_WIDTH : (head + 1) * HEAD_WIDTH]
                    .astype(BF)
                    .reshape(span // depth, depth, HEAD_WIDTH)
                )
        early_ref[:, 2 * depth :, :] = part_ref[...]
        store.wait()


def attend_back(plan, lengths, queries, heads, d_attn, wo_t, kv, lse, part):
    rows = queries.shape[0]
    total = kv.shape[0]
    steps = rows // (2 * BLK)
    everything = pl.BlockSpec(queries.shape, lambda i, *_: (0, 0))
    strip = pl.BlockSpec((1, 1, 4 * BLK), lambda i, *_: (i, 0, 0))
    sds = jax.ShapeDtypeStruct
    owners = part.shape[0]
    early_shape = (owners, part.shape[1] + 2 * d_attn.shape[1] // owners, HEAD_WIDTH)
    dkv_shape = (2, total // rows, 2, rows // 2, HEAD_WIDTH)
    return pl.pallas_call(
        backward_kernel,
        out_shape=(sds(queries.shape, F32), sds(dkv_shape, BF), sds(early_shape, BF)),
        grid_spec=pltpu.PrefetchScalarGridSpec(
            num_scalar_prefetch=2,
            grid=(steps,),
            in_specs=[
                everything,
                everything,
                ANY,
                pl.BlockSpec((wo_t.shape[0], queries.shape[1]), lambda i, *_: (0, 0)),
                pl.BlockSpec(kv.shape, lambda i, *_: (0, 0)),
                strip,
                pl.BlockSpec(part.shape, lambda i, *_: (0, 0, 0)),
            ],
            out_specs=[
                everything,
                ANY,
                pl.BlockSpec(early_shape, lambda i, *_: (0, 0, 0)),
            ],
            scratch_shapes=[
                pltpu.VMEM((total, HEAD_WIDTH), BF),
                pltpu.VMEM((total, HEAD_WIDTH), BF),
                pltpu.VMEM((HEAD_WIDTH, total), BF),
                pltpu.VMEM((total, HEAD_WIDTH), F32),
                pltpu.VMEM((total, HEAD_WIDTH), F32),
                pltpu.VMEM((HEAD_WIDTH, 4 * BLK), F32),
                pltpu.VMEM(d_attn.shape, BF),
                pltpu.VMEM(dkv_shape, BF),
                DMA((2,)),
            ],
        ),
        compiler_params=pltpu.CompilerParams(vmem_limit_bytes=ROOM),
        name="attend_back",
        cost_estimate=cost(24),
    )(plan, lengths, queries, heads, d_attn, wo_t, kv, lse, part)


def expert_kernel(side, x_ref, cot_ref, gate_ref, g_own, u_own, d_own, g_other, u_other, u_rest, d_other, y_ref, dx_ref, a_ref, dg_ref, du_ref, dy_ref, gate_w, up_w, down_w, gate_f, up_f, down_f, sems):
    half = gate_f.shape[1]
    own_copies, other_copies = [], []
    for at, (own, others, whole, stage) in enumerate(
        (
            (g_own, (g_other,), gate_w, gate_f),
            (u_own, (u_other, u_rest), up_w, up_f),
            (d_own, (d_other,), down_w, down_f),
        )
    ):
        own_copies.append(pltpu.make_async_copy(own.at[side[0]], stage, sems.at[at, 0]))
        begin = 0
        other_copies.append([])
        for which, part in enumerate(others):
            count = part.shape[0]
            if at < 2:
                target = whole.at[pl.ds(begin, count), pl.ds(half, half)]
            else:
                target = whole.at[pl.ds(half, half)]
            other_copies[at].append(pltpu.make_async_copy(part, target, sems.at[at, 1 + which]))
            begin += count

    @pl.when(pl.program_id(0) == 0)
    def _():
        for which in range(3):
            own_copies[which].start()
            for copy in other_copies[which]:
                copy.start()

    def ready(which, fill):
        @pl.when(pl.program_id(0) == 0)
        def _():
            own_copies[which].wait()
            fill()
            for copy in other_copies[which]:
                copy.wait()

    def fill_gate():
        gate_w[:, :half] = gate_f[...].astype(BF)

    def fill_up():
        up_w[:, :half] = up_f[...].astype(BF)

    def fill_down():
        down_w[:half, :] = down_f[...].astype(BF)

    x = x_ref[...]
    ready(0, fill_gate)
    gate_pre = matmul(x, gate_w[...])
    ready(1, fill_up)
    up_pre = matmul(x, up_w[...])
    ready(2, fill_down)
    sigma = 1.0 / (1.0 + jnp.exp(-gate_pre))
    silu = gate_pre * sigma
    activated = (silu * up_pre).astype(BF)
    a_ref[...] = activated
    gates = gate_ref[:, 0:1].astype(F32) + gate_ref[:, 64:65].astype(F32)
    cot = cot_ref[...].astype(F32)
    out = matmul(activated, down_w[...])
    y_ref[...] = (out * gates).astype(BF)
    dots = jnp.sum(out * cot, axis=1, keepdims=True)
    high = dots.astype(BF).astype(F32)
    lane = lax.broadcasted_iota(jnp.int32, (dots.shape[0], 128), 1)
    dx_ref[:, y_ref.shape[1] :] = jnp.where(lane < 64, high, dots - high).astype(BF)
    d_pairs = (cot * gates).astype(BF)
    dy_ref[...] = d_pairs
    d_act = times_transposed(d_pairs, down_w[...])
    d_gate = (d_act * up_pre * sigma * (1.0 + gate_pre * (1.0 - sigma))).astype(BF)
    d_up = (d_act * silu).astype(BF)
    dg_ref[...] = d_gate
    du_ref[...] = d_up
    dx_ref[:, : y_ref.shape[1]] = (times_transposed(d_gate, gate_w[...]) + times_transposed(d_up, up_w[...])).astype(BF)


def run_expert(side, rows_in, cot, gates, own, other):
    count, width = rows_in.shape
    half = own[0].shape[2]
    tile = 256
    sds = jax.ShapeDtypeStruct

    def by_rows(columns):
        return pl.BlockSpec((tile, columns), lambda i, side: (i, 0))

    return pl.pallas_call(
        expert_kernel,
        out_shape=(
            sds((count, width), BF),
            sds((count, width + 128), BF),
            sds((count, 2 * half), BF),
            sds((count, 2 * half), BF),
            sds((count, 2 * half), BF),
            sds((count, width), BF),
        ),
        grid_spec=pltpu.PrefetchScalarGridSpec(
            num_scalar_prefetch=1,
            grid=(count // tile,),
            in_specs=[by_rows(width), by_rows(width), by_rows(128)] + [ANY] * 7,
            out_specs=[
                by_rows(width),
                by_rows(width + 128),
                by_rows(2 * half),
                by_rows(2 * half),
                by_rows(2 * half),
                by_rows(width),
            ],
            scratch_shapes=[
                pltpu.VMEM((width, 2 * half), BF),
                pltpu.VMEM((width, 2 * half), BF),
                pltpu.VMEM((2 * half, width), BF),
                pltpu.VMEM((width, half), F32),
                pltpu.VMEM((width, half), F32),
                pltpu.VMEM((half, width), F32),
                DMA((3, 3)),
            ],
        ),
        compiler_params=pltpu.CompilerParams(vmem_limit_bytes=ROOM),
        name="run_expert",
        cost_estimate=cost(25),
    )(side, rows_in, cot, gates, *own, *other)


def gate_grads_kernel(side, x_ref, dg_ref, gate_ref, gate_out):
    half = gate_ref.shape[-1]
    value = matmul(x_ref[...].T, dg_ref[...])
    gate_ref[0] = value[:, :half]
    gate_out[...] = value[:, half:].astype(BF)


def gate_grads(side, rows_in, d_gate):
    count, width = rows_in.shape
    whole = d_gate.shape[1]
    half = whole // 2
    tile = 1024
    sds = jax.ShapeDtypeStruct
    return pl.pallas_call(
        gate_grads_kernel,
        out_shape=(sds((2, width, half), F32), sds((width, half), BF)),
        grid_spec=pltpu.PrefetchScalarGridSpec(
            num_scalar_prefetch=1,
            grid=(width // tile,),
            in_specs=[
                pl.BlockSpec((count, tile), lambda i, side: (0, i)),
                pl.BlockSpec((count, whole), lambda i, side: (0, 0)),
            ],
            out_specs=[
                pl.BlockSpec((1, tile, half), lambda i, side: (side[0], i, 0)),
                pl.BlockSpec((tile, half), lambda i, side: (i, 0)),
            ],
        ),
        compiler_params=pltpu.CompilerParams(vmem_limit_bytes=ROOM),
        name="gate_grads",
        cost_estimate=cost(5),
    )(side, rows_in, d_gate)


def expert_grads_kernel(side, x_ref, dy_ref, a_ref, du_ref, up_ref, down_ref, up_out, up_rest, down_out, down_rest, a_t):
    half = up_ref.shape[-1]
    step = pl.program_id(0)
    turn_at = up_out.shape[0]

    @pl.when(step == 0)
    def _():
        a_t[...] = a_ref[...].T

    value = matmul(x_ref[...].T, du_ref[...])
    up_ref[0] = value[:, :half]
    low = value[:, half:].astype(BF)

    @pl.when(step < UP_GRAD_CUT[0] // turn_at)
    def _():
        up_out[...] = low

    @pl.when(step >= UP_GRAD_CUT[0] // turn_at)
    def _():
        up_rest[...] = low

    value = matmul(a_t[...], dy_ref[...])
    down_ref[0] = value[:half]
    cut = half + down_out.shape[0]
    down_out[...] = value[half:cut].astype(BF)
    down_rest[...] = value[cut:].astype(BF)


def expert_grads(side, rows_in, d_pairs, activated, d_up):
    count, width = rows_in.shape
    whole = activated.shape[1]
    half = whole // 2
    tile = 256
    first = UP_GRAD_CUT[0] // tile
    sds = jax.ShapeDtypeStruct
    columns = pl.BlockSpec((count, tile), lambda i, side: (0, i))
    full = pl.BlockSpec((count, whole), lambda i, side: (0, 0))
    return pl.pallas_call(
        expert_grads_kernel,
        out_shape=(
            sds((2, width, half), F32),
            sds((2, half, width), F32),
            sds((UP_GRAD_CUT[0], half), BF),
            sds((UP_GRAD_CUT[1], half), BF),
            sds((DOWN_GRAD_CUT[0], width), BF),
            sds((DOWN_GRAD_CUT[1], width), BF),
        ),
        grid_spec=pltpu.PrefetchScalarGridSpec(
            num_scalar_prefetch=1,
            grid=(width // tile,),
            in_specs=[columns, columns, full, full],
            out_specs=[
                pl.BlockSpec((1, tile, half), lambda i, side: (side[0], i, 0)),
                pl.BlockSpec((1, half, tile), lambda i, side: (side[0], 0, i)),
                pl.BlockSpec((tile, half), lambda i, side: (jnp.minimum(i, first - 1), 0)),
                pl.BlockSpec((tile, half), lambda i, side: (jnp.maximum(i - first, 0), 0)),
                pl.BlockSpec((DOWN_GRAD_CUT[0], tile), lambda i, side: (0, i)),
                pl.BlockSpec((DOWN_GRAD_CUT[1], tile), lambda i, side: (0, i)),
            ],
            scratch_shapes=[pltpu.VMEM((whole, count), BF)],
        ),
        compiler_params=pltpu.CompilerParams(vmem_limit_bytes=ROOM),
        name="expert_grads",
        cost_estimate=cost(10),
    )(side, rows_in, d_pairs, activated, d_up)


def route_rows(where, routes_ref, cot_ref, pick_ref, turned_ref, of_ref, hits_ref, rows_ref):
    slots, rows = pick_ref.shape[0], routes_ref.shape[2]
    experts = of_ref.shape[1]
    slot = lax.broadcasted_iota(jnp.int32, (slots, experts), 0)
    lane = lax.broadcasted_iota(jnp.int32, (slots, experts), 1)
    chip = lax.div(slot, 2 * CAP)
    side = lax.rem(where[1] + lax.div(chip, 4) + where[2], 2)
    of_expert = (lane == 4 * chip + 2 * where[0] + side).astype(F32).astype(BF)
    of_ref[...] = of_expert
    expert = lax.broadcasted_iota(jnp.int32, (experts, rows), 0)
    before = (
        lax.broadcasted_iota(jnp.int32, (rows, rows), 0) < lax.broadcasted_iota(jnp.int32, (rows, rows), 1)
    ).astype(F32).astype(BF)
    hits, ranks = [], []
    for half in range(2):
        hit = jnp.zeros((experts, rows), F32)
        for choice in range(TOPK):
            hit = hit + (routes_ref[half, choice : choice + 1, :] == expert).astype(F32)
        rank = matmul(hit.astype(BF), before) + half * CAP
        hits.append(hit)
        ranks.append(jnp.where(hit > 0.5, rank, -1.0))
    hits_ref[...] = jnp.concatenate(hits, axis=1).T
    mine = matmul(of_expert, jnp.concatenate(ranks, axis=1).astype(BF))
    wanted = lax.rem(lax.broadcasted_iota(jnp.int32, mine.shape, 0), 2 * CAP).astype(F32)
    pick = (mine == wanted).astype(F32)
    pick_low = pick.astype(BF)
    pick_ref[...] = pick_low
    turned_ref[...] = pick.T.astype(BF)
    rows_ref[...] = matmul(pick_low, cot_ref[...]).astype(BF)


def middle_rows(t_ref, attn_ref, gain_ref, wr_ref, hits_ref, pick_ref, of_ref, res_ref, h_ref, inv_ref, gates_ref, rows_ref, tile_ref):
    residual = t_ref[...].astype(F32) + attn_ref[...]
    res_ref[...] = residual
    inverse = lax.rsqrt(jnp.mean(residual * residual, axis=1, keepdims=True) + EPSILON)
    inv_ref[...] = jnp.broadcast_to(inverse, inv_ref.shape)
    hidden = (residual * inverse * gain_ref[...]).astype(BF)
    h_ref[...] = hidden
    pick = pick_ref[...]
    rows_ref[...] = matmul(pick, hidden).astype(BF)
    hit = hits_ref[...] > 0.5
    logits = jnp.where(hit, matmul(hidden, wr_ref[...]), MASKED)
    exps = jnp.where(hit, jnp.exp(logits - jnp.max(logits, axis=1, keepdims=True)), 0.0)
    gates = exps / jnp.sum(exps, axis=1, keepdims=True)
    gates_ref[...] = gates
    high = gates.astype(BF)
    chosen = [
        jnp.sum(matmul(pick, part) * of_ref[...].astype(F32), axis=1, keepdims=True)
        for part in (high, (gates - high.astype(F32)).astype(BF))
    ]
    lane = lax.broadcasted_iota(jnp.int32, tile_ref.shape, 1)
    tile_ref[...] = jnp.where(lane < 64, chosen[0], chosen[1]).astype(BF)


def turn_rows(moe_ref, dg_ref, gates_ref, h_ref, res_ref, inv_ref, wr_ref, gain_ref, cot_ref, d_ref, low_ref, part_ref):
    gates = gates_ref[...]
    d_gates = dg_ref[...]
    d_logits = (gates * (d_gates - jnp.sum(gates * d_gates, axis=1, keepdims=True))).astype(BF)
    hidden = h_ref[...]
    gradient = moe_ref[...] + times_transposed(d_logits, wr_ref[...])
    residual, inverse = res_ref[...], inv_ref[:, 0:1]
    weighted = gradient * gain_ref[...]
    mean_term = jnp.mean(weighted * residual, axis=1, keepdims=True)
    back = inverse * weighted - residual * (inverse * inverse * inverse) * mean_term
    value = cot_ref[...].astype(F32) + back
    d_ref[...] = value
    low_ref[...] = value.astype(BF)
    owners, rows, _ = part_ref.shape
    depth = hidden.shape[1] // owners
    grad_router = transposed_times(hidden, d_logits).astype(BF)
    part_ref[:, :depth, :] = grad_router.reshape(owners, depth, grad_router.shape[1])
    terms = jnp.sum(gradient * residual * inverse, axis=0, keepdims=True)
    wide = jnp.broadcast_to(terms, (8, terms.shape[1]))
    by_owner = jnp.concatenate(
        [wide[:1, owner * depth : (owner + 1) * depth] for owner in range(owners)], axis=0
    )
    by_owner = jnp.concatenate([by_owner, jnp.zeros((owners, 128 - depth), F32)], axis=1)
    part_ref[:, depth:, :] = jnp.broadcast_to(
        by_owner[:, None, :], (owners, rows - depth, 128)
    ).astype(BF)


def last_kernel(side, g_in, u_in, u_rest, d_in, d_rest, *refs):
    (t_ref, dh_ref, dr_ref, moe_ref, res_ref, ga_ref, late_ref, early_ref, wq_ref, wk_ref, wv_ref), refs = refs[3:14], refs[14:]
    g_out, u_out, d_out, out_ref, gt_ref, gq_ref, gk_ref, gv_ref, go_ref, gr_ref, gains_ref, ffn_ref = refs[:12]
    keys, router, gains, ffn, dots = refs[12:]
    step = pl.program_id(0)
    g_out[0] = g_in[...].astype(F32)
    u_out[0] = jnp.where(step < UP_GRAD_CUT[0] // u_in.shape[0], u_in[...], u_rest[...]).astype(F32)
    d_out[0] = jnp.where(step < DOWN_GRAD_CUT[0] // d_in.shape[0], d_in[...], d_rest[...]).astype(F32)
    rows = t_ref[...].astype(F32)
    out_ref[...] = res_ref[...] + moe_ref[...]
    inverse = lax.rsqrt(jnp.mean(rows * rows, axis=1, keepdims=True) + EPSILON)
    weighted = dh_ref[...] * ga_ref[...]
    mean_term = jnp.mean(weighted * rows, axis=1, keepdims=True)
    gt_ref[...] = dr_ref[...] + (
        inverse * weighted - rows * (inverse * inverse * inverse) * mean_term
    )

    @pl.when(step == 0)
    def _():
        for ref in (keys, router, gains, ffn, dots):
            ref[...] = jnp.zeros_like(ref)

    depth = gq_ref.shape[0]
    late, early = late_ref[0].astype(F32), early_ref[0].astype(F32)
    query = jnp.concatenate([late[:depth], late[depth : 2 * depth]], axis=1)
    gq_ref[...] = query
    low_q = wq_ref[...].astype(BF).astype(F32)
    dots[...] += jnp.sum(low_q * query, axis=1, keepdims=True)
    keys[lax.div(step, 2)] += late[2 * depth : 3 * depth]
    gains[...] += late[3 * depth :]
    router[...] += early[2 * depth : 3 * depth]
    ffn[...] += early[3 * depth : 3 * depth + 8]
    go_ref[...] = jnp.concatenate([early[:depth], early[depth : 2 * depth]], axis=1)

    @pl.when(step == pl.num_programs(0) - 1)
    def _():
        gk_ref[...] = jnp.concatenate([keys[0], keys[2]], axis=1)
        gv_ref[...] = jnp.concatenate([keys[1], keys[3]], axis=1)
        gr_ref[...] = router[...]
        ffn_ref[...] = ffn[...]
        total = (
            dots[:, 0:1]
            + jnp.sum(wk_ref[...].astype(BF).astype(F32) * gk_ref[...], axis=1, keepdims=True)
            + jnp.sum(wv_ref[...].astype(BF).astype(F32) * gv_ref[...], axis=1, keepdims=True)
        )
        blank = jnp.zeros((128 - depth, 128), F32)
        square = jnp.concatenate([jnp.broadcast_to(total, (depth, 128)), blank], axis=0).T
        row = lax.broadcasted_iota(jnp.int32, gains_ref.shape, 0)
        gains_ref[...] = jnp.where(row < 2, gains[:8], square[:8])


def last(side, arrived, placed, tokens, d_hidden, d_residual, moe, residual, gain, late, early, weights):
    width, half = arrived[0].shape
    rows = tokens.shape[0]
    steps = 8
    tile, strip = width // steps, rows // steps
    depth = weights[0].shape[0]
    sds = jax.ShapeDtypeStruct

    def whole(*shape):
        return pl.BlockSpec(shape, lambda i, side: (0,) * len(shape))

    first = UP_GRAD_CUT[0] // tile
    rows_out = pl.BlockSpec((1, tile, half), lambda i, side: (1 - side[0], i, 0))
    short = half // steps
    short_first = DOWN_GRAD_CUT[0] // short
    short_out = pl.BlockSpec((1, short, width), lambda i, side: (1 - side[0], i, 0))
    strips = pl.BlockSpec((strip, width), lambda i, side: (i, 0))
    mine = pl.BlockSpec((strip, width), lambda i, side: (side[1] * steps + i, 0))
    place = pl.BlockSpec((1,) + late.shape[1:], lambda i, side: (i, 0, 0))
    query = pl.BlockSpec((depth, weights[0].shape[1] // steps), lambda i, side: (0, i))
    narrow = (depth, weights[1].shape[1])
    return pl.pallas_call(
        last_kernel,
        out_shape=[sds(value.shape, F32) for value in placed]
        + [
            sds((rows, width), F32),
            sds((rows, width), F32),
            sds(weights[0].shape, F32),
            sds(narrow, F32),
            sds(narrow, F32),
            sds(weights[0].shape, F32),
            sds((depth, 128), F32),
            sds((8, 128), F32),
            sds((8, 128), F32),
        ],
        grid_spec=pltpu.PrefetchScalarGridSpec(
            num_scalar_prefetch=1,
            grid=(steps,),
            in_specs=[
                pl.BlockSpec((tile, half), lambda i, side: (i, 0)),
                pl.BlockSpec((tile, half), lambda i, side: (jnp.minimum(i, first - 1), 0)),
                pl.BlockSpec((tile, half), lambda i, side: (jnp.maximum(i - first, 0), 0)),
                pl.BlockSpec((short, width), lambda i, side: (jnp.minimum(i, short_first - 1), 0)),
                pl.BlockSpec((short, width), lambda i, side: (jnp.maximum(i - short_first, 0), 0)),
            ]
            + [ANY] * 3
            + [
                strips,
                strips,
                strips,
                strips,
                mine,
                whole(1, width),
                place,
                place,
                query,
                whole(*narrow),
                whole(*narrow),
            ],
            out_specs=[
                rows_out,
                rows_out,
                short_out,
                strips,
                strips,
                query,
                whole(*narrow),
                whole(*narrow),
                query,
                whole(depth, 128),
                whole(8, 128),
                whole(8, 128),
            ],
            scratch_shapes=[
                pltpu.VMEM((4, depth, 128), F32),
                pltpu.VMEM((depth, 128), F32),
                pltpu.VMEM((16, 128), F32),
                pltpu.VMEM((8, 128), F32),
                pltpu.VMEM((depth, 128), F32),
            ],
        ),
        input_output_aliases={6: 0, 7: 1, 8: 2},
        compiler_params=pltpu.CompilerParams(vmem_limit_bytes=ROOM),
        name="last",
        cost_estimate=cost(9),
    )(side, *arrived, *placed, tokens, d_hidden, d_residual, moe, residual, gain, late, early, *weights)


def project_kernel(block_order, lengths, group, t_ref, w_ref, side_ref, flag_ref, freq_ref, ga_ref, gq_ref, gk_ref, h_ref, q_ref, kv_ref, qp_ref, kp_ref, cos_ref, sin_ref):
    tile = t_ref.shape[0]
    row = lax.broadcasted_iota(jnp.int32, (tile, HEAD_WIDTH), 0)
    lane = lax.broadcasted_iota(jnp.int32, (tile, HEAD_WIDTH), 1)
    first_block = group[0] * 16 + pl.program_id(0) * (tile // BLK)
    position = row * 0
    for at in range(tile // BLK):
        inside = block_order[first_block + at] * BLK + row - at * BLK
        position = jnp.where(row >= at * BLK, inside, position)
    angles = (position - start_of(lengths, position)).astype(F32) * freq_ref[...]
    cosine = jnp.cos(angles)
    sine_tab = jnp.where(lane < HEAD_WIDTH // 2, -1.0, 1.0) * jnp.sin(angles)
    cos_ref[...] = cosine
    sin_ref[...] = sine_tab
    rows = t_ref[...].astype(F32)
    inverse = lax.rsqrt(jnp.mean(rows * rows, axis=1, keepdims=True) + EPSILON)
    hidden = (rows * inverse * ga_ref[...]).astype(BF)
    h_ref[...] = hidden
    qkv = matmul(hidden, w_ref[...])
    own = qkv[:, 2 * HEAD_WIDTH :]
    other = matmul(hidden, side_ref[...])
    first = flag_ref[0:1, :] > 0.5

    def turned(value, gain):
        root = lax.rsqrt(jnp.mean(value * value, axis=1, keepdims=True) + EPSILON)
        value = value * root * gain
        return (value * cosine + pltpu.roll(value, HEAD_WIDTH // 2, 1) * sine_tab).astype(BF)

    for head in range(2):
        span = slice(head * HEAD_WIDTH, (head + 1) * HEAD_WIDTH)
        q_ref[:, span] = turned(qkv[:, span], gq_ref[...])
    qp_ref[...] = qkv[:, : 2 * HEAD_WIDTH]
    keys = jnp.where(first, own, other)
    kp_ref[...] = keys
    kv_ref[:, :HEAD_WIDTH] = turned(keys, gk_ref[...])
    kv_ref[:, HEAD_WIDTH:] = jnp.where(first, other, own).astype(BF)


def project(block_order, lengths, group, tokens, weights, side, first, frequency, gain, gain_query, gain_key):
    rows, width = tokens.shape
    tile = 256
    sds = jax.ShapeDtypeStruct

    def by_rows(columns):
        return pl.BlockSpec((tile, columns), lambda i, *_: (i, 0))

    def whole(value):
        return pl.BlockSpec(value.shape, lambda i, *_: (0, 0))

    return pl.pallas_call(
        project_kernel,
        out_shape=(
            sds((rows, width), BF),
            sds((rows, 256), BF),
            sds((rows, 256), BF),
            sds((rows, 256), F32),
            sds((rows, 128), F32),
            sds((rows, 128), F32),
            sds((rows, 128), F32),
        ),
        grid_spec=pltpu.PrefetchScalarGridSpec(
            num_scalar_prefetch=3,
            grid=(rows // tile,),
            in_specs=[
                by_rows(width),
                whole(weights),
                whole(side),
                whole(first),
                whole(frequency),
                whole(gain),
                whole(gain_query),
                whole(gain_key),
            ],
            out_specs=[
                by_rows(width),
                by_rows(256),
                by_rows(256),
                by_rows(256),
                by_rows(128),
                by_rows(128),
                by_rows(128),
            ],
        ),
        compiler_params=pltpu.CompilerParams(vmem_limit_bytes=ROOM),
        name="project",
        cost_estimate=cost(8),
    )(block_order, lengths, group, tokens, weights, side, first, frequency, gain, gain_query, gain_key)


def project_back_kernel(dq_ref, ds_ref, qp_ref, kp_ref, cos_ref, sin_ref, h_ref, w_ref, side_ref, gq_ref, gk_ref, flag_ref, part_ref, late_ref, side_w, total, gains):
    step = pl.program_id(0)
    cosine, sine_tab = cos_ref[...], sin_ref[...]
    key, first, own = flag_ref[0:1, :], flag_ref[1:2, :], flag_ref[2:3, :]
    heads = 2 * HEAD_WIDTH

    @pl.when(step == 0)
    def _():
        gains[...] = jnp.zeros_like(gains)
        total[...] = jnp.zeros_like(total)
        side_w[...] = jnp.where(
            own > 0.5, w_ref[:, heads:].astype(F32), side_ref[...].astype(F32)
        ).astype(BF)

    def back(gradient, value, gain):
        gradient = gradient * cosine - pltpu.roll(gradient, HEAD_WIDTH // 2, 1) * sine_tab
        root = lax.rsqrt(jnp.mean(value * value, axis=1, keepdims=True) + EPSILON)
        weighted = gradient * gain
        mean_term = jnp.mean(weighted * value, axis=1, keepdims=True)
        terms = jnp.sum(gradient * value * root, axis=0, keepdims=True)
        return root * weighted - value * (root * root * root) * mean_term, terms

    columns = []
    for head in range(2):
        span = slice(head * HEAD_WIDTH, (head + 1) * HEAD_WIDTH)
        value, terms = back(dq_ref[:, span], qp_ref[:, span], gq_ref[...])
        columns.append(value.astype(BF))
        gains[0:1, :] += terms
    d_side = ds_ref[...]
    value, terms = back(d_side, kp_ref[...], gk_ref[...])
    mine = jnp.where(first == (step // 2).astype(F32), 1.0, 0.0)
    columns.append((jnp.where(key > 0.5, value, d_side) * mine).astype(BF))
    gains[1:2, :] += terms * key * mine
    d_all = jnp.concatenate(columns, axis=1)
    part_ref[...] = (
        times_transposed(d_all[:, :heads], w_ref[:, :heads])
        + times_transposed(d_all[:, heads:], side_w[...])
    ).astype(BF)
    total[...] += transposed_times(h_ref[...], d_all)

    @pl.when(step == pl.num_programs(0) - 1)
    def _():
        pieces, depth = late_ref.shape[0], h_ref.shape[1] // late_ref.shape[0]
        for at in range(3):
            value = total[:, at * HEAD_WIDTH : (at + 1) * HEAD_WIDTH].astype(BF)
            late_ref[:, at * depth : (at + 1) * depth, :] = value.reshape(pieces, depth, HEAD_WIDTH)
        late_ref[:, 3 * depth :, :] = jnp.broadcast_to(
            gains[...].astype(BF)[None], (pieces,) + gains.shape
        )


def project_back(d_queries, d_side, q_pre, k_pre, cosine, sine_tab, hidden, weights, side, gain_query, gain_key, flags):
    rows = d_queries.shape[0]
    width = hidden.shape[1]
    tile = 256
    tiles = rows // tile
    owners = 64
    sds = jax.ShapeDtypeStruct
    late = (owners, 3 * width // owners + 16, 128)

    def by_rows(columns):
        return pl.BlockSpec((tile, columns), lambda i: (i, 0))

    def whole(value):
        return pl.BlockSpec(value.shape, lambda i: (0, 0))

    half_rows = pl.BlockSpec((tile, 128), lambda i: (i % (tiles // 2), 0))
    return pl.pallas_call(
        project_back_kernel,
        grid=(tiles,),
        out_shape=(sds((rows, width), BF), sds(late, BF)),
        in_specs=[
            by_rows(256),
            half_rows,
            by_rows(256),
            by_rows(128),
            by_rows(128),
            by_rows(128),
            by_rows(width),
            whole(weights),
            whole(side),
            whole(gain_query),
            whole(gain_key),
            whole(flags),
        ],
        out_specs=[by_rows(width), pl.BlockSpec(late, lambda i: (0, 0, 0))],
        scratch_shapes=[
            pltpu.VMEM((width, 128), BF),
            pltpu.VMEM((width, 384), F32),
            pltpu.VMEM((16, 128), F32),
        ],
        compiler_params=pltpu.CompilerParams(vmem_limit_bytes=ROOM),
        name="project_back",
        cost_estimate=cost(12),
    )(
        d_queries, d_side, q_pre, k_pre, cosine, sine_tab, hidden, weights, side, gain_query, gain_key, flags
    )


def after(value, earlier):
    return lax.optimization_barrier((value, earlier))


def lanes_to(row, lanes=128):
    return jnp.pad(row, ((0, 0),) * (row.ndim - 1) + ((0, lanes - row.shape[-1]),))


def local(
    tokens,
    cotangent,
    seq_lengths,
    block_order,
    routes,
    w_query,
    key_weight,
    value_weight,
    w_out,
    gain_attn,
    gain_query,
    gain_key,
    gain_ffn,
    w_router,
    w_gate,
    w_up,
    w_down,
):
    rows = tokens.shape[0]
    width = tokens.shape[1]
    experts = w_router.shape[1]
    block_count = block_order.shape[0]
    wsh = lax.axis_index("wsh")
    me = lax.axis_index("ctx")
    core = lax.rem(me, 2)
    place = lax.rem(me, 8)
    group = lax.div(me, 8)
    row_tokens = 8 * rows

    def swap(value):
        return lax.ppermute(value, "wsh", [(0, 1), (1, 0)])

    depth = w_query.shape[0]
    (
        w_all,
        row_rows,
        small_all,
        chip_routes,
        chip_cot,
        other_gate,
        up_first,
        other_up,
        other_down,
        w_side,
        late_pack,
    ) = gather_first(
        (w_query, key_weight, value_weight),
        w_out.T,
        w_router,
        (gain_attn[None, :], gain_ffn[None, :]),
        tokens,
        routes.T,
        cotangent,
        (w_gate, w_up, w_down),
    )
    w_main = w_all.reshape(width, 384)
    w_side = w_side.reshape(width, 128)
    is_key = lax.rem(lax.div(me, 2), 2) == 0

    def flag(value):
        return jnp.broadcast_to(value.astype(F32).reshape(1, 1), (8, 128))

    g_attn = to_low(small_all[:, 0, :depth].reshape(width)).astype(F32)
    g_ffn = to_low(small_all[:, 1, :depth].reshape(width)).astype(F32)
    g_query = rounded(gain_query)
    g_key = rounded(gain_key)

    late_all = lax.all_to_all(late_pack, "ctx", split_axis=0, concat_axis=0, tiled=True).reshape(width, 384)

    chips = experts // 4
    slots = 2 * CAP

    half_dim = HEAD_WIDTH // 2
    frequency = jnp.power(ROPE_BASE, -2.0 * jnp.arange(half_dim, dtype=jnp.float32) / HEAD_WIDTH)
    frequency = jnp.concatenate([frequency, frequency])[None, :]
    row_rows = row_rows.reshape(row_tokens, width)
    hidden_one, queries, kv, q_pre, k_pre, cosine, sine_tab = project(
        block_order,
        seq_lengths,
        group.reshape(1),
        row_rows,
        w_main,
        w_side,
        flag(core == 0),
        frequency,
        g_attn[None, :],
        g_query[None, :],
        g_key[None, :],
    )
    kv_all, pick_low, pick_turned, of_expert, hits, cot_rows = gather_keys(
        kv, chip_routes, chip_cot.reshape(2 * rows, width), experts, 1
    )
    kv_all = kv_all.reshape(block_count * BLK, 256)
    late_all, kv_all = after(late_all, kv_all)
    (cot_rows, other_gate), kv_all = after((cot_rows, other_gate), kv_all)
    gate_back = swap(other_gate)
    cot_there = exchange_behind(cot_rows.reshape(chips, slots, width)).reshape(chips * slots, width)
    heads, lse, plan = attend(block_order, seq_lengths, group.reshape(1), queries, kv_all)

    (other_up, other_down), heads = after((other_up, other_down), heads)
    residual, hidden_two, inverse_two, gates, out_rows, gate_tile, up_first = reduce_row(
        (heads, late_all),
        2,
        closing=(row_rows, g_ffn[None, :], hits, pick_low, of_expert),
        swapped_whole=up_first,
    )

    out_rows = out_rows.reshape(chips, slots, width)
    gate_tile = gate_tile.reshape(chips, slots, 128)
    (gate_back, cot_there, other_down, other_up), gate_tile = after(
        (gate_back, cot_there, other_down, other_up), gate_tile
    )
    down_back = swap(other_down)
    up_back = (up_first, swap(other_up))
    arrived, gate_there = exchange([out_rows, gate_tile], 3)
    arrived = arrived.reshape(chips * slots, width)
    side = wsh.reshape(1)
    gate_there = gate_there.reshape(chips * slots, 128)
    y_rows, d_rows, activated, d_gate_pre, d_up_pre, d_pairs = run_expert(
        side, arrived, cot_there, gate_there, (w_gate, w_up, w_down), (gate_back, *up_back, down_back)
    )
    own_gate, other_gate = gate_grads(side, arrived, d_gate_pre)
    activated, other_gate = after(activated, other_gate)
    own_up, own_down, up_first, other_up, other_down, down_rest = expert_grads(
        side, arrived, d_pairs, activated, d_up_pre
    )
    own_grads = (own_gate, own_up, own_down)
    gate_grad_back = swap(other_gate)
    d_back = exchange_behind(d_rows.reshape(chips, slots, width + 128))
    d_back = d_back.reshape(chips * slots, width + 128)
    (gate_grad_back, other_up, other_down, down_rest), d_back = after(
        (gate_grad_back, other_up, other_down, down_rest), d_back
    )
    d_residual, d_residual_low, part = reduce_chip(
        pick_turned,
        d_back,
        of_expert,
        gates,
        hidden_two,
        residual,
        inverse_two,
        late_all,
        g_ffn[None, :],
        cotangent,
        5,
    )

    d_attn, up_first = gather_row(d_residual_low, up_first, 7)
    d_attn = d_attn.reshape(row_tokens, width)
    (y_rows, other_up, other_down), d_attn_late = after((y_rows, other_up, other_down), d_attn)
    y_back = exchange_behind(y_rows.reshape(chips, slots, width))
    up_grad_back = swap(other_up)
    down_grad_back = swap(other_down)
    d_queries, d_kv, early = attend_back(
        plan, seq_lengths, queries, heads, d_attn_late, late_all, kv_all, lse, part
    )
    (y_back, up_grad_back, down_grad_back), d_kv = after((y_back, up_grad_back, down_grad_back), d_kv)
    d_side, early, down_rest = reduce_keys(d_kv, early, down_rest, 8)
    swapped_grads = (gate_grad_back, up_first, up_grad_back, down_grad_back, down_rest)
    flags = jnp.concatenate(
        [
            flag(is_key)[:1],
            flag(core)[:1],
            flag(is_key == (core == 0))[:1],
            jnp.zeros((5, 128), F32),
        ],
        axis=0,
    )
    d_hidden_parts, late = project_back(
        d_queries,
        d_side,
        q_pre,
        k_pre,
        cosine,
        sine_tab,
        hidden_one,
        w_main,
        w_side,
        g_query[None, :],
        g_key[None, :],
        flags,
    )
    d_hidden_parts = d_hidden_parts.reshape(8, rows, width)
    d_hidden_one, moe_total, late = reduce_row(
        d_hidden_parts,
        9,
        extra=(pick_turned, y_back.reshape(chips * slots, width)),
        owned=(late,),
    )
    (
        grad_gate,
        grad_up,
        grad_down,
        out_stream,
        grad_tokens,
        grad_query,
        grad_key,
        grad_value,
        grad_out_t,
        grad_router,
        gain_parts,
        grad_gain_ffn,
    ) = last(
        jnp.stack([wsh, core]),
        swapped_grads,
        own_grads,
        tokens,
        d_hidden_one,
        d_residual,
        moe_total,
        residual,
        g_attn[None, :],
        late,
        early,
        (w_query, key_weight, value_weight),
    )
    gain_parts = lax.psum(gain_parts, "wsh")
    return (
        out_stream,
        grad_tokens,
        grad_query,
        grad_key,
        grad_value,
        grad_out_t.T,
        gain_parts[2, :depth] / rounded(gain_attn),
        gain_parts[0],
        gain_parts[1],
        grad_gain_ffn[0, :depth],
        grad_router,
        grad_gate,
        grad_up,
        grad_down,
    )


def solution(mesh):
    in_specs = (
        P("ctx", None),
        P("ctx", None),
        P(),
        P(),
        P("ctx", None),
        P("ctx", "wsh"),
        P("ctx", "wsh"),
        P("ctx", "wsh"),
        P("wsh", "ctx"),
        P("ctx"),
        P(),
        P(),
        P("ctx"),
        P("ctx", None),
        P("ctx", None, "wsh"),
        P("ctx", None, "wsh"),
        P("ctx", "wsh", None),
    )
    out_specs = (
        P("ctx", None),
        P("ctx", None),
        P("ctx", "wsh"),
        P("ctx", "wsh"),
        P("ctx", "wsh"),
        P("wsh", "ctx"),
        P("ctx"),
        P(),
        P(),
        P("ctx"),
        P("ctx", None),
        P("ctx", None, "wsh"),
        P("ctx", None, "wsh"),
        P("ctx", "wsh", None),
    )
    return jax.shard_map(local, mesh=mesh, in_specs=in_specs, out_specs=out_specs, check_vma=False)
```
